32 devices in a mesh: exp: 8 (over y, x, core), dp: 4 (over z).
Axes of the slice: x: 2, y: 2, z: 4, core: 2. Of those that a mesh axis runs over, the one named last changes fastest.
Arguments:
- tokens: bfloat16 [49152, 768], P(('exp', 'dp')), may hold values from -6 to 6
- w_query: bfloat16 [768, 768], replicated, may hold values from -0.21875 to 0.21875
- w_key: bfloat16 [768, 768], replicated, may hold values from -0.21875 to 0.21875
- w_value: bfloat16 [768, 768], replicated, may hold values from -0.21875 to 0.21875
- w_output: bfloat16 [768, 768], replicated, may hold values from -1.75 to 1.75
- norm_attn: float32 [768], replicated, may hold values from 0.5 to 1.5
- norm_ffn: float32 [768], replicated, may hold values from 0.5 to 1.5
- relative_bias_table: float32 [32, 12], replicated, may hold values from -4 to 4
- w_router: float32 [768, 32], replicated, may hold values from -0.2 to 0.2
- w_in: bfloat16 [32, 768, 3072], P('exp'), may hold values from -0.21875 to 0.21875
- w_out: bfloat16 [32, 3072, 768], P('exp'), may hold values from -5 to 5
- expert_index: int32 [49152, 1], P(('exp', 'dp')), may hold values from 0 to 31
- priority: int32 [32, 1536], P(('exp', 'dp')), may hold values from 0 to 1535, each once within a row
- cotangent: bfloat16 [49152, 768], P(('exp', 'dp')), may hold values from -6 to 6
Outputs:
- mixed_out: bfloat16 [49152, 768], P(('exp', 'dp'))
- grad_tokens: float32 [49152, 768], P(('exp', 'dp'))
- grad_query: float32 [768, 768], replicated
- grad_key: float32 [768, 768], replicated
- grad_value: float32 [768, 768], replicated
- grad_output: float32 [768, 768], replicated
- grad_norm_attn: float32 [768], replicated
- grad_norm_ffn: float32 [768], replicated
- grad_table: float32 [32, 12], replicated
- grad_router: float32 [768, 32], replicated
- grad_in: float32 [32, 768, 3072], P('exp', None, 'dp')
- grad_out: float32 [32, 3072, 768], P('exp', 'dp')
The draws below stay inside these ranges and needn't reach their ends.
Inputs may be any that keep to these rules, and one draw needn't show every extreme that they name: `expert_index`: the expert of each token; skewed over the experts. `priority`: each row orders the 1536 tokens of one device block, each value once; a lower value takes a slot first.
All inputs are finite; a program needn't handle non-finite values.
Results may differ from the reference program's by a relative error of at most 0.015.
Values may be sent and summed in bfloat16 or wider, within the bound.
A program may use at most 320 MiB of HBM per device.

```python
import jax
import jax.numpy as jnp
from jax import lax

D = 768
HEADS = 12
HEAD_DIM = 64
FF = 3072
BUCKETS = 32
SEQ = 512
TOK_DEV = 1536
TOKENS = 49152
EXPERTS = 32
CAP = 60
DEVICES = 32


def steps_of(own_key, shape, cuts, smallest, top_value):
    level, own = 1.0, jax.random.fold_in(own_key, 6)
    for dim, shards_of in cuts:
        draws = jnp.exp(jax.random.uniform(jax.random.fold_in(own, dim), (shards_of,), jnp.float32, smallest / len(cuts), top_value / len(cuts)))
        level = level * jnp.repeat(draws, shape[dim] // shards_of).reshape([-1 if axis == dim else 1 for axis in range(len(shape))])
    return level


def picks_of(key, rows, amount, top, lift):
    sequence = jax.random.permutation(jax.random.fold_in(key, 1), amount)
    favour = sequence
    for power in range(3):
        favour = favour * favour // amount
    favour = favour * lift // amount
    chance = jax.random.randint(jax.random.fold_in(key, 2), (rows, amount), 0, 4096) + favour
    fixed_rows = jax.random.permutation(jax.random.fold_in(key, 3), rows)[jnp.arange(amount) % rows]
    chance = jnp.where(jnp.arange(rows)[:, None] == fixed_rows[None, :], 1 << 14, chance)
    score = chance * amount + jnp.arange(amount)
    return lax.top_k(score.astype(jnp.int32), top)[1].astype(jnp.int32)


def centred(stream_key, extent, scale, most, shards=(), kind=jnp.bfloat16):
    level = steps_of(stream_key, extent, shards, -0.22, 0.18) if shards else 1.0
    array = jax.random.normal(stream_key, extent, jnp.float32) * scale * level
    return jnp.minimum(jnp.maximum(array, -most), most).astype(kind)


def setup_inputs(seed: int = 0) -> dict:
    keys = jax.random.split(jax.random.key(seed), 15)
    tokens = centred(keys[0], (TOKENS, D), 1.0, 6.0, ((0, 32),))
    w_query = centred(keys[1], (D, D), D ** -0.5, 0.21875)
    w_key = centred(keys[2], (D, D), D ** -0.5, 0.21875)
    w_value = centred(keys[3], (D, D), D ** -0.5, 0.21875)
    w_output = centred(keys[4], (D, D), (D // 64) ** -0.5, 1.75)
    norm_attn = jnp.clip(1.0 + 0.1 * jax.random.normal(keys[5], (D,), jnp.float32), 0.5, 1.5)
    norm_ffn = jnp.clip(1.0 + 0.1 * jax.random.normal(keys[6], (D,), jnp.float32), 0.5, 1.5)
    relative_bias_table = centred(keys[7], (BUCKETS, HEADS), 1.0, 4.0, (), jnp.float32)
    w_router = centred(keys[8], (D, EXPERTS), 0.027, 0.2, (), jnp.float32)
    w_in = centred(keys[9], (EXPERTS, D, FF), D ** -0.5, 0.21875, ((0, 8),))
    w_out = centred(keys[10], (EXPERTS, FF, D), (EXPERTS / 36), 5.0, ((0, 8),))
    expert_index = picks_of(keys[11], TOKENS, EXPERTS, 1, 512)
    priority = jax.vmap(lambda own: jax.random.permutation(own, TOK_DEV))(jax.random.split(keys[12], DEVICES)).reshape((DEVICES, TOK_DEV)).astype(jnp.int32)
    cotangent = centred(keys[13], (TOKENS, D), 1.0, 6.0, ((0, 32),))
    return dict(tokens=tokens, w_query=w_query, w_key=w_key, w_value=w_value, w_output=w_output, norm_attn=norm_attn, norm_ffn=norm_ffn, relative_bias_table=relative_bias_table, w_router=w_router, w_in=w_in, w_out=w_out, expert_index=expert_index, priority=priority, cotangent=cotangent)


@jax.custom_vjp
def low(v):
    return lax.optimization_barrier(v.astype(jnp.bfloat16)).astype(jnp.float32)

@jax.custom_vjp
def low_back(v):
    return v

def low_keep(v):
    return (low(v), None)

def low_pass(kept, grad):
    return (grad,)

def back_keep(v):
    return (v, None)

def back_low(kept, grad):
    return (low(grad),)
low.defvjp(low_keep, low_pass)
low_back.defvjp(back_keep, back_low)
LIMITS = (12, 16, 23, 32, 46, 64, 91)
EPSILON = 1e-06
FULL_PRECISION = lax.Precision.HIGHEST

def bucket_table(length):
    places = jnp.arange(length, dtype=jnp.int32)
    offset = places[None, :] - places[:, None]
    distance = jnp.abs(offset)
    farther = jnp.zeros_like(distance)
    for limit in LIMITS:
        farther = farther + (distance >= limit).astype(jnp.int32)
    nearer = jnp.where(distance < 8, distance, 8 + farther)
    return (nearer + jnp.where(offset > 0, 16, 0)).astype(jnp.int32)

def rms_norm(values, gain):
    return values * lax.rsqrt(lax.optimization_barrier(jnp.mean(values * values, axis=-1, keepdims=True)) + EPSILON) * gain

def smooth(values):
    return jax.nn.gelu(values, approximate=True)

def expert_slots(expert_index, priority):
    chosen_rows = expert_index[:, 0].reshape(DEVICES, TOK_DEV)

    def ranks(pair):
        chosen, order = pair
        ahead = (chosen[:, None] == chosen[None, :]) & (order[None, :] < order[:, None])
        return lax.optimization_barrier(jnp.sum(ahead.astype(jnp.int32), axis=1)).astype(jnp.int32)
    rank = lax.map(ranks, (chosen_rows, priority))
    device = jnp.arange(DEVICES, dtype=jnp.int32)[:, None]
    slot = (device * EXPERTS + chosen_rows) * CAP + rank
    return jnp.where(rank < CAP, slot, DEVICES * EXPERTS * CAP).reshape(-1).astype(jnp.int32)

def reference(tokens, w_query, w_key, w_value, w_output, norm_attn, norm_ffn, relative_bias_table, w_router, w_in, w_out, expert_index, priority, cotangent):
    slots = expert_slots(expert_index, priority)
    buckets = bucket_table(SEQ)
    scale = HEAD_DIM ** (-0.5)

    def forward(inputs, wq, wk, wv, wo, gain_attn, gain_ffn, table, router, first_all, second_all):

        def attention_forward(rows):
            normed = low(rms_norm(rows, gain_attn))

            def project(weight):
                return low(low_back(jnp.dot(normed, weight, precision=FULL_PRECISION))).reshape(SEQ, HEADS, HEAD_DIM)
            query, key_rows, value_rows = (project(wq), project(wk), project(wv))
            position_bias = jnp.transpose(table[buckets], (2, 0, 1))
            scores = low_back(jnp.einsum('qhd,khd->hqk', query, key_rows, precision=FULL_PRECISION) * scale) + position_bias
            weights = low(jax.nn.softmax(scores, axis=-1))
            context = low(low_back(jnp.einsum('hqk,khd->qhd', weights, value_rows, precision=FULL_PRECISION))).reshape(SEQ, D)
            return rows + low_back(jnp.dot(context, wo, precision=FULL_PRECISION))
        mixed = lax.map(jax.checkpoint(attention_forward), inputs.reshape(TOKENS // SEQ, SEQ, D)).reshape(TOKENS, D)
        normed_ffn = rms_norm(mixed, gain_ffn)
        logits = jnp.dot(normed_ffn, router, precision=FULL_PRECISION)
        probs = jax.nn.softmax(logits, axis=-1)
        gate = jnp.take_along_axis(probs, expert_index, axis=1)
        sent = low(low_back(normed_ffn))
        buffer = jnp.zeros((DEVICES * EXPERTS * CAP, D), jnp.float32).at[slots].set(sent, mode='drop')
        buffer = jnp.transpose(buffer.reshape(DEVICES, EXPERTS, CAP, D), (1, 0, 2, 3)).reshape(EXPERTS, DEVICES * CAP, D)

        def expert(triple):
            rows, first, second = triple
            inner = low_back(jnp.dot(rows, first, precision=FULL_PRECISION))
            return low(low_back(jnp.dot(low(smooth(inner)), second, precision=FULL_PRECISION)))
        produced = lax.map(jax.checkpoint(expert), (buffer, first_all, second_all))
        produced = jnp.transpose(produced.reshape(EXPERTS, DEVICES, CAP, D), (1, 0, 2, 3)).reshape(DEVICES * EXPERTS * CAP, D)
        returned = jnp.take(produced, slots, axis=0, mode='fill', fill_value=0.0)
        return mixed + gate * returned
    floats = (tokens.astype(jnp.float32), w_query.astype(jnp.float32), w_key.astype(jnp.float32), w_value.astype(jnp.float32), w_output.astype(jnp.float32), norm_attn.astype(jnp.float32), norm_ffn.astype(jnp.float32), relative_bias_table.astype(jnp.float32), w_router.astype(jnp.float32), w_in.astype(jnp.float32), w_out.astype(jnp.float32))
    result, pull = jax.vjp(forward, *floats)
    grads = pull(cotangent.astype(jnp.float32))
    return (result.astype(jnp.bfloat16), grads[0], grads[1], grads[2], grads[3], grads[4], grads[5], grads[6], grads[7], grads[8], grads[9], grads[10])
```

```python
import functools

import jax
import jax.numpy as jnp
from jax import lax
from jax.experimental import pallas as pl
from jax.experimental.pallas import tpu as pltpu
from jax.sharding import PartitionSpec as P

HEADS = 12
HEAD_DIM = 64
SEQ = 512
LIMITS = (12, 16, 23, 32, 46, 64, 91)
EPSILON = 1e-06
FULL_PRECISION = lax.Precision.HIGHEST
BF = jnp.bfloat16
F32 = jnp.float32
PAIR = 2 * HEAD_DIM
TILE = 128
CHUNK = 256
GELU_A = 0.7978845608028654
GELU_B = 0.044715 * GELU_A
VMEM_MIB = 50


def params(**more):
    return pltpu.CompilerParams(vmem_limit_bytes=VMEM_MIB * 2**20, **more)


def mm(left, right):
    return jnp.dot(left, right, preferred_element_type=F32)


def mm_nt(left, right):
    return lax.dot_general(left, right, (((1,), (1,)), ((), ())), preferred_element_type=F32)


def bucket_of(offset):
    distance = jnp.abs(offset)
    farther = jnp.zeros_like(distance)
    for limit in LIMITS:
        farther = farther + (distance >= limit).astype(jnp.int32)
    return jnp.where(distance < 8, distance, 8 + farther) + jnp.where(offset > 0, 16, 0)


def diagonal_onehot(count):
    places = jnp.arange(TILE, dtype=jnp.int32)
    offsets = jnp.concatenate([-places, TILE - places, 0 * places - SEQ, 0 * places + SEQ])
    return (bucket_of(offsets)[:, None] == jnp.arange(count, dtype=jnp.int32)[None, :]).astype(F32)


def dispatch_kernel(slot_ref, rows_ref, out_ref):
    block, tokens = out_ref.shape[0], rows_ref.shape[0]
    ids = lax.broadcasted_iota(jnp.int32, (block, tokens), 0) + pl.program_id(0) * block
    picks = jnp.where(slot_ref[...] == ids, 1.0, 0.0).astype(BF)
    out_ref[...] = mm(picks, rows_ref[...]).astype(BF)


def dispatch_gate_kernel(experts, capacity, padded, slot_ref, gate_ref, rows_ref, out_ref):
    block, tokens = out_ref.shape[0], rows_ref.shape[0]
    width = out_ref.shape[1]
    step = pl.program_id(0)
    ids = lax.broadcasted_iota(jnp.int32, (block, tokens), 0) + step * block
    picks = jnp.where(slot_ref[...] == ids, 1.0, 0.0).astype(BF)
    out = mm(picks, rows_ref[...])
    gates = jnp.broadcast_to(gate_ref[...].astype(BF), (8, tokens))
    lanes = pl.num_programs(0) * padded
    in_slots = mm_nt(gates, picks)
    in_slots = jnp.concatenate([in_slots, jnp.zeros((8, lanes - block), F32)], axis=1)
    lane = lax.broadcasted_iota(jnp.int32, (8, lanes), 1)
    row = lax.broadcasted_iota(jnp.int32, (block, 1), 0)
    left = out[:, :lanes]
    for expert in range(experts):
        shift = lax.rem(step * padded - expert * padded + lanes, lanes)
        moved = pltpu.roll(in_slots, shift, 1)
        mine = (lane >= step * padded) & (lane < step * padded + capacity)
        moved = jnp.where(mine, moved, 0.0)[:1]
        left = jnp.where(row == expert * padded + capacity, moved, left)
    out_ref[:, :lanes] = left.astype(BF)
    out_ref[:, lanes:] = out[:, lanes:].astype(BF)


def dispatch(slot_row, rows, blocks, block, gate=None):
    tokens, width = rows.shape
    grid_spec = dict(
        grid=(blocks,),
        out_specs=pl.BlockSpec((block, width), lambda k: (k, 0)),
        out_shape=jax.ShapeDtypeStruct((blocks * block, width), BF),
    )
    line = pl.BlockSpec((1, tokens), lambda k: (0, 0))
    full = pl.BlockSpec((tokens, width), lambda k: (0, 0))
    cost = pl.CostEstimate(
        flops=2 * blocks * block * tokens * width,
        bytes_accessed=2 * width * (tokens + blocks * block),
        transcendentals=0,
    )
    if gate is None:
        return pl.pallas_call(
            dispatch_kernel, in_specs=[line, full], compiler_params=params(), cost_estimate=cost, **grid_spec
        )(slot_row, rows)
    values, experts, capacity, padded = gate
    return pl.pallas_call(
        functools.partial(dispatch_gate_kernel, experts, capacity, padded),
        in_specs=[line, line, full],
        compiler_params=params(),
        cost_estimate=cost,
        **grid_spec,
    )(slot_row, values, rows)


def qkv_kernel(x_ref, gain_ref, wq_ref, wk_ref, wv_ref, q_ref, k_ref, v_ref):
    rows = x_ref[...].astype(F32)
    inv = lax.rsqrt(jnp.mean(rows * rows, axis=-1, keepdims=True) + EPSILON)
    normed = (rows * inv * gain_ref[...]).astype(BF)
    q_ref[...] = (mm(normed, wq_ref[...]).astype(BF).astype(F32) * HEAD_DIM**-0.5).astype(BF)
    k_ref[...] = mm(normed, wk_ref[...]).astype(BF)
    v_ref[...] = mm(normed, wv_ref[...]).astype(BF)


def qkv(x, gain, wq, wk, wv):
    tokens, width = x.shape
    rows = pl.BlockSpec((SEQ, width), lambda t: (t, 0))
    square = pl.BlockSpec((width, width), lambda t: (0, 0))
    one = pl.BlockSpec((1, width), lambda t: (0, 0))
    return pl.pallas_call(
        qkv_kernel,
        grid=(tokens // SEQ,),
        in_specs=[rows, one, square, square, square],
        out_specs=[rows] * 3,
        out_shape=[jax.ShapeDtypeStruct((tokens, width), BF)] * 3,
        compiler_params=params(),
        cost_estimate=pl.CostEstimate(
            flops=6 * tokens * width * width, bytes_accessed=8 * tokens * width, transcendentals=0
        ),
    )(x, gain, wq, wk, wv)


def fill_bias(lines_ref, bias_ref):
    upper_right = lax.broadcasted_iota(jnp.int32, (TILE, TILE), 0) <= lax.broadcasted_iota(
        jnp.int32, (TILE, TILE), 1
    )
    tiles = SEQ // TILE
    for head in range(2):

        def sheared(line):
            whole = jnp.broadcast_to(lines_ref[head, line : line + 1, :], (TILE, TILE))
            return pltpu.roll(whole, 0, 1, stride=1, stride_axis=0)

        negative, positive = sheared(0), sheared(1)
        far_negative = jnp.broadcast_to(lines_ref[head, 2:3, :], (TILE, TILE))
        far_positive = jnp.broadcast_to(lines_ref[head, 3:4, :], (TILE, TILE))
        same = jnp.where(upper_right, negative, positive)
        above = jnp.where(upper_right, positive, far_positive)
        below = jnp.where(upper_right, far_negative, negative)
        for key in range(tiles):
            for query in range(tiles):
                gap = key - query
                tile = (
                    same
                    if gap == 0
                    else above
                    if gap == 1
                    else below
                    if gap == -1
                    else far_positive
                    if gap > 0
                    else far_negative
                )
                bias_ref[head, pl.ds(key * TILE, TILE), pl.ds(query * TILE, TILE)] = tile


def head_lanes(head):
    lane = lax.broadcasted_iota(jnp.int32, (1, PAIR), 1)
    return (lane >= head * HEAD_DIM) & (lane < (head + 1) * HEAD_DIM)


def only(head, array):
    return jnp.where(head_lanes(head), array, jnp.zeros_like(array))


def attention_kernel(lines_ref, q_ref, k_ref, v_ref, o_ref, lse_ref, bias_ref):
    @pl.when(pl.program_id(1) == 0)
    def _():
        fill_bias(lines_ref, bias_ref)

    keys = k_ref[...]
    values_t = v_ref[...].T
    masked = [only(head, keys) for head in range(2)]
    row = lax.broadcasted_iota(jnp.int32, (PAIR, 1), 0)
    for part in range(SEQ // CHUNK):
        places = pl.ds(part * CHUNK, CHUNK)
        queries = q_ref[places, :]
        out = None
        for head in range(2):
            scores = mm_nt(masked[head], queries) + bias_ref[head, :, places]
            highest = jnp.max(scores, axis=0, keepdims=True)
            weights = jnp.exp(scores - highest)
            total = jnp.sum(weights, axis=0, keepdims=True)
            lse_ref[0, 0, head : head + 1, places] = highest + jnp.log(total)
            mixed = mm(values_t, weights.astype(BF)) * (1.0 / total)
            out = mixed if out is None else jnp.where(row < HEAD_DIM, out, mixed)
        o_ref[places, :] = out.T.astype(BF)


def attention(lines, q, k, v):
    tokens, width = q.shape
    seqs, pairs = tokens // SEQ, width // PAIR
    block = pl.BlockSpec((SEQ, PAIR), lambda h, s: (s, h))
    return pl.pallas_call(
        attention_kernel,
        grid=(pairs, seqs),
        in_specs=[pl.BlockSpec((2, 8, TILE), lambda h, s: (h, 0, 0)), block, block, block],
        out_specs=[block, pl.BlockSpec((1, 1, 2, SEQ), lambda h, s: (h, s, 0, 0))],
        out_shape=[
            jax.ShapeDtypeStruct((tokens, width), BF),
            jax.ShapeDtypeStruct((pairs, seqs, 2, SEQ), F32),
        ],
        scratch_shapes=[pltpu.VMEM((2, SEQ, SEQ), F32)],
        compiler_params=params(),
        cost_estimate=pl.CostEstimate(
            flops=16 * pairs * seqs * SEQ * SEQ * PAIR,
            bytes_accessed=8 * tokens * width,
            transcendentals=2 * pairs * seqs * SEQ * SEQ,
        ),
    )(lines, q, k, v)


def attention_back_kernel(
    lines_ref, q_ref, k_ref, v_ref, do_ref, lse_ref, dq_ref, dk_ref, dv_ref, sums_ref, bias_ref, diag_ref
):
    seq = pl.program_id(1)

    @pl.when(seq == 0)
    def _():
        fill_bias(lines_ref, bias_ref)
        diag_ref[...] = jnp.zeros_like(diag_ref)

    keys, values = k_ref[...], v_ref[...]
    keys_t = keys.T
    masked_k = [only(head, keys) for head in range(2)]
    masked_v = [only(head, values) for head in range(2)]
    row = lax.broadcasted_iota(jnp.int32, (PAIR, 1), 0)
    grads_k, grads_v = [None, None], [None, None]
    tiles = SEQ // TILE
    for part in range(SEQ // CHUNK):
        places = pl.ds(part * CHUNK, CHUNK)
        queries, upstream = q_ref[places, :], do_ref[places, :]
        grad_q = None
        for head in range(2):
            scores = mm_nt(masked_k[head], queries) + bias_ref[head, :, places]
            weights = jnp.exp(scores - lse_ref[0, 0, head : head + 1, places])
            products = weights * mm_nt(masked_v[head], upstream)
            scores_grad = products - weights * jnp.sum(products, axis=0, keepdims=True)
            low = scores_grad.astype(BF)
            value_term = mm(weights.astype(BF), upstream)
            key_term = mm(low, queries)
            grads_v[head] = value_term if part == 0 else grads_v[head] + value_term
            grads_k[head] = key_term if part == 0 else grads_k[head] + key_term
            query_term = mm(keys_t, low)
            grad_q = query_term if head == 0 else jnp.where(row < HEAD_DIM, grad_q, query_term)
            groups = {}
            for query in range(CHUNK // TILE):
                for key in range(tiles):
                    gap = key - (query + part * (CHUNK // TILE))
                    kind = 0 if gap == 0 else 1 if gap == 1 else 2 if gap == -1 else 3 if gap > 0 else 4
                    tile = scores_grad[
                        key * TILE : (key + 1) * TILE, query * TILE : (query + 1) * TILE
                    ]
                    groups[kind] = tile if kind not in groups else groups[kind] + tile
            for kind, tile in groups.items():
                diag_ref[head, kind] += tile
        dq_ref[places, :] = (grad_q * HEAD_DIM**-0.5).T.astype(BF)
    first = head_lanes(0)
    dk_ref[...] = jnp.where(first, grads_k[0], grads_k[1]).astype(BF)
    dv_ref[...] = jnp.where(first, grads_v[0], grads_v[1]).astype(BF)

    @pl.when(seq == pl.num_programs(1) - 1)
    def _():
        upper_right = lax.broadcasted_iota(jnp.int32, (TILE, TILE), 0) <= lax.broadcasted_iota(
            jnp.int32, (TILE, TILE), 1
        )
        sums_ref[...] = jnp.zeros_like(sums_ref)
        for head in range(2):
            same, above, below = diag_ref[head, 0], diag_ref[head, 1], diag_ref[head, 2]

            def gathered(array):
                row_id = lax.broadcasted_iota(jnp.int32, (TILE, 1), 0)
                bit = 1
                while bit < TILE:
                    turned = pltpu.roll(array, TILE - bit, 1)
                    array = jnp.where((row_id & bit) != 0, turned, array)
                    bit *= 2
                return jnp.sum(array, axis=0, keepdims=True)

            zero = jnp.zeros_like(same)
            sums_ref[head, 0:1, :] = gathered(jnp.where(upper_right, same, below))
            sums_ref[head, 1:2, :] = gathered(jnp.where(upper_right, above, same))
            sums_ref[head, 2:3, :] = jnp.sum(
                diag_ref[head, 4] + jnp.where(upper_right, below, zero), axis=0, keepdims=True
            )
            sums_ref[head, 3:4, :] = jnp.sum(
                diag_ref[head, 3] + jnp.where(upper_right, zero, above), axis=0, keepdims=True
            )


def attention_back(lines, q, k, v, do, lse):
    tokens, width = q.shape
    seqs, pairs = tokens // SEQ, width // PAIR
    block = pl.BlockSpec((SEQ, PAIR), lambda h, s: (s, h))
    lines_spec = pl.BlockSpec((2, 8, TILE), lambda h, s: (h, 0, 0))
    return pl.pallas_call(
        attention_back_kernel,
        grid=(pairs, seqs),
        in_specs=[lines_spec, block, block, block, block]
        + [pl.BlockSpec((1, 1, 2, SEQ), lambda h, s: (h, s, 0, 0))],
        out_specs=[block, block, block, lines_spec],
        out_shape=[jax.ShapeDtypeStruct((tokens, width), BF)] * 3
        + [jax.ShapeDtypeStruct((2 * pairs, 8, TILE), F32)],
        scratch_shapes=[pltpu.VMEM((2, SEQ, SEQ), F32), pltpu.VMEM((2, 5, TILE, TILE), F32)],
        compiler_params=params(),
        cost_estimate=pl.CostEstimate(
            flops=40 * pairs * seqs * SEQ * SEQ * PAIR,
            bytes_accessed=14 * tokens * width,
            transcendentals=2 * pairs * seqs * SEQ * SEQ,
        ),
    )(lines, q, k, v, do, lse)


def router_kernel(
    o_ref, x_ref, wo_ref, gain_ref, wr_ref, expert_ref, h_ref, u_ref, probs_ref, gate_ref, line_ref
):
    mixed = x_ref[...].astype(F32) + mm(o_ref[...], wo_ref[...])
    h_ref[...] = mixed
    inv = lax.rsqrt(jnp.mean(mixed * mixed, axis=-1, keepdims=True) + EPSILON)
    normed = mixed * inv * gain_ref[...]
    u_ref[...] = normed.astype(BF)
    logits = jnp.dot(normed, wr_ref[...], precision=FULL_PRECISION, preferred_element_type=F32)
    spread = jnp.exp(logits - jnp.max(logits, axis=-1, keepdims=True))
    probs = spread / jnp.sum(spread, axis=-1, keepdims=True)
    probs_ref[...] = probs
    picked = expert_ref[...] == lax.broadcasted_iota(jnp.int32, probs.shape, 1)
    gate = jnp.sum(jnp.where(picked, probs, 0.0), axis=-1, keepdims=True)
    gate_ref[...] = gate
    size = gate.shape[0]
    diagonal = lax.broadcasted_iota(jnp.int32, (size, size), 0) == lax.broadcasted_iota(
        jnp.int32, (size, size), 1
    )
    line_ref[...] = jnp.sum(jnp.where(diagonal, gate, 0.0), axis=0, keepdims=True)


def router(o, x, wo, gain, wr, expert):
    tokens, width = x.shape
    experts = wr.shape[1]
    size = 256

    def rows(columns):
        return pl.BlockSpec((size, columns), lambda t: (t, 0))

    def whole(*shape):
        return pl.BlockSpec(shape, lambda t: (0, 0))

    return pl.pallas_call(
        router_kernel,
        grid=(tokens // size,),
        in_specs=[rows(width), rows(width), whole(width, width), whole(1, width)]
        + [whole(width, experts), rows(1)],
        out_specs=[rows(width), rows(width), rows(experts), rows(1)]
        + [pl.BlockSpec((1, size), lambda t: (0, t))],
        out_shape=[
            jax.ShapeDtypeStruct((tokens, width), F32),
            jax.ShapeDtypeStruct((tokens, width), BF),
            jax.ShapeDtypeStruct((tokens, experts), F32),
            jax.ShapeDtypeStruct((tokens, 1), F32),
            jax.ShapeDtypeStruct((1, tokens), F32),
        ],
        compiler_params=params(),
        cost_estimate=pl.CostEstimate(
            flops=2 * tokens * width * width, bytes_accessed=10 * tokens * width, transcendentals=0
        ),
    )(o, x, wo, gain, wr, expert)


def gelu_and_slope(z):
    square = z * z
    half = 0.5 + 0.5 * jnp.tanh(z * (GELU_A + GELU_B * square))
    value = z * half
    slope = half + 2.0 * value * (1.0 - half) * (GELU_A + 3.0 * GELU_B * square)
    return value, slope


def expert_kernel(parts, u_ref, c_ref, first_ref, second_ref, e_ref, d_ref, e_sum, d_sum):
    step = pl.program_id(1)
    rows, upstream = u_ref[0], c_ref[0]
    columns = first_ref.shape[2] // parts

    @pl.when(step == 0)
    def _():
        e_sum[...] = jnp.zeros_like(e_sum)
        d_sum[...] = jnp.zeros_like(d_sum)

    for part in range(parts):
        places = slice(part * columns, (part + 1) * columns)
        first, second = first_ref[0, :, places], second_ref[0, places, :]
        value, slope = gelu_and_slope(mm(rows, first))
        inner = (mm_nt(upstream, second) * slope).astype(BF)
        e_sum[...] += mm(value.astype(BF), second)
        d_sum[...] += mm_nt(inner, first)

    @pl.when(step == pl.num_programs(1) - 1)
    def _():
        e_ref[0] = e_sum[...].astype(BF)
        d_ref[0] = d_sum[...].astype(BF)


def expert_pass(u, c, w_in, w_out):
    experts, rows, width = u.shape
    hidden = w_in.shape[2]
    size = 768
    block = pl.BlockSpec((1, rows, width), lambda e, f: (e, 0, 0))
    return pl.pallas_call(
        functools.partial(expert_kernel, 3),
        grid=(experts, hidden // size),
        in_specs=[
            block,
            block,
            pl.BlockSpec((1, width, size), lambda e, f: (e, 0, f)),
            pl.BlockSpec((1, size, width), lambda e, f: (e, f, 0)),
        ],
        out_specs=[block, block],
        out_shape=[jax.ShapeDtypeStruct(u.shape, BF)] * 2,
        scratch_shapes=[pltpu.VMEM((rows, width), F32)] * 2,
        compiler_params=params(),
        cost_estimate=pl.CostEstimate(
            flops=8 * experts * rows * width * hidden,
            bytes_accessed=4 * experts * width * (hidden + 2 * rows),
            transcendentals=experts * rows * hidden,
        ),
    )(u, c, w_in, w_out)


def weights_kernel(parts, sources, capacity, padded, place_ref, *refs):
    u_refs, c_refs = refs[:sources], refs[sources : 2 * sources]
    first_ref, second_ref, own_in, own_out, far_in, far_out, in_sum, out_sum = refs[2 * sources :]
    width, size = first_ref.shape[1:]
    rows = u_refs[0].shape[1]
    columns = size // parts
    first_t = first_ref[0].T
    for source in range(sources):
        inputs, upstream = u_refs[source][0], c_refs[source][0]
        gate = jnp.zeros((1, rows), F32)
        for block in range(rows // padded):
            place = block * padded + capacity
            gate = gate + inputs[place : place + 1, :rows].astype(F32)
        for part in range(parts):
            places = slice(part * columns, (part + 1) * columns)
            value, slope = gelu_and_slope(mm_nt(first_t[places, :], inputs))
            inner = (mm_nt(second_ref[0, places, :], upstream) * (slope * gate)).astype(BF)
            in_term = mm(inner, inputs)
            out_term = mm((value * gate).astype(BF), upstream)
            if source == 0:
                in_sum[places, :] = in_term
                out_sum[places, :] = out_term
            else:
                in_sum[places, :] += in_term
                out_sum[places, :] += out_term
    mine = pl.program_id(1) == place_ref[2]

    @pl.when(mine)
    def _():
        own_in[0] = in_sum[...].T
        own_out[0] = out_sum[...]

    @pl.when(jnp.logical_not(mine))
    def _():
        far_in[0] = in_sum[...].T.astype(BF)
        far_out[0] = out_sum[...].astype(BF)


def weight_grads(place, us, cs, w_in, w_out, size, capacity, padded):
    sources = len(us)
    experts, rows, width = us[0].shape
    local = w_in.shape[0]
    block = pl.BlockSpec((1, rows, width), lambda e, f, p: (e, 0, 0))
    tile = pl.BlockSpec((1, width, size), lambda e, f, p: (e, 0, 0))
    turned = pl.BlockSpec((1, size, width), lambda e, f, p: (e, 0, 0))
    return pl.pallas_call(
        functools.partial(weights_kernel, 3, sources, capacity, padded),
        grid_spec=pltpu.PrefetchScalarGridSpec(
            num_scalar_prefetch=1,
            grid=(experts, 2),
            in_specs=[block] * (2 * sources)
            + [
                pl.BlockSpec((1, width, size), lambda e, f, p: (p[0] + e, 0, p[1] + f)),
                pl.BlockSpec((1, size, width), lambda e, f, p: (p[0] + e, p[1] + f, 0)),
            ],
            out_specs=[
                pl.BlockSpec((1, width, size), lambda e, f, p: (p[0] + e, 0, 0)),
                pl.BlockSpec((1, size, width), lambda e, f, p: (p[0] + e, 0, 0)),
                tile,
                turned,
            ],
            scratch_shapes=[pltpu.VMEM((size, width), F32)] * 2,
        ),
        out_shape=[
            jax.ShapeDtypeStruct((local, width, size), F32),
            jax.ShapeDtypeStruct((local, size, width), F32),
            jax.ShapeDtypeStruct((experts, width, size), BF),
            jax.ShapeDtypeStruct((experts, size, width), BF),
        ],
        compiler_params=params(),
        cost_estimate=pl.CostEstimate(
            flops=16 * sources * experts * rows * width * size,
            bytes_accessed=4 * experts * (sources * rows * width + 6 * size * width),
            transcendentals=2 * sources * experts * rows * size,
        ),
    )(place, *us, *cs, w_in, w_out)


def finish_kernel(place_ref, a_ref, b_ref, x_ref, y_ref, a_out, b_out):
    a_out[...] = x_ref[...].astype(F32)
    b_out[...] = y_ref[...].astype(F32)


def finish(place, own_in, own_out, came_in, came_out):
    experts, width, size = came_in.shape

    def spec(shape, moved):
        return pl.BlockSpec((1,) + shape, lambda e, p: ((p[0] if moved else 0) + e, 0, 0))

    return pl.pallas_call(
        finish_kernel,
        grid_spec=pltpu.PrefetchScalarGridSpec(
            num_scalar_prefetch=1,
            grid=(experts,),
            in_specs=[pl.BlockSpec(memory_space=pl.ANY)] * 2
            + [spec((width, size), False), spec((size, width), False)],
            out_specs=[spec((width, size), True), spec((size, width), True)],
        ),
        out_shape=[
            jax.ShapeDtypeStruct(own_in.shape, F32),
            jax.ShapeDtypeStruct(own_out.shape, F32),
        ],
        input_output_aliases={1: 0, 2: 1},
        compiler_params=params(),
    )(place, own_in, own_out, came_in, came_out)


def combine_kernel(
    slot_ref, expert_ref, gate_ref, probs_ref, h_ref, c_ref, o_ref, e_ref, d_ref, wo_ref, wr_ref, gain_ref,
    mixed_ref, dh_ref, do_ref, wo_sum, wr_sum, gain_sum,
):
    step = pl.program_id(0)
    tokens, slots = slot_ref.shape[0], e_ref.shape[0]
    picks = jnp.where(
        slot_ref[...] == lax.broadcasted_iota(jnp.int32, (tokens, slots), 1), 1.0, 0.0
    ).astype(BF)
    returned, arrived = mm(picks, e_ref[...]), mm(picks, d_ref[...])
    gate, probs, mixed = gate_ref[...], probs_ref[...], h_ref[...]
    upstream = c_ref[...].astype(F32)
    mixed_ref[...] = (mixed + gate * returned).astype(BF)
    gate_grad = jnp.sum(upstream * returned, axis=-1, keepdims=True)
    picked = jnp.where(expert_ref[...] == lax.broadcasted_iota(jnp.int32, probs.shape, 1), 1.0, 0.0)
    logit_grad = gate_grad * gate * (picked - probs)
    inv = lax.rsqrt(jnp.mean(mixed * mixed, axis=-1, keepdims=True) + EPSILON)
    unit = mixed * inv
    gain = gain_ref[...]
    normed_grad = (
        lax.dot_general(
            logit_grad,
            wr_ref[...],
            (((1,), (1,)), ((), ())),
            precision=FULL_PRECISION,
            preferred_element_type=F32,
        )
        + gate * arrived
    )
    unit_grad = normed_grad * gain
    mixed_grad = upstream + inv * (
        unit_grad - unit * jnp.mean(unit_grad * unit, axis=-1, keepdims=True)
    )
    dh_ref[...] = mixed_grad
    low = mixed_grad.astype(BF)
    do_ref[...] = mm_nt(low, wo_ref[...]).astype(BF)

    @pl.when(step == 0)
    def _():
        wo_sum[...] = jnp.zeros_like(wo_sum)
        wr_sum[...] = jnp.zeros_like(wr_sum)
        gain_sum[...] = jnp.zeros_like(gain_sum)

    wo_sum[...] += mm(o_ref[...].T, low)
    wr_sum[...] += jnp.dot(
        (unit * gain).T, logit_grad, precision=FULL_PRECISION, preferred_element_type=F32
    )
    gain_sum[...] += jnp.sum(normed_grad * unit, axis=0, keepdims=True)


def combine(slot, expert, gate, probs, h, c, o, e_out, du, wo, wr, gain):
    tokens, width = h.shape
    slots, experts = e_out.shape[0], wr.shape[1]
    size = 256

    def rows(columns):
        return pl.BlockSpec((size, columns), lambda t: (t, 0))

    def whole(*shape):
        return pl.BlockSpec(shape, lambda t: (0, 0))

    return pl.pallas_call(
        combine_kernel,
        grid=(tokens // size,),
        in_specs=[rows(1), rows(1), rows(1), rows(experts), rows(width), rows(width), rows(width)]
        + [whole(slots, width), whole(slots, width), whole(width, width), whole(width, experts)]
        + [whole(1, width)],
        out_specs=[rows(width), rows(width), rows(width), whole(width, width), whole(width, experts)]
        + [whole(1, width)],
        out_shape=[
            jax.ShapeDtypeStruct((tokens, width), BF),
            jax.ShapeDtypeStruct((tokens, width), F32),
            jax.ShapeDtypeStruct((tokens, width), BF),
            jax.ShapeDtypeStruct((width, width), F32),
            jax.ShapeDtypeStruct((width, experts), F32),
            jax.ShapeDtypeStruct((1, width), F32),
        ],
        compiler_params=params(),
        cost_estimate=pl.CostEstimate(
            flops=4 * tokens * width * (slots + width),
            bytes_accessed=16 * tokens * width + 4 * slots * width,
            transcendentals=0,
        ),
    )(slot, expert, gate, probs, h, c, o, e_out, du, wo, wr, gain)


def last_kernel(
    x_ref, dh_ref, dq_ref, dk_ref, dv_ref, wq_ref, wk_ref, wv_ref, gain_ref,
    grad_ref, q_sum, k_sum, v_sum, gain_sum,
):
    step = pl.program_id(0)

    @pl.when(step == 0)
    def _():
        for total in (q_sum, k_sum, v_sum, gain_sum):
            total[...] = jnp.zeros_like(total)

    rows = x_ref[...].astype(F32)
    inv = lax.rsqrt(jnp.mean(rows * rows, axis=-1, keepdims=True) + EPSILON)
    unit = rows * inv
    gain = gain_ref[...]
    normed_t = (unit * gain).astype(BF).T
    normed_grad = None
    for grad_ref_in, weight_ref, total in (
        (dq_ref, wq_ref, q_sum),
        (dk_ref, wk_ref, k_sum),
        (dv_ref, wv_ref, v_sum),
    ):
        grad = grad_ref_in[...]
        total[...] += mm(normed_t, grad)
        term = mm_nt(grad, weight_ref[...])
        normed_grad = term if normed_grad is None else normed_grad + term
    unit_grad = normed_grad * gain
    grad_ref[...] = dh_ref[...] + inv * (
        unit_grad - unit * jnp.mean(unit_grad * unit, axis=-1, keepdims=True)
    )
    gain_sum[...] += jnp.sum(normed_grad * unit, axis=0, keepdims=True)


def last(x, dh, dq, dk, dv, wq, wk, wv, gain):
    tokens, width = x.shape
    size = 256
    rows = pl.BlockSpec((size, width), lambda t: (t, 0))
    square = pl.BlockSpec((width, width), lambda t: (0, 0))
    one = pl.BlockSpec((1, width), lambda t: (0, 0))
    return pl.pallas_call(
        last_kernel,
        grid=(tokens // size,),
        in_specs=[rows] * 5 + [square] * 3 + [one],
        out_specs=[rows, square, square, square, one],
        out_shape=[jax.ShapeDtypeStruct((tokens, width), F32)]
        + [jax.ShapeDtypeStruct((width, width), F32)] * 3
        + [jax.ShapeDtypeStruct((1, width), F32)],
        compiler_params=params(),
        cost_estimate=pl.CostEstimate(
            flops=12 * tokens * width * width, bytes_accessed=16 * tokens * width, transcendentals=0
        ),
    )(x, dh, dq, dk, dv, wq, wk, wv, gain)


def per_device(
    tokens,
    w_query,
    w_key,
    w_value,
    w_output,
    norm_attn,
    norm_ffn,
    relative_bias_table,
    w_router,
    w_in,
    w_out,
    expert_index,
    priority,
    cotangent,
):
    tok_rows, width = tokens.shape
    local = w_in.shape[0]
    exp_n, dp_n = lax.axis_size("exp"), lax.axis_size("dp")
    exp_me, dp_me = lax.axis_index("exp"), lax.axis_index("dp")
    all_experts = local * exp_n
    capacity = (5 * tok_rows + 4 * all_experts - 1) // (4 * all_experts)
    padded = (capacity + 1 + 15) // 16 * 16
    block = local * padded
    buckets = relative_bias_table.shape[0]

    chosen = expert_index[:, 0]
    order = priority[0]
    ahead = (chosen[:, None] == chosen[None, :]) & (order[None, :] < order[:, None])
    rank = jnp.sum(ahead.astype(jnp.int32), axis=1)
    place = ((chosen // local) ^ exp_me) * block + (chosen % local) * padded + rank
    slots = jnp.where(rank < capacity, place, -1)
    slot_row, slot_column = slots[None, :], slots[:, None]

    def over_exp(array):
        pieces = [array[0]]
        for step in range(1, exp_n):
            pairs = [(i, i ^ step) for i in range(exp_n)]
            pieces.append(lax.ppermute(array[step], "exp", pairs))
        return pieces

    def to_experts(rows):
        pieces = over_exp(rows.reshape(exp_n, local, padded, width))
        return jnp.concatenate(pieces, axis=1)

    def to_tokens(rows):
        pieces = rows.reshape(local, exp_n, padded, width).transpose(1, 0, 2, 3)
        return jnp.concatenate(over_exp(pieces), axis=0).reshape(exp_n * block, width)

    half = local // 2
    group = dp_me % 2

    def over_dp(rows):
        mine = lax.dynamic_slice_in_dim(rows, group * half, half, 0)
        other = lax.dynamic_slice_in_dim(rows, (1 - group) * half, half, 0)
        pieces = [mine]
        for step in range(1, dp_n):
            pairs = [(i, i ^ step) for i in range(dp_n)]
            pieces.append(lax.ppermute(other if step % 2 else mine, "dp", pairs))
        return pieces

    c_rows = to_experts(dispatch(slot_row, cotangent, exp_n, block))
    c_all = over_dp(c_rows)

    lines = jnp.dot(
        relative_bias_table.T, diagonal_onehot(buckets).T, precision=FULL_PRECISION
    ).reshape(HEADS, 4, TILE)
    lines = jnp.concatenate([lines, jnp.zeros_like(lines)], axis=1)
    gain_attn, gain_ffn = norm_attn[None, :], norm_ffn[None, :]
    q, k, v = qkv(tokens, gain_attn, w_query, w_key, w_value)
    context, lse = attention(lines, q, k, v)
    mixed, u, probs, gate, gate_row = router(
        context, tokens, w_output, gain_ffn, w_router, expert_index
    )
    sent = dispatch(slot_row, u, exp_n, block, gate=(gate_row, local, capacity, padded))
    u_rows = to_experts(sent)
    u_all = over_dp(u_rows)
    e_rows, d_rows = expert_pass(u_rows, c_rows, w_in, w_out)
    e_back, d_back = to_tokens(e_rows), to_tokens(d_rows)
    mixed_out, mixed_grad, context_grad, output_part, router_part, norm_ffn_part = combine(
        slot_column, expert_index, gate, probs, mixed, cotangent, context,
        e_back, d_back, w_output, w_router, gain_ffn,
    )
    query_grad, key_grad, value_grad, sums = attention_back(lines, q, k, v, context_grad, lse)
    table_part = jnp.dot(
        diagonal_onehot(buckets).T,
        sums[:, :4].reshape(HEADS, 4 * TILE).T,
        precision=FULL_PRECISION,
    )
    grad_tokens, query_part, key_part, value_part, norm_attn_part = last(
        tokens, mixed_grad, query_grad, key_grad, value_grad, w_query, w_key, w_value, gain_attn
    )

    size = w_in.shape[2] // dp_n
    where = jnp.stack([group * half, (dp_me // 2) * 2, group]).astype(jnp.int32)
    own_in, own_out, far_in, far_out = weight_grads(
        where, u_all, c_all, w_in, w_out, size, capacity, padded
    )
    swap = [(i, i ^ 1) for i in range(dp_n)]
    came_in, came_out = lax.ppermute(far_in, "dp", swap), lax.ppermute(far_out, "dp", swap)
    there = ((1 - group) * half).astype(jnp.int32)[None]
    grad_in, grad_out = finish(there, own_in, own_out, came_in, came_out)

    axes = ("exp", "dp")
    big = lax.psum(
        tuple(part.astype(BF) for part in (query_part, key_part, value_part, output_part)), axes
    )
    small = lax.psum((norm_attn_part, norm_ffn_part, table_part, router_part), axes)
    return (
        mixed_out,
        grad_tokens,
        *(part.astype(F32) for part in big),
        small[0][0],
        small[1][0],
        small[2],
        small[3],
        grad_in,
        grad_out,
    )


def solution(mesh):
    return jax.shard_map(
        per_device,
        mesh=mesh,
        in_specs=(
            P(("exp", "dp"), None),
            P(),
            P(),
            P(),
            P(),
            P(),
            P(),
            P(),
            P(),
            P("exp", None, None),
            P("exp", None, None),
            P(("exp", "dp"), None),
            P(("exp", "dp"), None),
            P(("exp", "dp"), None),
        ),
        out_specs=(
            P(("exp", "dp"), None),
            P(("exp", "dp"), None),
            P(),
            P(),
            P(),
            P(),
            P(),
            P(),
            P(),
            P(),
            P("exp", None, "dp"),
            P("exp", "dp", None),
        ),
        check_vma=False,
    )
```

```python
import functools

import jax
import jax.numpy as jnp
from jax import lax
from jax.experimental import pallas as pl
from jax.experimental.pallas import tpu as pltpu
from jax.sharding import PartitionSpec as P

HEADS = 12
HEAD_DIM = 64
SEQ = 512
LIMITS = (12, 16, 23, 32, 46, 64, 91)
EPSILON = 1e-06
FULL_PRECISION = lax.Precision.HIGHEST
BF = jnp.bfloat16
F32 = jnp.float32
PAIR = 2 * HEAD_DIM
TILE = 128
CHUNK = 256
GELU_A = 0.7978845608028654
GELU_B = 0.044715 * GELU_A
VMEM_MIB = 50


def params(**more):
    return pltpu.CompilerParams(vmem_limit_bytes=VMEM_MIB * 2**20, **more)


def mm(left, right):
    return jnp.dot(left, right, preferred_element_type=F32)


def mm_nt(left, right):
    return lax.dot_general(left, right, (((1,), (1,)), ((), ())), preferred_element_type=F32)


def flipped(index, step):
    bit = 1
    while bit <= step:
        if step & bit:
            index = index + bit * (1 - 2 * ((index // bit) % 2))
        bit *= 2
    return index


def bucket_of(offset):
    distance = jnp.abs(offset)
    farther = jnp.zeros_like(distance)
    for limit in LIMITS:
        farther = farther + (distance >= limit).astype(jnp.int32)
    return jnp.where(distance < 8, distance, 8 + farther) + jnp.where(offset > 0, 16, 0)


def diagonal_onehot(count):
    places = jnp.arange(TILE, dtype=jnp.int32)
    offsets = jnp.concatenate([-places, TILE - places, 0 * places - SEQ, 0 * places + SEQ])
    return (bucket_of(offsets)[:, None] == jnp.arange(count, dtype=jnp.int32)[None, :]).astype(F32)


def dispatch_kernel(slot_ref, rows_ref, out_ref):
    block, tokens = out_ref.shape[0], rows_ref.shape[0]
    ids = lax.broadcasted_iota(jnp.int32, (block, tokens), 0) + pl.program_id(0) * block
    picks = jnp.where(slot_ref[...] == ids, 1.0, 0.0).astype(BF)
    out_ref[...] = mm(picks, rows_ref[...]).astype(BF)


def dispatch_gate_kernel(experts, capacity, padded, slot_ref, gate_ref, rows_ref, out_ref):
    block, tokens = out_ref.shape[0], rows_ref.shape[0]
    width = out_ref.shape[1]
    step = pl.program_id(0)
    ids = lax.broadcasted_iota(jnp.int32, (block, tokens), 0) + step * block
    picks = jnp.where(slot_ref[...] == ids, 1.0, 0.0).astype(BF)
    out = mm(picks, rows_ref[...])
    gates = jnp.broadcast_to(gate_ref[...].astype(BF), (8, tokens))
    lanes = pl.num_programs(0) * padded
    in_slots = mm_nt(gates, picks)
    in_slots = jnp.concatenate([in_slots, jnp.zeros((8, lanes - block), F32)], axis=1)
    lane = lax.broadcasted_iota(jnp.int32, (8, lanes), 1)
    row = lax.broadcasted_iota(jnp.int32, (block, 1), 0)
    left = out[:, :lanes]
    for expert in range(experts):
        shift = lax.rem(step * padded - expert * padded + lanes, lanes)
        moved = pltpu.roll(in_slots, shift, 1)
        mine = (lane >= step * padded) & (lane < step * padded + capacity)
        moved = jnp.where(mine, moved, 0.0)[:1]
        left = jnp.where(row == expert * padded + capacity, moved, left)
    out_ref[:, :lanes] = left.astype(BF)
    out_ref[:, lanes:] = out[:, lanes:].astype(BF)


def dispatch(slot_row, rows, blocks, block, gate=None):
    tokens, width = rows.shape
    grid_spec = dict(
        grid=(blocks,),
        out_specs=pl.BlockSpec((block, width), lambda k: (k, 0)),
        out_shape=jax.ShapeDtypeStruct((blocks * block, width), BF),
    )
    line = pl.BlockSpec((1, tokens), lambda k: (0, 0))
    full = pl.BlockSpec((tokens, width), lambda k: (0, 0))
    cost = pl.CostEstimate(
        flops=2 * blocks * block * tokens * width,
        bytes_accessed=2 * width * (tokens + blocks * block),
        transcendentals=0,
    )
    if gate is None:
        return pl.pallas_call(
            dispatch_kernel, in_specs=[line, full], compiler_params=params(), cost_estimate=cost, **grid_spec
        )(slot_row, rows)
    values, experts, capacity, padded = gate
    return pl.pallas_call(
        functools.partial(dispatch_gate_kernel, experts, capacity, padded),
        in_specs=[line, line, full],
        compiler_params=params(),
        cost_estimate=cost,
        **grid_spec,
    )(slot_row, values, rows)


def qkv_kernel(x_ref, gain_ref, wq_ref, wk_ref, wv_ref, q_ref, k_ref, v_ref):
    rows = x_ref[...].astype(F32)
    inv = lax.rsqrt(jnp.mean(rows * rows, axis=-1, keepdims=True) + EPSILON)
    normed = (rows * inv * gain_ref[...]).astype(BF)
    q_ref[...] = (mm(normed, wq_ref[...]).astype(BF).astype(F32) * HEAD_DIM**-0.5).astype(BF)
    k_ref[...] = mm(normed, wk_ref[...]).astype(BF)
    v_ref[...] = mm(normed, wv_ref[...]).astype(BF)


def qkv(x, gain, wq, wk, wv):
    tokens, width = x.shape
    rows = pl.BlockSpec((SEQ, width), lambda t: (t, 0))
    square = pl.BlockSpec((width, width), lambda t: (0, 0))
    one = pl.BlockSpec((1, width), lambda t: (0, 0))
    return pl.pallas_call(
        qkv_kernel,
        grid=(tokens // SEQ,),
        in_specs=[rows, one, square, square, square],
        out_specs=[rows] * 3,
        out_shape=[jax.ShapeDtypeStruct((tokens, width), BF)] * 3,
        compiler_params=params(),
        cost_estimate=pl.CostEstimate(
            flops=6 * tokens * width * width, bytes_accessed=8 * tokens * width, transcendentals=0
        ),
    )(x, gain, wq, wk, wv)


def fill_bias(lines_ref, bias_ref):
    upper_right = lax.broadcasted_iota(jnp.int32, (TILE, TILE), 0) <= lax.broadcasted_iota(
        jnp.int32, (TILE, TILE), 1
    )
    tiles = SEQ // TILE
    for head in range(2):

        def sheared(line):
            whole = jnp.broadcast_to(lines_ref[head, line : line + 1, :], (TILE, TILE))
            return pltpu.roll(whole, 0, 1, stride=1, stride_axis=0)

        negative, positive = sheared(0), sheared(1)
        far_negative = jnp.broadcast_to(lines_ref[head, 2:3, :], (TILE, TILE))
        far_positive = jnp.broadcast_to(lines_ref[head, 3:4, :], (TILE, TILE))
        same = jnp.where(upper_right, negative, positive)
        above = jnp.where(upper_right, positive, far_positive)
        below = jnp.where(upper_right, far_negative, negative)
        for key in range(tiles):
            for query in range(tiles):
                gap = key - query
                tile = (
                    same
                    if gap == 0
                    else above
                    if gap == 1
                    else below
                    if gap == -1
                    else far_positive
                    if gap > 0
                    else far_negative
                )
                bias_ref[head, pl.ds(key * TILE, TILE), pl.ds(query * TILE, TILE)] = tile


def head_lanes(head):
    lane = lax.broadcasted_iota(jnp.int32, (1, PAIR), 1)
    return (lane >= head * HEAD_DIM) & (lane < (head + 1) * HEAD_DIM)


def only(head, array):
    return jnp.where(head_lanes(head), array, jnp.zeros_like(array))


def attention_kernel(
    lines_ref, sent_ref, q_ref, k_ref, v_ref, o_ref, lse_ref, came_ref, bias_ref, local_sem, send_sem, recv_sem
):
    pair, seq = pl.program_id(0), pl.program_id(1)
    blocks = sent_ref.shape[0]
    me = lax.axis_index("exp")

    def there(block):
        return {"exp": flipped(me, block)}

    def outgoing(block):
        return pltpu.make_async_remote_copy(
            src_ref=sent_ref.at[block],
            dst_ref=came_ref.at[:, block],
            send_sem=send_sem.at[block],
            recv_sem=recv_sem.at[block],
            device_id=there(block),
            device_id_type=pl.DeviceIdType.MESH,
        )

    own = pltpu.make_async_copy(sent_ref.at[0], came_ref.at[:, 0], local_sem)

    @pl.when((pair == 0) & (seq == 0))
    def _():
        barrier = pltpu.get_barrier_semaphore()
        for block in range(1, blocks):
            pl.semaphore_signal(
                barrier, inc=1, device_id=there(block), device_id_type=pl.DeviceIdType.MESH
            )
        pl.semaphore_wait(barrier, blocks - 1)
        own.start()
        for block in range(1, blocks):
            outgoing(block).start()

    @pl.when(seq == 0)
    def _():
        fill_bias(lines_ref, bias_ref)

    keys = k_ref[...]
    values_t = v_ref[...].T
    masked = [only(head, keys) for head in range(2)]
    row = lax.broadcasted_iota(jnp.int32, (PAIR, 1), 0)
    for part in range(SEQ // CHUNK):
        places = pl.ds(part * CHUNK, CHUNK)
        queries = q_ref[places, :]
        out = None
        for head in range(2):
            scores = mm_nt(masked[head], queries) + bias_ref[head, :, places]
            highest = jnp.max(scores, axis=0, keepdims=True)
            weights = jnp.exp(scores - highest)
            total = jnp.sum(weights, axis=0, keepdims=True)
            lse_ref[0, 0, head : head + 1, places] = highest + jnp.log(total)
            mixed = mm(values_t, weights.astype(BF)) * (1.0 / total)
            out = mixed if out is None else jnp.where(row < HEAD_DIM, out, mixed)
        o_ref[places, :] = out.T.astype(BF)

    @pl.when((pair == pl.num_programs(0) - 1) & (seq == pl.num_programs(1) - 1))
    def _():
        own.wait()
        for block in range(1, blocks):
            outgoing(block).wait()


def attention(lines, sent, q, k, v):
    blocks, experts, padded, width = sent.shape
    tokens, width = q.shape
    seqs, pairs = tokens // SEQ, width // PAIR
    block = pl.BlockSpec((SEQ, PAIR), lambda h, s: (s, h))
    return pl.pallas_call(
        attention_kernel,
        grid=(pairs, seqs),
        in_specs=[pl.BlockSpec((2, 8, TILE), lambda h, s: (h, 0, 0)), pl.BlockSpec(memory_space=pl.ANY)]
        + [block, block, block],
        out_specs=[block, pl.BlockSpec((1, 1, 2, SEQ), lambda h, s: (h, s, 0, 0))]
        + [pl.BlockSpec(memory_space=pl.ANY)],
        out_shape=[
            jax.ShapeDtypeStruct((tokens, width), BF),
            jax.ShapeDtypeStruct((pairs, seqs, 2, SEQ), F32),
            jax.ShapeDtypeStruct((experts, blocks, padded, width), BF),
        ],
        scratch_shapes=[
            pltpu.VMEM((2, SEQ, SEQ), F32),
            pltpu.SemaphoreType.DMA,
            pltpu.SemaphoreType.DMA((blocks,)),
            pltpu.SemaphoreType.DMA((blocks,)),
        ],
        compiler_params=params(collective_id=1, has_side_effects=True),
        cost_estimate=pl.CostEstimate(
            flops=16 * pairs * seqs * SEQ * SEQ * PAIR,
            bytes_accessed=8 * tokens * width,
            transcendentals=2 * pairs * seqs * SEQ * SEQ,
        ),
    )(lines, sent, q, k, v)


def attention_back_kernel(
    lines_ref, q_ref, k_ref, v_ref, do_ref, lse_ref, dq_ref, dk_ref, dv_ref, sums_ref, bias_ref, diag_ref
):
    seq = pl.program_id(1)

    @pl.when(seq == 0)
    def _():
        fill_bias(lines_ref, bias_ref)
        diag_ref[...] = jnp.zeros_like(diag_ref)

    keys, values = k_ref[...], v_ref[...]
    keys_t = keys.T
    masked_k = [only(head, keys) for head in range(2)]
    masked_v = [only(head, values) for head in range(2)]
    row = lax.broadcasted_iota(jnp.int32, (PAIR, 1), 0)
    grads_k, grads_v = [None, None], [None, None]
    tiles = SEQ // TILE
    for part in range(SEQ // CHUNK):
        places = pl.ds(part * CHUNK, CHUNK)
        queries, upstream = q_ref[places, :], do_ref[places, :]
        grad_q = None
        for head in range(2):
            scores = mm_nt(masked_k[head], queries) + bias_ref[head, :, places]
            weights = jnp.exp(scores - lse_ref[0, 0, head : head + 1, places])
            products = weights * mm_nt(masked_v[head], upstream)
            scores_grad = products - weights * jnp.sum(products, axis=0, keepdims=True)
            low = scores_grad.astype(BF)
            value_term = mm(weights.astype(BF), upstream)
            key_term = mm(low, queries)
            grads_v[head] = value_term if part == 0 else grads_v[head] + value_term
            grads_k[head] = key_term if part == 0 else grads_k[head] + key_term
            query_term = mm(keys_t, low)
            grad_q = query_term if head == 0 else jnp.where(row < HEAD_DIM, grad_q, query_term)
            groups = {}
            for query in range(CHUNK // TILE):
                for key in range(tiles):
                    gap = key - (query + part * (CHUNK // TILE))
                    kind = 0 if gap == 0 else 1 if gap == 1 else 2 if gap == -1 else 3 if gap > 0 else 4
                    tile = scores_grad[
                        key * TILE : (key + 1) * TILE, query * TILE : (query + 1) * TILE
                    ]
                    groups[kind] = tile if kind not in groups else groups[kind] + tile
            for kind, tile in groups.items():
                diag_ref[head, kind] += tile
        dq_ref[places, :] = (grad_q * HEAD_DIM**-0.5).T.astype(BF)
    first = head_lanes(0)
    dk_ref[...] = jnp.where(first, grads_k[0], grads_k[1]).astype(BF)
    dv_ref[...] = jnp.where(first, grads_v[0], grads_v[1]).astype(BF)

    @pl.when(seq == pl.num_programs(1) - 1)
    def _():
        upper_right = lax.broadcasted_iota(jnp.int32, (TILE, TILE), 0) <= lax.broadcasted_iota(
            jnp.int32, (TILE, TILE), 1
        )
        sums_ref[...] = jnp.zeros_like(sums_ref)
        for head in range(2):
            same, above, below = diag_ref[head, 0], diag_ref[head, 1], diag_ref[head, 2]

            def gathered(array):
                row_id = lax.broadcasted_iota(jnp.int32, (TILE, 1), 0)
                bit = 1
                while bit < TILE:
                    turned = pltpu.roll(array, TILE - bit, 1)
                    array = jnp.where((row_id & bit) != 0, turned, array)
                    bit *= 2
                return jnp.sum(array, axis=0, keepdims=True)

            zero = jnp.zeros_like(same)
            sums_ref[head, 0:1, :] = gathered(jnp.where(upper_right, same, below))
            sums_ref[head, 1:2, :] = gathered(jnp.where(upper_right, above, same))
            sums_ref[head, 2:3, :] = jnp.sum(
                diag_ref[head, 4] + jnp.where(upper_right, below, zero), axis=0, keepdims=True
            )
            sums_ref[head, 3:4, :] = jnp.sum(
                diag_ref[head, 3] + jnp.where(upper_right, zero, above), axis=0, keepdims=True
            )


def attention_back(lines, q, k, v, do, lse):
    tokens, width = q.shape
    seqs, pairs = tokens // SEQ, width // PAIR
    block = pl.BlockSpec((SEQ, PAIR), lambda h, s: (s, h))
    lines_spec = pl.BlockSpec((2, 8, TILE), lambda h, s: (h, 0, 0))
    return pl.pallas_call(
        attention_back_kernel,
        grid=(pairs, seqs),
        in_specs=[lines_spec, block, block, block, block]
        + [pl.BlockSpec((1, 1, 2, SEQ), lambda h, s: (h, s, 0, 0))],
        out_specs=[block, block, block, lines_spec],
        out_shape=[jax.ShapeDtypeStruct((tokens, width), BF)] * 3
        + [jax.ShapeDtypeStruct((2 * pairs, 8, TILE), F32)],
        scratch_shapes=[pltpu.VMEM((2, SEQ, SEQ), F32), pltpu.VMEM((2, 5, TILE, TILE), F32)],
        compiler_params=params(),
        cost_estimate=pl.CostEstimate(
            flops=40 * pairs * seqs * SEQ * SEQ * PAIR,
            bytes_accessed=14 * tokens * width,
            transcendentals=2 * pairs * seqs * SEQ * SEQ,
        ),
    )(lines, q, k, v, do, lse)


def router_kernel(
    o_ref, x_ref, wo_ref, gain_ref, wr_ref, expert_ref, h_ref, u_ref, probs_ref, gate_ref, line_ref
):
    mixed = x_ref[...].astype(F32) + mm(o_ref[...], wo_ref[...])
    h_ref[...] = mixed
    inv = lax.rsqrt(jnp.mean(mixed * mixed, axis=-1, keepdims=True) + EPSILON)
    normed = mixed * inv * gain_ref[...]
    u_ref[...] = normed.astype(BF)
    logits = jnp.dot(normed, wr_ref[...], precision=FULL_PRECISION, preferred_element_type=F32)
    spread = jnp.exp(logits - jnp.max(logits, axis=-1, keepdims=True))
    probs = spread / jnp.sum(spread, axis=-1, keepdims=True)
    probs_ref[...] = probs
    picked = expert_ref[...] == lax.broadcasted_iota(jnp.int32, probs.shape, 1)
    gate = jnp.sum(jnp.where(picked, probs, 0.0), axis=-1, keepdims=True)
    gate_ref[...] = gate
    size = gate.shape[0]
    diagonal = lax.broadcasted_iota(jnp.int32, (size, size), 0) == lax.broadcasted_iota(
        jnp.int32, (size, size), 1
    )
    line_ref[...] = jnp.sum(jnp.where(diagonal, gate, 0.0), axis=0, keepdims=True)


def router(o, x, wo, gain, wr, expert):
    tokens, width = x.shape
    experts = wr.shape[1]
    size = 256

    def rows(columns):
        return pl.BlockSpec((size, columns), lambda t: (t, 0))

    def whole(*shape):
        return pl.BlockSpec(shape, lambda t: (0, 0))

    return pl.pallas_call(
        router_kernel,
        grid=(tokens // size,),
        in_specs=[rows(width), rows(width), whole(width, width), whole(1, width)]
        + [whole(width, experts), rows(1)],
        out_specs=[rows(width), rows(width), rows(experts), rows(1)]
        + [pl.BlockSpec((1, size), lambda t: (0, t))],
        out_shape=[
            jax.ShapeDtypeStruct((tokens, width), F32),
            jax.ShapeDtypeStruct((tokens, width), BF),
            jax.ShapeDtypeStruct((tokens, experts), F32),
            jax.ShapeDtypeStruct((tokens, 1), F32),
            jax.ShapeDtypeStruct((1, tokens), F32),
        ],
        compiler_params=params(),
        cost_estimate=pl.CostEstimate(
            flops=2 * tokens * width * width, bytes_accessed=10 * tokens * width, transcendentals=0
        ),
    )(o, x, wo, gain, wr, expert)


def gelu_and_slope(z):
    square = z * z
    half = 0.5 + 0.5 * jnp.tanh(z * (GELU_A + GELU_B * square))
    value = z * half
    slope = half + 2.0 * value * (1.0 - half) * (GELU_A + 3.0 * GELU_B * square)
    return value, slope


def expert_kernel(
    parts, sent_ref, c_ref, first_ref, second_ref, u_ref, e_ref, d_ref,
    rows_ref, e_sum, d_sum, e_held, d_held, local_sem, send_sem, recv_sem, back_send, back_recv,
):
    expert, step = pl.program_id(0), pl.program_id(1)
    experts, last_step = pl.num_programs(0), pl.num_programs(1) - 1
    blocks, padded, width = rows_ref.shape[1:]
    me = lax.axis_index("exp")
    columns = first_ref.shape[2] // parts

    def there(block):
        return {"exp": flipped(me, block)}

    def outgoing(which, block):
        return pltpu.make_async_remote_copy(
            src_ref=sent_ref.at[block, which],
            dst_ref=rows_ref.at[which, block],
            send_sem=send_sem.at[which, block],
            recv_sem=recv_sem.at[which, block],
            device_id=there(block),
            device_id_type=pl.DeviceIdType.MESH,
        )

    def returning(kind, which, block):
        held, target = (e_held, e_ref) if kind == 0 else (d_held, d_ref)
        return pltpu.make_async_remote_copy(
            src_ref=held.at[which, block],
            dst_ref=target.at[block, which],
            send_sem=back_send.at[kind, which, block],
            recv_sem=back_recv.at[kind, which, block],
            device_id=there(block),
            device_id_type=pl.DeviceIdType.MESH,
        )

    def own_in(which):
        return pltpu.make_async_copy(sent_ref.at[0, which], rows_ref.at[which, 0], local_sem.at[0, which])

    def own_back(kind, which):
        held, target = (e_held, e_ref) if kind == 0 else (d_held, d_ref)
        return pltpu.make_async_copy(
            held.at[which, 0], target.at[0, which], local_sem.at[1 + kind, which]
        )

    def keep(which):
        return pltpu.make_async_copy(rows_ref.at[which], u_ref.at[which], local_sem.at[3, which])

    @pl.when((expert == 0) & (step == 0))
    def _():
        barrier = pltpu.get_barrier_semaphore()
        for block in range(1, blocks):
            pl.semaphore_signal(
                barrier, inc=1, device_id=there(block), device_id_type=pl.DeviceIdType.MESH
            )
        pl.semaphore_wait(barrier, blocks - 1)
        for which in range(rows_ref.shape[0]):
            own_in(which).start()
            for block in range(1, blocks):
                outgoing(which, block).start()

    @pl.when(step == 0)
    def _():
        own_in(expert).wait()
        for block in range(1, blocks):
            outgoing(expert, block).wait_recv()
        keep(expert).start()
        e_sum[...] = jnp.zeros_like(e_sum)
        d_sum[...] = jnp.zeros_like(d_sum)

    rows, upstream = rows_ref[expert].reshape(blocks * padded, width), c_ref[0]
    for part in range(parts):
        places = slice(part * columns, (part + 1) * columns)
        first, second = first_ref[0, :, places], second_ref[0, places, :]
        value, slope = gelu_and_slope(mm(rows, first))
        inner = (mm_nt(upstream, second) * slope).astype(BF)
        e_sum[...] += mm(value.astype(BF), second)
        d_sum[...] += mm_nt(inner, first)

    @pl.when(step == last_step)
    def _():
        e_held[expert] = e_sum[...].astype(BF).reshape(blocks, padded, width)
        d_held[expert] = d_sum[...].astype(BF).reshape(blocks, padded, width)
        for kind in range(2):
            own_back(kind, expert).start()
            for block in range(1, blocks):
                returning(kind, expert, block).start()

    @pl.when((step == last_step) & (expert == experts - 1))
    def _():
        for which in range(rows_ref.shape[0]):
            keep(which).wait()
            for block in range(1, blocks):
                outgoing(which, block).wait_send()
            for kind in range(2):
                own_back(kind, which).wait()
                for block in range(1, blocks):
                    returning(kind, which, block).wait()


def expert_pass(sent, c, w_in, w_out):
    blocks, experts, padded, width = sent.shape
    hidden = w_in.shape[2]
    size = 768
    rows = blocks * padded
    anywhere = pl.BlockSpec(memory_space=pl.ANY)
    return pl.pallas_call(
        functools.partial(expert_kernel, 3),
        grid=(experts, hidden // size),
        in_specs=[
            anywhere,
            pl.BlockSpec((1, rows, width), lambda e, f: (e, 0, 0)),
            pl.BlockSpec((1, width, size), lambda e, f: (e, 0, f)),
            pl.BlockSpec((1, size, width), lambda e, f: (e, f, 0)),
        ],
        out_specs=[anywhere] * 3,
        out_shape=[
            jax.ShapeDtypeStruct((experts, blocks, padded, width), BF),
            jax.ShapeDtypeStruct(sent.shape, BF),
            jax.ShapeDtypeStruct(sent.shape, BF),
        ],
        scratch_shapes=[
            pltpu.VMEM((experts, blocks, padded, width), BF),
            pltpu.VMEM((rows, width), F32),
            pltpu.VMEM((rows, width), F32),
            pltpu.VMEM((experts, blocks, padded, width), BF),
            pltpu.VMEM((experts, blocks, padded, width), BF),
            pltpu.SemaphoreType.DMA((4, experts)),
            pltpu.SemaphoreType.DMA((experts, blocks)),
            pltpu.SemaphoreType.DMA((experts, blocks)),
            pltpu.SemaphoreType.DMA((2, experts, blocks)),
            pltpu.SemaphoreType.DMA((2, experts, blocks)),
        ],
        compiler_params=params(collective_id=0, has_side_effects=True),
        cost_estimate=pl.CostEstimate(
            flops=8 * experts * rows * width * hidden,
            bytes_accessed=4 * experts * width * (hidden + 2 * rows),
            transcendentals=experts * rows * hidden,
        ),
    )(sent, c, w_in, w_out)


def weights_kernel(parts, sources, capacity, padded, place_ref, *refs):
    u_refs, c_refs = refs[:sources], refs[sources : 2 * sources]
    first_ref, second_ref, own_in, own_out, far_in, far_out, in_sum, out_sum = refs[2 * sources :]
    width, size = first_ref.shape[1:]
    rows = u_refs[0].shape[1]
    columns = size // parts
    first_t = first_ref[0].T
    for source in range(sources):
        inputs, upstream = u_refs[source][0], c_refs[source][0]
        gate = jnp.zeros((1, rows), F32)
        for block in range(rows // padded):
            place = block * padded + capacity
            gate = gate + inputs[place : place + 1, :rows].astype(F32)
        for part in range(parts):
            places = slice(part * columns, (part + 1) * columns)
            value, slope = gelu_and_slope(mm_nt(first_t[places, :], inputs))
            inner = (mm_nt(second_ref[0, places, :], upstream) * (slope * gate)).astype(BF)
            in_term = mm(inner, inputs)
            out_term = mm((value * gate).astype(BF), upstream)
            if source == 0:
                in_sum[places, :] = in_term
                out_sum[places, :] = out_term
            else:
                in_sum[places, :] += in_term
                out_sum[places, :] += out_term
    mine = pl.program_id(1) == place_ref[2]

    @pl.when(mine)
    def _():
        own_in[0] = in_sum[...].T
        own_out[0] = out_sum[...]

    @pl.when(jnp.logical_not(mine))
    def _():
        far_in[0] = in_sum[...].T.astype(BF)
        far_out[0] = out_sum[...].astype(BF)


def weight_grads(place, us, cs, w_in, w_out, size, capacity, padded):
    sources = len(us)
    experts, rows, width = us[0].shape
    local = w_in.shape[0]
    block = pl.BlockSpec((1, rows, width), lambda e, f, p: (e, 0, 0))
    tile = pl.BlockSpec((1, width, size), lambda e, f, p: (e, 0, 0))
    turned = pl.BlockSpec((1, size, width), lambda e, f, p: (e, 0, 0))
    return pl.pallas_call(
        functools.partial(weights_kernel, 3, sources, capacity, padded),
        grid_spec=pltpu.PrefetchScalarGridSpec(
            num_scalar_prefetch=1,
            grid=(experts, 2),
            in_specs=[block] * (2 * sources)
            + [
                pl.BlockSpec((1, width, size), lambda e, f, p: (p[0] + e, 0, p[1] + f)),
                pl.BlockSpec((1, size, width), lambda e, f, p: (p[0] + e, p[1] + f, 0)),
            ],
            out_specs=[
                pl.BlockSpec((1, width, size), lambda e, f, p: (p[0] + e, 0, 0)),
                pl.BlockSpec((1, size, width), lambda e, f, p: (p[0] + e, 0, 0)),
                tile,
                turned,
            ],
            scratch_shapes=[pltpu.VMEM((size, width), F32)] * 2,
        ),
        out_shape=[
            jax.ShapeDtypeStruct((local, width, size), F32),
            jax.ShapeDtypeStruct((local, size, width), F32),
            jax.ShapeDtypeStruct((experts, width, size), BF),
            jax.ShapeDtypeStruct((experts, size, width), BF),
        ],
        compiler_params=params(),
        cost_estimate=pl.CostEstimate(
            flops=16 * sources * experts * rows * width * size,
            bytes_accessed=4 * experts * (sources * rows * width + 6 * size * width),
            transcendentals=2 * sources * experts * rows * size,
        ),
    )(place, *us, *cs, w_in, w_out)


def finish_kernel(place_ref, a_ref, b_ref, x_ref, y_ref, a_out, b_out):
    a_out[...] = x_ref[...].astype(F32)
    b_out[...] = y_ref[...].astype(F32)


def finish(place, own_in, own_out, came_in, came_out):
    experts, width, size = came_in.shape

    def spec(shape, moved):
        return pl.BlockSpec((1,) + shape, lambda e, p: ((p[0] if moved else 0) + e, 0, 0))

    return pl.pallas_call(
        finish_kernel,
        grid_spec=pltpu.PrefetchScalarGridSpec(
            num_scalar_prefetch=1,
            grid=(experts,),
            in_specs=[pl.BlockSpec(memory_space=pl.ANY)] * 2
            + [spec((width, size), False), spec((size, width), False)],
            out_specs=[spec((width, size), True), spec((size, width), True)],
        ),
        out_shape=[
            jax.ShapeDtypeStruct(own_in.shape, F32),
            jax.ShapeDtypeStruct(own_out.shape, F32),
        ],
        input_output_aliases={1: 0, 2: 1},
        compiler_params=params(),
    )(place, own_in, own_out, came_in, came_out)


def combine_kernel(
    slot_ref, expert_ref, gate_ref, probs_ref, h_ref, c_ref, o_ref, e_ref, d_ref, wo_ref, wr_ref, gain_ref,
    mixed_ref, dh_ref, do_ref, wo_sum, wr_sum, gain_sum,
):
    step = pl.program_id(0)
    tokens, slots = slot_ref.shape[0], e_ref.shape[0]
    picks = jnp.where(
        slot_ref[...] == lax.broadcasted_iota(jnp.int32, (tokens, slots), 1), 1.0, 0.0
    ).astype(BF)
    returned, arrived = mm(picks, e_ref[...]), mm(picks, d_ref[...])
    gate, probs, mixed = gate_ref[...], probs_ref[...], h_ref[...]
    upstream = c_ref[...].astype(F32)
    mixed_ref[...] = (mixed + gate * returned).astype(BF)
    gate_grad = jnp.sum(upstream * returned, axis=-1, keepdims=True)
    picked = jnp.where(expert_ref[...] == lax.broadcasted_iota(jnp.int32, probs.shape, 1), 1.0, 0.0)
    logit_grad = gate_grad * gate * (picked - probs)
    inv = lax.rsqrt(jnp.mean(mixed * mixed, axis=-1, keepdims=True) + EPSILON)
    unit = mixed * inv
    gain = gain_ref[...]
    normed_grad = (
        lax.dot_general(
            logit_grad,
            wr_ref[...],
            (((1,), (1,)), ((), ())),
            precision=FULL_PRECISION,
            preferred_element_type=F32,
        )
        + gate * arrived
    )
    unit_grad = normed_grad * gain
    mixed_grad = upstream + inv * (
        unit_grad - unit * jnp.mean(unit_grad * unit, axis=-1, keepdims=True)
    )
    dh_ref[...] = mixed_grad
    low = mixed_grad.astype(BF)
    do_ref[...] = mm_nt(low, wo_ref[...]).astype(BF)

    @pl.when(step == 0)
    def _():
        wo_sum[...] = jnp.zeros_like(wo_sum)
        wr_sum[...] = jnp.zeros_like(wr_sum)
        gain_sum[...] = jnp.zeros_like(gain_sum)

    wo_sum[...] += mm(o_ref[...].T, low)
    wr_sum[...] += jnp.dot(
        (unit * gain).T, logit_grad, precision=FULL_PRECISION, preferred_element_type=F32
    )
    gain_sum[...] += jnp.sum(normed_grad * unit, axis=0, keepdims=True)


def combine(slot, expert, gate, probs, h, c, o, e_out, du, wo, wr, gain):
    tokens, width = h.shape
    slots, experts = e_out.shape[0], wr.shape[1]
    size = 256

    def rows(columns):
        return pl.BlockSpec((size, columns), lambda t: (t, 0))

    def whole(*shape):
        return pl.BlockSpec(shape, lambda t: (0, 0))

    return pl.pallas_call(
        combine_kernel,
        grid=(tokens // size,),
        in_specs=[rows(1), rows(1), rows(1), rows(experts), rows(width), rows(width), rows(width)]
        + [whole(slots, width), whole(slots, width), whole(width, width), whole(width, experts)]
        + [whole(1, width)],
        out_specs=[rows(width), rows(width), rows(width), whole(width, width), whole(width, experts)]
        + [whole(1, width)],
        out_shape=[
            jax.ShapeDtypeStruct((tokens, width), BF),
            jax.ShapeDtypeStruct((tokens, width), F32),
            jax.ShapeDtypeStruct((tokens, width), BF),
            jax.ShapeDtypeStruct((width, width), F32),
            jax.ShapeDtypeStruct((width, experts), F32),
            jax.ShapeDtypeStruct((1, width), F32),
        ],
        compiler_params=params(),
        cost_estimate=pl.CostEstimate(
            flops=4 * tokens * width * (slots + width),
            bytes_accessed=16 * tokens * width + 4 * slots * width,
            transcendentals=0,
        ),
    )(slot, expert, gate, probs, h, c, o, e_out, du, wo, wr, gain)


def last_kernel(
    x_ref, dh_ref, dq_ref, dk_ref, dv_ref, wq_ref, wk_ref, wv_ref, gain_ref,
    grad_ref, q_sum, k_sum, v_sum, gain_sum,
):
    step = pl.program_id(0)

    @pl.when(step == 0)
    def _():
        for total in (q_sum, k_sum, v_sum, gain_sum):
            total[...] = jnp.zeros_like(total)

    rows = x_ref[...].astype(F32)
    inv = lax.rsqrt(jnp.mean(rows * rows, axis=-1, keepdims=True) + EPSILON)
    unit = rows * inv
    gain = gain_ref[...]
    normed_t = (unit * gain).astype(BF).T
    normed_grad = None
    for grad_ref_in, weight_ref, total in (
        (dq_ref, wq_ref, q_sum),
        (dk_ref, wk_ref, k_sum),
        (dv_ref, wv_ref, v_sum),
    ):
        grad = grad_ref_in[...]
        total[...] += mm(normed_t, grad)
        term = mm_nt(grad, weight_ref[...])
        normed_grad = term if normed_grad is None else normed_grad + term
    unit_grad = normed_grad * gain
    grad_ref[...] = dh_ref[...] + inv * (
        unit_grad - unit * jnp.mean(unit_grad * unit, axis=-1, keepdims=True)
    )
    gain_sum[...] += jnp.sum(normed_grad * unit, axis=0, keepdims=True)


def last(x, dh, dq, dk, dv, wq, wk, wv, gain):
    tokens, width = x.shape
    size = 256
    rows = pl.BlockSpec((size, width), lambda t: (t, 0))
    square = pl.BlockSpec((width, width), lambda t: (0, 0))
    one = pl.BlockSpec((1, width), lambda t: (0, 0))
    return pl.pallas_call(
        last_kernel,
        grid=(tokens // size,),
        in_specs=[rows] * 5 + [square] * 3 + [one],
        out_specs=[rows, square, square, square, one],
        out_shape=[jax.ShapeDtypeStruct((tokens, width), F32)]
        + [jax.ShapeDtypeStruct((width, width), F32)] * 3
        + [jax.ShapeDtypeStruct((1, width), F32)],
        compiler_params=params(),
        cost_estimate=pl.CostEstimate(
            flops=12 * tokens * width * width, bytes_accessed=16 * tokens * width, transcendentals=0
        ),
    )(x, dh, dq, dk, dv, wq, wk, wv, gain)


def per_device(
    tokens,
    w_query,
    w_key,
    w_value,
    w_output,
    norm_attn,
    norm_ffn,
    relative_bias_table,
    w_router,
    w_in,
    w_out,
    expert_index,
    priority,
    cotangent,
):
    tok_rows, width = tokens.shape
    local = w_in.shape[0]
    exp_n, dp_n = lax.axis_size("exp"), lax.axis_size("dp")
    exp_me, dp_me = lax.axis_index("exp"), lax.axis_index("dp")
    all_experts = local * exp_n
    capacity = (5 * tok_rows + 4 * all_experts - 1) // (4 * all_experts)
    padded = (capacity + 1 + 15) // 16 * 16
    block = local * padded
    buckets = relative_bias_table.shape[0]

    chosen = expert_index[:, 0]
    order = priority[0]
    ahead = (chosen[:, None] == chosen[None, :]) & (order[None, :] < order[:, None])
    rank = jnp.sum(ahead.astype(jnp.int32), axis=1)
    place = ((chosen // local) ^ exp_me) * block + (chosen % local) * padded + rank
    slots = jnp.where(rank < capacity, place, -1)
    slot_row, slot_column = slots[None, :], slots[:, None]

    half = local // 2
    group = dp_me % 2

    def over_dp(rows):
        mine = lax.dynamic_slice_in_dim(rows, group * half, half, 0)
        other = lax.dynamic_slice_in_dim(rows, (1 - group) * half, half, 0)
        pieces = [mine]
        for step in range(1, dp_n):
            pairs = [(i, i ^ step) for i in range(dp_n)]
            pieces.append(lax.ppermute(other if step % 2 else mine, "dp", pairs))
        return pieces

    lines = jnp.dot(
        relative_bias_table.T, diagonal_onehot(buckets).T, precision=FULL_PRECISION
    ).reshape(HEADS, 4, TILE)
    lines = jnp.concatenate([lines, jnp.zeros_like(lines)], axis=1)
    gain_attn, gain_ffn = norm_attn[None, :], norm_ffn[None, :]
    q, k, v = qkv(tokens, gain_attn, w_query, w_key, w_value)
    c_sent = dispatch(slot_row, cotangent, exp_n, block).reshape(exp_n, local, padded, width)
    context, lse, c_rows = attention(lines, c_sent, q, k, v)
    c_rows = c_rows.reshape(local, exp_n * padded, width)
    c_all = over_dp(c_rows)
    mixed, u, probs, gate, gate_row = router(
        context, tokens, w_output, gain_ffn, w_router, expert_index
    )
    sent = dispatch(slot_row, u, exp_n, block, gate=(gate_row, local, capacity, padded))
    u_rows, e_back, d_back = expert_pass(
        sent.reshape(exp_n, local, padded, width), c_rows, w_in, w_out
    )
    e_back, *c_all = lax.optimization_barrier((e_back, *c_all))
    e_back, d_back = e_back.reshape(exp_n * block, width), d_back.reshape(exp_n * block, width)
    u_all = over_dp(u_rows.reshape(local, exp_n * padded, width))
    mixed_out, mixed_grad, context_grad, output_part, router_part, norm_ffn_part = combine(
        slot_column, expert_index, gate, probs, mixed, cotangent, context,
        e_back, d_back, w_output, w_router, gain_ffn,
    )
    query_grad, key_grad, value_grad, sums = attention_back(lines, q, k, v, context_grad, lse)
    table_part = jnp.dot(
        diagonal_onehot(buckets).T,
        sums[:, :4].reshape(HEADS, 4 * TILE).T,
        precision=FULL_PRECISION,
    )
    grad_tokens, query_part, key_part, value_part, norm_attn_part = last(
        tokens, mixed_grad, query_grad, key_grad, value_grad, w_query, w_key, w_value, gain_attn
    )

    size = w_in.shape[2] // dp_n
    where = jnp.stack([group * half, (dp_me // 2) * 2, group]).astype(jnp.int32)
    own_in, own_out, far_in, far_out = weight_grads(
        where, u_all, c_all, w_in, w_out, size, capacity, padded
    )
    swap = [(i, i ^ 1) for i in range(dp_n)]
    came_in, came_out = lax.ppermute(far_in, "dp", swap), lax.ppermute(far_out, "dp", swap)
    there = ((1 - group) * half).astype(jnp.int32)[None]
    grad_in, grad_out = finish(there, own_in, own_out, came_in, came_out)

    axes = ("exp", "dp")
    big = lax.psum(
        tuple(part.astype(BF) for part in (query_part, key_part, value_part, output_part)), axes
    )
    small = lax.psum((norm_attn_part, norm_ffn_part, table_part, router_part), axes)
    return (
        mixed_out,
        grad_tokens,
        *(part.astype(F32) for part in big),
        small[0][0],
        small[1][0],
        small[2],
        small[3],
        grad_in,
        grad_out,
    )


def solution(mesh):
    return jax.shard_map(
        per_device,
        mesh=mesh,
        in_specs=(
            P(("exp", "dp"), None),
            P(),
            P(),
            P(),
            P(),
            P(),
            P(),
            P(),
            P(),
            P("exp", None, None),
            P("exp", None, None),
            P(("exp", "dp"), None),
            P(("exp", "dp"), None),
            P(("exp", "dp"), None),
        ),
        out_specs=(
            P(("exp", "dp"), None),
            P(("exp", "dp"), None),
            P(),
            P(),
            P(),
            P(),
            P(),
            P(),
            P(),
            P(),
            P("exp", None, "dp"),
            P("exp", "dp", None),
        ),
        check_vma=False,
    )
```

```python
import functools

import jax
import jax.numpy as jnp
from jax import lax
from jax.experimental import pallas as pl
from jax.experimental.pallas import tpu as pltpu
from jax.sharding import PartitionSpec as P

HEADS = 12
HEAD_DIM = 64
SEQ = 512
LIMITS = (12, 16, 23, 32, 46, 64, 91)
EPSILON = 1e-06
FULL_PRECISION = lax.Precision.HIGHEST
BF = jnp.bfloat16
F32 = jnp.float32
PAIR = 2 * HEAD_DIM
TILE = 128
CHUNK = 256
GELU_A = 0.7978845608028654
GELU_B = 0.044715 * GELU_A
VMEM_MIB = 50


def params(**more):
    return pltpu.CompilerParams(vmem_limit_bytes=VMEM_MIB * 2**20, **more)


def mm(left, right):
    return jnp.dot(left, right, preferred_element_type=F32)


def mm_nt(left, right):
    return lax.dot_general(left, right, (((1,), (1,)), ((), ())), preferred_element_type=F32)


def flipped(index, step):
    bit = 1
    while bit <= step:
        if step & bit:
            index = index + bit * (1 - 2 * ((index // bit) % 2))
        bit *= 2
    return index


def bucket_of(offset):
    distance = jnp.abs(offset)
    farther = jnp.zeros_like(distance)
    for limit in LIMITS:
        farther = farther + (distance >= limit).astype(jnp.int32)
    return jnp.where(distance < 8, distance, 8 + farther) + jnp.where(offset > 0, 16, 0)


def diagonal_onehot(count):
    places = jnp.arange(TILE, dtype=jnp.int32)
    offsets = jnp.concatenate([-places, TILE - places, 0 * places - SEQ, 0 * places + SEQ])
    return (bucket_of(offsets)[:, None] == jnp.arange(count, dtype=jnp.int32)[None, :]).astype(F32)


def dispatch_kernel(slot_ref, rows_ref, out_ref):
    block, tokens = out_ref.shape[0], rows_ref.shape[0]
    ids = lax.broadcasted_iota(jnp.int32, (block, tokens), 0) + pl.program_id(0) * block
    picks = jnp.where(slot_ref[...] == ids, 1.0, 0.0).astype(BF)
    out_ref[...] = mm(picks, rows_ref[...]).astype(BF)


def dispatch_gate_kernel(experts, capacity, padded, slot_ref, gate_ref, rows_ref, out_ref):
    block, tokens = out_ref.shape[0], rows_ref.shape[0]
    width = out_ref.shape[1]
    step = pl.program_id(0)
    ids = lax.broadcasted_iota(jnp.int32, (block, tokens), 0) + step * block
    picks = jnp.where(slot_ref[...] == ids, 1.0, 0.0).astype(BF)
    out = mm(picks, rows_ref[...])
    gates = jnp.broadcast_to(gate_ref[...].astype(BF), (8, tokens))
    lanes = pl.num_programs(0) * padded
    in_slots = mm_nt(gates, picks)
    in_slots = jnp.concatenate([in_slots, jnp.zeros((8, lanes - block), F32)], axis=1)
    lane = lax.broadcasted_iota(jnp.int32, (8, lanes), 1)
    row = lax.broadcasted_iota(jnp.int32, (block, 1), 0)
    left = out[:, :lanes]
    for expert in range(experts):
        shift = lax.rem(step * padded - expert * padded + lanes, lanes)
        moved = pltpu.roll(in_slots, shift, 1)
        mine = (lane >= step * padded) & (lane < step * padded + capacity)
        moved = jnp.where(mine, moved, 0.0)[:1]
        left = jnp.where(row == expert * padded + capacity, moved, left)
    out_ref[:, :lanes] = left.astype(BF)
    out_ref[:, lanes:] = out[:, lanes:].astype(BF)


def dispatch(slot_row, rows, blocks, block, gate=None):
    tokens, width = rows.shape
    grid_spec = dict(
        grid=(blocks,),
        out_specs=pl.BlockSpec((block, width), lambda k: (k, 0)),
        out_shape=jax.ShapeDtypeStruct((blocks * block, width), BF),
    )
    line = pl.BlockSpec((1, tokens), lambda k: (0, 0))
    full = pl.BlockSpec((tokens, width), lambda k: (0, 0))
    cost = pl.CostEstimate(
        flops=2 * blocks * block * tokens * width,
        bytes_accessed=2 * width * (tokens + blocks * block),
        transcendentals=0,
    )
    if gate is None:
        return pl.pallas_call(
            dispatch_kernel, in_specs=[line, full], compiler_params=params(), cost_estimate=cost, **grid_spec
        )(slot_row, rows)
    values, experts, capacity, padded = gate
    return pl.pallas_call(
        functools.partial(dispatch_gate_kernel, experts, capacity, padded),
        in_specs=[line, line, full],
        compiler_params=params(),
        cost_estimate=cost,
        **grid_spec,
    )(slot_row, values, rows)


def qkv_kernel(x_ref, gain_ref, wq_ref, wk_ref, wv_ref, q_ref, k_ref, v_ref):
    rows = x_ref[...].astype(F32)
    inv = lax.rsqrt(jnp.mean(rows * rows, axis=-1, keepdims=True) + EPSILON)
    normed = (rows * inv * gain_ref[...]).astype(BF)
    q_ref[...] = (mm(normed, wq_ref[...]).astype(BF).astype(F32) * HEAD_DIM**-0.5).astype(BF)
    k_ref[...] = mm(normed, wk_ref[...]).astype(BF)
    v_ref[...] = mm(normed, wv_ref[...]).astype(BF)


def qkv(x, gain, wq, wk, wv):
    tokens, width = x.shape
    rows = pl.BlockSpec((SEQ, width), lambda t: (t, 0))
    square = pl.BlockSpec((width, width), lambda t: (0, 0))
    one = pl.BlockSpec((1, width), lambda t: (0, 0))
    return pl.pallas_call(
        qkv_kernel,
        grid=(tokens // SEQ,),
        in_specs=[rows, one, square, square, square],
        out_specs=[rows] * 3,
        out_shape=[jax.ShapeDtypeStruct((tokens, width), BF)] * 3,
        compiler_params=params(),
        cost_estimate=pl.CostEstimate(
            flops=6 * tokens * width * width, bytes_accessed=8 * tokens * width, transcendentals=0
        ),
    )(x, gain, wq, wk, wv)


def fill_bias(lines_ref, bias_ref):
    upper_right = lax.broadcasted_iota(jnp.int32, (TILE, TILE), 0) <= lax.broadcasted_iota(
        jnp.int32, (TILE, TILE), 1
    )
    tiles = SEQ // TILE
    for head in range(2):

        def sheared(line):
            whole = jnp.broadcast_to(lines_ref[head, line : line + 1, :], (TILE, TILE))
            return pltpu.roll(whole, 0, 1, stride=1, stride_axis=0)

        negative, positive = sheared(0), sheared(1)
        far_negative = jnp.broadcast_to(lines_ref[head, 2:3, :], (TILE, TILE))
        far_positive = jnp.broadcast_to(lines_ref[head, 3:4, :], (TILE, TILE))
        same = jnp.where(upper_right, negative, positive)
        above = jnp.where(upper_right, positive, far_positive)
        below = jnp.where(upper_right, far_negative, negative)
        for key in range(tiles):
            for query in range(tiles):
                gap = key - query
                tile = (
                    same
                    if gap == 0
                    else above
                    if gap == 1
                    else below
                    if gap == -1
                    else far_positive
                    if gap > 0
                    else far_negative
                )
                bias_ref[head, pl.ds(key * TILE, TILE), pl.ds(query * TILE, TILE)] = tile


def head_lanes(head):
    lane = lax.broadcasted_iota(jnp.int32, (1, PAIR), 1)
    return (lane >= head * HEAD_DIM) & (lane < (head + 1) * HEAD_DIM)


def only(head, array):
    return jnp.where(head_lanes(head), array, jnp.zeros_like(array))


def attention_kernel(
    lines_ref, sent_ref, q_ref, k_ref, v_ref, o_ref, lse_ref, came_ref, bias_ref, local_sem, send_sem, recv_sem
):
    pair, seq = pl.program_id(0), pl.program_id(1)
    blocks = sent_ref.shape[0]
    me = lax.axis_index("exp")

    def there(block):
        return {"exp": flipped(me, block)}

    def outgoing(block):
        return pltpu.make_async_remote_copy(
            src_ref=sent_ref.at[block],
            dst_ref=came_ref.at[:, block],
            send_sem=send_sem.at[block],
            recv_sem=recv_sem.at[block],
            device_id=there(block),
            device_id_type=pl.DeviceIdType.MESH,
        )

    own = pltpu.make_async_copy(sent_ref.at[0], came_ref.at[:, 0], local_sem)

    @pl.when((pair == 0) & (seq == 0))
    def _():
        barrier = pltpu.get_barrier_semaphore()
        for block in range(1, blocks):
            pl.semaphore_signal(
                barrier, inc=1, device_id=there(block), device_id_type=pl.DeviceIdType.MESH
            )
        pl.semaphore_wait(barrier, blocks - 1)
        own.start()
        for block in range(1, blocks):
            outgoing(block).start()

    @pl.when(seq == 0)
    def _():
        fill_bias(lines_ref, bias_ref)

    keys = k_ref[...]
    values_t = v_ref[...].T
    masked = [only(head, keys) for head in range(2)]
    row = lax.broadcasted_iota(jnp.int32, (PAIR, 1), 0)
    for part in range(SEQ // CHUNK):
        places = pl.ds(part * CHUNK, CHUNK)
        queries = q_ref[places, :]
        out = None
        for head in range(2):
            scores = mm_nt(masked[head], queries) + bias_ref[head, :, places]
            highest = jnp.max(scores, axis=0, keepdims=True)
            weights = jnp.exp(scores - highest)
            total = jnp.sum(weights, axis=0, keepdims=True)
            lse_ref[0, 0, head : head + 1, places] = highest + jnp.log(total)
            mixed = mm(values_t, weights.astype(BF)) * (1.0 / total)
            out = mixed if out is None else jnp.where(row < HEAD_DIM, out, mixed)
        o_ref[places, :] = out.T.astype(BF)

    @pl.when((pair == pl.num_programs(0) - 1) & (seq == pl.num_programs(1) - 1))
    def _():
        own.wait()
        for block in range(1, blocks):
            outgoing(block).wait()


def attention(lines, sent, q, k, v):
    blocks, experts, padded, width = sent.shape
    tokens, width = q.shape
    seqs, pairs = tokens // SEQ, width // PAIR
    block = pl.BlockSpec((SEQ, PAIR), lambda h, s: (s, h))
    return pl.pallas_call(
        attention_kernel,
        grid=(pairs, seqs),
        in_specs=[pl.BlockSpec((2, 8, TILE), lambda h, s: (h, 0, 0)), pl.BlockSpec(memory_space=pl.ANY)]
        + [block, block, block],
        out_specs=[block, pl.BlockSpec((1, 1, 2, SEQ), lambda h, s: (h, s, 0, 0))]
        + [pl.BlockSpec(memory_space=pl.ANY)],
        out_shape=[
            jax.ShapeDtypeStruct((tokens, width), BF),
            jax.ShapeDtypeStruct((pairs, seqs, 2, SEQ), F32),
            jax.ShapeDtypeStruct((experts, blocks, padded, width), BF),
        ],
        scratch_shapes=[
            pltpu.VMEM((2, SEQ, SEQ), F32),
            pltpu.SemaphoreType.DMA,
            pltpu.SemaphoreType.DMA((blocks,)),
            pltpu.SemaphoreType.DMA((blocks,)),
        ],
        compiler_params=params(collective_id=1, has_side_effects=True),
        cost_estimate=pl.CostEstimate(
            flops=16 * pairs * seqs * SEQ * SEQ * PAIR,
            bytes_accessed=8 * tokens * width,
            transcendentals=2 * pairs * seqs * SEQ * SEQ,
        ),
    )(lines, sent, q, k, v)


def attention_back_kernel(
    lines_ref, q_ref, k_ref, v_ref, do_ref, lse_ref, dq_ref, dk_ref, dv_ref, sums_ref, bias_ref, diag_ref
):
    seq = pl.program_id(1)

    @pl.when(seq == 0)
    def _():
        fill_bias(lines_ref, bias_ref)
        diag_ref[...] = jnp.zeros_like(diag_ref)

    keys, values = k_ref[...], v_ref[...]
    keys_t = keys.T
    masked_k = [only(head, keys) for head in range(2)]
    masked_v = [only(head, values) for head in range(2)]
    row = lax.broadcasted_iota(jnp.int32, (PAIR, 1), 0)
    grads_k, grads_v = [None, None], [None, None]
    tiles = SEQ // TILE
    for part in range(SEQ // CHUNK):
        places = pl.ds(part * CHUNK, CHUNK)
        queries, upstream = q_ref[places, :], do_ref[places, :]
        grad_q = None
        for head in range(2):
            scores = mm_nt(masked_k[head], queries) + bias_ref[head, :, places]
            weights = jnp.exp(scores - lse_ref[0, 0, head : head + 1, places])
            products = weights * mm_nt(masked_v[head], upstream)
            scores_grad = products - weights * jnp.sum(products, axis=0, keepdims=True)
            low = scores_grad.astype(BF)
            value_term = mm(weights.astype(BF), upstream)
            key_term = mm(low, queries)
            grads_v[head] = value_term if part == 0 else grads_v[head] + value_term
            grads_k[head] = key_term if part == 0 else grads_k[head] + key_term
            query_term = mm(keys_t, low)
            grad_q = query_term if head == 0 else jnp.where(row < HEAD_DIM, grad_q, query_term)
            groups = {}
            for query in range(CHUNK // TILE):
                for key in range(tiles):
                    gap = key - (query + part * (CHUNK // TILE))
                    kind = 0 if gap == 0 else 1 if gap == 1 else 2 if gap == -1 else 3 if gap > 0 else 4
                    tile = scores_grad[
                        key * TILE : (key + 1) * TILE, query * TILE : (query + 1) * TILE
                    ]
                    groups[kind] = tile if kind not in groups else groups[kind] + tile
            for kind, tile in groups.items():
                diag_ref[head, kind] += tile
        dq_ref[places, :] = (grad_q * HEAD_DIM**-0.5).T.astype(BF)
    first = head_lanes(0)
    dk_ref[...] = jnp.where(first, grads_k[0], grads_k[1]).astype(BF)
    dv_ref[...] = jnp.where(first, grads_v[0], grads_v[1]).astype(BF)

    @pl.when(seq == pl.num_programs(1) - 1)
    def _():
        upper_right = lax.broadcasted_iota(jnp.int32, (TILE, TILE), 0) <= lax.broadcasted_iota(
            jnp.int32, (TILE, TILE), 1
        )
        sums_ref[...] = jnp.zeros_like(sums_ref)
        for head in range(2):
            same, above, below = diag_ref[head, 0], diag_ref[head, 1], diag_ref[head, 2]

            def gathered(array):
                row_id = lax.broadcasted_iota(jnp.int32, (TILE, 1), 0)
                bit = 1
                while bit < TILE:
                    turned = pltpu.roll(array, TILE - bit, 1)
                    array = jnp.where((row_id & bit) != 0, turned, array)
                    bit *= 2
                return jnp.sum(array, axis=0, keepdims=True)

            zero = jnp.zeros_like(same)
            sums_ref[head, 0:1, :] = gathered(jnp.where(upper_right, same, below))
            sums_ref[head, 1:2, :] = gathered(jnp.where(upper_right, above, same))
            sums_ref[head, 2:3, :] = jnp.sum(
                diag_ref[head, 4] + jnp.where(upper_right, below, zero), axis=0, keepdims=True
            )
            sums_ref[head, 3:4, :] = jnp.sum(
                diag_ref[head, 3] + jnp.where(upper_right, zero, above), axis=0, keepdims=True
            )


def attention_back(lines, q, k, v, do, lse):
    tokens, width = q.shape
    seqs, pairs = tokens // SEQ, width // PAIR
    block = pl.BlockSpec((SEQ, PAIR), lambda h, s: (s, h))
    lines_spec = pl.BlockSpec((2, 8, TILE), lambda h, s: (h, 0, 0))
    return pl.pallas_call(
        attention_back_kernel,
        grid=(pairs, seqs),
        in_specs=[lines_spec, block, block, block, block]
        + [pl.BlockSpec((1, 1, 2, SEQ), lambda h, s: (h, s, 0, 0))],
        out_specs=[block, block, block, lines_spec],
        out_shape=[jax.ShapeDtypeStruct((tokens, width), BF)] * 3
        + [jax.ShapeDtypeStruct((2 * pairs, 8, TILE), F32)],
        scratch_shapes=[pltpu.VMEM((2, SEQ, SEQ), F32), pltpu.VMEM((2, 5, TILE, TILE), F32)],
        compiler_params=params(),
        cost_estimate=pl.CostEstimate(
            flops=40 * pairs * seqs * SEQ * SEQ * PAIR,
            bytes_accessed=14 * tokens * width,
            transcendentals=2 * pairs * seqs * SEQ * SEQ,
        ),
    )(lines, q, k, v, do, lse)


def router_kernel(
    o_ref, x_ref, wo_ref, gain_ref, wr_ref, expert_ref, h_ref, u_ref, probs_ref, gate_ref, line_ref
):
    mixed = x_ref[...].astype(F32) + mm(o_ref[...], wo_ref[...])
    h_ref[...] = mixed
    inv = lax.rsqrt(jnp.mean(mixed * mixed, axis=-1, keepdims=True) + EPSILON)
    normed = mixed * inv * gain_ref[...]
    u_ref[...] = normed.astype(BF)
    logits = jnp.dot(normed, wr_ref[...], precision=FULL_PRECISION, preferred_element_type=F32)
    spread = jnp.exp(logits - jnp.max(logits, axis=-1, keepdims=True))
    probs = spread / jnp.sum(spread, axis=-1, keepdims=True)
    probs_ref[...] = probs
    picked = expert_ref[...] == lax.broadcasted_iota(jnp.int32, probs.shape, 1)
    gate = jnp.sum(jnp.where(picked, probs, 0.0), axis=-1, keepdims=True)
    gate_ref[...] = gate
    size = gate.shape[0]
    diagonal = lax.broadcasted_iota(jnp.int32, (size, size), 0) == lax.broadcasted_iota(
        jnp.int32, (size, size), 1
    )
    line_ref[...] = jnp.sum(jnp.where(diagonal, gate, 0.0), axis=0, keepdims=True)


def router(o, x, wo, gain, wr, expert):
    tokens, width = x.shape
    experts = wr.shape[1]
    size = 256

    def rows(columns):
        return pl.BlockSpec((size, columns), lambda t: (t, 0))

    def whole(*shape):
        return pl.BlockSpec(shape, lambda t: (0, 0))

    return pl.pallas_call(
        router_kernel,
        grid=(tokens // size,),
        in_specs=[rows(width), rows(width), whole(width, width), whole(1, width)]
        + [whole(width, experts), rows(1)],
        out_specs=[rows(width), rows(width), rows(experts), rows(1)]
        + [pl.BlockSpec((1, size), lambda t: (0, t))],
        out_shape=[
            jax.ShapeDtypeStruct((tokens, width), F32),
            jax.ShapeDtypeStruct((tokens, width), BF),
            jax.ShapeDtypeStruct((tokens, experts), F32),
            jax.ShapeDtypeStruct((tokens, 1), F32),
            jax.ShapeDtypeStruct((1, tokens), F32),
        ],
        compiler_params=params(),
        cost_estimate=pl.CostEstimate(
            flops=2 * tokens * width * width, bytes_accessed=10 * tokens * width, transcendentals=0
        ),
    )(o, x, wo, gain, wr, expert)


def gelu_and_slope(z):
    square = z * z
    half = 0.5 + 0.5 * jnp.tanh(z * (GELU_A + GELU_B * square))
    value = z * half
    slope = half + 2.0 * value * (1.0 - half) * (GELU_A + 3.0 * GELU_B * square)
    return value, slope


def expert_kernel(
    parts, sent_ref, c_ref, first_ref, second_ref, u_ref, e_ref, d_ref,
    rows_ref, e_sum, d_sum, e_held, d_held, local_sem, send_sem, recv_sem, back_send, back_recv,
):
    expert, step = pl.program_id(0), pl.program_id(1)
    experts, last_step = pl.num_programs(0), pl.num_programs(1) - 1
    blocks, padded, width = rows_ref.shape[1:]
    me = lax.axis_index("exp")
    columns = first_ref.shape[2] // parts

    def there(block):
        return {"exp": flipped(me, block)}

    def outgoing(which, block):
        return pltpu.make_async_remote_copy(
            src_ref=sent_ref.at[block, which],
            dst_ref=rows_ref.at[which, block],
            send_sem=send_sem.at[which, block],
            recv_sem=recv_sem.at[which, block],
            device_id=there(block),
            device_id_type=pl.DeviceIdType.MESH,
        )

    def returning(kind, which, block):
        held, target = (e_held, e_ref) if kind == 0 else (d_held, d_ref)
        return pltpu.make_async_remote_copy(
            src_ref=held.at[which, block],
            dst_ref=target.at[block, which],
            send_sem=back_send.at[kind, which, block],
            recv_sem=back_recv.at[kind, which, block],
            device_id=there(block),
            device_id_type=pl.DeviceIdType.MESH,
        )

    def own_in(which):
        return pltpu.make_async_copy(sent_ref.at[0, which], rows_ref.at[which, 0], local_sem.at[0, which])

    def own_back(kind, which):
        held, target = (e_held, e_ref) if kind == 0 else (d_held, d_ref)
        return pltpu.make_async_copy(
            held.at[which, 0], target.at[0, which], local_sem.at[1 + kind, which]
        )

    def keep(which):
        return pltpu.make_async_copy(rows_ref.at[which], u_ref.at[which], local_sem.at[3, which])

    @pl.when((expert == 0) & (step == 0))
    def _():
        barrier = pltpu.get_barrier_semaphore()
        for block in range(1, blocks):
            pl.semaphore_signal(
                barrier, inc=1, device_id=there(block), device_id_type=pl.DeviceIdType.MESH
            )
        pl.semaphore_wait(barrier, blocks - 1)
        for which in range(rows_ref.shape[0]):
            own_in(which).start()
            for block in range(1, blocks):
                outgoing(which, block).start()

    @pl.when(step == 0)
    def _():
        own_in(expert).wait()
        for block in range(1, blocks):
            outgoing(expert, block).wait_recv()
        keep(expert).start()
        e_sum[...] = jnp.zeros_like(e_sum)
        d_sum[...] = jnp.zeros_like(d_sum)

    rows, upstream = rows_ref[expert].reshape(blocks * padded, width), c_ref[0]
    for part in range(parts):
        places = slice(part * columns, (part + 1) * columns)
        first, second = first_ref[0, :, places], second_ref[0, places, :]
        value, slope = gelu_and_slope(mm(rows, first))
        inner = (mm_nt(upstream, second) * slope).astype(BF)
        e_sum[...] += mm(value.astype(BF), second)
        d_sum[...] += mm_nt(inner, first)

    @pl.when(step == last_step)
    def _():
        e_held[expert] = e_sum[...].astype(BF).reshape(blocks, padded, width)
        d_held[expert] = d_sum[...].astype(BF).reshape(blocks, padded, width)
        for kind in range(2):
            own_back(kind, expert).start()
            for block in range(1, blocks):
                returning(kind, expert, block).start()

    @pl.when((step == last_step) & (expert == experts - 1))
    def _():
        for which in range(rows_ref.shape[0]):
            keep(which).wait()
            for block in range(1, blocks):
                outgoing(which, block).wait_send()
            for kind in range(2):
                own_back(kind, which).wait()
                for block in range(1, blocks):
                    returning(kind, which, block).wait()


def expert_pass(sent, c, w_in, w_out):
    blocks, experts, padded, width = sent.shape
    hidden = w_in.shape[2]
    size = 768
    rows = blocks * padded
    anywhere = pl.BlockSpec(memory_space=pl.ANY)
    return pl.pallas_call(
        functools.partial(expert_kernel, 3),
        grid=(experts, hidden // size),
        in_specs=[
            anywhere,
            pl.BlockSpec((1, rows, width), lambda e, f: (e, 0, 0)),
            pl.BlockSpec((1, width, size), lambda e, f: (e, 0, f)),
            pl.BlockSpec((1, size, width), lambda e, f: (e, f, 0)),
        ],
        out_specs=[anywhere] * 3,
        out_shape=[
            jax.ShapeDtypeStruct((experts, blocks, padded, width), BF),
            jax.ShapeDtypeStruct(sent.shape, BF),
            jax.ShapeDtypeStruct(sent.shape, BF),
        ],
        scratch_shapes=[
            pltpu.VMEM((experts, blocks, padded, width), BF),
            pltpu.VMEM((rows, width), F32),
            pltpu.VMEM((rows, width), F32),
            pltpu.VMEM((experts, blocks, padded, width), BF),
            pltpu.VMEM((experts, blocks, padded, width), BF),
            pltpu.SemaphoreType.DMA((4, experts)),
            pltpu.SemaphoreType.DMA((experts, blocks)),
            pltpu.SemaphoreType.DMA((experts, blocks)),
            pltpu.SemaphoreType.DMA((2, experts, blocks)),
            pltpu.SemaphoreType.DMA((2, experts, blocks)),
        ],
        compiler_params=params(collective_id=0, has_side_effects=True),
        cost_estimate=pl.CostEstimate(
            flops=8 * experts * rows * width * hidden,
            bytes_accessed=4 * experts * width * (hidden + 2 * rows),
            transcendentals=experts * rows * hidden,
        ),
    )(sent, c, w_in, w_out)


def finish_kernel(steps, place_ref, *refs):
    ins, outs, (a_out, b_out) = refs[:steps], refs[steps : 2 * steps], refs[2 * steps :]
    for step in range(steps):

        @pl.when(pl.program_id(0) == step)
        def _(step=step):
            a_out[0] = ins[step][...].astype(F32)
            b_out[0] = outs[step][...].astype(F32)


def finish(places, ins, outs):
    steps = len(ins)
    width, size = ins[0].shape

    def whole(*shape):
        return pl.BlockSpec(shape, lambda e, p: (0, 0))

    def spec(*shape):
        return pl.BlockSpec((1,) + shape, lambda e, p: (p[e], 0, 0))

    return pl.pallas_call(
        functools.partial(finish_kernel, steps),
        grid_spec=pltpu.PrefetchScalarGridSpec(
            num_scalar_prefetch=1,
            grid=(steps,),
            in_specs=[whole(width, size)] * steps + [whole(size, width)] * steps,
            out_specs=[spec(width, size), spec(size, width)],
        ),
        out_shape=[
            jax.ShapeDtypeStruct((steps, width, size), F32),
            jax.ShapeDtypeStruct((steps, size, width), F32),
        ],
        compiler_params=params(),
    )(places, *ins, *outs)


def tail_kernel(parts, sources, experts, capacity, padded, *refs):
    u_refs, refs = refs[:sources], refs[sources:]
    c_refs, refs = refs[:sources], refs[sources:]
    (
        first_ref, second_ref, dense_o, dense_qkv, small_ref,
        own_in_ref, own_out_ref, came_in_ref, came_out_ref, dense_ref, total_ref,
        rows_u, rows_c, first_held, second_held, first_t, in_sum, out_sum, far_in, far_out, own_in, own_out,
        dense, dense_came, dense_over_dp, small, small_came,
        rows_sem, weight_sem, load_sem, far_send, far_recv, own_sem,
        half_send, half_recv, over_send, over_recv, back_send, back_recv, small_send, small_recv, keep_sem,
    ) = refs
    rows, width = rows_u.shape[2:]
    size = in_sum.shape[0]
    columns = size // parts
    exp_me, dp_me = lax.axis_index("exp"), lax.axis_index("dp")
    exp_bits, dp_bits = half_send.shape[2], over_send.shape[0]
    group, pair = dp_me % 2, dp_me // 2
    mesh_id = pl.DeviceIdType.MESH

    def exp_peer(bit):
        return {"exp": flipped(exp_me, 1 << bit)}

    def dp_peer(bit):
        return {"dp": flipped(dp_me, 1 << bit)}

    chain = dense.shape[0] // 2
    bits = list(range(exp_bits))
    split = 1 + (exp_bits - 1) // 2
    orders = (bits, bits[:1] + bits[split:] + bits[1:split])

    def region(which, depth):
        start = which * chain
        for level in range(depth):
            start = start + (exp_me // (1 << orders[which][level])) % 2 * (chain >> (level + 1))
        return pl.ds(pl.multiple_of(start, 16), chain >> depth)

    def other_half(which, depth):
        start = which * chain
        for level in range(depth):
            start = start + (exp_me // (1 << orders[which][level])) % 2 * (chain >> (level + 1))
        start = start + (1 - (exp_me // (1 << orders[which][depth])) % 2) * (chain >> (depth + 1))
        return pl.ds(pl.multiple_of(start, 16), chain >> (depth + 1))

    def came(which, depth):
        return pl.ds(which * chain + chain - (chain >> depth), chain >> (depth + 1))

    def columns_of(side):
        return pl.ds(side * (width // 2), width // 2)

    def halving(side, which, depth):
        return pltpu.make_async_remote_copy(
            src_ref=dense.at[other_half(which, depth), columns_of(side)],
            dst_ref=dense_came.at[came(which, depth), columns_of(side)],
            send_sem=half_send.at[side, which, depth],
            recv_sem=half_recv.at[side, which, depth],
            device_id=exp_peer(orders[which][depth]),
            device_id_type=mesh_id,
        )

    def over(side, which, bit):
        mine = dense.at[region(which, exp_bits), columns_of(side)]
        return pltpu.make_async_remote_copy(
            src_ref=mine if bit == 0 else dense_over_dp.at[1, bit - 1, side, which],
            dst_ref=dense_over_dp.at[0, bit, side, which],
            send_sem=over_send.at[bit, side, which],
            recv_sem=over_recv.at[bit, side, which],
            device_id=dp_peer(dp_bits - 1 - bit),
            device_id_type=mesh_id,
        )

    def keeping(side, which):
        return pltpu.make_async_copy(
            dense_over_dp.at[1, dp_bits - 1, side, which],
            dense_ref.at[region(which, exp_bits), columns_of(side)],
            keep_sem.at[side, which],
        )

    def returning(side, which, depth):
        place = dense_ref.at[region(which, depth + 1), columns_of(side)]
        return pltpu.make_async_remote_copy(
            src_ref=place,
            dst_ref=place,
            send_sem=back_send.at[side, which, depth],
            recv_sem=back_recv.at[side, which, depth],
            device_id=exp_peer(orders[which][depth]),
            device_id_type=mesh_id,
        )

    def small_copy(depth):
        return pltpu.make_async_remote_copy(
            src_ref=small.at[depth],
            dst_ref=small_came.at[depth],
            send_sem=small_send.at[depth],
            recv_sem=small_recv.at[depth],
            device_id=exp_peer(depth) if depth < exp_bits else dp_peer(depth - exp_bits),
            device_id_type=mesh_id,
        )

    def loads():
        return [
            pltpu.make_async_copy(dense_o, dense.at[pl.ds(3 * width, width)], load_sem.at[0]),
            pltpu.make_async_copy(dense_qkv, dense.at[pl.ds(0, 3 * width)], load_sem.at[1]),
            pltpu.make_async_copy(small_ref, small.at[0], load_sem.at[2]),
        ]

    def add_small(depth):
        small_copy(depth).wait_recv()
        small[depth + 1] = small[depth] + small_came[depth]

    def begin(side):
        if side == 0:
            for load in loads():
                load.wait()
            small_copy(0).start()
        for which in range(2):
            halving(side, which, 0).start()

    def halve(depth):
        def act(side):
            for which in range(2):
                halving(side, which, depth).wait_recv()
                place, new, here = region(which, depth + 1), came(which, depth), columns_of(side)
                dense[place, here] = (
                    dense[place, here].astype(F32) + dense_came[new, here].astype(F32)
                ).astype(BF)
                if depth + 1 < exp_bits:
                    halving(side, which, depth + 1).start()
                else:
                    over(side, which, 0).start()
            if side == 0:
                add_small(depth)
                small_copy(depth + 1).start()

        return act

    def sum_over(bit):
        def act(side):
            for which in range(2):
                over(side, which, bit).wait_recv()
                if bit == 0:
                    mine = dense[region(which, exp_bits), columns_of(side)]
                else:
                    mine = dense_over_dp[1, bit - 1, side, which]
                dense_over_dp[1, bit, side, which] = (
                    mine.astype(F32) + dense_over_dp[0, bit, side, which].astype(F32)
                ).astype(BF)
                if bit + 1 < dp_bits:
                    over(side, which, bit + 1).start()
                else:
                    keeping(side, which).start()
            if side == 0:
                add_small(exp_bits + bit)
                if bit + 1 < dp_bits:
                    small_copy(exp_bits + bit + 1).start()
            if bit + 1 == dp_bits:
                for which in range(2):
                    keeping(side, which).wait()
                    returning(side, which, exp_bits - 1).start()

        return act

    def give_back(depth):
        def act(side):
            for which in range(2):
                returning(side, which, depth).wait_recv()
                if depth > 0:
                    returning(side, which, depth - 1).start()

        return act

    stages = [begin] + [halve(depth) for depth in range(exp_bits)]
    stages += [sum_over(bit) for bit in range(dp_bits)]
    stages += [give_back(depth) for depth in reversed(range(exp_bits))]
    stages = [functools.partial(stage, side) for stage in stages for side in range(2)]

    steps, turns = 2 * experts, 2 * experts * sources

    def rows_copy(source, expert):
        return [
            pltpu.make_async_copy(
                u_refs[source].at[expert],
                rows_u.at[source, expert],
                rows_sem.at[0, source, expert],
            ),
            pltpu.make_async_copy(
                c_refs[source].at[expert], rows_c.at[source, expert], rows_sem.at[1, source, expert]
            ),
        ]

    def weight_copy(step):
        far = step < experts
        expert = group * experts + step % experts
        place = (pair * 2 + jnp.where(far, 1 - group, group)) * size
        place = pl.ds(pl.multiple_of(place, 128), size)
        slot = step % 2
        return [
            pltpu.make_async_copy(
                first_ref.at[expert, :, place], first_held.at[slot], weight_sem.at[0, slot]
            ),
            pltpu.make_async_copy(
                second_ref.at[expert, place, :], second_held.at[slot], weight_sem.at[1, slot]
            ),
        ]

    far_parts = far_send.shape[2]

    def far_copy(index):
        expert, kind, part = index // (2 * far_parts), index % 2, index // 2 % far_parts
        held, target = ((far_in, came_in_ref), (far_out, came_out_ref))[kind]
        lines = held.shape[1] // far_parts
        place = pl.ds(part * lines, lines)
        return pltpu.make_async_remote_copy(
            src_ref=held.at[expert, place],
            dst_ref=target.at[expert, place],
            send_sem=far_send.at[expert, kind, part],
            recv_sem=far_recv.at[expert, kind, part],
            device_id=dp_peer(0),
            device_id_type=mesh_id,
        )

    def own_copy(expert):
        return [
            pltpu.make_async_copy(held.at[expert], target.at[expert], own_sem.at[kind, expert])
            for kind, (held, target) in enumerate(((own_in, own_in_ref), (own_out, own_out_ref)))
        ]

    for load in loads():
        load.start()
    for copy in weight_copy(0):
        copy.start()
    for expert in reversed(range(experts)):
        for source in range(sources):
            for copy in rows_copy(source, expert):
                copy.start()
    barrier = pltpu.get_barrier_semaphore()
    for bit in range(exp_bits):
        pl.semaphore_signal(barrier, inc=1, device_id=exp_peer(bit), device_id_type=mesh_id)
    for bit in range(dp_bits):
        pl.semaphore_signal(barrier, inc=1, device_id=dp_peer(bit), device_id_type=mesh_id)
    pl.semaphore_wait(barrier, exp_bits + dp_bits)

    places = [0, 0] + [2 + index + 2 * max(0, index // 2 - 2) for index in range(len(stages) - 2)]
    places = [place for place in places if place < turns]
    starts = {5: 2, 8: 3, 9: 4, 12: 5, 13: 6, 15: 7}
    starts = {place: index for place, index in starts.items() if place < turns}
    pieces = 2 * far_parts * experts

    def turn(at, carry):
        step, source = at // sources, at % sources
        expert, slot = step % experts, step % 2
        for place, stage in zip(places, stages):
            pl.when(at == place)(stage)
        for place, index in starts.items():
            pl.when(at == place)(far_copy(index).start)

        @pl.when(source == 0)
        def _():
            for copy in weight_copy(step):
                copy.wait()

            @pl.when(step + 1 < steps)
            def _():
                for copy in weight_copy(step + 1):
                    copy.start()

            first_t[...] = first_held[slot].T

        for each_expert in range(experts):
            for each in range(sources):

                @pl.when(at == each_expert * sources + each)
                def _(each=each, each_expert=each_expert):
                    for copy in rows_copy(each, each_expert):
                        copy.wait()

        inputs, upstream = rows_u[source, expert], rows_c[source, expert]
        gate = jnp.zeros((1, rows), F32)
        for block in range(rows // padded):
            place = block * padded + capacity
            gate = gate + inputs[place : place + 1, :rows].astype(F32)
        for part in range(parts):
            here = slice(part * columns, (part + 1) * columns)
            value, slope = gelu_and_slope(mm_nt(first_t[here, :], inputs))
            inner = (mm_nt(second_held[slot, here, :], upstream) * (slope * gate)).astype(BF)
            in_term = mm(inner, inputs)
            out_term = mm((value * gate).astype(BF), upstream)
            fresh = source == 0
            in_sum[here, :] = jnp.where(fresh, 0.0, in_sum[here, :]) + in_term
            out_sum[here, :] = jnp.where(fresh, 0.0, out_sum[here, :]) + out_term

        for each in range(experts):

            @pl.when((source == sources - 1) & (step == each))
            def _(each=each):
                far_in[each] = in_sum[...].T.astype(BF)
                far_out[each] = out_sum[...].astype(BF)
                if each == 0:
                    for index in range(2):
                        far_copy(index).start()

            @pl.when((source == sources - 1) & (step == experts + each))
            def _(each=each):
                own_in[each] = in_sum[...].T.astype(BF)
                own_out[each] = out_sum[...].astype(BF)
                for copy in own_copy(each):
                    copy.start()

        return carry

    lax.fori_loop(0, turns, turn, 0)
    for index in range(2 + len(starts), pieces):
        far_copy(index).start()
    for stage in stages[len(places) :]:
        stage()
    total_ref[...] = small[exp_bits + dp_bits]
    for index in range(pieces):
        far_copy(index).wait()
    for expert in range(experts):
        for copy in own_copy(expert):
            copy.wait()
    for side in range(2):
        for which in range(2):
            for depth in range(exp_bits):
                halving(side, which, depth).wait_send()
                returning(side, which, depth).wait_send()
            for bit in range(dp_bits):
                over(side, which, bit).wait_send()
    for depth in range(exp_bits + dp_bits):
        small_copy(depth).wait_send()


def tail(us, cs, w_in, w_out, size, dense_o, dense_qkv, small, capacity, padded, exp_n):
    sources = len(us)
    experts, rows, width = us[0].shape
    far_parts = 4
    exp_bits, dp_bits = exp_n.bit_length() - 1, sources.bit_length() - 1
    lines = 4 * width
    anywhere = pl.BlockSpec(memory_space=pl.ANY)
    dma = pltpu.SemaphoreType.DMA
    return pl.pallas_call(
        functools.partial(tail_kernel, 3, sources, experts, capacity, padded),
        in_specs=[anywhere] * (2 * sources + 5),
        out_specs=[anywhere] * 5 + [pl.BlockSpec(memory_space=pltpu.VMEM)],
        out_shape=[
            jax.ShapeDtypeStruct((experts, width, size), BF),
            jax.ShapeDtypeStruct((experts, size, width), BF),
            jax.ShapeDtypeStruct((experts, width, size), BF),
            jax.ShapeDtypeStruct((experts, size, width), BF),
            jax.ShapeDtypeStruct((lines, width), BF),
            jax.ShapeDtypeStruct(small.shape, F32),
        ],
        scratch_shapes=[
            pltpu.VMEM((sources, experts, rows, width), BF),
            pltpu.VMEM((sources, experts, rows, width), BF),
            pltpu.VMEM((2, width, size), BF),
            pltpu.VMEM((2, size, width), BF),
            pltpu.VMEM((size, width), BF),
            pltpu.VMEM((size, width), F32),
            pltpu.VMEM((size, width), F32),
            pltpu.VMEM((experts, width, size), BF),
            pltpu.VMEM((experts, size, width), BF),
            pltpu.VMEM((experts, width, size), BF),
            pltpu.VMEM((experts, size, width), BF),
            pltpu.VMEM((lines, width), BF),
            pltpu.VMEM((lines, width), BF),
            pltpu.VMEM((2, dp_bits, 2, 2, lines // 2 >> exp_bits, width // 2), BF),
            pltpu.VMEM((exp_bits + dp_bits + 1,) + small.shape, F32),
            pltpu.VMEM((exp_bits + dp_bits,) + small.shape, F32),
            dma((2, sources, experts)),
            dma((2, 2)),
            dma((3,)),
            dma((experts, 2, far_parts)),
            dma((experts, 2, far_parts)),
            dma((2, experts)),
            dma((2, 2, exp_bits)),
            dma((2, 2, exp_bits)),
            dma((dp_bits, 2, 2)),
            dma((dp_bits, 2, 2)),
            dma((2, 2, exp_bits)),
            dma((2, 2, exp_bits)),
            dma((exp_bits + dp_bits,)),
            dma((exp_bits + dp_bits,)),
            dma((2, 2)),
        ],
        compiler_params=pltpu.CompilerParams(
            vmem_limit_bytes=58 * 2**20, collective_id=2, has_side_effects=True
        ),
        cost_estimate=pl.CostEstimate(flops=0, bytes_accessed=2**16, transcendentals=0),
    )(*us, *cs, w_in, w_out, dense_o, dense_qkv, small)


def combine_kernel(
    slot_ref, expert_ref, gate_ref, probs_ref, h_ref, c_ref, o_ref, e_ref, d_ref, wo_ref, wr_ref, gain_ref,
    mixed_ref, dh_ref, do_ref, wo_ref_out, wr_sum, gain_sum, wo_sum,
):
    step = pl.program_id(0)
    tokens, slots = slot_ref.shape[0], e_ref.shape[0]
    picks = jnp.where(
        slot_ref[...] == lax.broadcasted_iota(jnp.int32, (tokens, slots), 1), 1.0, 0.0
    ).astype(BF)
    returned, arrived = mm(picks, e_ref[...]), mm(picks, d_ref[...])
    gate, probs, mixed = gate_ref[...], probs_ref[...], h_ref[...]
    upstream = c_ref[...].astype(F32)
    mixed_ref[...] = (mixed + gate * returned).astype(BF)
    gate_grad = jnp.sum(upstream * returned, axis=-1, keepdims=True)
    picked = jnp.where(expert_ref[...] == lax.broadcasted_iota(jnp.int32, probs.shape, 1), 1.0, 0.0)
    logit_grad = gate_grad * gate * (picked - probs)
    inv = lax.rsqrt(jnp.mean(mixed * mixed, axis=-1, keepdims=True) + EPSILON)
    unit = mixed * inv
    gain = gain_ref[...]
    normed_grad = (
        lax.dot_general(
            logit_grad,
            wr_ref[...],
            (((1,), (1,)), ((), ())),
            precision=FULL_PRECISION,
            preferred_element_type=F32,
        )
        + gate * arrived
    )
    unit_grad = normed_grad * gain
    mixed_grad = upstream + inv * (
        unit_grad - unit * jnp.mean(unit_grad * unit, axis=-1, keepdims=True)
    )
    dh_ref[...] = mixed_grad
    low = mixed_grad.astype(BF)
    do_ref[...] = mm_nt(low, wo_ref[...]).astype(BF)

    @pl.when(step == 0)
    def _():
        wo_sum[...] = jnp.zeros_like(wo_sum)
        wr_sum[...] = jnp.zeros_like(wr_sum)
        gain_sum[...] = jnp.zeros_like(gain_sum)

    wo_sum[...] += mm(o_ref[...].T, low)
    wr_sum[...] += jnp.dot(
        logit_grad.T, unit * gain, precision=FULL_PRECISION, preferred_element_type=F32
    )
    gain_sum[...] += jnp.sum(normed_grad * unit, axis=0, keepdims=True)

    @pl.when(step == pl.num_programs(0) - 1)
    def _():
        wo_ref_out[...] = wo_sum[...].astype(BF)


def combine(slot, expert, gate, probs, h, c, o, e_out, du, wo, wr, gain):
    tokens, width = h.shape
    slots, experts = e_out.shape[0], wr.shape[1]
    size = 256

    def rows(columns):
        return pl.BlockSpec((size, columns), lambda t: (t, 0))

    def whole(*shape):
        return pl.BlockSpec(shape, lambda t: (0, 0))

    return pl.pallas_call(
        combine_kernel,
        grid=(tokens // size,),
        in_specs=[rows(1), rows(1), rows(1), rows(experts), rows(width), rows(width), rows(width)]
        + [whole(slots, width), whole(slots, width), whole(width, width), whole(width, experts)]
        + [whole(1, width)],
        out_specs=[rows(width), rows(width), rows(width), whole(width, width), whole(experts, width)]
        + [whole(1, width)],
        out_shape=[
            jax.ShapeDtypeStruct((tokens, width), BF),
            jax.ShapeDtypeStruct((tokens, width), F32),
            jax.ShapeDtypeStruct((tokens, width), BF),
            jax.ShapeDtypeStruct((width, width), BF),
            jax.ShapeDtypeStruct((experts, width), F32),
            jax.ShapeDtypeStruct((1, width), F32),
        ],
        scratch_shapes=[pltpu.VMEM((width, width), F32)],
        compiler_params=params(),
        cost_estimate=pl.CostEstimate(
            flops=4 * tokens * width * (slots + width),
            bytes_accessed=16 * tokens * width + 4 * slots * width,
            transcendentals=0,
        ),
    )(slot, expert, gate, probs, h, c, o, e_out, du, wo, wr, gain)


def last_kernel(
    x_ref, dh_ref, dq_ref, dk_ref, dv_ref, wq_ref, wk_ref, wv_ref, gain_ref,
    grad_ref, sums_ref, gain_sum, q_sum, k_sum, v_sum,
):
    step = pl.program_id(0)
    width = x_ref.shape[1]

    @pl.when(step == 0)
    def _():
        for total in (q_sum, k_sum, v_sum, gain_sum):
            total[...] = jnp.zeros_like(total)

    rows = x_ref[...].astype(F32)
    inv = lax.rsqrt(jnp.mean(rows * rows, axis=-1, keepdims=True) + EPSILON)
    unit = rows * inv
    gain = gain_ref[...]
    normed_t = (unit * gain).astype(BF).T
    normed_grad = None
    for grad_ref_in, weight_ref, total in (
        (dq_ref, wq_ref, q_sum),
        (dk_ref, wk_ref, k_sum),
        (dv_ref, wv_ref, v_sum),
    ):
        grad = grad_ref_in[...]
        total[...] += mm(normed_t, grad)
        term = mm_nt(grad, weight_ref[...])
        normed_grad = term if normed_grad is None else normed_grad + term
    unit_grad = normed_grad * gain
    grad_ref[...] = dh_ref[...] + inv * (
        unit_grad - unit * jnp.mean(unit_grad * unit, axis=-1, keepdims=True)
    )
    gain_sum[...] += jnp.sum(normed_grad * unit, axis=0, keepdims=True)

    @pl.when(step == pl.num_programs(0) - 1)
    def _():
        for which, total in enumerate((q_sum, k_sum, v_sum)):
            sums_ref[which * width : (which + 1) * width, :] = total[...].astype(BF)


def last(x, dh, dq, dk, dv, wq, wk, wv, gain):
    tokens, width = x.shape
    size = 256
    rows = pl.BlockSpec((size, width), lambda t: (t, 0))
    square = pl.BlockSpec((width, width), lambda t: (0, 0))
    one = pl.BlockSpec((1, width), lambda t: (0, 0))
    return pl.pallas_call(
        last_kernel,
        grid=(tokens // size,),
        in_specs=[rows] * 5 + [square] * 3 + [one],
        out_specs=[rows, pl.BlockSpec((3 * width, width), lambda t: (0, 0)), one],
        out_shape=[
            jax.ShapeDtypeStruct((tokens, width), F32),
            jax.ShapeDtypeStruct((3 * width, width), BF),
            jax.ShapeDtypeStruct((1, width), F32),
        ],
        scratch_shapes=[pltpu.VMEM((width, width), F32)] * 3,
        compiler_params=params(),
        cost_estimate=pl.CostEstimate(
            flops=12 * tokens * width * width, bytes_accessed=16 * tokens * width, transcendentals=0
        ),
    )(x, dh, dq, dk, dv, wq, wk, wv, gain)


def per_device(
    tokens,
    w_query,
    w_key,
    w_value,
    w_output,
    norm_attn,
    norm_ffn,
    relative_bias_table,
    w_router,
    w_in,
    w_out,
    expert_index,
    priority,
    cotangent,
):
    tok_rows, width = tokens.shape
    local = w_in.shape[0]
    exp_n, dp_n = lax.axis_size("exp"), lax.axis_size("dp")
    exp_me, dp_me = lax.axis_index("exp"), lax.axis_index("dp")
    all_experts = local * exp_n
    capacity = (5 * tok_rows + 4 * all_experts - 1) // (4 * all_experts)
    padded = (capacity + 1 + 15) // 16 * 16
    block = local * padded
    buckets = relative_bias_table.shape[0]

    chosen = expert_index[:, 0]
    order = priority[0]
    ahead = (chosen[:, None] == chosen[None, :]) & (order[None, :] < order[:, None])
    rank = jnp.sum(ahead.astype(jnp.int32), axis=1)
    place = ((chosen // local) ^ exp_me) * block + (chosen % local) * padded + rank
    slots = jnp.where(rank < capacity, place, -1)
    slot_row, slot_column = slots[None, :], slots[:, None]

    half = local // 2
    group = dp_me % 2

    def over_dp(mine, other):
        pieces = [mine]
        for step in range(1, dp_n):
            pairs = [(i, i ^ step) for i in range(dp_n)]
            pieces.append(lax.ppermute(other if step % 2 else mine, "dp", pairs))
        return pieces

    def groups(rows, start, count):
        return (
            lax.dynamic_slice_in_dim(rows, group * half + start, count, 0),
            lax.dynamic_slice_in_dim(rows, (1 - group) * half + start, count, 0),
        )

    lines = jnp.dot(
        relative_bias_table.T, diagonal_onehot(buckets).T, precision=FULL_PRECISION
    ).reshape(HEADS, 4, TILE)
    lines = jnp.concatenate([lines, jnp.zeros_like(lines)], axis=1)
    gain_attn, gain_ffn = norm_attn[None, :], norm_ffn[None, :]
    q, k, v = qkv(tokens, gain_attn, w_query, w_key, w_value)
    c_sent = dispatch(slot_row, cotangent, exp_n, block).reshape(exp_n, local, padded, width)
    context, lse, c_rows = attention(lines, c_sent, q, k, v)
    c_rows = c_rows.reshape(local, exp_n * padded, width)
    c_all = over_dp(*groups(c_rows, 0, half))
    mixed, u, probs, gate, gate_row = router(
        context, tokens, w_output, gain_ffn, w_router, expert_index
    )
    sent = dispatch(slot_row, u, exp_n, block, gate=(gate_row, local, capacity, padded))
    u_rows, e_back, d_back = expert_pass(
        sent.reshape(exp_n, local, padded, width), c_rows, w_in, w_out
    )
    e_back, *c_all = lax.optimization_barrier((e_back, *c_all))
    e_back, d_back = e_back.reshape(exp_n * block, width), d_back.reshape(exp_n * block, width)
    u_rows = u_rows.reshape(local, exp_n * padded, width)
    u_all = over_dp(*groups(u_rows, 0, half))
    mixed_out, mixed_grad, context_grad, output_part, router_part, norm_ffn_part = combine(
        slot_column, expert_index, gate, probs, mixed, cotangent, context,
        e_back, d_back, w_output, w_router, gain_ffn,
    )
    query_grad, key_grad, value_grad, sums = attention_back(lines, q, k, v, context_grad, lse)
    size = w_in.shape[2] // dp_n
    table_part = jnp.dot(
        diagonal_onehot(buckets).T,
        sums[:, :4].reshape(HEADS, 4 * TILE).T,
        precision=FULL_PRECISION,
    )
    grad_tokens, qkv_part, norm_attn_part = last(
        tokens, mixed_grad, query_grad, key_grad, value_grad, w_query, w_key, w_value, gain_attn
    )

    table_line = jnp.pad(table_part.reshape(1, -1), ((0, 0), (0, width - table_part.size)))
    small = jnp.concatenate([router_part, norm_attn_part, norm_ffn_part, table_line], axis=0)
    small = jnp.pad(small, ((0, -small.shape[0] % 8), (0, 0)))
    own_in, own_out, came_in, came_out, dense, total = tail(
        u_all, c_all, w_in, w_out, size, output_part, qkv_part, small, capacity, padded, exp_n
    )
    experts = jnp.arange(local, dtype=jnp.int32)
    grad_in, grad_out = finish(
        jnp.where(group == 0, experts, (experts + half) % local),
        list(own_in) + list(came_in),
        list(own_out) + list(came_out),
    )
    dense = dense.reshape(4, width, width).astype(F32)
    return (
        mixed_out,
        grad_tokens,
        dense[0],
        dense[1],
        dense[2],
        dense[3],
        total[all_experts],
        total[all_experts + 1],
        total[all_experts + 2, : table_part.size].reshape(table_part.shape),
        total[:all_experts].T,
        grad_in,
        grad_out,
    )


def solution(mesh):
    return jax.shard_map(
        per_device,
        mesh=mesh,
        in_specs=(
            P(("exp", "dp"), None),
            P(),
            P(),
            P(),
            P(),
            P(),
            P(),
            P(),
            P(),
            P("exp", None, None),
            P("exp", None, None),
            P(("exp", "dp"), None),
            P(("exp", "dp"), None),
            P(("exp", "dp"), None),
        ),
        out_specs=(
            P(("exp", "dp"), None),
            P(("exp", "dp"), None),
            P(),
            P(),
            P(),
            P(),
            P(),
            P(),
            P(),
            P(),
            P("exp", None, "dp"),
            P("exp", "dp", None),
        ),
        check_vma=False,
    )
```

```python
import functools

import jax
import jax.numpy as jnp
from jax import lax
from jax.experimental import pallas as pl
from jax.experimental.pallas import tpu as pltpu
from jax.sharding import PartitionSpec as P

HEADS = 12
HEAD_DIM = 64
SEQ = 512
LIMITS = (12, 16, 23, 32, 46, 64, 91)
EPSILON = 1e-06
FULL_PRECISION = lax.Precision.HIGHEST
BF = jnp.bfloat16
F32 = jnp.float32
PAIR = 2 * HEAD_DIM
TILE = 128
CHUNK = 256
GELU_A = 0.7978845608028654
GELU_B = 0.044715 * GELU_A
VMEM_MIB = 58
NO_COST = pl.CostEstimate(flops=0, bytes_accessed=2**16, transcendentals=0)


def params(**more):
    return pltpu.CompilerParams(vmem_limit_bytes=VMEM_MIB * 2**20, **more)


def mm(left, right):
    return jnp.dot(left, right, preferred_element_type=F32)


def mm_nt(left, right):
    return lax.dot_general(left, right, (((1,), (1,)), ((), ())), preferred_element_type=F32)


def flipped(index, step):
    bit = 1
    while bit <= step:
        if step & bit:
            index = index + bit * (1 - 2 * ((index // bit) % 2))
        bit *= 2
    return index


def greet(me, blocks, others=()):
    barrier = pltpu.get_barrier_semaphore()
    devices = [{"exp": flipped(me, block)} for block in range(1, blocks)] + list(others)
    for device in devices:
        pl.semaphore_signal(barrier, inc=1, device_id=device, device_id_type=pl.DeviceIdType.MESH)
    pl.semaphore_wait(barrier, len(devices))


def spread(me, sent, expert, came, sems, index):
    local_sem, send_sem, recv_sem = sems
    copies = [pltpu.make_async_copy(sent.at[0, expert], came.at[0], local_sem.at[index])]
    for block in range(1, came.shape[0]):
        copies.append(
            pltpu.make_async_remote_copy(
                src_ref=sent.at[block, expert],
                dst_ref=came.at[block],
                send_sem=send_sem.at[index, block],
                recv_sem=recv_sem.at[index, block],
                device_id={"exp": flipped(me, block)},
                device_id_type=pl.DeviceIdType.MESH,
            )
        )
    return copies


def spread_sems(count, blocks):
    dma = pltpu.SemaphoreType.DMA
    return [dma((count,)), dma((count, blocks)), dma((count, blocks))]


def halves(array):
    high = array.astype(BF)
    return high, (array - high.astype(F32)).astype(BF)


def as_column(line):
    size = line.shape[1]
    diagonal = lax.broadcasted_iota(jnp.int32, (size, size), 0) == lax.broadcasted_iota(
        jnp.int32, (size, size), 1
    )
    return jnp.sum(jnp.where(diagonal, line, 0.0), axis=1, keepdims=True)


def bucket_of(offset):
    distance = jnp.abs(offset)
    farther = jnp.zeros_like(distance)
    for limit in LIMITS:
        farther = farther + (distance >= limit).astype(jnp.int32)
    return jnp.where(distance < 8, distance, 8 + farther) + jnp.where(offset > 0, 16, 0)


def diagonal_onehot(count):
    places = jnp.arange(TILE, dtype=jnp.int32)
    offsets = jnp.concatenate([-places, TILE - places, 0 * places - SEQ, 0 * places + SEQ])
    return (bucket_of(offsets)[:, None] == jnp.arange(count, dtype=jnp.int32)[None, :]).astype(F32)


def dispatch_kernel(slot_ref, rows_ref, out_ref):
    block, tokens = out_ref.shape[0], rows_ref.shape[0]
    ids = lax.broadcasted_iota(jnp.int32, (block, tokens), 0) + pl.program_id(0) * block
    picks = jnp.where(slot_ref[...] == ids, 1.0, 0.0).astype(BF)
    out_ref[...] = mm(picks, rows_ref[...]).astype(BF)


def dispatch_gate_kernel(experts, capacity, padded, slot_ref, gate_ref, rows_ref, out_ref):
    block, tokens = out_ref.shape[0], rows_ref.shape[0]
    width = out_ref.shape[1]
    step = pl.program_id(0)
    ids = lax.broadcasted_iota(jnp.int32, (block, tokens), 0) + step * block
    picks = jnp.where(slot_ref[...] == ids, 1.0, 0.0).astype(BF)
    out = mm(picks, rows_ref[...])
    gates = jnp.broadcast_to(gate_ref[...].astype(BF), (8, tokens))
    lanes = pl.num_programs(0) * padded
    in_slots = mm_nt(gates, picks)
    in_slots = jnp.concatenate([in_slots, jnp.zeros((8, lanes - block), F32)], axis=1)
    lane = lax.broadcasted_iota(jnp.int32, (8, lanes), 1)
    row = lax.broadcasted_iota(jnp.int32, (block, 1), 0)
    left = out[:, :lanes]
    for expert in range(experts):
        shift = lax.rem(step * padded - expert * padded + lanes, lanes)
        moved = pltpu.roll(in_slots, shift, 1)
        mine = (lane >= step * padded) & (lane < step * padded + capacity)
        moved = jnp.where(mine, moved, 0.0)[:1]
        left = jnp.where(row == expert * padded + capacity, moved, left)
    out_ref[:, :lanes] = left.astype(BF)
    out_ref[:, lanes:] = out[:, lanes:].astype(BF)


def dispatch(slot_row, rows, blocks, block, gate=None):
    tokens, width = rows.shape
    grid_spec = dict(
        grid=(blocks,),
        out_specs=pl.BlockSpec((block, width), lambda k: (k, 0)),
        out_shape=jax.ShapeDtypeStruct((blocks * block, width), BF),
    )
    line = pl.BlockSpec((1, tokens), lambda k: (0, 0))
    full = pl.BlockSpec((tokens, width), lambda k: (0, 0))
    cost = NO_COST
    if gate is None:
        return pl.pallas_call(
            dispatch_kernel, in_specs=[line, full], compiler_params=params(), cost_estimate=cost, **grid_spec
        )(slot_row, rows)
    values, experts, capacity, padded = gate
    return pl.pallas_call(
        functools.partial(dispatch_gate_kernel, experts, capacity, padded),
        in_specs=[line, line, full],
        compiler_params=params(),
        cost_estimate=cost,
        **grid_spec,
    )(slot_row, values, rows)


def qkv_kernel(x_ref, gain_ref, wq_ref, wk_ref, wv_ref, q_ref, k_ref, v_ref):
    rows = x_ref[...].astype(F32)
    inv = lax.rsqrt(jnp.mean(rows * rows, axis=-1, keepdims=True) + EPSILON)
    normed = (rows * inv * gain_ref[...]).astype(BF)
    q_ref[...] = (mm(normed, wq_ref[...]).astype(BF).astype(F32) * HEAD_DIM**-0.5).astype(BF)
    k_ref[...] = mm(normed, wk_ref[...]).astype(BF)
    v_ref[...] = mm(normed, wv_ref[...]).astype(BF)


def qkv(x, gain, wq, wk, wv):
    tokens, width = x.shape
    rows = pl.BlockSpec((SEQ, width), lambda t: (t, 0))
    square = pl.BlockSpec((width, width), lambda t: (0, 0))
    one = pl.BlockSpec((1, width), lambda t: (0, 0))
    return pl.pallas_call(
        qkv_kernel,
        grid=(tokens // SEQ,),
        in_specs=[rows, one, square, square, square],
        out_specs=[rows] * 3,
        out_shape=[jax.ShapeDtypeStruct((tokens, width), BF)] * 3,
        compiler_params=params(),
        cost_estimate=NO_COST,
    )(x, gain, wq, wk, wv)


def fill_bias(lines_ref, bias_ref):
    upper_right = lax.broadcasted_iota(jnp.int32, (TILE, TILE), 0) <= lax.broadcasted_iota(
        jnp.int32, (TILE, TILE), 1
    )
    tiles = SEQ // TILE
    for head in range(2):

        def sheared(line):
            whole = jnp.broadcast_to(lines_ref[head, line : line + 1, :], (TILE, TILE))
            return pltpu.roll(whole, 0, 1, stride=1, stride_axis=0)

        negative, positive = sheared(0), sheared(1)
        far_negative = jnp.broadcast_to(lines_ref[head, 2:3, :], (TILE, TILE))
        far_positive = jnp.broadcast_to(lines_ref[head, 3:4, :], (TILE, TILE))
        same = jnp.where(upper_right, negative, positive)
        above = jnp.where(upper_right, positive, far_positive)
        below = jnp.where(upper_right, far_negative, negative)
        for key in range(tiles):
            for query in range(tiles):
                gap = key - query
                tile = (
                    same
                    if gap == 0
                    else above
                    if gap == 1
                    else below
                    if gap == -1
                    else far_positive
                    if gap > 0
                    else far_negative
                )
                bias_ref[head, pl.ds(key * TILE, TILE), pl.ds(query * TILE, TILE)] = tile


def head_lanes(head):
    lane = lax.broadcasted_iota(jnp.int32, (1, PAIR), 1)
    return (lane >= head * HEAD_DIM) & (lane < (head + 1) * HEAD_DIM)


def only(head, array):
    return jnp.where(head_lanes(head), array, jnp.zeros_like(array))


def attention_kernel(
    lines_ref, sent_ref, q_ref, k_ref, v_ref, o_ref, lse_ref, came_ref, bias_ref, local_sem, send_sem, recv_sem
):
    pair, seq = pl.program_id(0), pl.program_id(1)
    blocks = sent_ref.shape[0]
    me = lax.axis_index("exp")

    def there(block):
        return {"exp": flipped(me, block)}

    def outgoing(block):
        return pltpu.make_async_remote_copy(
            src_ref=sent_ref.at[block],
            dst_ref=came_ref.at[:, block],
            send_sem=send_sem.at[block],
            recv_sem=recv_sem.at[block],
            device_id=there(block),
            device_id_type=pl.DeviceIdType.MESH,
        )

    own = pltpu.make_async_copy(sent_ref.at[0], came_ref.at[:, 0], local_sem)

    @pl.when((pair == 0) & (seq == 0))
    def _():
        barrier = pltpu.get_barrier_semaphore()
        for block in range(1, blocks):
            pl.semaphore_signal(
                barrier, inc=1, device_id=there(block), device_id_type=pl.DeviceIdType.MESH
            )
        pl.semaphore_wait(barrier, blocks - 1)
        own.start()
        for block in range(1, blocks):
            outgoing(block).start()

    @pl.when(seq == 0)
    def _():
        fill_bias(lines_ref, bias_ref)

    keys = k_ref[...]
    values_t = v_ref[...].T
    masked = [only(head, keys) for head in range(2)]
    row = lax.broadcasted_iota(jnp.int32, (PAIR, 1), 0)
    for part in range(SEQ // CHUNK):
        places = pl.ds(part * CHUNK, CHUNK)
        queries = q_ref[places, :]
        out = None
        for head in range(2):
            scores = mm_nt(masked[head], queries) + bias_ref[head, :, places]
            highest = jnp.max(scores, axis=0, keepdims=True)
            weights = jnp.exp(scores - highest)
            total = jnp.sum(weights, axis=0, keepdims=True)
            lse_ref[0, 0, head : head + 1, places] = highest + jnp.log(total)
            mixed = mm(values_t, weights.astype(BF)) * (1.0 / total)
            out = mixed if out is None else jnp.where(row < HEAD_DIM, out, mixed)
        o_ref[places, :] = out.T.astype(BF)

    @pl.when((pair == pl.num_programs(0) - 1) & (seq == pl.num_programs(1) - 1))
    def _():
        own.wait()
        for block in range(1, blocks):
            outgoing(block).wait()


def attention(lines, sent, q, k, v):
    blocks, experts, padded, width = sent.shape
    tokens, width = q.shape
    seqs, pairs = tokens // SEQ, width // PAIR
    block = pl.BlockSpec((SEQ, PAIR), lambda h, s: (s, h))
    return pl.pallas_call(
        attention_kernel,
        grid=(pairs, seqs),
        in_specs=[pl.BlockSpec((2, 8, TILE), lambda h, s: (h, 0, 0)), pl.BlockSpec(memory_space=pl.ANY)]
        + [block, block, block],
        out_specs=[block, pl.BlockSpec((1, 1, 2, SEQ), lambda h, s: (h, s, 0, 0))]
        + [pl.BlockSpec(memory_space=pl.ANY)],
        out_shape=[
            jax.ShapeDtypeStruct((tokens, width), BF),
            jax.ShapeDtypeStruct((pairs, seqs, 2, SEQ), F32),
            jax.ShapeDtypeStruct((experts, blocks, padded, width), BF),
        ],
        scratch_shapes=[
            pltpu.VMEM((2, SEQ, SEQ), F32),
            pltpu.SemaphoreType.DMA,
            pltpu.SemaphoreType.DMA((blocks,)),
            pltpu.SemaphoreType.DMA((blocks,)),
        ],
        compiler_params=params(collective_id=1, has_side_effects=True),
        cost_estimate=NO_COST,
    )(lines, sent, q, k, v)


def attention_back_kernel(parts, swaps, lines_ref, q_ref, k_ref, v_ref, do_ref, lse_ref, *refs):
    sent_refs, swap_refs, refs = refs[:parts], refs[parts : parts + swaps], refs[parts + swaps :]
    dq_ref, dk_ref, dv_ref, sums_ref = refs[:4]
    came_refs, got_refs, refs = refs[4 : 4 + parts], refs[4 + parts : 4 + parts + swaps], refs[4 + parts + swaps :]
    bias_ref, diag_ref, *sems = refs
    sems, swap_send, swap_recv = sems[:3], sems[3], sems[4]
    pair, seq = pl.program_id(0), pl.program_id(1)
    blocks, expert = came_refs[0].shape[0], sent_refs[0].shape[1] - 1
    me = lax.axis_index("exp")
    partner = {"dp": flipped(lax.axis_index("dp"), 1)}

    def transfers():
        copies = []
        for index in range(swaps):
            copies.append(
                pltpu.make_async_remote_copy(
                    src_ref=swap_refs[index],
                    dst_ref=got_refs[index],
                    send_sem=swap_send.at[index],
                    recv_sem=swap_recv.at[index],
                    device_id=partner,
                    device_id_type=pl.DeviceIdType.MESH,
                )
            )
        for part in range(parts):
            copies += spread(me, sent_refs[part], expert, came_refs[part], sems, part)
        return copies

    @pl.when((pair == 0) & (seq == 0))
    def _():
        greet(me, blocks, [partner])
        for copy in transfers():
            copy.start()

    @pl.when((pair == pl.num_programs(0) - 1) & (seq == pl.num_programs(1) - 1))
    def _():
        for copy in transfers():
            copy.wait()

    @pl.when(seq == 0)
    def _():
        fill_bias(lines_ref, bias_ref)
        diag_ref[...] = jnp.zeros_like(diag_ref)

    keys, values = k_ref[...], v_ref[...]
    keys_t = keys.T
    masked_k = [only(head, keys) for head in range(2)]
    masked_v = [only(head, values) for head in range(2)]
    row = lax.broadcasted_iota(jnp.int32, (PAIR, 1), 0)
    grads_k, grads_v = [None, None], [None, None]
    tiles = SEQ // TILE
    for part in range(SEQ // CHUNK):
        places = pl.ds(part * CHUNK, CHUNK)
        queries, upstream = q_ref[places, :], do_ref[places, :]
        grad_q = None
        for head in range(2):
            scores = mm_nt(masked_k[head], queries) + bias_ref[head, :, places]
            weights = jnp.exp(scores - lse_ref[0, 0, head : head + 1, places])
            products = weights * mm_nt(masked_v[head], upstream)
            scores_grad = products - weights * jnp.sum(products, axis=0, keepdims=True)
            low = scores_grad.astype(BF)
            value_term = mm(weights.astype(BF), upstream)
            key_term = mm(low, queries)
            grads_v[head] = value_term if part == 0 else grads_v[head] + value_term
            grads_k[head] = key_term if part == 0 else grads_k[head] + key_term
            query_term = mm(keys_t, low)
            grad_q = query_term if head == 0 else jnp.where(row < HEAD_DIM, grad_q, query_term)
            groups = {}
            for query in range(CHUNK // TILE):
                for key in range(tiles):
                    gap = key - (query + part * (CHUNK // TILE))
                    kind = 0 if gap == 0 else 1 if gap == 1 else 2 if gap == -1 else 3 if gap > 0 else 4
                    tile = scores_grad[
                        key * TILE : (key + 1) * TILE, query * TILE : (query + 1) * TILE
                    ]
                    groups[kind] = tile if kind not in groups else groups[kind] + tile
            for kind, tile in groups.items():
                diag_ref[head, kind] += tile
        dq_ref[places, :] = (grad_q * HEAD_DIM**-0.5).T.astype(BF)
    first = head_lanes(0)
    dk_ref[...] = jnp.where(first, grads_k[0], grads_k[1]).astype(BF)
    dv_ref[...] = jnp.where(first, grads_v[0], grads_v[1]).astype(BF)

    @pl.when(seq == pl.num_programs(1) - 1)
    def _():
        upper_right = lax.broadcasted_iota(jnp.int32, (TILE, TILE), 0) <= lax.broadcasted_iota(
            jnp.int32, (TILE, TILE), 1
        )
        sums_ref[...] = jnp.zeros_like(sums_ref)
        for head in range(2):
            same, above, below = diag_ref[head, 0], diag_ref[head, 1], diag_ref[head, 2]

            def gathered(array):
                row_id = lax.broadcasted_iota(jnp.int32, (TILE, 1), 0)
                bit = 1
                while bit < TILE:
                    turned = pltpu.roll(array, TILE - bit, 1)
                    array = jnp.where((row_id & bit) != 0, turned, array)
                    bit *= 2
                return jnp.sum(array, axis=0, keepdims=True)

            zero = jnp.zeros_like(same)
            sums_ref[head, 0:1, :] = gathered(jnp.where(upper_right, same, below))
            sums_ref[head, 1:2, :] = gathered(jnp.where(upper_right, above, same))
            sums_ref[head, 2:3, :] = jnp.sum(
                diag_ref[head, 4] + jnp.where(upper_right, below, zero), axis=0, keepdims=True
            )
            sums_ref[head, 3:4, :] = jnp.sum(
                diag_ref[head, 3] + jnp.where(upper_right, zero, above), axis=0, keepdims=True
            )


def attention_back(lines, q, k, v, do, lse, sent, swapped):
    parts, swaps = len(sent), len(swapped)
    blocks, _, padded, _ = sent[0].shape
    anywhere = pl.BlockSpec(memory_space=pl.ANY)
    tokens, width = q.shape
    seqs, pairs = tokens // SEQ, width // PAIR
    block = pl.BlockSpec((SEQ, PAIR), lambda h, s: (s, h))
    lines_spec = pl.BlockSpec((2, 8, TILE), lambda h, s: (h, 0, 0))
    return pl.pallas_call(
        functools.partial(attention_back_kernel, parts, swaps),
        grid=(pairs, seqs),
        in_specs=[lines_spec, block, block, block, block]
        + [pl.BlockSpec((1, 1, 2, SEQ), lambda h, s: (h, s, 0, 0))]
        + [anywhere] * (parts + swaps),
        out_specs=[block, block, block, lines_spec] + [anywhere] * (parts + swaps),
        out_shape=[jax.ShapeDtypeStruct((tokens, width), BF)] * 3
        + [jax.ShapeDtypeStruct((2 * pairs, 8, TILE), F32)]
        + [jax.ShapeDtypeStruct((blocks, padded, width), BF)] * parts
        + [jax.ShapeDtypeStruct(array.shape, BF) for array in swapped],
        scratch_shapes=[
            pltpu.VMEM((2, SEQ, SEQ), F32),
            pltpu.VMEM((2, 5, TILE, TILE), F32),
            *spread_sems(parts, blocks),
            pltpu.SemaphoreType.DMA((swaps,)),
            pltpu.SemaphoreType.DMA((swaps,)),
        ],
        compiler_params=params(collective_id=4, has_side_effects=True),
        cost_estimate=NO_COST,
    )(lines, q, k, v, do, lse, *sent, *swapped)


def router_kernel(
    o_ref, x_ref, wo_ref, gain_ref, wr_ref, expert_ref, h_ref, u_ref, probs_ref, gate_ref, line_ref
):
    mixed = x_ref[...].astype(F32) + mm(o_ref[...], wo_ref[...])
    h_ref[...] = mixed
    inv = lax.rsqrt(jnp.mean(mixed * mixed, axis=-1, keepdims=True) + EPSILON)
    normed = mixed * inv * gain_ref[...]
    u_ref[...] = normed.astype(BF)
    high, low = halves(normed)
    wr_high, wr_low = halves(wr_ref[...])
    logits = mm(high, wr_high) + (mm(high, wr_low) + mm(low, wr_high))
    spread = jnp.exp(logits - jnp.max(logits, axis=-1, keepdims=True))
    probs = spread / jnp.sum(spread, axis=-1, keepdims=True)
    probs_ref[...] = probs
    picked = expert_ref[...] == lax.broadcasted_iota(jnp.int32, probs.shape, 1)
    gate = jnp.sum(jnp.where(picked, probs, 0.0), axis=-1, keepdims=True)
    gate_ref[...] = gate
    size = gate.shape[0]
    diagonal = lax.broadcasted_iota(jnp.int32, (size, size), 0) == lax.broadcasted_iota(
        jnp.int32, (size, size), 1
    )
    line_ref[...] = jnp.sum(jnp.where(diagonal, gate, 0.0), axis=0, keepdims=True)


def router(o, x, wo, gain, wr, expert):
    tokens, width = x.shape
    experts = wr.shape[1]
    size = 256

    def rows(columns):
        return pl.BlockSpec((size, columns), lambda t: (t, 0))

    def whole(*shape):
        return pl.BlockSpec(shape, lambda t: (0, 0))

    return pl.pallas_call(
        router_kernel,
        grid=(tokens // size,),
        in_specs=[rows(width), rows(width), whole(width, width), whole(1, width)]
        + [whole(width, experts), rows(1)],
        out_specs=[rows(width), rows(width), rows(experts), rows(1)]
        + [pl.BlockSpec((1, size), lambda t: (0, t))],
        out_shape=[
            jax.ShapeDtypeStruct((tokens, width), F32),
            jax.ShapeDtypeStruct((tokens, width), BF),
            jax.ShapeDtypeStruct((tokens, experts), F32),
            jax.ShapeDtypeStruct((tokens, 1), F32),
            jax.ShapeDtypeStruct((1, tokens), F32),
        ],
        compiler_params=params(),
        cost_estimate=NO_COST,
    )(o, x, wo, gain, wr, expert)


def gelu_and_slope(z):
    square = z * z
    half = 0.5 + 0.5 * jnp.tanh(z * (GELU_A + GELU_B * square))
    value = z * half
    slope = half + 2.0 * value * (1.0 - half) * (GELU_A + 3.0 * GELU_B * square)
    return value, slope


def send_back(me, held, target, which, place, sems, kind):
    send_sem, recv_sem, local_sem = sems
    copies = [pltpu.make_async_copy(held.at[0], target.at[0, which], local_sem.at[kind, place])]
    for block in range(1, held.shape[0]):
        copies.append(
            pltpu.make_async_remote_copy(
                src_ref=held.at[block],
                dst_ref=target.at[block, which],
                send_sem=send_sem.at[kind, place, block],
                recv_sem=recv_sem.at[kind, place, block],
                device_id={"exp": flipped(me, block)},
                device_id_type=pl.DeviceIdType.MESH,
            )
        )
    return copies


def expert_step(parts, rows, upstream, first_ref, second_ref, e_sum, d_sum):
    columns = first_ref.shape[2] // parts
    for part in range(parts):
        places = slice(part * columns, (part + 1) * columns)
        first, second = first_ref[0, :, places], second_ref[0, places, :]
        value, slope = gelu_and_slope(mm(rows, first))
        inner = (mm_nt(upstream, second) * slope).astype(BF)
        e_sum[...] += mm(value.astype(BF), second)
        d_sum[...] += mm_nt(inner, first)


def expert_kernel(
    parts, sent_ref, c_ref, first_ref, second_ref, *refs
):
    expert, step = pl.program_id(0), pl.program_id(1)
    count, last_step = pl.num_programs(0), pl.num_programs(1) - 1
    all_experts = count + 1
    u_refs, u_last, refs = refs[:all_experts], refs[all_experts], refs[all_experts + 1 :]
    e_kept, d_kept, e_ref, d_ref, rows_ref, e_sum, d_sum, e_held, d_held = refs[:9]
    local_sem, send_sem, recv_sem, back_send, back_recv, back_local = refs[9:]
    _, blocks, padded, width = rows_ref.shape
    me = lax.axis_index("exp")
    group, half = lax.axis_index("dp") % 2, all_experts // 2
    sems = (back_send, back_recv, back_local)

    def outgoing(which, block):
        return pltpu.make_async_remote_copy(
            src_ref=sent_ref.at[block, which],
            dst_ref=rows_ref.at[which, block],
            send_sem=send_sem.at[which, block],
            recv_sem=recv_sem.at[which, block],
            device_id={"exp": flipped(me, block)},
            device_id_type=pl.DeviceIdType.MESH,
        )

    def own_in(which):
        return pltpu.make_async_copy(sent_ref.at[0, which], rows_ref.at[which, 0], local_sem.at[0, which])

    def keep(which, act):
        for each in range(2):
            target = u_refs[(which // half + each) % 2 * half + which % half]

            @pl.when(group == each)
            def _(target=target):
                act(pltpu.make_async_copy(rows_ref.at[which], target, local_sem.at[1, which]))

        if which == all_experts - 1:
            act(pltpu.make_async_copy(rows_ref.at[which], u_last, local_sem.at[2, 0]))

    def arrive(which):
        own_in(which).wait()
        for block in range(1, blocks):
            outgoing(which, block).wait_recv()
        keep(which, lambda copy: copy.start())

    def keep_result(which):
        return [
            pltpu.make_async_copy(e_held.at[which], e_kept.at[which - 1], local_sem.at[2, which]),
            pltpu.make_async_copy(d_held.at[which], d_kept.at[which - 1], local_sem.at[3, which]),
        ]

    def back():
        return send_back(me, e_held.at[0], e_ref, 0, 0, sems, 0) + send_back(
            me, d_held.at[0], d_ref, 0, 0, sems, 1
        )

    @pl.when((expert == 0) & (step == 0))
    def _():
        greet(me, blocks)
        for which in range(all_experts):
            own_in(which).start()
            for block in range(1, blocks):
                outgoing(which, block).start()

    @pl.when(step == 0)
    def _():
        for which in range(all_experts - 1):

            @pl.when(expert == which)
            def _(which=which):
                arrive(which)

        e_sum[...] = jnp.zeros_like(e_sum)
        d_sum[...] = jnp.zeros_like(d_sum)

    rows = rows_ref[expert].reshape(blocks * padded, width)
    expert_step(parts, rows, c_ref[0], first_ref, second_ref, e_sum, d_sum)

    @pl.when(step == last_step)
    def _():
        e_held[expert] = e_sum[...].astype(BF).reshape(blocks, padded, width)
        d_held[expert] = d_sum[...].astype(BF).reshape(blocks, padded, width)

        @pl.when(expert == 0)
        def _():
            for copy in back():
                copy.start()

        for which in range(1, all_experts - 1):

            @pl.when(expert == which)
            def _(which=which):
                for copy in keep_result(which):
                    copy.start()

    @pl.when((step == last_step) & (expert == count - 1))
    def _():
        arrive(all_experts - 1)
        for which in range(all_experts):
            keep(which, lambda copy: copy.wait())
            for block in range(1, blocks):
                outgoing(which, block).wait_send()
        for which in range(1, all_experts - 1):
            for copy in keep_result(which):
                copy.wait()
        for copy in back():
            copy.wait()


def expert_rest_kernel(
    parts, kept, u_ref, c_ref, first_ref, second_ref, e_kept, d_kept, e_ref, d_ref,
    e_sum, d_sum, e_held, d_held, back_send, back_recv, back_local,
):
    step, last_step = pl.program_id(0), pl.num_programs(0) - 1
    blocks, padded, width = e_held.shape
    me = lax.axis_index("exp")
    sems = (back_send, back_recv, back_local)

    def back(which):
        e_from, d_from = (e_kept.at[which], d_kept.at[which]) if which < kept else (e_held, d_held)
        return send_back(me, e_from, e_ref, which, which, sems, 0) + send_back(
            me, d_from, d_ref, which, which, sems, 1
        )

    @pl.when(step == 0)
    def _():
        greet(me, blocks)
        for which in range(kept):
            for copy in back(which):
                copy.start()
        e_sum[...] = jnp.zeros_like(e_sum)
        d_sum[...] = jnp.zeros_like(d_sum)

    expert_step(parts, u_ref[...], c_ref[0], first_ref, second_ref, e_sum, d_sum)

    @pl.when(step == last_step)
    def _():
        e_held[...] = e_sum[...].astype(BF).reshape(blocks, padded, width)
        d_held[...] = d_sum[...].astype(BF).reshape(blocks, padded, width)
        for copy in back(kept):
            copy.start()
        for which in range(kept + 1):
            for copy in back(which):
                copy.wait()


def expert_pass(sent, c, w_in, w_out):
    blocks, experts, padded, width = sent.shape
    hidden = w_in.shape[2]
    size = 768
    rows = blocks * padded
    kept = experts - 2
    anywhere = pl.BlockSpec(memory_space=pl.ANY)
    dma = pltpu.SemaphoreType.DMA
    *u_rows, u_last, e_kept, d_kept, e_first, d_first = pl.pallas_call(
        functools.partial(expert_kernel, 3),
        grid=(experts - 1, hidden // size),
        in_specs=[
            anywhere,
            pl.BlockSpec((1, rows, width), lambda e, f: (e, 0, 0)),
            pl.BlockSpec((1, width, size), lambda e, f: (e, 0, f)),
            pl.BlockSpec((1, size, width), lambda e, f: (e, f, 0)),
        ],
        out_specs=[anywhere] * (experts + 5),
        out_shape=[jax.ShapeDtypeStruct((blocks, padded, width), BF)] * (experts + 1)
        + [
            jax.ShapeDtypeStruct((kept, blocks, padded, width), BF),
            jax.ShapeDtypeStruct((kept, blocks, padded, width), BF),
            jax.ShapeDtypeStruct((blocks, 1, padded, width), BF),
            jax.ShapeDtypeStruct((blocks, 1, padded, width), BF),
        ],
        scratch_shapes=[
            pltpu.VMEM((experts, blocks, padded, width), BF),
            pltpu.VMEM((rows, width), F32),
            pltpu.VMEM((rows, width), F32),
            pltpu.VMEM((experts - 1, blocks, padded, width), BF),
            pltpu.VMEM((experts - 1, blocks, padded, width), BF),
            dma((4, experts)),
            dma((experts, blocks)),
            dma((experts, blocks)),
            dma((2, 1, blocks)),
            dma((2, 1, blocks)),
            dma((2, 1)),
        ],
        compiler_params=params(collective_id=0, has_side_effects=True),
        cost_estimate=NO_COST,
    )(sent, c, w_in, w_out)
    u_rows = [part.reshape(rows, width) for part in u_rows]
    last = experts - 1
    e_rest, d_rest = pl.pallas_call(
        functools.partial(expert_rest_kernel, 3, kept),
        grid=(hidden // size,),
        in_specs=[
            pl.BlockSpec((rows, width), lambda f: (0, 0)),
            pl.BlockSpec((1, rows, width), lambda f: (last, 0, 0)),
            pl.BlockSpec((1, width, size), lambda f: (last, 0, f)),
            pl.BlockSpec((1, size, width), lambda f: (last, f, 0)),
            anywhere,
            anywhere,
        ],
        out_specs=[anywhere] * 2,
        out_shape=[jax.ShapeDtypeStruct((blocks, kept + 1, padded, width), BF)] * 2,
        scratch_shapes=[
            pltpu.VMEM((rows, width), F32),
            pltpu.VMEM((rows, width), F32),
            pltpu.VMEM((blocks, padded, width), BF),
            pltpu.VMEM((blocks, padded, width), BF),
            dma((2, kept + 1, blocks)),
            dma((2, kept + 1, blocks)),
            dma((2, kept + 1)),
        ],
        compiler_params=params(collective_id=3, has_side_effects=True),
        cost_estimate=pl.CostEstimate(
            flops=32 * rows * width * hidden, bytes_accessed=4 * width * hidden, transcendentals=0
        ),
    )(u_last.reshape(rows, width), c, w_in, w_out, e_kept, d_kept)
    return u_rows, (e_first, e_rest), (d_first, d_rest)


def weights_kernel(parts, sources, capacity, padded, place_ref, *refs):
    u_refs, c_refs = refs[:sources], refs[sources : 2 * sources]
    first_ref, second_ref, far_in, far_out, in_sum, out_sum = refs[2 * sources :]
    size = first_ref.shape[2]
    rows = u_refs[0].shape[0]
    columns = size // parts
    first_t = first_ref[0].T
    for source in range(sources):
        inputs, upstream = u_refs[source][...], c_refs[source][...].reshape(u_refs[source].shape)
        gate = jnp.zeros((1, rows), F32)
        for block in range(rows // padded):
            place = block * padded + capacity
            gate = gate + inputs[place : place + 1, :rows].astype(F32)
        for part in range(parts):
            places = slice(part * columns, (part + 1) * columns)
            value, slope = gelu_and_slope(mm_nt(first_t[places, :], inputs))
            inner = (mm_nt(second_ref[0, places, :], upstream) * (slope * gate)).astype(BF)
            in_term = mm(inner, inputs)
            out_term = mm((value * gate).astype(BF), upstream)
            if source == 0:
                in_sum[places, :] = in_term
                out_sum[places, :] = out_term
            else:
                in_sum[places, :] += in_term
                out_sum[places, :] += out_term
    far_in[...] = in_sum[...].T.astype(BF)
    far_out[...] = out_sum[...].astype(BF)


def weight_grads(place, us, c_rows, c_far, w_in, w_out, size, capacity, padded):
    sources = len(us)
    rows, width = us[0].shape
    block = pl.BlockSpec((rows, width), lambda f, p: (0, 0))
    return pl.pallas_call(
        functools.partial(weights_kernel, 3, sources, capacity, padded),
        grid_spec=pltpu.PrefetchScalarGridSpec(
            num_scalar_prefetch=1,
            grid=(1,),
            in_specs=[block] * sources
            + [pl.BlockSpec((1, rows, width), lambda f, p: (p[0], 0, 0))]
            + [block] * (sources - 1)
            + [
                pl.BlockSpec((1, width, size), lambda f, p: (p[0], 0, p[1])),
                pl.BlockSpec((1, size, width), lambda f, p: (p[0], p[1], 0)),
            ],
            out_specs=[
                pl.BlockSpec((width, size), lambda f, p: (0, 0)),
                pl.BlockSpec((size, width), lambda f, p: (0, 0)),
            ],
            scratch_shapes=[pltpu.VMEM((size, width), F32)] * 2,
        ),
        out_shape=[
            jax.ShapeDtypeStruct((width, size), BF),
            jax.ShapeDtypeStruct((size, width), BF),
        ],
        compiler_params=params(),
        cost_estimate=NO_COST,
    )(place, *us, c_rows, *c_far, w_in, w_out)


def finish_kernel(half, place_ref, *refs):
    own_in, own_out, refs = refs[0], refs[1], refs[2:]
    came_in, came_out, dense_ref = refs[:half], refs[half : 2 * half], refs[2 * half]
    a_out, b_out, *dense_outs = refs[2 * half + 1 :]
    width = dense_ref.shape[1]
    for step in range(2 * half):

        @pl.when(pl.program_id(0) == step)
        def _(step=step):
            a_out[0] = (own_in[step] if step < half else came_in[step - half][...]).astype(F32)
            b_out[0] = (own_out[step] if step < half else came_out[step - half][...]).astype(F32)
            for which in range(step, 4, 2 * half):
                dense_outs[which][...] = dense_ref[which * width : (which + 1) * width, :].astype(F32)


def finish(places, own_in, own_out, came_in, came_out, dense):
    half, width, size = own_in.shape

    def whole(*shape):
        return pl.BlockSpec(shape, lambda e, p: (0,) * len(shape))

    def spec(*shape):
        return pl.BlockSpec((1,) + shape, lambda e, p: (p[e], 0, 0))

    return pl.pallas_call(
        functools.partial(finish_kernel, half),
        grid_spec=pltpu.PrefetchScalarGridSpec(
            num_scalar_prefetch=1,
            grid=(2 * half,),
            in_specs=[whole(half, width, size), whole(half, size, width)]
            + [whole(width, size)] * half
            + [whole(size, width)] * half
            + [whole(4 * width, width)],
            out_specs=[spec(width, size), spec(size, width)] + [whole(width, width)] * 4,
        ),
        out_shape=[
            jax.ShapeDtypeStruct((2 * half, width, size), F32),
            jax.ShapeDtypeStruct((2 * half, size, width), F32),
        ]
        + [jax.ShapeDtypeStruct((width, width), F32)] * 4,
        compiler_params=params(),
    )(places, own_in, own_out, *came_in, *came_out, dense)


def tail_kernel(parts, sources, experts, capacity, padded, *refs):
    u_refs, refs = refs[: sources * experts], refs[sources * experts :]
    c_own, c_far, refs = refs[0], refs[1 : 1 + (sources - 1) * experts], refs[1 + (sources - 1) * experts :]
    (
        first_ref, second_ref, dense_o, dense_qkv, small_ref,
        own_in_ref, own_out_ref, came_in_ref, came_out_ref, dense_ref, total_ref,
        rows_u, rows_c, first_held, second_held, first_t, in_sum, out_sum, far_in, far_out, own_in, own_out,
        dense, dense_came, dense_over_dp, small, small_came,
        rows_sem, weight_sem, load_sem, far_send, far_recv, own_sem,
        half_send, half_recv, over_send, over_recv, back_send, back_recv, small_send, small_recv, keep_sem,
    ) = refs
    rows, width = rows_u.shape[2:]
    size = in_sum.shape[0]
    columns = size // parts
    exp_me, dp_me = lax.axis_index("exp"), lax.axis_index("dp")
    exp_bits, dp_bits = half_send.shape[2], over_send.shape[0]
    group, pair = dp_me % 2, dp_me // 2
    mesh_id = pl.DeviceIdType.MESH

    def exp_peer(bit):
        return {"exp": flipped(exp_me, 1 << bit)}

    def dp_peer(bit):
        return {"dp": flipped(dp_me, 1 << bit)}

    chain = dense.shape[0] // 2
    bits = list(range(exp_bits))
    split = 1 + (exp_bits - 1) // 2
    orders = (bits, bits[:1] + bits[split:] + bits[1:split])

    def region(which, depth):
        start = which * chain
        for level in range(depth):
            start = start + (exp_me // (1 << orders[which][level])) % 2 * (chain >> (level + 1))
        return pl.ds(pl.multiple_of(start, 16), chain >> depth)

    def other_half(which, depth):
        start = which * chain
        for level in range(depth):
            start = start + (exp_me // (1 << orders[which][level])) % 2 * (chain >> (level + 1))
        start = start + (1 - (exp_me // (1 << orders[which][depth])) % 2) * (chain >> (depth + 1))
        return pl.ds(pl.multiple_of(start, 16), chain >> (depth + 1))

    def came(which, depth):
        return pl.ds(which * chain + chain - (chain >> depth), chain >> (depth + 1))

    def columns_of(side):
        return pl.ds(side * (width // 2), width // 2)

    def halving(side, which, depth):
        return pltpu.make_async_remote_copy(
            src_ref=dense.at[other_half(which, depth), columns_of(side)],
            dst_ref=dense_came.at[came(which, depth), columns_of(side)],
            send_sem=half_send.at[side, which, depth],
            recv_sem=half_recv.at[side, which, depth],
            device_id=exp_peer(orders[which][depth]),
            device_id_type=mesh_id,
        )

    def over(side, which, bit):
        mine = dense.at[region(which, exp_bits), columns_of(side)]
        return pltpu.make_async_remote_copy(
            src_ref=mine if bit == 0 else dense_over_dp.at[1, bit - 1, side, which],
            dst_ref=dense_over_dp.at[0, bit, side, which],
            send_sem=over_send.at[bit, side, which],
            recv_sem=over_recv.at[bit, side, which],
            device_id=dp_peer(dp_bits - 1 - bit),
            device_id_type=mesh_id,
        )

    def keeping(side, which):
        return pltpu.make_async_copy(
            dense_over_dp.at[1, dp_bits - 1, side, which],
            dense_ref.at[region(which, exp_bits), columns_of(side)],
            keep_sem.at[side, which],
        )

    def returning(side, which, depth):
        place = dense_ref.at[region(which, depth + 1), columns_of(side)]
        return pltpu.make_async_remote_copy(
            src_ref=place,
            dst_ref=place,
            send_sem=back_send.at[side, which, depth],
            recv_sem=back_recv.at[side, which, depth],
            device_id=exp_peer(orders[which][depth]),
            device_id_type=mesh_id,
        )

    def small_copy(depth):
        return pltpu.make_async_remote_copy(
            src_ref=small.at[depth],
            dst_ref=small_came.at[depth],
            send_sem=small_send.at[depth],
            recv_sem=small_recv.at[depth],
            device_id=exp_peer(depth) if depth < exp_bits else dp_peer(depth - exp_bits),
            device_id_type=mesh_id,
        )

    def loads():
        return [
            pltpu.make_async_copy(dense_o, dense.at[pl.ds(3 * width, width)], load_sem.at[0]),
            pltpu.make_async_copy(dense_qkv, dense.at[pl.ds(0, 3 * width)], load_sem.at[1]),
            pltpu.make_async_copy(small_ref, small.at[0], load_sem.at[2]),
        ]

    def add_small(depth):
        small_copy(depth).wait_recv()
        small[depth + 1] = small[depth] + small_came[depth]

    def begin(side):
        if side == 0:
            for load in loads():
                load.wait()
            small_copy(0).start()
        for which in range(2):
            halving(side, which, 0).start()

    def halve(depth):
        def act(side):
            for which in range(2):
                halving(side, which, depth).wait_recv()
                place, new, here = region(which, depth + 1), came(which, depth), columns_of(side)
                dense[place, here] = (
                    dense[place, here].astype(F32) + dense_came[new, here].astype(F32)
                ).astype(BF)
                if depth + 1 < exp_bits:
                    halving(side, which, depth + 1).start()
                else:
                    over(side, which, 0).start()
            if side == 0:
                add_small(depth)
                small_copy(depth + 1).start()

        return act

    def sum_over(bit):
        def act(side):
            for which in range(2):
                over(side, which, bit).wait_recv()
                if bit == 0:
                    mine = dense[region(which, exp_bits), columns_of(side)]
                else:
                    mine = dense_over_dp[1, bit - 1, side, which]
                dense_over_dp[1, bit, side, which] = (
                    mine.astype(F32) + dense_over_dp[0, bit, side, which].astype(F32)
                ).astype(BF)
                if bit + 1 < dp_bits:
                    over(side, which, bit + 1).start()
                else:
                    keeping(side, which).start()
            if side == 0:
                add_small(exp_bits + bit)
                if bit + 1 < dp_bits:
                    small_copy(exp_bits + bit + 1).start()
            if bit + 1 == dp_bits:
                for which in range(2):
                    keeping(side, which).wait()
                    returning(side, which, exp_bits - 1).start()

        return act

    def give_back(depth):
        def act(side):
            for which in range(2):
                returning(side, which, depth).wait_recv()
                if depth > 0:
                    returning(side, which, depth - 1).start()

        return act

    stages = [begin] + [halve(depth) for depth in range(exp_bits)]
    stages += [sum_over(bit) for bit in range(dp_bits)]
    stages += [give_back(depth) for depth in reversed(range(exp_bits))]
    stages = [functools.partial(stage, side) for stage in stages for side in range(2)]

    steps, turns = 1 + experts, (1 + experts) * sources

    def rows_copy(source, expert):
        if source == 0:
            c_from = c_own.at[group * experts + expert]
        else:
            c_from = c_far[expert * (sources - 1) + source - 1]
        return [
            pltpu.make_async_copy(
                u_refs[expert * sources + source],
                rows_u.at[source, expert],
                rows_sem.at[0, source, expert],
            ),
            pltpu.make_async_copy(
                c_from, rows_c.at[source, expert], rows_sem.at[1, source, expert]
            ),
        ]

    def weight_copy(step):
        far = step == 0
        expert = group * experts + jnp.where(far, experts - 1, step - 1)
        place = (pair * 2 + jnp.where(far, 1 - group, group)) * size
        place = pl.ds(pl.multiple_of(place, 128), size)
        slot = step % 2
        return [
            pltpu.make_async_copy(
                first_ref.at[expert, :, place], first_held.at[slot], weight_sem.at[0, slot]
            ),
            pltpu.make_async_copy(
                second_ref.at[expert, place, :], second_held.at[slot], weight_sem.at[1, slot]
            ),
        ]

    far_parts = far_send.shape[1]

    def far_copy(index):
        kind, part = index % 2, index // 2
        held, target = ((far_in, came_in_ref), (far_out, came_out_ref))[kind]
        lines = held.shape[0] // far_parts
        place = pl.ds(part * lines, lines)
        return pltpu.make_async_remote_copy(
            src_ref=held.at[place],
            dst_ref=target.at[place],
            send_sem=far_send.at[kind, part],
            recv_sem=far_recv.at[kind, part],
            device_id=dp_peer(0),
            device_id_type=mesh_id,
        )

    def own_copy(expert):
        return [
            pltpu.make_async_copy(held.at[expert], target.at[expert], own_sem.at[kind, expert])
            for kind, (held, target) in enumerate(((own_in, own_in_ref), (own_out, own_out_ref)))
        ]

    for load in loads():
        load.start()
    for copy in weight_copy(0):
        copy.start()
    for expert in reversed(range(experts)):
        for source in range(sources):
            for copy in rows_copy(source, expert):
                copy.start()
    barrier = pltpu.get_barrier_semaphore()
    for bit in range(exp_bits):
        pl.semaphore_signal(barrier, inc=1, device_id=exp_peer(bit), device_id_type=mesh_id)
    for bit in range(dp_bits):
        pl.semaphore_signal(barrier, inc=1, device_id=dp_peer(bit), device_id_type=mesh_id)
    pl.semaphore_wait(barrier, exp_bits + dp_bits)

    places = [0, 0, 1, 2, 3, 4, 5, 6]
    places = [place for place in places if place < turns][: len(stages)]
    starts = {7: 2, 9: 3}
    starts = {place: index for place, index in starts.items() if place < turns}
    pieces = 2 * far_parts

    def turn(at, carry):
        step, source = at // sources, at % sources
        expert, slot = jnp.where(step == 0, experts - 1, step - 1), step % 2
        for place, stage in zip(places, stages):
            pl.when(at == place)(stage)
        for place, index in starts.items():
            pl.when(at == place)(far_copy(index).start)

        @pl.when(source == 0)
        def _():
            for copy in weight_copy(step):
                copy.wait()

            @pl.when(step + 1 < steps)
            def _():
                for copy in weight_copy(step + 1):
                    copy.start()

            first_t[...] = first_held[slot].T

        for each_expert in range(experts):
            for each in range(sources):
                first_step = 0 if each_expert == experts - 1 else each_expert + 1

                @pl.when(at == first_step * sources + each)
                def _(each=each, each_expert=each_expert):
                    for copy in rows_copy(each, each_expert):
                        copy.wait()

        inputs, upstream = rows_u[source, expert], rows_c[source, expert]
        gate = jnp.zeros((1, rows), F32)
        for block in range(rows // padded):
            place = block * padded + capacity
            gate = gate + inputs[place : place + 1, :rows].astype(F32)
        for part in range(parts):
            here = slice(part * columns, (part + 1) * columns)
            value, slope = gelu_and_slope(mm_nt(first_t[here, :], inputs))
            inner = (mm_nt(second_held[slot, here, :], upstream) * (slope * gate)).astype(BF)
            in_term = mm(inner, inputs)
            out_term = mm((value * gate).astype(BF), upstream)
            fresh = source == 0
            in_sum[here, :] = jnp.where(fresh, 0.0, in_sum[here, :]) + in_term
            out_sum[here, :] = jnp.where(fresh, 0.0, out_sum[here, :]) + out_term

        @pl.when((source == sources - 1) & (step == 0))
        def _():
            far_in[...] = in_sum[...].T.astype(BF)
            far_out[...] = out_sum[...].astype(BF)
            for index in range(2):
                far_copy(index).start()

        for each_expert in range(experts):

            @pl.when((source == sources - 1) & (step == each_expert + 1))
            def _(each_expert=each_expert):
                own_in[each_expert] = in_sum[...].T.astype(BF)
                own_out[each_expert] = out_sum[...].astype(BF)
                for copy in own_copy(each_expert):
                    copy.start()

        return carry

    lax.fori_loop(0, turns, turn, 0)
    for stage in stages[len(places) : len(places) + 2]:
        stage()
    for index in range(2 + len(starts), pieces):
        far_copy(index).start()
    for stage in stages[len(places) + 2 :]:
        stage()
    total_ref[...] = small[exp_bits + dp_bits]
    for index in range(pieces):
        far_copy(index).wait()
    for expert in range(experts):
        for copy in own_copy(expert):
            copy.wait()
    for side in range(2):
        for which in range(2):
            for depth in range(exp_bits):
                halving(side, which, depth).wait_send()
                returning(side, which, depth).wait_send()
            for bit in range(dp_bits):
                over(side, which, bit).wait_send()
    for depth in range(exp_bits + dp_bits):
        small_copy(depth).wait_send()


def tail(us, c_rows, c_far, w_in, w_out, size, dense_o, dense_qkv, small, capacity, padded, exp_n):
    sources, experts = len(us[0]), len(us)
    rows, width = us[0][0].shape
    far_parts = 4
    exp_bits, dp_bits = exp_n.bit_length() - 1, sources.bit_length() - 1
    lines = 4 * width
    anywhere = pl.BlockSpec(memory_space=pl.ANY)
    dma = pltpu.SemaphoreType.DMA
    return pl.pallas_call(
        functools.partial(tail_kernel, 3, sources, experts, capacity, padded),
        in_specs=[anywhere] * (experts * (2 * sources - 1) + 6),
        out_specs=[anywhere] * 5 + [pl.BlockSpec(memory_space=pltpu.VMEM)],
        out_shape=[
            jax.ShapeDtypeStruct((experts, width, size), BF),
            jax.ShapeDtypeStruct((experts, size, width), BF),
            jax.ShapeDtypeStruct((width, size), BF),
            jax.ShapeDtypeStruct((size, width), BF),
            jax.ShapeDtypeStruct((lines, width), BF),
            jax.ShapeDtypeStruct(small.shape, F32),
        ],
        scratch_shapes=[
            pltpu.VMEM((sources, experts, rows, width), BF),
            pltpu.VMEM((sources, experts, rows, width), BF),
            pltpu.VMEM((2, width, size), BF),
            pltpu.VMEM((2, size, width), BF),
            pltpu.VMEM((size, width), BF),
            pltpu.VMEM((size, width), F32),
            pltpu.VMEM((size, width), F32),
            pltpu.VMEM((width, size), BF),
            pltpu.VMEM((size, width), BF),
            pltpu.VMEM((experts, width, size), BF),
            pltpu.VMEM((experts, size, width), BF),
            pltpu.VMEM((lines, width), BF),
            pltpu.VMEM((lines, width), BF),
            pltpu.VMEM((2, dp_bits, 2, 2, lines // 2 >> exp_bits, width // 2), BF),
            pltpu.VMEM((exp_bits + dp_bits + 1,) + small.shape, F32),
            pltpu.VMEM((exp_bits + dp_bits,) + small.shape, F32),
            dma((2, sources, experts)),
            dma((2, 2)),
            dma((3,)),
            dma((2, far_parts)),
            dma((2, far_parts)),
            dma((2, experts)),
            dma((2, 2, exp_bits)),
            dma((2, 2, exp_bits)),
            dma((dp_bits, 2, 2)),
            dma((dp_bits, 2, 2)),
            dma((2, 2, exp_bits)),
            dma((2, 2, exp_bits)),
            dma((exp_bits + dp_bits,)),
            dma((exp_bits + dp_bits,)),
            dma((2, 2)),
        ],
        compiler_params=pltpu.CompilerParams(
            vmem_limit_bytes=58 * 2**20, collective_id=2, has_side_effects=True
        ),
        cost_estimate=NO_COST,
    )(*sum(us, []), c_rows, *sum(c_far, []), w_in, w_out, dense_o, dense_qkv, small)


def combine_kernel(
    parts, experts, slot_ref, expert_ref, gate_ref, probs_ref, h_ref, c_ref, o_ref,
    e_first, e_rest, d_first, d_rest, wo_ref, wr_ref, gain_ref, *refs
):
    sent_refs, refs = refs[:parts], refs[parts:]
    mixed_ref, dh_ref, do_ref, wo_ref_out, wr_sum, gain_sum = refs[:6]
    came_refs, refs = refs[6 : 6 + parts * experts], refs[6 + parts * experts :]
    wo_sum, *sems = refs
    step = pl.program_id(0)
    me, blocks = lax.axis_index("exp"), sent_refs[0].shape[0]

    def transfers():
        copies = []
        for expert in range(experts):
            for part in range(parts):
                index = expert * parts + part
                copies += spread(me, sent_refs[part], expert, came_refs[index], sems, index)
        return copies

    @pl.when(step == 0)
    def _():
        greet(me, blocks)
        for copy in transfers():
            copy.start()

    @pl.when(step == pl.num_programs(0) - 1)
    def _():
        for copy in transfers():
            copy.wait()

    tokens, early = slot_ref.shape[1], e_first.shape[0]
    slots = early + e_rest.shape[0]
    slot = as_column(slot_ref[...].astype(F32)).astype(jnp.int32)
    picks = jnp.where(
        slot == lax.broadcasted_iota(jnp.int32, (tokens, slots), 1), 1.0, 0.0
    ).astype(BF)
    returned = mm(picks[:, :early], e_first[...]) + mm(picks[:, early:], e_rest[...])
    arrived = mm(picks[:, :early], d_first[...]) + mm(picks[:, early:], d_rest[...])
    gate, probs, mixed = gate_ref[...], probs_ref[...], h_ref[...]
    upstream = c_ref[...].astype(F32)
    mixed_ref[...] = (mixed + gate * returned).astype(BF)
    gate_grad = jnp.sum(upstream * returned, axis=-1, keepdims=True)
    picked = jnp.where(expert_ref[...] == lax.broadcasted_iota(jnp.int32, probs.shape, 1), 1.0, 0.0)
    logit_grad = gate_grad * gate * (picked - probs)
    inv = lax.rsqrt(jnp.mean(mixed * mixed, axis=-1, keepdims=True) + EPSILON)
    unit = mixed * inv
    gain = gain_ref[...]
    lg_high, lg_low = halves(logit_grad)
    wr_high, wr_low = halves(wr_ref[...])
    through_router = mm_nt(lg_high, wr_high) + (mm_nt(lg_low, wr_high) + mm_nt(lg_high, wr_low))
    normed_grad = through_router + gate * arrived
    unit_grad = normed_grad * gain
    mixed_grad = upstream + inv * (
        unit_grad - unit * jnp.mean(unit_grad * unit, axis=-1, keepdims=True)
    )
    dh_ref[...] = mixed_grad
    low = mixed_grad.astype(BF)
    do_ref[...] = mm_nt(low, wo_ref[...]).astype(BF)

    @pl.when(step == 0)
    def _():
        wo_sum[...] = jnp.zeros_like(wo_sum)
        wr_sum[...] = jnp.zeros_like(wr_sum)
        gain_sum[...] = jnp.zeros_like(gain_sum)

    wo_sum[...] += mm(o_ref[...].T, low)
    n_high, n_low = halves(unit * gain)
    lg_high, lg_low = lg_high.T, lg_low.T
    wr_sum[...] += mm(lg_high, n_high) + (mm(lg_low, n_high) + mm(lg_high, n_low))
    gain_sum[...] += jnp.sum(normed_grad * unit, axis=0, keepdims=True)

    @pl.when(step == pl.num_programs(0) - 1)
    def _():
        wo_ref_out[...] = wo_sum[...].astype(BF)


def combine(slot, expert, gate, probs, h, c, o, e_out, du, wo, wr, gain, sent):
    parts, (blocks, local, padded, _) = len(sent), sent[0].shape
    spreads = parts * (local - 1)
    anywhere = pl.BlockSpec(memory_space=pl.ANY)
    tokens, width = h.shape
    early, rest = (part.shape[0] for part in e_out)
    slots, experts = early + rest, wr.shape[1]
    size = 256

    def rows(columns):
        return pl.BlockSpec((size, columns), lambda t: (t, 0))

    def whole(*shape):
        return pl.BlockSpec(shape, lambda t: (0, 0))

    return pl.pallas_call(
        functools.partial(combine_kernel, parts, local - 1),
        grid=(tokens // size,),
        in_specs=[pl.BlockSpec((1, size), lambda t: (0, t)), rows(1), rows(1), rows(experts), rows(width), rows(width), rows(width)]
        + [whole(early, width), whole(rest, width)] * 2
        + [whole(width, width), whole(width, experts)]
        + [whole(1, width)]
        + [anywhere] * parts,
        out_specs=[rows(width), rows(width), rows(width), whole(width, width), whole(experts, width)]
        + [whole(1, width)]
        + [anywhere] * spreads,
        out_shape=[
            jax.ShapeDtypeStruct((tokens, width), BF),
            jax.ShapeDtypeStruct((tokens, width), F32),
            jax.ShapeDtypeStruct((tokens, width), BF),
            jax.ShapeDtypeStruct((width, width), BF),
            jax.ShapeDtypeStruct((experts, width), F32),
            jax.ShapeDtypeStruct((1, width), F32),
        ]
        + [jax.ShapeDtypeStruct((blocks, padded, width), BF)] * spreads,
        scratch_shapes=[pltpu.VMEM((width, width), F32)] + spread_sems(spreads, blocks),
        compiler_params=params(collective_id=5, has_side_effects=True),
        cost_estimate=NO_COST,
    )(slot, expert, gate, probs, h, c, o, *e_out, *du, wo, wr, gain, *sent)


def last_kernel(
    x_ref, dh_ref, dq_ref, dk_ref, dv_ref, wq_ref, wk_ref, wv_ref, gain_ref,
    grad_ref, sums_ref, gain_sum, q_sum, k_sum, v_sum,
):
    step = pl.program_id(0)
    width = x_ref.shape[1]

    @pl.when(step == 0)
    def _():
        for total in (q_sum, k_sum, v_sum, gain_sum):
            total[...] = jnp.zeros_like(total)

    rows = x_ref[...].astype(F32)
    inv = lax.rsqrt(jnp.mean(rows * rows, axis=-1, keepdims=True) + EPSILON)
    unit = rows * inv
    gain = gain_ref[...]
    normed_t = (unit * gain).astype(BF).T
    normed_grad = None
    for grad_ref_in, weight_ref, total in (
        (dq_ref, wq_ref, q_sum),
        (dk_ref, wk_ref, k_sum),
        (dv_ref, wv_ref, v_sum),
    ):
        grad = grad_ref_in[...]
        total[...] += mm(normed_t, grad)
        term = mm_nt(grad, weight_ref[...])
        normed_grad = term if normed_grad is None else normed_grad + term
    unit_grad = normed_grad * gain
    grad_ref[...] = dh_ref[...] + inv * (
        unit_grad - unit * jnp.mean(unit_grad * unit, axis=-1, keepdims=True)
    )
    gain_sum[...] += jnp.sum(normed_grad * unit, axis=0, keepdims=True)

    @pl.when(step == pl.num_programs(0) - 1)
    def _():
        for which, total in enumerate((q_sum, k_sum, v_sum)):
            sums_ref[which * width : (which + 1) * width, :] = total[...].astype(BF)


def last(x, dh, dq, dk, dv, wq, wk, wv, gain):
    tokens, width = x.shape
    size = 256
    rows = pl.BlockSpec((size, width), lambda t: (t, 0))
    square = pl.BlockSpec((width, width), lambda t: (0, 0))
    one = pl.BlockSpec((1, width), lambda t: (0, 0))
    return pl.pallas_call(
        last_kernel,
        grid=(tokens // size,),
        in_specs=[rows] * 5 + [square] * 3 + [one],
        out_specs=[rows, pl.BlockSpec((3 * width, width), lambda t: (0, 0)), one],
        out_shape=[
            jax.ShapeDtypeStruct((tokens, width), F32),
            jax.ShapeDtypeStruct((3 * width, width), BF),
            jax.ShapeDtypeStruct((1, width), F32),
        ],
        scratch_shapes=[pltpu.VMEM((width, width), F32)] * 3,
        compiler_params=params(),
        cost_estimate=NO_COST,
    )(x, dh, dq, dk, dv, wq, wk, wv, gain)


def per_device(
    tokens,
    w_query,
    w_key,
    w_value,
    w_output,
    norm_attn,
    norm_ffn,
    relative_bias_table,
    w_router,
    w_in,
    w_out,
    expert_index,
    priority,
    cotangent,
):
    tok_rows, width = tokens.shape
    local = w_in.shape[0]
    exp_n, dp_n = lax.axis_size("exp"), lax.axis_size("dp")
    exp_me, dp_me = lax.axis_index("exp"), lax.axis_index("dp")
    all_experts = local * exp_n
    capacity = (5 * tok_rows + 4 * all_experts - 1) // (4 * all_experts)
    padded = (capacity + 1 + 15) // 16 * 16
    block = local * padded
    buckets = relative_bias_table.shape[0]

    chosen = expert_index[:, 0]
    order = priority[0]
    ahead = (chosen[:, None] == chosen[None, :]) & (order[None, :] < order[:, None])
    rank = jnp.sum(ahead.astype(jnp.int32), axis=1)
    place = ((chosen // local) ^ exp_me) * block + (chosen % local) * padded + rank
    slots = jnp.where(rank < capacity, place, -1)
    chunk, inside = slots // block, slots % block
    later = exp_n * padded + chunk * (block - padded) + inside - padded
    returned_slots = jnp.where(inside < padded, chunk * padded + inside, later)
    returned_slots = jnp.where(slots < 0, -1, returned_slots)
    slot_row, returned_row = slots[None, :], returned_slots[None, :]

    half = local // 2
    group = dp_me % 2

    def over_dp(mine, other):
        pieces = [mine]
        for step in range(1, dp_n):
            pairs = [(i, i ^ step) for i in range(dp_n)]
            pieces.append(lax.ppermute(other if step % 2 else mine, "dp", pairs))
        return pieces

    lines = jnp.dot(
        relative_bias_table.T, diagonal_onehot(buckets).T, precision=FULL_PRECISION
    ).reshape(HEADS, 4, TILE)
    lines = jnp.concatenate([lines, jnp.zeros_like(lines)], axis=1)
    gain_attn, gain_ffn = norm_attn[None, :], norm_ffn[None, :]
    q, k, v = qkv(tokens, gain_attn, w_query, w_key, w_value)
    c_sent = dispatch(slot_row, cotangent, exp_n, block).reshape(exp_n, local, padded, width)
    c_far = over_dp(
        lax.dynamic_slice_in_dim(c_sent, group * half, half, 1),
        lax.dynamic_slice_in_dim(c_sent, (1 - group) * half, half, 1),
    )[1:]
    context, lse, c_rows = attention(lines, c_sent, q, k, v)
    c_rows = c_rows.reshape(local, exp_n * padded, width)
    mixed, u, probs, gate, gate_row = router(
        context, tokens, w_output, gain_ffn, w_router, expert_index
    )
    sent = dispatch(slot_row, u, exp_n, block, gate=(gate_row, local, capacity, padded))
    u_rows, e_back, d_back = expert_pass(
        sent.reshape(exp_n, local, padded, width), c_rows, w_in, w_out
    )
    mine, other = u_rows[:half], u_rows[half:]
    mine[0], *c_far = lax.optimization_barrier((mine[0], *c_far))
    u_all = [over_dp(mine[0], other[0])]
    for expert in range(1, half):
        late, *u_all[-1], mine[expert], other[expert] = lax.optimization_barrier(
            (e_back[1], *u_all[-1], mine[expert], other[expert])
        )
        e_back = (e_back[0], late)
        u_all.append(over_dp(mine[expert], other[expert]))
    e_back, d_back = ([part.reshape(-1, width) for part in parts] for parts in (e_back, d_back))
    mixed_out, mixed_grad, context_grad, output_part, router_part, norm_ffn_part, *c_early = combine(
        returned_row, expert_index, gate, probs, mixed, cotangent, context,
        e_back, d_back, w_output, w_router, gain_ffn, c_far,
    )
    size = w_in.shape[2] // dp_n
    rows = exp_n * padded
    c_early = [part.reshape(rows, width) for part in c_early]
    c_spread = [c_early[at : at + dp_n - 1] for at in range(0, len(c_early), dp_n - 1)]
    swapped = []
    for expert in range(half - 1):
        where = jnp.stack([group * half + expert, dp_me // 2 * 2 + 1 - group]).astype(jnp.int32)
        swapped += weight_grads(
            where, u_all[expert], c_rows, c_spread[expert], w_in, w_out, size, capacity, padded
        )
    query_grad, key_grad, value_grad, sums, *moved = attention_back(
        lines, q, k, v, context_grad, lse, c_far, swapped
    )
    c_late, got = moved[: dp_n - 1], moved[dp_n - 1 :]
    c_spread.append([part.reshape(rows, width) for part in c_late])
    table_part = jnp.dot(
        diagonal_onehot(buckets).T,
        sums[:, :4].reshape(HEADS, 4 * TILE).T,
        precision=FULL_PRECISION,
    )
    grad_tokens, qkv_part, norm_attn_part = last(
        tokens, mixed_grad, query_grad, key_grad, value_grad, w_query, w_key, w_value, gain_attn
    )

    table_line = jnp.pad(table_part.reshape(1, -1), ((0, 0), (0, width - table_part.size)))
    small = jnp.concatenate([router_part, norm_attn_part, norm_ffn_part, table_line], axis=0)
    small = jnp.pad(small, ((0, -small.shape[0] % 8), (0, 0)))
    own_in, own_out, came_in, came_out, dense, total = tail(
        u_all, c_rows, c_spread, w_in, w_out, size, output_part, qkv_part, small, capacity, padded, exp_n
    )
    experts = jnp.arange(local, dtype=jnp.int32)
    grad_in, grad_out, *dense_grads = finish(
        jnp.where(group == 0, experts, (experts + half) % local),
        own_in,
        own_out,
        got[0::2] + [came_in],
        got[1::2] + [came_out],
        dense,
    )
    return (
        mixed_out,
        grad_tokens,
        *dense_grads,
        total[all_experts],
        total[all_experts + 1],
        total[all_experts + 2, : table_part.size].reshape(table_part.shape),
        total[:all_experts].T,
        grad_in,
        grad_out,
    )


def solution(mesh):
    return jax.shard_map(
        per_device,
        mesh=mesh,
        in_specs=(
            P(("exp", "dp"), None),
            P(),
            P(),
            P(),
            P(),
            P(),
            P(),
            P(),
            P(),
            P("exp", None, None),
            P("exp", None, None),
            P(("exp", "dp"), None),
            P(("exp", "dp"), None),
            P(("exp", "dp"), None),
        ),
        out_specs=(
            P(("exp", "dp"), None),
            P(("exp", "dp"), None),
            P(),
            P(),
            P(),
            P(),
            P(),
            P(),
            P(),
            P(),
            P("exp", None, "dp"),
            P("exp", "dp", None),
        ),
        check_vma=False,
    )
```

```python
import functools

import jax
import jax.numpy as jnp
from jax import lax
from jax.experimental import pallas as pl
from jax.experimental.pallas import tpu as pltpu
from jax.sharding import PartitionSpec as P

HEADS = 12
HEAD_DIM = 64
SEQ = 512
LIMITS = (12, 16, 23, 32, 46, 64, 91)
EPSILON = 1e-06
FULL_PRECISION = lax.Precision.HIGHEST
BF = jnp.bfloat16
F32 = jnp.float32
PAIR = 2 * HEAD_DIM
TILE = 128
CHUNK = 256
GELU_A = 0.7978845608028654
GELU_B = 0.044715 * GELU_A
VMEM_MIB = 58
NO_COST = pl.CostEstimate(flops=0, bytes_accessed=2**16, transcendentals=0)


def params(**more):
    return pltpu.CompilerParams(vmem_limit_bytes=VMEM_MIB * 2**20, **more)


def mm(left, right):
    return jnp.dot(left, right, preferred_element_type=F32)


def mm_nt(left, right):
    return lax.dot_general(left, right, (((1,), (1,)), ((), ())), preferred_element_type=F32)


def flipped(index, step):
    bit = 1
    while bit <= step:
        if step & bit:
            index = index + bit * (1 - 2 * ((index // bit) % 2))
        bit *= 2
    return index


def greet(me, blocks, others=()):
    barrier = pltpu.get_barrier_semaphore()
    devices = [{"exp": flipped(me, block)} for block in range(1, blocks)] + list(others)
    for device in devices:
        pl.semaphore_signal(barrier, inc=1, device_id=device, device_id_type=pl.DeviceIdType.MESH)
    pl.semaphore_wait(barrier, len(devices))


def spread(me, sent, expert, came, sems, index):
    local_sem, send_sem, recv_sem = sems
    copies = [pltpu.make_async_copy(sent.at[0, expert], came.at[0], local_sem.at[index])]
    for block in range(1, came.shape[0]):
        copies.append(
            pltpu.make_async_remote_copy(
                src_ref=sent.at[block, expert],
                dst_ref=came.at[block],
                send_sem=send_sem.at[index, block],
                recv_sem=recv_sem.at[index, block],
                device_id={"exp": flipped(me, block)},
                device_id_type=pl.DeviceIdType.MESH,
            )
        )
    return copies


def spread_sems(count, blocks):
    dma = pltpu.SemaphoreType.DMA
    return [dma((count,)), dma((count, blocks)), dma((count, blocks))]


def halves(array):
    high = array.astype(BF)
    return high, (array - high.astype(F32)).astype(BF)


def as_column(line):
    size = line.shape[1]
    diagonal = lax.broadcasted_iota(jnp.int32, (size, size), 0) == lax.broadcasted_iota(
        jnp.int32, (size, size), 1
    )
    return jnp.sum(jnp.where(diagonal, line, 0.0), axis=1, keepdims=True)


def bucket_of(offset):
    distance = jnp.abs(offset)
    farther = jnp.zeros_like(distance)
    for limit in LIMITS:
        farther = farther + (distance >= limit).astype(jnp.int32)
    return jnp.where(distance < 8, distance, 8 + farther) + jnp.where(offset > 0, 16, 0)


def diagonal_onehot(count):
    places = jnp.arange(TILE, dtype=jnp.int32)
    offsets = jnp.concatenate([-places, TILE - places, 0 * places - SEQ, 0 * places + SEQ])
    return (bucket_of(offsets)[:, None] == jnp.arange(count, dtype=jnp.int32)[None, :]).astype(F32)


def dispatch_gate_kernel(experts, capacity, padded, slot_ref, gate_ref, rows_ref, out_ref):
    block, tokens = out_ref.shape[0], rows_ref.shape[0]
    width = out_ref.shape[1]
    step = pl.program_id(0)
    ids = lax.broadcasted_iota(jnp.int32, (block, tokens), 0) + step * block
    picks = jnp.where(slot_ref[...] == ids, 1.0, 0.0).astype(BF)
    out = mm(picks, rows_ref[...])
    gates = jnp.broadcast_to(gate_ref[...].astype(BF), (8, tokens))
    lanes = pl.num_programs(0) * padded
    in_slots = mm_nt(gates, picks)
    in_slots = jnp.concatenate([in_slots, jnp.zeros((8, lanes - block), F32)], axis=1)
    lane = lax.broadcasted_iota(jnp.int32, (8, lanes), 1)
    row = lax.broadcasted_iota(jnp.int32, (block, 1), 0)
    left = out[:, :lanes]
    for expert in range(experts):
        shift = lax.rem(step * padded - expert * padded + lanes, lanes)
        moved = pltpu.roll(in_slots, shift, 1)
        mine = (lane >= step * padded) & (lane < step * padded + capacity)
        moved = jnp.where(mine, moved, 0.0)[:1]
        left = jnp.where(row == expert * padded + capacity, moved, left)
    out_ref[:, :lanes] = left.astype(BF)
    out_ref[:, lanes:] = out[:, lanes:].astype(BF)


def dispatch(slot_row, rows, blocks, block, gate):
    tokens, width = rows.shape
    grid_spec = dict(
        grid=(blocks,),
        out_specs=pl.BlockSpec((block, width), lambda k: (k, 0)),
        out_shape=jax.ShapeDtypeStruct((blocks * block, width), BF),
    )
    line = pl.BlockSpec((1, tokens), lambda k: (0, 0))
    full = pl.BlockSpec((tokens, width), lambda k: (0, 0))
    values, experts, capacity, padded = gate
    return pl.pallas_call(
        functools.partial(dispatch_gate_kernel, experts, capacity, padded),
        in_specs=[line, line, full],
        compiler_params=params(),
        cost_estimate=NO_COST,
        **grid_spec,
    )(slot_row, values, rows)


def dispatch_by_group_kernel(slot_ref, rows_ref, mine_ref, other_ref):
    block, tokens = mine_ref.shape[0], rows_ref.shape[0]
    step = pl.program_id(0)
    ids = lax.broadcasted_iota(jnp.int32, (block, tokens), 0) + step * block
    picks = jnp.where(slot_ref[...] == ids, 1.0, 0.0).astype(BF)
    out = mm(picks, rows_ref[...]).astype(BF)
    first = step < pl.num_programs(0) // 2

    @pl.when(first)
    def _():
        mine_ref[...] = out

    @pl.when(jnp.logical_not(first))
    def _():
        other_ref[...] = out


def dispatch_by_group(slot_row, rows, slots):
    tokens, width = rows.shape
    block = 256
    steps = slots // block
    return pl.pallas_call(
        dispatch_by_group_kernel,
        grid=(2 * steps,),
        in_specs=[
            pl.BlockSpec((1, tokens), lambda k: (0, 0)),
            pl.BlockSpec((tokens, width), lambda k: (0, 0)),
        ],
        out_specs=[
            pl.BlockSpec((block, width), lambda k: (jnp.minimum(k, steps - 1), 0)),
            pl.BlockSpec((block, width), lambda k: (jnp.maximum(k - steps, 0), 0)),
        ],
        out_shape=[jax.ShapeDtypeStruct((slots, width), BF)] * 2,
        compiler_params=params(),
        cost_estimate=NO_COST,
    )(slot_row, rows)


def qkv_kernel(x_ref, gain_ref, wq_ref, wk_ref, wv_ref, q_ref, k_ref, v_ref):
    rows = x_ref[...].astype(F32)
    inv = lax.rsqrt(jnp.mean(rows * rows, axis=-1, keepdims=True) + EPSILON)
    normed = (rows * inv * gain_ref[...]).astype(BF)
    q_ref[...] = (mm(normed, wq_ref[...]).astype(BF).astype(F32) * HEAD_DIM**-0.5).astype(BF)
    k_ref[...] = mm(normed, wk_ref[...]).astype(BF)
    v_ref[...] = mm(normed, wv_ref[...]).astype(BF)


def qkv(x, gain, wq, wk, wv):
    tokens, width = x.shape
    rows = pl.BlockSpec((SEQ, width), lambda t: (t, 0))
    square = pl.BlockSpec((width, width), lambda t: (0, 0))
    one = pl.BlockSpec((1, width), lambda t: (0, 0))
    return pl.pallas_call(
        qkv_kernel,
        grid=(tokens // SEQ,),
        in_specs=[rows, one, square, square, square],
        out_specs=[rows] * 3,
        out_shape=[jax.ShapeDtypeStruct((tokens, width), BF)] * 3,
        compiler_params=params(),
        cost_estimate=NO_COST,
    )(x, gain, wq, wk, wv)


def fill_bias(lines_ref, bias_ref):
    upper_right = lax.broadcasted_iota(jnp.int32, (TILE, TILE), 0) <= lax.broadcasted_iota(
        jnp.int32, (TILE, TILE), 1
    )
    tiles = SEQ // TILE
    for head in range(2):

        def sheared(line):
            whole = jnp.broadcast_to(lines_ref[head, line : line + 1, :], (TILE, TILE))
            return pltpu.roll(whole, 0, 1, stride=1, stride_axis=0)

        negative, positive = sheared(0), sheared(1)
        far_negative = jnp.broadcast_to(lines_ref[head, 2:3, :], (TILE, TILE))
        far_positive = jnp.broadcast_to(lines_ref[head, 3:4, :], (TILE, TILE))
        same = jnp.where(upper_right, negative, positive)
        above = jnp.where(upper_right, positive, far_positive)
        below = jnp.where(upper_right, far_negative, negative)
        for key in range(tiles):
            for query in range(tiles):
                gap = key - query
                tile = (
                    same
                    if gap == 0
                    else above
                    if gap == 1
                    else below
                    if gap == -1
                    else far_positive
                    if gap > 0
                    else far_negative
                )
                bias_ref[head, pl.ds(key * TILE, TILE), pl.ds(query * TILE, TILE)] = tile


def head_lanes(head):
    lane = lax.broadcasted_iota(jnp.int32, (1, PAIR), 1)
    return (lane >= head * HEAD_DIM) & (lane < (head + 1) * HEAD_DIM)


def only(head, array):
    return jnp.where(head_lanes(head), array, jnp.zeros_like(array))


def attention_kernel(
    lines_ref, mine_ref, other_ref, q_ref, k_ref, v_ref, o_ref, lse_ref, came_ref,
    bias_ref, local_sem, send_sem, recv_sem
):
    pair, seq = pl.program_id(0), pl.program_id(1)
    blocks, half = mine_ref.shape[:2]
    me, group = lax.axis_index("exp"), lax.axis_index("dp") % 2

    def transfers():
        copies = []
        for kind, sent in enumerate((mine_ref, other_ref)):
            experts = pl.ds((group + kind) % 2 * half, half)
            copies.append(
                pltpu.make_async_copy(sent.at[0], came_ref.at[experts, 0], local_sem.at[kind])
            )
            for block in range(1, blocks):
                copies.append(
                    pltpu.make_async_remote_copy(
                        src_ref=sent.at[block],
                        dst_ref=came_ref.at[experts, block],
                        send_sem=send_sem.at[kind, block],
                        recv_sem=recv_sem.at[kind, block],
                        device_id={"exp": flipped(me, block)},
                        device_id_type=pl.DeviceIdType.MESH,
                    )
                )
        return copies

    @pl.when((pair == 0) & (seq == 0))
    def _():
        greet(me, blocks)
        for copy in transfers():
            copy.start()

    @pl.when(seq == 0)
    def _():
        fill_bias(lines_ref, bias_ref)

    keys = k_ref[...]
    values_t = v_ref[...].T
    masked = [only(head, keys) for head in range(2)]
    row = lax.broadcasted_iota(jnp.int32, (PAIR, 1), 0)
    for part in range(SEQ // CHUNK):
        places = pl.ds(part * CHUNK, CHUNK)
        queries = q_ref[places, :]
        out = None
        for head in range(2):
            scores = mm_nt(masked[head], queries) + bias_ref[head, :, places]
            highest = jnp.max(scores, axis=0, keepdims=True)
            weights = jnp.exp(scores - highest)
            total = jnp.sum(weights, axis=0, keepdims=True)
            lse_ref[0, 0, head : head + 1, places] = highest + jnp.log(total)
            mixed = mm(values_t, weights.astype(BF)) * (1.0 / total)
            out = mixed if out is None else jnp.where(row < HEAD_DIM, out, mixed)
        o_ref[places, :] = out.T.astype(BF)

    @pl.when((pair == pl.num_programs(0) - 1) & (seq == pl.num_programs(1) - 1))
    def _():
        for copy in transfers():
            copy.wait()


def attention(lines, sent, q, k, v):
    blocks, half, padded, width = sent[0].shape
    tokens, width = q.shape
    seqs, pairs = tokens // SEQ, width // PAIR
    block = pl.BlockSpec((SEQ, PAIR), lambda h, s: (s, h))
    return pl.pallas_call(
        attention_kernel,
        grid=(pairs, seqs),
        in_specs=[pl.BlockSpec((2, 8, TILE), lambda h, s: (h, 0, 0))]
        + [pl.BlockSpec(memory_space=pl.ANY)] * 2
        + [block, block, block],
        out_specs=[block, pl.BlockSpec((1, 1, 2, SEQ), lambda h, s: (h, s, 0, 0))]
        + [pl.BlockSpec(memory_space=pl.ANY)],
        out_shape=[
            jax.ShapeDtypeStruct((tokens, width), BF),
            jax.ShapeDtypeStruct((pairs, seqs, 2, SEQ), F32),
            jax.ShapeDtypeStruct((2 * half, blocks, padded, width), BF),
        ],
        scratch_shapes=[pltpu.VMEM((2, SEQ, SEQ), F32)] + spread_sems(2, blocks),
        compiler_params=params(collective_id=1, has_side_effects=True),
        cost_estimate=NO_COST,
    )(lines, *sent, q, k, v)


def attention_back_kernel(parts, lines_ref, q_ref, k_ref, v_ref, do_ref, lse_ref, *refs):
    sent_refs, refs = refs[:parts], refs[parts:]
    dq_ref, dk_ref, dv_ref, sums_ref = refs[:4]
    came_refs, refs = refs[4 : 4 + parts], refs[4 + parts :]
    bias_ref, diag_ref, *sems = refs
    pair, seq = pl.program_id(0), pl.program_id(1)
    blocks, expert = came_refs[0].shape[0], sent_refs[0].shape[1] - 1
    me = lax.axis_index("exp")

    def transfers():
        copies = []
        for part in range(parts):
            copies += spread(me, sent_refs[part], expert, came_refs[part], sems, part)
        return copies

    @pl.when((pair == 0) & (seq == 0))
    def _():
        greet(me, blocks)
        for copy in transfers():
            copy.start()

    @pl.when((pair == pl.num_programs(0) - 1) & (seq == pl.num_programs(1) - 1))
    def _():
        for copy in transfers():
            copy.wait()

    @pl.when(seq == 0)
    def _():
        fill_bias(lines_ref, bias_ref)
        diag_ref[...] = jnp.zeros_like(diag_ref)

    keys, values = k_ref[...], v_ref[...]
    keys_t = keys.T
    masked_k = [only(head, keys) for head in range(2)]
    masked_v = [only(head, values) for head in range(2)]
    row = lax.broadcasted_iota(jnp.int32, (PAIR, 1), 0)
    grads_k, grads_v = [None, None], [None, None]
    tiles = SEQ // TILE
    for part in range(SEQ // CHUNK):
        places = pl.ds(part * CHUNK, CHUNK)
        queries, upstream = q_ref[places, :], do_ref[places, :]
        grad_q = None
        for head in range(2):
            scores = mm_nt(masked_k[head], queries) + bias_ref[head, :, places]
            weights = jnp.exp(scores - lse_ref[0, 0, head : head + 1, places])
            products = weights * mm_nt(masked_v[head], upstream)
            scores_grad = products - weights * jnp.sum(products, axis=0, keepdims=True)
            low = scores_grad.astype(BF)
            value_term = mm(weights.astype(BF), upstream)
            key_term = mm(low, queries)
            grads_v[head] = value_term if part == 0 else grads_v[head] + value_term
            grads_k[head] = key_term if part == 0 else grads_k[head] + key_term
            query_term = mm(keys_t, low)
            grad_q = query_term if head == 0 else jnp.where(row < HEAD_DIM, grad_q, query_term)
            groups = {}
            for query in range(CHUNK // TILE):
                for key in range(tiles):
                    gap = key - (query + part * (CHUNK // TILE))
                    kind = 0 if gap == 0 else 1 if gap == 1 else 2 if gap == -1 else 3 if gap > 0 else 4
                    tile = scores_grad[
                        key * TILE : (key + 1) * TILE, query * TILE : (query + 1) * TILE
                    ]
                    groups[kind] = tile if kind not in groups else groups[kind] + tile
            for kind, tile in groups.items():
                diag_ref[head, kind] += tile
        dq_ref[places, :] = (grad_q * HEAD_DIM**-0.5).T.astype(BF)
    first = head_lanes(0)
    dk_ref[...] = jnp.where(first, grads_k[0], grads_k[1]).astype(BF)
    dv_ref[...] = jnp.where(first, grads_v[0], grads_v[1]).astype(BF)

    @pl.when(seq == pl.num_programs(1) - 1)
    def _():
        upper_right = lax.broadcasted_iota(jnp.int32, (TILE, TILE), 0) <= lax.broadcasted_iota(
            jnp.int32, (TILE, TILE), 1
        )
        sums_ref[...] = jnp.zeros_like(sums_ref)
        for head in range(2):
            same, above, below = diag_ref[head, 0], diag_ref[head, 1], diag_ref[head, 2]

            def gathered(array):
                row_id = lax.broadcasted_iota(jnp.int32, (TILE, 1), 0)
                bit = 1
                while bit < TILE:
                    turned = pltpu.roll(array, TILE - bit, 1)
                    array = jnp.where((row_id & bit) != 0, turned, array)
                    bit *= 2
                return jnp.sum(array, axis=0, keepdims=True)

            zero = jnp.zeros_like(same)
            sums_ref[head, 0:1, :] = gathered(jnp.where(upper_right, same, below))
            sums_ref[head, 1:2, :] = gathered(jnp.where(upper_right, above, same))
            sums_ref[head, 2:3, :] = jnp.sum(
                diag_ref[head, 4] + jnp.where(upper_right, below, zero), axis=0, keepdims=True
            )
            sums_ref[head, 3:4, :] = jnp.sum(
                diag_ref[head, 3] + jnp.where(upper_right, zero, above), axis=0, keepdims=True
            )


def attention_back(lines, q, k, v, do, lse, sent):
    parts = len(sent)
    blocks, _, padded, _ = sent[0].shape
    anywhere = pl.BlockSpec(memory_space=pl.ANY)
    tokens, width = q.shape
    seqs, pairs = tokens // SEQ, width // PAIR
    block = pl.BlockSpec((SEQ, PAIR), lambda h, s: (s, h))
    lines_spec = pl.BlockSpec((2, 8, TILE), lambda h, s: (h, 0, 0))
    return pl.pallas_call(
        functools.partial(attention_back_kernel, parts),
        grid=(pairs, seqs),
        in_specs=[lines_spec, block, block, block, block]
        + [pl.BlockSpec((1, 1, 2, SEQ), lambda h, s: (h, s, 0, 0))]
        + [anywhere] * parts,
        out_specs=[block, block, block, lines_spec] + [anywhere] * parts,
        out_shape=[jax.ShapeDtypeStruct((tokens, width), BF)] * 3
        + [jax.ShapeDtypeStruct((2 * pairs, 8, TILE), F32)]
        + [jax.ShapeDtypeStruct((blocks, padded, width), BF)] * parts,
        scratch_shapes=[
            pltpu.VMEM((2, SEQ, SEQ), F32),
            pltpu.VMEM((2, 5, TILE, TILE), F32),
            *spread_sems(parts, blocks),
        ],
        compiler_params=params(collective_id=4, has_side_effects=True),
        cost_estimate=pl.CostEstimate(
            flops=40 * pairs * seqs * SEQ * SEQ * PAIR,
            bytes_accessed=14 * tokens * width,
            transcendentals=2 * pairs * seqs * SEQ * SEQ,
        ),
    )(lines, q, k, v, do, lse, *sent)


def router_kernel(
    o_ref, x_ref, wo_ref, gain_ref, wr_ref, expert_ref, h_ref, u_ref, probs_ref, gate_ref, line_ref
):
    mixed = x_ref[...].astype(F32) + mm(o_ref[...], wo_ref[...])
    h_ref[...] = mixed
    inv = lax.rsqrt(jnp.mean(mixed * mixed, axis=-1, keepdims=True) + EPSILON)
    normed = mixed * inv * gain_ref[...]
    u_ref[...] = normed.astype(BF)
    high, low = halves(normed)
    wr_high, wr_low = halves(wr_ref[...])
    logits = mm(high, wr_high) + (mm(high, wr_low) + mm(low, wr_high))
    spread = jnp.exp(logits - jnp.max(logits, axis=-1, keepdims=True))
    probs = spread / jnp.sum(spread, axis=-1, keepdims=True)
    probs_ref[...] = probs
    picked = expert_ref[...] == lax.broadcasted_iota(jnp.int32, probs.shape, 1)
    gate = jnp.sum(jnp.where(picked, probs, 0.0), axis=-1, keepdims=True)
    gate_ref[...] = gate
    size = gate.shape[0]
    diagonal = lax.broadcasted_iota(jnp.int32, (size, size), 0) == lax.broadcasted_iota(
        jnp.int32, (size, size), 1
    )
    line_ref[...] = jnp.sum(jnp.where(diagonal, gate, 0.0), axis=0, keepdims=True)


def router(o, x, wo, gain, wr, expert):
    tokens, width = x.shape
    experts = wr.shape[1]
    size = 256

    def rows(columns):
        return pl.BlockSpec((size, columns), lambda t: (t, 0))

    def whole(*shape):
        return pl.BlockSpec(shape, lambda t: (0, 0))

    return pl.pallas_call(
        router_kernel,
        grid=(tokens // size,),
        in_specs=[rows(width), rows(width), whole(width, width), whole(1, width)]
        + [whole(width, experts), rows(1)],
        out_specs=[rows(width), rows(width), rows(experts), rows(1)]
        + [pl.BlockSpec((1, size), lambda t: (0, t))],
        out_shape=[
            jax.ShapeDtypeStruct((tokens, width), F32),
            jax.ShapeDtypeStruct((tokens, width), BF),
            jax.ShapeDtypeStruct((tokens, experts), F32),
            jax.ShapeDtypeStruct((tokens, 1), F32),
            jax.ShapeDtypeStruct((1, tokens), F32),
        ],
        compiler_params=params(),
        cost_estimate=NO_COST,
    )(o, x, wo, gain, wr, expert)


def gelu_and_slope(z):
    square = z * z
    half = 0.5 + 0.5 * jnp.tanh(z * (GELU_A + GELU_B * square))
    value = z * half
    slope = half + 2.0 * value * (1.0 - half) * (GELU_A + 3.0 * GELU_B * square)
    return value, slope


def send_back(me, held, target, which, place, sems, kind):
    send_sem, recv_sem, local_sem = sems
    copies = [pltpu.make_async_copy(held.at[0], target.at[0, which], local_sem.at[kind, place])]
    for block in range(1, held.shape[0]):
        copies.append(
            pltpu.make_async_remote_copy(
                src_ref=held.at[block],
                dst_ref=target.at[block, which],
                send_sem=send_sem.at[kind, place, block],
                recv_sem=recv_sem.at[kind, place, block],
                device_id={"exp": flipped(me, block)},
                device_id_type=pl.DeviceIdType.MESH,
            )
        )
    return copies


def expert_step(parts, rows, upstream, first_ref, second_ref, e_sum, d_sum):
    columns = first_ref.shape[2] // parts
    for part in range(parts):
        places = slice(part * columns, (part + 1) * columns)
        first, second = first_ref[0, :, places], second_ref[0, places, :]
        value, slope = gelu_and_slope(mm(rows, first))
        inner = (mm_nt(upstream, second) * slope).astype(BF)
        e_sum[...] += mm(value.astype(BF), second)
        d_sum[...] += mm_nt(inner, first)


def expert_kernel(parts, all_experts, sent_ref, c_ref, first_ref, second_ref, *refs):
    expert, step = pl.program_id(0), pl.program_id(1)
    count, last_step = pl.num_programs(0), pl.num_programs(1) - 1
    u_refs, u_late, refs = refs[:all_experts], refs[all_experts], refs[all_experts + 1 :]
    e_kept, d_kept, rows_ref, e_sum, d_sum, e_held, d_held, local_sem, send_sem, recv_sem = refs
    early, blocks, padded, width = e_held.shape
    me = lax.axis_index("exp")
    group, half = lax.axis_index("dp") % 2, all_experts // 2

    def outgoing(which, block):
        return pltpu.make_async_remote_copy(
            src_ref=sent_ref.at[block, which],
            dst_ref=rows_ref.at[which, block],
            send_sem=send_sem.at[which, block],
            recv_sem=recv_sem.at[which, block],
            device_id={"exp": flipped(me, block)},
            device_id_type=pl.DeviceIdType.MESH,
        )

    def own_in(which):
        return pltpu.make_async_copy(sent_ref.at[0, which], rows_ref.at[which, 0], local_sem.at[0, which])

    def keep(which, act):
        for each in range(2):
            target = u_refs[(which // half + each) % 2 * half + which % half]

            @pl.when(group == each)
            def _(target=target):
                act(pltpu.make_async_copy(rows_ref.at[which], target, local_sem.at[1, which]))

        if which >= early:
            act(
                pltpu.make_async_copy(
                    rows_ref.at[which], u_late.at[which - early], local_sem.at[2, which - early]
                )
            )

    def arrive(which):
        own_in(which).wait()
        for block in range(1, blocks):
            outgoing(which, block).wait_recv()
        keep(which, lambda copy: copy.start())

    def keep_result(which):
        return [
            pltpu.make_async_copy(e_held.at[which], e_kept.at[which], local_sem.at[3, which]),
            pltpu.make_async_copy(d_held.at[which], d_kept.at[which], local_sem.at[4, which]),
        ]

    @pl.when((expert == 0) & (step == 0))
    def _():
        greet(me, blocks)
        for which in range(all_experts):
            own_in(which).start()
            for block in range(1, blocks):
                outgoing(which, block).start()

    @pl.when(step == 0)
    def _():
        for which in range(early):

            @pl.when(expert == which)
            def _(which=which):
                arrive(which)

        e_sum[...] = jnp.zeros_like(e_sum)
        d_sum[...] = jnp.zeros_like(d_sum)

    rows = rows_ref[expert].reshape(blocks * padded, width)
    expert_step(parts, rows, c_ref[0], first_ref, second_ref, e_sum, d_sum)

    @pl.when(step == last_step)
    def _():
        e_held[expert] = e_sum[...].astype(BF).reshape(blocks, padded, width)
        d_held[expert] = d_sum[...].astype(BF).reshape(blocks, padded, width)
        for which in range(early):

            @pl.when(expert == which)
            def _(which=which):
                for copy in keep_result(which):
                    copy.start()

    @pl.when((step == last_step) & (expert == count - 1))
    def _():
        for which in range(early, all_experts):
            arrive(which)
        for which in range(all_experts):
            keep(which, lambda copy: copy.wait())
            for block in range(1, blocks):
                outgoing(which, block).wait_send()
        for which in range(early):
            for copy in keep_result(which):
                copy.wait()


def expert_rest_kernel(
    parts, u_ref, c_ref, first_ref, second_ref, e_kept, d_kept, e_ref, d_ref,
    e_sum, d_sum, e_held, d_held, back_send, back_recv, back_local,
):
    expert, step = pl.program_id(0), pl.program_id(1)
    count, last_step = pl.num_programs(0), pl.num_programs(1) - 1
    late, blocks, padded, width = e_held.shape
    kept = e_kept.shape[0]
    me = lax.axis_index("exp")
    sems = (back_send, back_recv, back_local)

    def back(which):
        if which < kept:
            e_from, d_from = e_kept.at[which], d_kept.at[which]
        else:
            e_from, d_from = e_held.at[which - kept], d_held.at[which - kept]
        return send_back(me, e_from, e_ref, which, which, sems, 0) + send_back(
            me, d_from, d_ref, which, which, sems, 1
        )

    @pl.when((expert == 0) & (step == 0))
    def _():
        greet(me, blocks)
        for which in range(kept):
            for copy in back(which):
                copy.start()

    @pl.when(step == 0)
    def _():
        e_sum[...] = jnp.zeros_like(e_sum)
        d_sum[...] = jnp.zeros_like(d_sum)

    rows = u_ref[0].reshape(blocks * padded, width)
    expert_step(parts, rows, c_ref[0], first_ref, second_ref, e_sum, d_sum)

    @pl.when(step == last_step)
    def _():
        e_held[expert] = e_sum[...].astype(BF).reshape(blocks, padded, width)
        d_held[expert] = d_sum[...].astype(BF).reshape(blocks, padded, width)
        for which in range(late):

            @pl.when(expert == which)
            def _(which=which):
                for copy in back(kept + which):
                    copy.start()

    @pl.when((step == last_step) & (expert == count - 1))
    def _():
        for which in range(kept + late):
            for copy in back(which):
                copy.wait()


def expert_pass(sent, c, w_in, w_out):
    blocks, experts, padded, width = sent.shape
    hidden = w_in.shape[2]
    size = 768
    rows = blocks * padded
    early = experts // 2
    late = experts - early
    anywhere = pl.BlockSpec(memory_space=pl.ANY)
    dma = pltpu.SemaphoreType.DMA

    def results(count):
        return jax.ShapeDtypeStruct((count, blocks, padded, width), BF)

    def weights(first):
        return [
            pl.BlockSpec((1, rows, width), lambda e, f: (first + e, 0, 0)),
            pl.BlockSpec((1, width, size), lambda e, f: (first + e, 0, f)),
            pl.BlockSpec((1, size, width), lambda e, f: (first + e, f, 0)),
        ]

    *u_rows, u_late, e_kept, d_kept = pl.pallas_call(
        functools.partial(expert_kernel, 3, experts),
        grid=(early, hidden // size),
        in_specs=[anywhere] + weights(0),
        out_specs=[anywhere] * (experts + 3),
        out_shape=[jax.ShapeDtypeStruct((blocks, padded, width), BF)] * experts
        + [results(late), results(early), results(early)],
        scratch_shapes=[
            pltpu.VMEM((experts, blocks, padded, width), BF),
            pltpu.VMEM((rows, width), F32),
            pltpu.VMEM((rows, width), F32),
            pltpu.VMEM((early, blocks, padded, width), BF),
            pltpu.VMEM((early, blocks, padded, width), BF),
            dma((5, experts)),
            dma((experts, blocks)),
            dma((experts, blocks)),
        ],
        compiler_params=params(collective_id=0, has_side_effects=True),
        cost_estimate=NO_COST,
    )(sent, c, w_in, w_out)
    u_rows = [part.reshape(rows, width) for part in u_rows]
    e_back, d_back = pl.pallas_call(
        functools.partial(expert_rest_kernel, 3),
        grid=(late, hidden // size),
        in_specs=[pl.BlockSpec((1, blocks, padded, width), lambda e, f: (e, 0, 0, 0))]
        + weights(early)
        + [anywhere] * 2,
        out_specs=[anywhere] * 2,
        out_shape=[jax.ShapeDtypeStruct((blocks, experts, padded, width), BF)] * 2,
        scratch_shapes=[
            pltpu.VMEM((rows, width), F32),
            pltpu.VMEM((rows, width), F32),
            pltpu.VMEM((late, blocks, padded, width), BF),
            pltpu.VMEM((late, blocks, padded, width), BF),
            dma((2, experts, blocks)),
            dma((2, experts, blocks)),
            dma((2, experts)),
        ],
        compiler_params=params(collective_id=3, has_side_effects=True),
        cost_estimate=pl.CostEstimate(
            flops=32 * rows * width * hidden, bytes_accessed=4 * width * hidden, transcendentals=0
        ),
    )(u_late, c, w_in, w_out, e_kept, d_kept)
    return u_rows, e_back, d_back


def weights_kernel(parts, sources, capacity, padded, place_ref, *refs):
    u_refs, c_refs = refs[:sources], refs[sources : 2 * sources]
    first_ref, second_ref, far_in, far_out, in_sum, out_sum = refs[2 * sources :]
    size = first_ref.shape[2]
    rows = u_refs[0].shape[0]
    columns = size // parts
    first_t = first_ref[0].T
    for source in range(sources):
        inputs, upstream = u_refs[source][...], c_refs[source][...].reshape(u_refs[source].shape)
        gate = jnp.zeros((1, rows), F32)
        for block in range(rows // padded):
            place = block * padded + capacity
            gate = gate + inputs[place : place + 1, :rows].astype(F32)
        for part in range(parts):
            places = slice(part * columns, (part + 1) * columns)
            value, slope = gelu_and_slope(mm_nt(first_t[places, :], inputs))
            inner = (mm_nt(second_ref[0, places, :], upstream) * (slope * gate)).astype(BF)
            in_term = mm(inner, inputs)
            out_term = mm((value * gate).astype(BF), upstream)
            if source == 0:
                in_sum[places, :] = in_term
                out_sum[places, :] = out_term
            else:
                in_sum[places, :] += in_term
                out_sum[places, :] += out_term
    far_in[...] = in_sum[...].T.astype(BF)
    far_out[...] = out_sum[...].astype(BF)


def weight_grads(place, us, c_rows, c_far, w_in, w_out, size, capacity, padded):
    sources = len(us)
    rows, width = us[0].shape
    block = pl.BlockSpec((rows, width), lambda f, p: (0, 0))
    return pl.pallas_call(
        functools.partial(weights_kernel, 3, sources, capacity, padded),
        grid_spec=pltpu.PrefetchScalarGridSpec(
            num_scalar_prefetch=1,
            grid=(1,),
            in_specs=[block] * sources
            + [pl.BlockSpec((1, rows, width), lambda f, p: (p[0], 0, 0))]
            + [block] * (sources - 1)
            + [
                pl.BlockSpec((1, width, size), lambda f, p: (p[0], 0, p[1])),
                pl.BlockSpec((1, size, width), lambda f, p: (p[0], p[1], 0)),
            ],
            out_specs=[
                pl.BlockSpec((width, size), lambda f, p: (0, 0)),
                pl.BlockSpec((size, width), lambda f, p: (0, 0)),
            ],
            scratch_shapes=[pltpu.VMEM((size, width), F32)] * 2,
        ),
        out_shape=[
            jax.ShapeDtypeStruct((width, size), BF),
            jax.ShapeDtypeStruct((size, width), BF),
        ],
        compiler_params=params(),
        cost_estimate=NO_COST,
    )(place, *us, c_rows, *c_far, w_in, w_out)


def finish_kernel(half, place_ref, *refs):
    own_in, own_out, refs = refs[0], refs[1], refs[2:]
    came_in, came_out, dense_ref = refs[:half], refs[half : 2 * half], refs[2 * half]
    a_out, b_out, *dense_outs = refs[2 * half + 1 :]
    width = dense_ref.shape[1]
    for step in range(2 * half):

        @pl.when(pl.program_id(0) == step)
        def _(step=step):
            a_out[0] = (own_in[step] if step < half else came_in[step - half][...]).astype(F32)
            b_out[0] = (own_out[step] if step < half else came_out[step - half][...]).astype(F32)
            for which in range(step, 4, 2 * half):
                dense_outs[which][...] = dense_ref[which * width : (which + 1) * width, :].astype(F32)


def finish(places, own_in, own_out, came_in, came_out, dense):
    half, width, size = own_in.shape

    def whole(*shape):
        return pl.BlockSpec(shape, lambda e, p: (0,) * len(shape))

    def spec(*shape):
        return pl.BlockSpec((1,) + shape, lambda e, p: (p[e], 0, 0))

    return pl.pallas_call(
        functools.partial(finish_kernel, half),
        grid_spec=pltpu.PrefetchScalarGridSpec(
            num_scalar_prefetch=1,
            grid=(2 * half,),
            in_specs=[whole(half, width, size), whole(half, size, width)]
            + [whole(width, size)] * half
            + [whole(size, width)] * half
            + [whole(4 * width, width)],
            out_specs=[spec(width, size), spec(size, width)] + [whole(width, width)] * 4,
        ),
        out_shape=[
            jax.ShapeDtypeStruct((2 * half, width, size), F32),
            jax.ShapeDtypeStruct((2 * half, size, width), F32),
        ]
        + [jax.ShapeDtypeStruct((width, width), F32)] * 4,
        compiler_params=params(),
    )(places, own_in, own_out, *came_in, *came_out, dense)


def tail_kernel(parts, sources, experts, capacity, padded, *refs):
    u_refs, refs = refs[: sources * experts], refs[sources * experts :]
    c_own, c_far, refs = refs[0], refs[1 : 1 + (sources - 1) * experts], refs[1 + (sources - 1) * experts :]
    (
        first_ref, second_ref, far_in, far_out, dense_o, dense_qkv, small_ref,
        own_in_ref, own_out_ref, came_in_ref, came_out_ref, dense_ref, total_ref,
        rows_u, rows_c, first_held, second_held, first_t, in_sum, out_sum, own_in, own_out,
        dense, dense_came, dense_over_dp, small, small_came,
        rows_sem, weight_sem, load_sem, far_send, far_recv, own_sem,
        half_send, half_recv, over_send, over_recv, back_send, back_recv, small_send, small_recv, keep_sem,
    ) = refs
    rows, width = rows_u.shape[2:]
    size = in_sum.shape[0]
    columns = size // parts
    exp_me, dp_me = lax.axis_index("exp"), lax.axis_index("dp")
    exp_bits, dp_bits = half_send.shape[2], over_send.shape[0]
    group, pair = dp_me % 2, dp_me // 2
    mesh_id = pl.DeviceIdType.MESH

    def exp_peer(bit):
        return {"exp": flipped(exp_me, 1 << bit)}

    def dp_peer(bit):
        return {"dp": flipped(dp_me, 1 << bit)}

    chain = dense.shape[0] // 2
    bits = list(range(exp_bits))
    split = 1 + (exp_bits - 1) // 2
    orders = (bits, bits[:1] + bits[split:] + bits[1:split])

    def region(which, depth):
        start = which * chain
        for level in range(depth):
            start = start + (exp_me // (1 << orders[which][level])) % 2 * (chain >> (level + 1))
        return pl.ds(pl.multiple_of(start, 16), chain >> depth)

    def other_half(which, depth):
        start = which * chain
        for level in range(depth):
            start = start + (exp_me // (1 << orders[which][level])) % 2 * (chain >> (level + 1))
        start = start + (1 - (exp_me // (1 << orders[which][depth])) % 2) * (chain >> (depth + 1))
        return pl.ds(pl.multiple_of(start, 16), chain >> (depth + 1))

    def came(which, depth):
        return pl.ds(which * chain + chain - (chain >> depth), chain >> (depth + 1))

    def columns_of(side):
        return pl.ds(side * (width // 2), width // 2)

    def halving(side, which, depth):
        return pltpu.make_async_remote_copy(
            src_ref=dense.at[other_half(which, depth), columns_of(side)],
            dst_ref=dense_came.at[came(which, depth), columns_of(side)],
            send_sem=half_send.at[side, which, depth],
            recv_sem=half_recv.at[side, which, depth],
            device_id=exp_peer(orders[which][depth]),
            device_id_type=mesh_id,
        )

    def over(side, which, bit):
        mine = dense.at[region(which, exp_bits), columns_of(side)]
        return pltpu.make_async_remote_copy(
            src_ref=mine if bit == 0 else dense_over_dp.at[1, bit - 1, side, which],
            dst_ref=dense_over_dp.at[0, bit, side, which],
            send_sem=over_send.at[bit, side, which],
            recv_sem=over_recv.at[bit, side, which],
            device_id=dp_peer(dp_bits - 1 - bit),
            device_id_type=mesh_id,
        )

    def keeping(side, which):
        return pltpu.make_async_copy(
            dense_over_dp.at[1, dp_bits - 1, side, which],
            dense_ref.at[region(which, exp_bits), columns_of(side)],
            keep_sem.at[side, which],
        )

    def returning(side, which, depth):
        place = dense_ref.at[region(which, depth + 1), columns_of(side)]
        return pltpu.make_async_remote_copy(
            src_ref=place,
            dst_ref=place,
            send_sem=back_send.at[side, which, depth],
            recv_sem=back_recv.at[side, which, depth],
            device_id=exp_peer(orders[which][depth]),
            device_id_type=mesh_id,
        )

    def small_copy(depth):
        return pltpu.make_async_remote_copy(
            src_ref=small.at[depth],
            dst_ref=small_came.at[depth],
            send_sem=small_send.at[depth],
            recv_sem=small_recv.at[depth],
            device_id=exp_peer(depth) if depth < exp_bits else dp_peer(depth - exp_bits),
            device_id_type=mesh_id,
        )

    def loads():
        return [
            pltpu.make_async_copy(dense_o, dense.at[pl.ds(3 * width, width)], load_sem.at[0]),
            pltpu.make_async_copy(dense_qkv, dense.at[pl.ds(0, 3 * width)], load_sem.at[1]),
            pltpu.make_async_copy(small_ref, small.at[0], load_sem.at[2]),
        ]

    def add_small(depth):
        small_copy(depth).wait_recv()
        small[depth + 1] = small[depth] + small_came[depth]

    def begin(side):
        if side == 0:
            for load in loads():
                load.wait()
            small_copy(0).start()
        for which in range(2):
            halving(side, which, 0).start()

    def halve(depth):
        def act(side):
            for which in range(2):
                halving(side, which, depth).wait_recv()
                place, new, here = region(which, depth + 1), came(which, depth), columns_of(side)
                dense[place, here] = (
                    dense[place, here].astype(F32) + dense_came[new, here].astype(F32)
                ).astype(BF)
                if depth + 1 < exp_bits:
                    halving(side, which, depth + 1).start()
                else:
                    over(side, which, 0).start()
            if side == 0:
                add_small(depth)
                small_copy(depth + 1).start()

        return act

    def sum_over(bit):
        def act(side):
            for which in range(2):
                over(side, which, bit).wait_recv()
                if bit == 0:
                    mine = dense[region(which, exp_bits), columns_of(side)]
                else:
                    mine = dense_over_dp[1, bit - 1, side, which]
                dense_over_dp[1, bit, side, which] = (
                    mine.astype(F32) + dense_over_dp[0, bit, side, which].astype(F32)
                ).astype(BF)
                if bit + 1 < dp_bits:
                    over(side, which, bit + 1).start()
                else:
                    keeping(side, which).start()
            if side == 0:
                add_small(exp_bits + bit)
                if bit + 1 < dp_bits:
                    small_copy(exp_bits + bit + 1).start()
            if bit + 1 == dp_bits:
                for which in range(2):
                    keeping(side, which).wait()
                    returning(side, which, exp_bits - 1).start()

        return act

    def give_back(depth):
        def act(side):
            for which in range(2):
                returning(side, which, depth).wait_recv()
                if depth > 0:
                    returning(side, which, depth - 1).start()

        return act

    stages = [begin] + [halve(depth) for depth in range(exp_bits)]
    stages += [sum_over(bit) for bit in range(dp_bits)]
    stages += [give_back(depth) for depth in reversed(range(exp_bits))]
    stages = [functools.partial(stage, side) for stage in stages for side in range(2)]

    steps, turns = experts, experts * sources

    def rows_copy(source, expert):
        if source == 0:
            c_from = c_own.at[group * experts + expert]
        else:
            c_from = c_far[expert * (sources - 1) + source - 1]
        return [
            pltpu.make_async_copy(
                u_refs[expert * sources + source],
                rows_u.at[source, expert],
                rows_sem.at[0, source, expert],
            ),
            pltpu.make_async_copy(
                c_from, rows_c.at[source, expert], rows_sem.at[1, source, expert]
            ),
        ]

    def weight_copy(step):
        expert = group * experts + step
        place = (pair * 2 + group) * size
        place = pl.ds(pl.multiple_of(place, 128), size)
        slot = step % 2
        return [
            pltpu.make_async_copy(
                first_ref.at[expert, :, place], first_held.at[slot], weight_sem.at[0, slot]
            ),
            pltpu.make_async_copy(
                second_ref.at[expert, place, :], second_held.at[slot], weight_sem.at[1, slot]
            ),
        ]

    far_parts = far_send.shape[1]

    def far_copy(index):
        kind, part = index % 2, index // 2
        held, target = ((far_in, came_in_ref), (far_out, came_out_ref))[kind]
        lines = held.shape[0] // far_parts
        place = pl.ds(part * lines, lines)
        return pltpu.make_async_remote_copy(
            src_ref=held.at[place],
            dst_ref=target.at[place],
            send_sem=far_send.at[kind, part],
            recv_sem=far_recv.at[kind, part],
            device_id=dp_peer(0),
            device_id_type=mesh_id,
        )

    def own_copy(expert):
        return [
            pltpu.make_async_copy(held.at[expert], target.at[expert], own_sem.at[kind, expert])
            for kind, (held, target) in enumerate(((own_in, own_in_ref), (own_out, own_out_ref)))
        ]

    for load in loads():
        load.start()
    for copy in weight_copy(0):
        copy.start()
    for expert in range(experts):
        for source in range(sources):
            for copy in rows_copy(source, expert):
                copy.start()
    barrier = pltpu.get_barrier_semaphore()
    for bit in range(exp_bits):
        pl.semaphore_signal(barrier, inc=1, device_id=exp_peer(bit), device_id_type=mesh_id)
    for bit in range(dp_bits):
        pl.semaphore_signal(barrier, inc=1, device_id=dp_peer(bit), device_id_type=mesh_id)
    pl.semaphore_wait(barrier, exp_bits + dp_bits)

    places = [0, 0, 1, 2, 3, 4, 5, 6]
    places = [place for place in places if place < turns][: len(stages)]
    starts = {4: 3}
    starts = {place: index for place, index in starts.items() if place < turns}
    pieces = 2 * far_parts

    def turn(at, carry):
        step, source = at // sources, at % sources
        expert, slot = step, step % 2
        for place, stage in zip(places, stages):
            pl.when(at == place)(stage)
        for place, index in starts.items():
            pl.when(at == place)(far_copy(index).start)

        @pl.when(source == 0)
        def _():
            for copy in weight_copy(step):
                copy.wait()

            @pl.when(step + 1 < steps)
            def _():
                for copy in weight_copy(step + 1):
                    copy.start()

            first_t[...] = first_held[slot].T

        for each_expert in range(experts):
            for each in range(sources):

                @pl.when(at == each_expert * sources + each)
                def _(each=each, each_expert=each_expert):
                    for copy in rows_copy(each, each_expert):
                        copy.wait()

        inputs, upstream = rows_u[source, expert], rows_c[source, expert]
        gate = jnp.zeros((1, rows), F32)
        for block in range(rows // padded):
            place = block * padded + capacity
            gate = gate + inputs[place : place + 1, :rows].astype(F32)
        for part in range(parts):
            here = slice(part * columns, (part + 1) * columns)
            value, slope = gelu_and_slope(mm_nt(first_t[here, :], inputs))
            inner = (mm_nt(second_held[slot, here, :], upstream) * (slope * gate)).astype(BF)
            in_term = mm(inner, inputs)
            out_term = mm((value * gate).astype(BF), upstream)
            fresh = source == 0
            in_sum[here, :] = jnp.where(fresh, 0.0, in_sum[here, :]) + in_term
            out_sum[here, :] = jnp.where(fresh, 0.0, out_sum[here, :]) + out_term

        for each_expert in range(experts):

            @pl.when((source == sources - 1) & (step == each_expert))
            def _(each_expert=each_expert):
                own_in[each_expert] = in_sum[...].T.astype(BF)
                own_out[each_expert] = out_sum[...].astype(BF)
                for copy in own_copy(each_expert):
                    copy.start()

        return carry

    for index in range(3):
        far_copy(index).start()
    lax.fori_loop(0, turns, turn, 0)
    for stage in stages[len(places) : len(places) + 2]:
        stage()
    for index in range(3 + len(starts), pieces):
        far_copy(index).start()
    for stage in stages[len(places) + 2 :]:
        stage()
    total_ref[...] = small[exp_bits + dp_bits]
    for index in range(pieces):
        far_copy(index).wait()
    for expert in range(experts):
        for copy in own_copy(expert):
            copy.wait()
    for side in range(2):
        for which in range(2):
            for depth in range(exp_bits):
                halving(side, which, depth).wait_send()
                returning(side, which, depth).wait_send()
            for bit in range(dp_bits):
                over(side, which, bit).wait_send()
    for depth in range(exp_bits + dp_bits):
        small_copy(depth).wait_send()


def tail(us, c_rows, c_far, w_in, w_out, far_in, far_out, size, dense_o, dense_qkv, small, capacity, padded, exp_n):
    sources, experts = len(us[0]), len(us)
    rows, width = us[0][0].shape
    far_parts = 4
    exp_bits, dp_bits = exp_n.bit_length() - 1, sources.bit_length() - 1
    lines = 4 * width
    anywhere = pl.BlockSpec(memory_space=pl.ANY)
    dma = pltpu.SemaphoreType.DMA
    return pl.pallas_call(
        functools.partial(tail_kernel, 3, sources, experts, capacity, padded),
        in_specs=[anywhere] * (experts * (2 * sources - 1) + 8),
        out_specs=[anywhere] * 5 + [pl.BlockSpec(memory_space=pltpu.VMEM)],
        out_shape=[
            jax.ShapeDtypeStruct((experts, width, size), BF),
            jax.ShapeDtypeStruct((experts, size, width), BF),
            jax.ShapeDtypeStruct((width, size), BF),
            jax.ShapeDtypeStruct((size, width), BF),
            jax.ShapeDtypeStruct((lines, width), BF),
            jax.ShapeDtypeStruct(small.shape, F32),
        ],
        scratch_shapes=[
            pltpu.VMEM((sources, experts, rows, width), BF),
            pltpu.VMEM((sources, experts, rows, width), BF),
            pltpu.VMEM((2, width, size), BF),
            pltpu.VMEM((2, size, width), BF),
            pltpu.VMEM((size, width), BF),
            pltpu.VMEM((size, width), F32),
            pltpu.VMEM((size, width), F32),
            pltpu.VMEM((experts, width, size), BF),
            pltpu.VMEM((experts, size, width), BF),
            pltpu.VMEM((lines, width), BF),
            pltpu.VMEM((lines, width), BF),
            pltpu.VMEM((2, dp_bits, 2, 2, lines // 2 >> exp_bits, width // 2), BF),
            pltpu.VMEM((exp_bits + dp_bits + 1,) + small.shape, F32),
            pltpu.VMEM((exp_bits + dp_bits,) + small.shape, F32),
            dma((2, sources, experts)),
            dma((2, 2)),
            dma((3,)),
            dma((2, far_parts)),
            dma((2, far_parts)),
            dma((2, experts)),
            dma((2, 2, exp_bits)),
            dma((2, 2, exp_bits)),
            dma((dp_bits, 2, 2)),
            dma((dp_bits, 2, 2)),
            dma((2, 2, exp_bits)),
            dma((2, 2, exp_bits)),
            dma((exp_bits + dp_bits,)),
            dma((exp_bits + dp_bits,)),
            dma((2, 2)),
        ],
        compiler_params=pltpu.CompilerParams(
            vmem_limit_bytes=58 * 2**20, collective_id=2, has_side_effects=True
        ),
        cost_estimate=NO_COST,
    )(*sum(us, []), c_rows, *sum(c_far, []), w_in, w_out, far_in, far_out, dense_o, dense_qkv, small)


def combine_kernel(
    parts, experts, slot_ref, expert_ref, gate_ref, probs_ref, h_ref, c_ref, o_ref,
    e_ref, d_ref, wo_ref, wr_ref, gain_ref, *refs
):
    sent_refs, refs = refs[:parts], refs[parts:]
    mixed_ref, dh_ref, do_ref, wo_ref_out, wr_sum, gain_sum = refs[:6]
    came_refs, refs = refs[6 : 6 + parts * experts], refs[6 + parts * experts :]
    wo_sum, *sems = refs
    step = pl.program_id(0)
    me, blocks = lax.axis_index("exp"), sent_refs[0].shape[0]

    def transfers():
        copies = []
        for expert in range(experts):
            for part in range(parts):
                index = expert * parts + part
                copies += spread(me, sent_refs[part], expert, came_refs[index], sems, index)
        return copies

    @pl.when(step == 0)
    def _():
        greet(me, blocks)
        for copy in transfers():
            copy.start()

    @pl.when(step == pl.num_programs(0) - 1)
    def _():
        for copy in transfers():
            copy.wait()

    tokens, slots = slot_ref.shape[1], e_ref.shape[0]
    slot = as_column(slot_ref[...].astype(F32)).astype(jnp.int32)
    picks = jnp.where(
        slot == lax.broadcasted_iota(jnp.int32, (tokens, slots), 1), 1.0, 0.0
    ).astype(BF)
    returned, arrived = mm(picks, e_ref[...]), mm(picks, d_ref[...])
    gate, probs, mixed = gate_ref[...], probs_ref[...], h_ref[...]
    upstream = c_ref[...].astype(F32)
    mixed_ref[...] = (mixed + gate * returned).astype(BF)
    gate_grad = jnp.sum(upstream * returned, axis=-1, keepdims=True)
    picked = jnp.where(expert_ref[...] == lax.broadcasted_iota(jnp.int32, probs.shape, 1), 1.0, 0.0)
    logit_grad = gate_grad * gate * (picked - probs)
    inv = lax.rsqrt(jnp.mean(mixed * mixed, axis=-1, keepdims=True) + EPSILON)
    unit = mixed * inv
    gain = gain_ref[...]
    lg_high, lg_low = halves(logit_grad)
    wr_high, wr_low = halves(wr_ref[...])
    through_router = mm_nt(lg_high, wr_high) + (mm_nt(lg_low, wr_high) + mm_nt(lg_high, wr_low))
    normed_grad = through_router + gate * arrived
    unit_grad = normed_grad * gain
    mixed_grad = upstream + inv * (
        unit_grad - unit * jnp.mean(unit_grad * unit, axis=-1, keepdims=True)
    )
    dh_ref[...] = mixed_grad
    low = mixed_grad.astype(BF)
    do_ref[...] = mm_nt(low, wo_ref[...]).astype(BF)

    @pl.when(step == 0)
    def _():
        wo_sum[...] = jnp.zeros_like(wo_sum)
        wr_sum[...] = jnp.zeros_like(wr_sum)
        gain_sum[...] = jnp.zeros_like(gain_sum)

    wo_sum[...] += mm(o_ref[...].T, low)
    n_high, n_low = halves(unit * gain)
    lg_high, lg_low = lg_high.T, lg_low.T
    wr_sum[...] += mm(lg_high, n_high) + (mm(lg_low, n_high) + mm(lg_high, n_low))
    gain_sum[...] += jnp.sum(normed_grad * unit, axis=0, keepdims=True)

    @pl.when(step == pl.num_programs(0) - 1)
    def _():
        wo_ref_out[...] = wo_sum[...].astype(BF)


def combine(slot, expert, gate, probs, h, c, o, e_out, du, wo, wr, gain, sent):
    parts, (blocks, local, padded, _) = len(sent), sent[0].shape
    spreads = parts * (local - 1)
    anywhere = pl.BlockSpec(memory_space=pl.ANY)
    tokens, width = h.shape
    slots, experts = e_out.shape[0], wr.shape[1]
    size = 256

    def rows(columns):
        return pl.BlockSpec((size, columns), lambda t: (t, 0))

    def whole(*shape):
        return pl.BlockSpec(shape, lambda t: (0, 0))

    return pl.pallas_call(
        functools.partial(combine_kernel, parts, local - 1),
        grid=(tokens // size,),
        in_specs=[pl.BlockSpec((1, size), lambda t: (0, t)), rows(1), rows(1), rows(experts), rows(width), rows(width), rows(width)]
        + [whole(slots, width)] * 2
        + [whole(width, width), whole(width, experts)]
        + [whole(1, width)]
        + [anywhere] * parts,
        out_specs=[rows(width), rows(width), rows(width), whole(width, width), whole(experts, width)]
        + [whole(1, width)]
        + [anywhere] * spreads,
        out_shape=[
            jax.ShapeDtypeStruct((tokens, width), BF),
            jax.ShapeDtypeStruct((tokens, width), F32),
            jax.ShapeDtypeStruct((tokens, width), BF),
            jax.ShapeDtypeStruct((width, width), BF),
            jax.ShapeDtypeStruct((experts, width), F32),
            jax.ShapeDtypeStruct((1, width), F32),
        ]
        + [jax.ShapeDtypeStruct((blocks, padded, width), BF)] * spreads,
        scratch_shapes=[pltpu.VMEM((width, width), F32)] + spread_sems(spreads, blocks),
        compiler_params=params(collective_id=5, has_side_effects=True),
        cost_estimate=NO_COST,
    )(slot, expert, gate, probs, h, c, o, e_out, du, wo, wr, gain, *sent)


def last_kernel(
    x_ref, dh_ref, dq_ref, dk_ref, dv_ref, wq_ref, wk_ref, wv_ref, gain_ref,
    grad_ref, sums_ref, gain_sum, q_sum, k_sum, v_sum,
):
    step = pl.program_id(0)
    width = x_ref.shape[1]

    @pl.when(step == 0)
    def _():
        for total in (q_sum, k_sum, v_sum, gain_sum):
            total[...] = jnp.zeros_like(total)

    rows = x_ref[...].astype(F32)
    inv = lax.rsqrt(jnp.mean(rows * rows, axis=-1, keepdims=True) + EPSILON)
    unit = rows * inv
    gain = gain_ref[...]
    normed_t = (unit * gain).astype(BF).T
    normed_grad = None
    for grad_ref_in, weight_ref, total in (
        (dq_ref, wq_ref, q_sum),
        (dk_ref, wk_ref, k_sum),
        (dv_ref, wv_ref, v_sum),
    ):
        grad = grad_ref_in[...]
        total[...] += mm(normed_t, grad)
        term = mm_nt(grad, weight_ref[...])
        normed_grad = term if normed_grad is None else normed_grad + term
    unit_grad = normed_grad * gain
    grad_ref[...] = dh_ref[...] + inv * (
        unit_grad - unit * jnp.mean(unit_grad * unit, axis=-1, keepdims=True)
    )
    gain_sum[...] += jnp.sum(normed_grad * unit, axis=0, keepdims=True)

    @pl.when(step == pl.num_programs(0) - 1)
    def _():
        for which, total in enumerate((q_sum, k_sum, v_sum)):
            sums_ref[which * width : (which + 1) * width, :] = total[...].astype(BF)


def last(x, dh, dq, dk, dv, wq, wk, wv, gain):
    tokens, width = x.shape
    size = 256
    rows = pl.BlockSpec((size, width), lambda t: (t, 0))
    square = pl.BlockSpec((width, width), lambda t: (0, 0))
    one = pl.BlockSpec((1, width), lambda t: (0, 0))
    return pl.pallas_call(
        last_kernel,
        grid=(tokens // size,),
        in_specs=[rows] * 5 + [square] * 3 + [one],
        out_specs=[rows, pl.BlockSpec((3 * width, width), lambda t: (0, 0)), one],
        out_shape=[
            jax.ShapeDtypeStruct((tokens, width), F32),
            jax.ShapeDtypeStruct((3 * width, width), BF),
            jax.ShapeDtypeStruct((1, width), F32),
        ],
        scratch_shapes=[pltpu.VMEM((width, width), F32)] * 3,
        compiler_params=params(),
        cost_estimate=NO_COST,
    )(x, dh, dq, dk, dv, wq, wk, wv, gain)


def per_device(
    tokens,
    w_query,
    w_key,
    w_value,
    w_output,
    norm_attn,
    norm_ffn,
    relative_bias_table,
    w_router,
    w_in,
    w_out,
    expert_index,
    priority,
    cotangent,
):
    tok_rows, width = tokens.shape
    local = w_in.shape[0]
    exp_n, dp_n = lax.axis_size("exp"), lax.axis_size("dp")
    exp_me, dp_me = lax.axis_index("exp"), lax.axis_index("dp")
    all_experts = local * exp_n
    capacity = (5 * tok_rows + 4 * all_experts - 1) // (4 * all_experts)
    padded = (capacity + 1 + 15) // 16 * 16
    block = local * padded
    buckets = relative_bias_table.shape[0]

    chosen = expert_index[:, 0]
    order = priority[0]
    ahead = (chosen[:, None] == chosen[None, :]) & (order[None, :] < order[:, None])
    rank = jnp.sum(ahead.astype(jnp.int32), axis=1)
    place = ((chosen // local) ^ exp_me) * block + (chosen % local) * padded + rank
    slots = jnp.where(rank < capacity, place, -1)
    slot_row = slots[None, :]
    half = local // 2
    group = dp_me % 2
    inside = chosen % local
    grouped = ((inside // half + group) % 2 * exp_n + place // block) * half + inside % half
    c_row = jnp.where(rank < capacity, grouped * padded + rank, -1)[None, :]

    def to_dp(rows, step):
        return lax.ppermute(rows, "dp", [(i, i ^ step) for i in range(dp_n)])

    def over_dp(mine, other):
        return [mine] + [to_dp(other if step % 2 else mine, step) for step in range(1, dp_n)]

    lines = jnp.dot(
        relative_bias_table.T, diagonal_onehot(buckets).T, precision=FULL_PRECISION
    ).reshape(HEADS, 4, TILE)
    lines = jnp.concatenate([lines, jnp.zeros_like(lines)], axis=1)
    gain_attn, gain_ffn = norm_attn[None, :], norm_ffn[None, :]
    q, k, v = qkv(tokens, gain_attn, w_query, w_key, w_value)
    c_sent = [
        part.reshape(exp_n, half, padded, width)
        for part in dispatch_by_group(c_row, cotangent, exp_n * half * padded)
    ]
    c_far = over_dp(*c_sent)[1:]
    context, lse, c_rows = attention(lines, c_sent, q, k, v)
    c_rows = c_rows.reshape(local, exp_n * padded, width)
    mixed, u, probs, gate, gate_row = router(
        context, tokens, w_output, gain_ffn, w_router, expert_index
    )
    sent = dispatch(slot_row, u, exp_n, block, gate=(gate_row, local, capacity, padded))
    u_rows, e_back, d_back = expert_pass(
        sent.reshape(exp_n, local, padded, width), c_rows, w_in, w_out
    )
    mine, other = u_rows[:half], u_rows[half:]
    mine[0], other[0], c_far[0] = lax.optimization_barrier((mine[0], other[0], c_far[0]))
    u_all = [over_dp(mine[0], other[0])]
    for expert in range(1, half):
        e_back, mine[expert], other[expert], *c_far[1:] = lax.optimization_barrier(
            (e_back, mine[expert], other[expert], *c_far[1:])
        )
        u_all.append([mine[expert], None] + [
            to_dp(other[expert] if step % 2 else mine[expert], step) for step in range(2, dp_n)
        ])
    e_back, d_back = e_back.reshape(-1, width), d_back.reshape(-1, width)
    mixed_out, mixed_grad, context_grad, output_part, router_part, norm_ffn_part, *c_early = combine(
        slot_row, expert_index, gate, probs, mixed, cotangent, context,
        e_back, d_back, w_output, w_router, gain_ffn, c_far,
    )
    for expert in range(1, half):
        context_grad, *u_all[0], other[expert] = lax.optimization_barrier(
            (context_grad, *u_all[0], other[expert])
        )
        u_all[expert][1] = to_dp(other[expert], 1)
    size = w_in.shape[2] // dp_n
    rows = exp_n * padded
    c_early = [part.reshape(rows, width) for part in c_early]
    c_spread = [c_early[at : at + dp_n - 1] for at in range(0, len(c_early), dp_n - 1)]

    def for_partner(expert):
        where = jnp.stack([group * half + expert, dp_me // 2 * 2 + 1 - group]).astype(jnp.int32)
        return weight_grads(
            where, u_all[expert], c_rows, c_spread[expert], w_in, w_out, size, capacity, padded
        )

    got = []
    for expert in range(half - 1):
        context_grad, *far = lax.optimization_barrier((context_grad, *for_partner(expert)))
        got += [to_dp(array, 1) for array in far]
    query_grad, key_grad, value_grad, sums, *c_late = attention_back(
        lines, q, k, v, context_grad, lse, c_far
    )
    c_spread.append([part.reshape(rows, width) for part in c_late])
    query_grad, far_in, far_out = lax.optimization_barrier((query_grad, *for_partner(half - 1)))
    table_part = jnp.dot(
        diagonal_onehot(buckets).T,
        sums[:, :4].reshape(HEADS, 4 * TILE).T,
        precision=FULL_PRECISION,
    )
    grad_tokens, qkv_part, norm_attn_part = last(
        tokens, mixed_grad, query_grad, key_grad, value_grad, w_query, w_key, w_value, gain_attn
    )

    table_line = jnp.pad(table_part.reshape(1, -1), ((0, 0), (0, width - table_part.size)))
    small = jnp.concatenate([router_part, norm_attn_part, norm_ffn_part, table_line], axis=0)
    small = jnp.pad(small, ((0, -small.shape[0] % 8), (0, 0)))
    own_in, own_out, came_in, came_out, dense, total = tail(
        u_all, c_rows, c_spread, w_in, w_out, far_in, far_out, size, output_part, qkv_part, small, capacity, padded, exp_n
    )
    experts = jnp.arange(local, dtype=jnp.int32)
    grad_in, grad_out, *dense_grads = finish(
        jnp.where(group == 0, experts, (experts + half) % local),
        own_in,
        own_out,
        got[0::2] + [came_in],
        got[1::2] + [came_out],
        dense,
    )
    return (
        mixed_out,
        grad_tokens,
        *dense_grads,
        total[all_experts],
        total[all_experts + 1],
        total[all_experts + 2, : table_part.size].reshape(table_part.shape),
        total[:all_experts].T,
        grad_in,
        grad_out,
    )


def solution(mesh):
    return jax.shard_map(
        per_device,
        mesh=mesh,
        in_specs=(
            P(("exp", "dp"), None),
            P(),
            P(),
            P(),
            P(),
            P(),
            P(),
            P(),
            P(),
            P("exp", None, None),
            P("exp", None, None),
            P(("exp", "dp"), None),
            P(("exp", "dp"), None),
            P(("exp", "dp"), None),
        ),
        out_specs=(
            P(("exp", "dp"), None),
            P(("exp", "dp"), None),
            P(),
            P(),
            P(),
            P(),
            P(),
            P(),
            P(),
            P(),
            P("exp", None, "dp"),
            P("exp", "dp", None),
        ),
        check_vma=False,
    )
```

```python
import functools

import jax
import jax.numpy as jnp
from jax import lax
from jax.experimental import pallas as pl
from jax.experimental.pallas import tpu as pltpu
from jax.sharding import PartitionSpec as P

HEADS = 12
HEAD_DIM = 64
SEQ = 512
LIMITS = (12, 16, 23, 32, 46, 64, 91)
EPSILON = 1e-06
FULL_PRECISION = lax.Precision.HIGHEST
BF = jnp.bfloat16
F32 = jnp.float32
PAIR = 2 * HEAD_DIM
TILE = 128
CHUNK = 256
GELU_A = 0.7978845608028654
GELU_B = 0.044715 * GELU_A
VMEM_MIB = 58
NO_COST = pl.CostEstimate(flops=0, bytes_accessed=2**16, transcendentals=0)


def params(**more):
    return pltpu.CompilerParams(vmem_limit_bytes=VMEM_MIB * 2**20, **more)


def mm(left, right):
    return jnp.dot(left, right, preferred_element_type=F32)


def mm_nt(left, right):
    return lax.dot_general(left, right, (((1,), (1,)), ((), ())), preferred_element_type=F32)


def flipped(index, step):
    bit = 1
    while bit <= step:
        if step & bit:
            index = index + bit * (1 - 2 * ((index // bit) % 2))
        bit *= 2
    return index


def greet(me, blocks, others=()):
    barrier = pltpu.get_barrier_semaphore()
    devices = [{"exp": flipped(me, block)} for block in range(1, blocks)] + list(others)
    for device in devices:
        pl.semaphore_signal(barrier, inc=1, device_id=device, device_id_type=pl.DeviceIdType.MESH)
    pl.semaphore_wait(barrier, len(devices))


def spread(me, sent, expert, came, sems, index):
    local_sem, send_sem, recv_sem = sems
    copies = [pltpu.make_async_copy(sent.at[0, expert], came.at[0], local_sem.at[index])]
    for block in range(1, came.shape[0]):
        copies.append(
            pltpu.make_async_remote_copy(
                src_ref=sent.at[block, expert],
                dst_ref=came.at[block],
                send_sem=send_sem.at[index, block],
                recv_sem=recv_sem.at[index, block],
                device_id={"exp": flipped(me, block)},
                device_id_type=pl.DeviceIdType.MESH,
            )
        )
    return copies


def spread_sems(count, blocks):
    dma = pltpu.SemaphoreType.DMA
    return [dma((count,)), dma((count, blocks)), dma((count, blocks))]


def halves(array):
    high = array.astype(BF)
    return high, (array - high.astype(F32)).astype(BF)


def as_column(line):
    size = line.shape[1]
    diagonal = lax.broadcasted_iota(jnp.int32, (size, size), 0) == lax.broadcasted_iota(
        jnp.int32, (size, size), 1
    )
    return jnp.sum(jnp.where(diagonal, line, 0.0), axis=1, keepdims=True)


def bucket_of(offset):
    distance = jnp.abs(offset)
    farther = jnp.zeros_like(distance)
    for limit in LIMITS:
        farther = farther + (distance >= limit).astype(jnp.int32)
    return jnp.where(distance < 8, distance, 8 + farther) + jnp.where(offset > 0, 16, 0)


def diagonal_onehot(count):
    places = jnp.arange(TILE, dtype=jnp.int32)
    offsets = jnp.concatenate([-places, TILE - places, 0 * places - SEQ, 0 * places + SEQ])
    return (bucket_of(offsets)[:, None] == jnp.arange(count, dtype=jnp.int32)[None, :]).astype(F32)


def dispatch_gate_kernel(experts, capacity, padded, slot_ref, gate_ref, rows_ref, out_ref):
    block, tokens = out_ref.shape[0], rows_ref.shape[0]
    width = out_ref.shape[1]
    step = pl.program_id(0)
    ids = lax.broadcasted_iota(jnp.int32, (block, tokens), 0) + step * block
    picks = jnp.where(slot_ref[...] == ids, 1.0, 0.0).astype(BF)
    out = mm(picks, rows_ref[...])
    gates = jnp.broadcast_to(gate_ref[...].astype(BF), (8, tokens))
    lanes = pl.num_programs(0) * padded
    in_slots = mm_nt(gates, picks)
    in_slots = jnp.concatenate([in_slots, jnp.zeros((8, lanes - block), F32)], axis=1)
    lane = lax.broadcasted_iota(jnp.int32, (8, lanes), 1)
    row = lax.broadcasted_iota(jnp.int32, (block, 1), 0)
    left = out[:, :lanes]
    for expert in range(experts):
        shift = lax.rem(step * padded - expert * padded + lanes, lanes)
        moved = pltpu.roll(in_slots, shift, 1)
        mine = (lane >= step * padded) & (lane < step * padded + capacity)
        moved = jnp.where(mine, moved, 0.0)[:1]
        left = jnp.where(row == expert * padded + capacity, moved, left)
    out_ref[:, :lanes] = left.astype(BF)
    out_ref[:, lanes:] = out[:, lanes:].astype(BF)


def dispatch(slot_row, rows, blocks, block, gate):
    tokens, width = rows.shape
    grid_spec = dict(
        grid=(blocks,),
        out_specs=pl.BlockSpec((block, width), lambda k: (k, 0)),
        out_shape=jax.ShapeDtypeStruct((blocks * block, width), BF),
    )
    line = pl.BlockSpec((1, tokens), lambda k: (0, 0))
    full = pl.BlockSpec((tokens, width), lambda k: (0, 0))
    values, experts, capacity, padded = gate
    return pl.pallas_call(
        functools.partial(dispatch_gate_kernel, experts, capacity, padded),
        in_specs=[line, line, full],
        compiler_params=params(),
        cost_estimate=NO_COST,
        **grid_spec,
    )(slot_row, values, rows)


def dispatch_by_group_kernel(slot_ref, rows_ref, mine_ref, other_ref):
    block, tokens = mine_ref.shape[0], rows_ref.shape[0]
    step = pl.program_id(0)
    ids = lax.broadcasted_iota(jnp.int32, (block, tokens), 0) + step * block
    picks = jnp.where(slot_ref[...] == ids, 1.0, 0.0).astype(BF)
    out = mm(picks, rows_ref[...]).astype(BF)
    first = step < pl.num_programs(0) // 2

    @pl.when(first)
    def _():
        mine_ref[...] = out

    @pl.when(jnp.logical_not(first))
    def _():
        other_ref[...] = out


def dispatch_by_group(slot_row, rows, slots):
    tokens, width = rows.shape
    block = 256
    steps = slots // block
    return pl.pallas_call(
        dispatch_by_group_kernel,
        grid=(2 * steps,),
        in_specs=[
            pl.BlockSpec((1, tokens), lambda k: (0, 0)),
            pl.BlockSpec((tokens, width), lambda k: (0, 0)),
        ],
        out_specs=[
            pl.BlockSpec((block, width), lambda k: (jnp.minimum(k, steps - 1), 0)),
            pl.BlockSpec((block, width), lambda k: (jnp.maximum(k - steps, 0), 0)),
        ],
        out_shape=[jax.ShapeDtypeStruct((slots, width), BF)] * 2,
        compiler_params=params(),
        cost_estimate=NO_COST,
    )(slot_row, rows)


def qkv_kernel(x_ref, gain_ref, wq_ref, wk_ref, wv_ref, q_ref, k_ref, v_ref):
    rows = x_ref[...].astype(F32)
    inv = lax.rsqrt(jnp.mean(rows * rows, axis=-1, keepdims=True) + EPSILON)
    normed = (rows * inv * gain_ref[...]).astype(BF)
    q_ref[...] = (mm(normed, wq_ref[...]).astype(BF).astype(F32) * HEAD_DIM**-0.5).astype(BF)
    k_ref[...] = mm(normed, wk_ref[...]).astype(BF)
    v_ref[...] = mm(normed, wv_ref[...]).astype(BF)


def qkv(x, gain, wq, wk, wv):
    tokens, width = x.shape
    rows = pl.BlockSpec((SEQ, width), lambda t: (t, 0))
    square = pl.BlockSpec((width, width), lambda t: (0, 0))
    one = pl.BlockSpec((1, width), lambda t: (0, 0))
    return pl.pallas_call(
        qkv_kernel,
        grid=(tokens // SEQ,),
        in_specs=[rows, one, square, square, square],
        out_specs=[rows] * 3,
        out_shape=[jax.ShapeDtypeStruct((tokens, width), BF)] * 3,
        compiler_params=params(),
        cost_estimate=NO_COST,
    )(x, gain, wq, wk, wv)


def fill_bias(lines_ref, bias_ref):
    upper_right = lax.broadcasted_iota(jnp.int32, (TILE, TILE), 0) <= lax.broadcasted_iota(
        jnp.int32, (TILE, TILE), 1
    )
    tiles = SEQ // TILE
    for head in range(2):

        def sheared(line):
            whole = jnp.broadcast_to(lines_ref[head, line : line + 1, :], (TILE, TILE))
            return pltpu.roll(whole, 0, 1, stride=1, stride_axis=0)

        negative, positive = sheared(0), sheared(1)
        far_negative = jnp.broadcast_to(lines_ref[head, 2:3, :], (TILE, TILE))
        far_positive = jnp.broadcast_to(lines_ref[head, 3:4, :], (TILE, TILE))
        same = jnp.where(upper_right, negative, positive)
        above = jnp.where(upper_right, positive, far_positive)
        below = jnp.where(upper_right, far_negative, negative)
        for key in range(tiles):
            for query in range(tiles):
                gap = key - query
                tile = (
                    same
                    if gap == 0
                    else above
                    if gap == 1
                    else below
                    if gap == -1
                    else far_positive
                    if gap > 0
                    else far_negative
                )
                bias_ref[head, pl.ds(key * TILE, TILE), pl.ds(query * TILE, TILE)] = tile


def head_lanes(head):
    lane = lax.broadcasted_iota(jnp.int32, (1, PAIR), 1)
    return (lane >= head * HEAD_DIM) & (lane < (head + 1) * HEAD_DIM)


def only(head, array):
    return jnp.where(head_lanes(head), array, jnp.zeros_like(array))


def attention_kernel(
    lines_ref, mine_ref, other_ref, q_ref, k_ref, v_ref, o_ref, lse_ref, came_ref,
    bias_ref, local_sem, send_sem, recv_sem
):
    pair, seq = pl.program_id(0), pl.program_id(1)
    blocks, half = mine_ref.shape[:2]
    me, group = lax.axis_index("exp"), lax.axis_index("dp") % 2

    def transfers():
        copies = []
        for kind, sent in enumerate((mine_ref, other_ref)):
            experts = pl.ds((group + kind) % 2 * half, half)
            copies.append(
                pltpu.make_async_copy(sent.at[0], came_ref.at[experts, 0], local_sem.at[kind])
            )
            for block in range(1, blocks):
                copies.append(
                    pltpu.make_async_remote_copy(
                        src_ref=sent.at[block],
                        dst_ref=came_ref.at[experts, block],
                        send_sem=send_sem.at[kind, block],
                        recv_sem=recv_sem.at[kind, block],
                        device_id={"exp": flipped(me, block)},
                        device_id_type=pl.DeviceIdType.MESH,
                    )
                )
        return copies

    @pl.when((pair == 0) & (seq == 0))
    def _():
        greet(me, blocks)
        for copy in transfers():
            copy.start()

    @pl.when(seq == 0)
    def _():
        fill_bias(lines_ref, bias_ref)

    keys = k_ref[...]
    values_t = v_ref[...].T
    masked = [only(head, keys) for head in range(2)]
    row = lax.broadcasted_iota(jnp.int32, (PAIR, 1), 0)
    for part in range(SEQ // CHUNK):
        places = pl.ds(part * CHUNK, CHUNK)
        queries = q_ref[places, :]
        out = None
        for head in range(2):
            scores = mm_nt(masked[head], queries) + bias_ref[head, :, places]
            highest = jnp.max(scores, axis=0, keepdims=True)
            weights = jnp.exp(scores - highest)
            total = jnp.sum(weights, axis=0, keepdims=True)
            lse_ref[0, 0, head : head + 1, places] = highest + jnp.log(total)
            mixed = mm(values_t, weights.astype(BF)) * (1.0 / total)
            out = mixed if out is None else jnp.where(row < HEAD_DIM, out, mixed)
        o_ref[places, :] = out.T.astype(BF)

    @pl.when((pair == pl.num_programs(0) - 1) & (seq == pl.num_programs(1) - 1))
    def _():
        for copy in transfers():
            copy.wait()


def attention(lines, sent, q, k, v):
    blocks, half, padded, width = sent[0].shape
    tokens, width = q.shape
    seqs, pairs = tokens // SEQ, width // PAIR
    block = pl.BlockSpec((SEQ, PAIR), lambda h, s: (s, h))
    return pl.pallas_call(
        attention_kernel,
        grid=(pairs, seqs),
        in_specs=[pl.BlockSpec((2, 8, TILE), lambda h, s: (h, 0, 0))]
        + [pl.BlockSpec(memory_space=pl.ANY)] * 2
        + [block, block, block],
        out_specs=[block, pl.BlockSpec((1, 1, 2, SEQ), lambda h, s: (h, s, 0, 0))]
        + [pl.BlockSpec(memory_space=pl.ANY)],
        out_shape=[
            jax.ShapeDtypeStruct((tokens, width), BF),
            jax.ShapeDtypeStruct((pairs, seqs, 2, SEQ), F32),
            jax.ShapeDtypeStruct((2 * half, blocks, padded, width), BF),
        ],
        scratch_shapes=[pltpu.VMEM((2, SEQ, SEQ), F32)] + spread_sems(2, blocks),
        compiler_params=params(collective_id=1, has_side_effects=True),
        cost_estimate=NO_COST,
    )(lines, *sent, q, k, v)


def attention_back_kernel(parts, lines_ref, q_ref, k_ref, v_ref, do_ref, lse_ref, *refs):
    sent_refs, refs = refs[:parts], refs[parts:]
    dq_ref, dk_ref, dv_ref, sums_ref = refs[:4]
    came_refs, refs = refs[4 : 4 + parts], refs[4 + parts :]
    bias_ref, diag_ref, *sems = refs
    pair, seq = pl.program_id(0), pl.program_id(1)
    blocks, expert = came_refs[0].shape[0], sent_refs[0].shape[1] - 1
    me = lax.axis_index("exp")

    def transfers():
        copies = []
        for part in range(parts):
            copies += spread(me, sent_refs[part], expert, came_refs[part], sems, part)
        return copies

    @pl.when((pair == 0) & (seq == 0))
    def _():
        greet(me, blocks)
        for copy in transfers():
            copy.start()

    @pl.when((pair == pl.num_programs(0) - 1) & (seq == pl.num_programs(1) - 1))
    def _():
        for copy in transfers():
            copy.wait()

    @pl.when(seq == 0)
    def _():
        fill_bias(lines_ref, bias_ref)
        diag_ref[...] = jnp.zeros_like(diag_ref)

    keys, values = k_ref[...], v_ref[...]
    keys_t = keys.T
    masked_k = [only(head, keys) for head in range(2)]
    masked_v = [only(head, values) for head in range(2)]
    row = lax.broadcasted_iota(jnp.int32, (PAIR, 1), 0)
    grads_k, grads_v = [None, None], [None, None]
    tiles = SEQ // TILE
    for part in range(SEQ // CHUNK):
        places = pl.ds(part * CHUNK, CHUNK)
        queries, upstream = q_ref[places, :], do_ref[places, :]
        grad_q = None
        for head in range(2):
            scores = mm_nt(masked_k[head], queries) + bias_ref[head, :, places]
            weights = jnp.exp(scores - lse_ref[0, 0, head : head + 1, places])
            products = weights * mm_nt(masked_v[head], upstream)
            scores_grad = products - weights * jnp.sum(products, axis=0, keepdims=True)
            low = scores_grad.astype(BF)
            value_term = mm(weights.astype(BF), upstream)
            key_term = mm(low, queries)
            grads_v[head] = value_term if part == 0 else grads_v[head] + value_term
            grads_k[head] = key_term if part == 0 else grads_k[head] + key_term
            query_term = mm(keys_t, low)
            grad_q = query_term if head == 0 else jnp.where(row < HEAD_DIM, grad_q, query_term)
            groups = {}
            for query in range(CHUNK // TILE):
                for key in range(tiles):
                    gap = key - (query + part * (CHUNK // TILE))
                    kind = 0 if gap == 0 else 1 if gap == 1 else 2 if gap == -1 else 3 if gap > 0 else 4
                    tile = scores_grad[
                        key * TILE : (key + 1) * TILE, query * TILE : (query + 1) * TILE
                    ]
                    groups[kind] = tile if kind not in groups else groups[kind] + tile
            for kind, tile in groups.items():
                diag_ref[head, kind] += tile
        dq_ref[places, :] = (grad_q * HEAD_DIM**-0.5).T.astype(BF)
    first = head_lanes(0)
    dk_ref[...] = jnp.where(first, grads_k[0], grads_k[1]).astype(BF)
    dv_ref[...] = jnp.where(first, grads_v[0], grads_v[1]).astype(BF)

    @pl.when(seq == pl.num_programs(1) - 1)
    def _():
        upper_right = lax.broadcasted_iota(jnp.int32, (TILE, TILE), 0) <= lax.broadcasted_iota(
            jnp.int32, (TILE, TILE), 1
        )
        sums_ref[...] = jnp.zeros_like(sums_ref)
        for head in range(2):
            same, above, below = diag_ref[head, 0], diag_ref[head, 1], diag_ref[head, 2]

            def gathered(array):
                row_id = lax.broadcasted_iota(jnp.int32, (TILE, 1), 0)
                bit = 1
                while bit < TILE:
                    turned = pltpu.roll(array, TILE - bit, 1)
                    array = jnp.where((row_id & bit) != 0, turned, array)
                    bit *= 2
                return jnp.sum(array, axis=0, keepdims=True)

            zero = jnp.zeros_like(same)
            sums_ref[head, 0:1, :] = gathered(jnp.where(upper_right, same, below))
            sums_ref[head, 1:2, :] = gathered(jnp.where(upper_right, above, same))
            sums_ref[head, 2:3, :] = jnp.sum(
                diag_ref[head, 4] + jnp.where(upper_right, below, zero), axis=0, keepdims=True
            )
            sums_ref[head, 3:4, :] = jnp.sum(
                diag_ref[head, 3] + jnp.where(upper_right, zero, above), axis=0, keepdims=True
            )


def attention_back(lines, q, k, v, do, lse, sent):
    parts = len(sent)
    blocks, _, padded, _ = sent[0].shape
    anywhere = pl.BlockSpec(memory_space=pl.ANY)
    tokens, width = q.shape
    seqs, pairs = tokens // SEQ, width // PAIR
    block = pl.BlockSpec((SEQ, PAIR), lambda h, s: (s, h))
    lines_spec = pl.BlockSpec((2, 8, TILE), lambda h, s: (h, 0, 0))
    return pl.pallas_call(
        functools.partial(attention_back_kernel, parts),
        grid=(pairs, seqs),
        in_specs=[lines_spec, block, block, block, block]
        + [pl.BlockSpec((1, 1, 2, SEQ), lambda h, s: (h, s, 0, 0))]
        + [anywhere] * parts,
        out_specs=[block, block, block, lines_spec] + [anywhere] * parts,
        out_shape=[jax.ShapeDtypeStruct((tokens, width), BF)] * 3
        + [jax.ShapeDtypeStruct((2 * pairs, 8, TILE), F32)]
        + [jax.ShapeDtypeStruct((blocks, padded, width), BF)] * parts,
        scratch_shapes=[
            pltpu.VMEM((2, SEQ, SEQ), F32),
            pltpu.VMEM((2, 5, TILE, TILE), F32),
            *spread_sems(parts, blocks),
        ],
        compiler_params=params(collective_id=4, has_side_effects=True),
        cost_estimate=pl.CostEstimate(
            flops=40 * pairs * seqs * SEQ * SEQ * PAIR,
            bytes_accessed=14 * tokens * width,
            transcendentals=2 * pairs * seqs * SEQ * SEQ,
        ),
    )(lines, q, k, v, do, lse, *sent)


def router_kernel(
    o_ref, x_ref, wo_ref, gain_ref, wr_ref, expert_ref, h_ref, u_ref, probs_ref, gate_ref, line_ref
):
    mixed = x_ref[...].astype(F32) + mm(o_ref[...], wo_ref[...])
    h_ref[...] = mixed
    inv = lax.rsqrt(jnp.mean(mixed * mixed, axis=-1, keepdims=True) + EPSILON)
    normed = mixed * inv * gain_ref[...]
    u_ref[...] = normed.astype(BF)
    high, low = halves(normed)
    wr_high, wr_low = halves(wr_ref[...])
    logits = mm(high, wr_high) + (mm(high, wr_low) + mm(low, wr_high))
    spread = jnp.exp(logits - jnp.max(logits, axis=-1, keepdims=True))
    probs = spread / jnp.sum(spread, axis=-1, keepdims=True)
    probs_ref[...] = probs
    picked = expert_ref[...] == lax.broadcasted_iota(jnp.int32, probs.shape, 1)
    gate = jnp.sum(jnp.where(picked, probs, 0.0), axis=-1, keepdims=True)
    gate_ref[...] = gate
    size = gate.shape[0]
    diagonal = lax.broadcasted_iota(jnp.int32, (size, size), 0) == lax.broadcasted_iota(
        jnp.int32, (size, size), 1
    )
    line_ref[...] = jnp.sum(jnp.where(diagonal, gate, 0.0), axis=0, keepdims=True)


def router(o, x, wo, gain, wr, expert):
    tokens, width = x.shape
    experts = wr.shape[1]
    size = 256

    def rows(columns):
        return pl.BlockSpec((size, columns), lambda t: (t, 0))

    def whole(*shape):
        return pl.BlockSpec(shape, lambda t: (0, 0))

    return pl.pallas_call(
        router_kernel,
        grid=(tokens // size,),
        in_specs=[rows(width), rows(width), whole(width, width), whole(1, width)]
        + [whole(width, experts), rows(1)],
        out_specs=[rows(width), rows(width), rows(experts), rows(1)]
        + [pl.BlockSpec((1, size), lambda t: (0, t))],
        out_shape=[
            jax.ShapeDtypeStruct((tokens, width), F32),
            jax.ShapeDtypeStruct((tokens, width), BF),
            jax.ShapeDtypeStruct((tokens, experts), F32),
            jax.ShapeDtypeStruct((tokens, 1), F32),
            jax.ShapeDtypeStruct((1, tokens), F32),
        ],
        compiler_params=params(),
        cost_estimate=NO_COST,
    )(o, x, wo, gain, wr, expert)


def gelu_and_slope(z):
    square = z * z
    half = 0.5 + 0.5 * jnp.tanh(z * (GELU_A + GELU_B * square))
    value = z * half
    slope = half + 2.0 * value * (1.0 - half) * (GELU_A + 3.0 * GELU_B * square)
    return value, slope


def send_back(me, held, target, which, place, sems, kind):
    send_sem, recv_sem, local_sem = sems
    copies = [pltpu.make_async_copy(held.at[0], target.at[0, which], local_sem.at[kind, place])]
    for block in range(1, held.shape[0]):
        copies.append(
            pltpu.make_async_remote_copy(
                src_ref=held.at[block],
                dst_ref=target.at[block, which],
                send_sem=send_sem.at[kind, place, block],
                recv_sem=recv_sem.at[kind, place, block],
                device_id={"exp": flipped(me, block)},
                device_id_type=pl.DeviceIdType.MESH,
            )
        )
    return copies


def expert_step(parts, rows, upstream, first_ref, second_ref, e_sum, d_sum):
    columns = first_ref.shape[2] // parts
    for part in range(parts):
        places = slice(part * columns, (part + 1) * columns)
        first, second = first_ref[0, :, places], second_ref[0, places, :]
        value, slope = gelu_and_slope(mm(rows, first))
        inner = (mm_nt(upstream, second) * slope).astype(BF)
        e_sum[...] += mm(value.astype(BF), second)
        d_sum[...] += mm_nt(inner, first)


def expert_kernel(parts, all_experts, sent_ref, c_ref, first_ref, second_ref, *refs):
    expert, step = pl.program_id(0), pl.program_id(1)
    count, last_step = pl.num_programs(0), pl.num_programs(1) - 1
    u_refs, u_late, refs = refs[:all_experts], refs[all_experts], refs[all_experts + 1 :]
    e_kept, d_kept, rows_ref, e_sum, d_sum, e_held, d_held, local_sem, send_sem, recv_sem = refs
    early, blocks, padded, width = e_held.shape
    me = lax.axis_index("exp")
    group, half = lax.axis_index("dp") % 2, all_experts // 2

    def outgoing(which, block):
        return pltpu.make_async_remote_copy(
            src_ref=sent_ref.at[block, which],
            dst_ref=rows_ref.at[which, block],
            send_sem=send_sem.at[which, block],
            recv_sem=recv_sem.at[which, block],
            device_id={"exp": flipped(me, block)},
            device_id_type=pl.DeviceIdType.MESH,
        )

    def own_in(which):
        return pltpu.make_async_copy(sent_ref.at[0, which], rows_ref.at[which, 0], local_sem.at[0, which])

    def keep(which, act):
        for each in range(2):
            target = u_refs[(which // half + each) % 2 * half + which % half]

            @pl.when(group == each)
            def _(target=target):
                act(pltpu.make_async_copy(rows_ref.at[which], target, local_sem.at[1, which]))

        if which >= early:
            act(
                pltpu.make_async_copy(
                    rows_ref.at[which], u_late.at[which - early], local_sem.at[2, which - early]
                )
            )

    def arrive(which):
        own_in(which).wait()
        for block in range(1, blocks):
            outgoing(which, block).wait_recv()
        keep(which, lambda copy: copy.start())

    def keep_result(which):
        return [
            pltpu.make_async_copy(e_held.at[which], e_kept.at[which], local_sem.at[3, which]),
            pltpu.make_async_copy(d_held.at[which], d_kept.at[which], local_sem.at[4, which]),
        ]

    @pl.when((expert == 0) & (step == 0))
    def _():
        greet(me, blocks)
        for which in range(all_experts):
            own_in(which).start()
            for block in range(1, blocks):
                outgoing(which, block).start()

    @pl.when(step == 0)
    def _():
        for which in range(early):

            @pl.when(expert == which)
            def _(which=which):
                arrive(which)

        e_sum[...] = jnp.zeros_like(e_sum)
        d_sum[...] = jnp.zeros_like(d_sum)

    rows = rows_ref[expert].reshape(blocks * padded, width)
    expert_step(parts, rows, c_ref[0], first_ref, second_ref, e_sum, d_sum)

    @pl.when(step == last_step)
    def _():
        e_held[expert] = e_sum[...].astype(BF).reshape(blocks, padded, width)
        d_held[expert] = d_sum[...].astype(BF).reshape(blocks, padded, width)
        for which in range(early):

            @pl.when(expert == which)
            def _(which=which):
                for copy in keep_result(which):
                    copy.start()

    @pl.when((step == last_step) & (expert == count - 1))
    def _():
        for which in range(early, all_experts):
            arrive(which)
        for which in range(all_experts):
            keep(which, lambda copy: copy.wait())
            for block in range(1, blocks):
                outgoing(which, block).wait_send()
        for which in range(early):
            for copy in keep_result(which):
                copy.wait()


def expert_rest_kernel(
    parts, u_ref, c_ref, first_ref, second_ref, e_kept, d_kept, e_ref, d_ref,
    e_sum, d_sum, e_held, d_held, back_send, back_recv, back_local,
):
    expert, step = pl.program_id(0), pl.program_id(1)
    count, last_step = pl.num_programs(0), pl.num_programs(1) - 1
    late, blocks, padded, width = e_held.shape
    kept = e_kept.shape[0]
    me = lax.axis_index("exp")
    sems = (back_send, back_recv, back_local)

    def back(which):
        if which < kept:
            e_from, d_from = e_kept.at[which], d_kept.at[which]
        else:
            e_from, d_from = e_held.at[which - kept], d_held.at[which - kept]
        return send_back(me, e_from, e_ref, which, which, sems, 0) + send_back(
            me, d_from, d_ref, which, which, sems, 1
        )

    @pl.when((expert == 0) & (step == 0))
    def _():
        greet(me, blocks)
        for which in range(kept):
            for copy in back(which):
                copy.start()

    @pl.when(step == 0)
    def _():
        e_sum[...] = jnp.zeros_like(e_sum)
        d_sum[...] = jnp.zeros_like(d_sum)

    rows = u_ref[0].reshape(blocks * padded, width)
    expert_step(parts, rows, c_ref[0], first_ref, second_ref, e_sum, d_sum)

    @pl.when(step == last_step)
    def _():
        e_held[expert] = e_sum[...].astype(BF).reshape(blocks, padded, width)
        d_held[expert] = d_sum[...].astype(BF).reshape(blocks, padded, width)
        for which in range(late):

            @pl.when(expert == which)
            def _(which=which):
                for copy in back(kept + which):
                    copy.start()

    @pl.when((step == last_step) & (expert == count - 1))
    def _():
        for which in range(kept + late):
            for copy in back(which):
                copy.wait()


def expert_pass(sent, c, w_in, w_out):
    blocks, experts, padded, width = sent.shape
    hidden = w_in.shape[2]
    size = 768
    rows = blocks * padded
    early = experts // 2
    late = experts - early
    anywhere = pl.BlockSpec(memory_space=pl.ANY)
    dma = pltpu.SemaphoreType.DMA

    def results(count):
        return jax.ShapeDtypeStruct((count, blocks, padded, width), BF)

    def weights(first):
        return [
            pl.BlockSpec((1, rows, width), lambda e, f: (first + e, 0, 0)),
            pl.BlockSpec((1, width, size), lambda e, f: (first + e, 0, f)),
            pl.BlockSpec((1, size, width), lambda e, f: (first + e, f, 0)),
        ]

    *u_rows, u_late, e_kept, d_kept = pl.pallas_call(
        functools.partial(expert_kernel, 3, experts),
        grid=(early, hidden // size),
        in_specs=[anywhere] + weights(0),
        out_specs=[anywhere] * (experts + 3),
        out_shape=[jax.ShapeDtypeStruct((blocks, padded, width), BF)] * experts
        + [results(late), results(early), results(early)],
        scratch_shapes=[
            pltpu.VMEM((experts, blocks, padded, width), BF),
            pltpu.VMEM((rows, width), F32),
            pltpu.VMEM((rows, width), F32),
            pltpu.VMEM((early, blocks, padded, width), BF),
            pltpu.VMEM((early, blocks, padded, width), BF),
            dma((5, experts)),
            dma((experts, blocks)),
            dma((experts, blocks)),
        ],
        compiler_params=params(collective_id=0, has_side_effects=True),
        cost_estimate=NO_COST,
    )(sent, c, w_in, w_out)
    u_rows = [part.reshape(rows, width) for part in u_rows]
    e_back, d_back = pl.pallas_call(
        functools.partial(expert_rest_kernel, 3),
        grid=(late, hidden // size),
        in_specs=[pl.BlockSpec((1, blocks, padded, width), lambda e, f: (e, 0, 0, 0))]
        + weights(early)
        + [anywhere] * 2,
        out_specs=[anywhere] * 2,
        out_shape=[jax.ShapeDtypeStruct((blocks, experts, padded, width), BF)] * 2,
        scratch_shapes=[
            pltpu.VMEM((rows, width), F32),
            pltpu.VMEM((rows, width), F32),
            pltpu.VMEM((late, blocks, padded, width), BF),
            pltpu.VMEM((late, blocks, padded, width), BF),
            dma((2, experts, blocks)),
            dma((2, experts, blocks)),
            dma((2, experts)),
        ],
        compiler_params=params(collective_id=3, has_side_effects=True),
        cost_estimate=pl.CostEstimate(
            flops=32 * rows * width * hidden, bytes_accessed=4 * width * hidden, transcendentals=0
        ),
    )(u_late, c, w_in, w_out, e_kept, d_kept)
    return u_rows, e_back, d_back


def weights_kernel(parts, sources, capacity, padded, place_ref, *refs):
    u_refs, c_refs = refs[:sources], refs[sources : 2 * sources]
    first_ref, second_ref, far_in, far_out, in_sum, out_sum = refs[2 * sources :]
    size = first_ref.shape[2]
    rows = u_refs[0].shape[0]
    columns = size // parts
    first_t = first_ref[0].T
    for source in range(sources):
        inputs, upstream = u_refs[source][...], c_refs[source][...].reshape(u_refs[source].shape)
        gate = jnp.zeros((1, rows), F32)
        for block in range(rows // padded):
            place = block * padded + capacity
            gate = gate + inputs[place : place + 1, :rows].astype(F32)
        for part in range(parts):
            places = slice(part * columns, (part + 1) * columns)
            value, slope = gelu_and_slope(mm_nt(first_t[places, :], inputs))
            inner = (mm_nt(second_ref[0, places, :], upstream) * (slope * gate)).astype(BF)
            in_term = mm(inner, inputs)
            out_term = mm((value * gate).astype(BF), upstream)
            if source == 0:
                in_sum[places, :] = in_term
                out_sum[places, :] = out_term
            else:
                in_sum[places, :] += in_term
                out_sum[places, :] += out_term
    far_in[...] = in_sum[...].T.astype(BF)
    far_out[...] = out_sum[...].astype(BF)


def weight_grads(place, us, c_rows, c_far, w_in, w_out, size, capacity, padded):
    sources = len(us)
    rows, width = us[0].shape
    block = pl.BlockSpec((rows, width), lambda f, p: (0, 0))
    return pl.pallas_call(
        functools.partial(weights_kernel, 3, sources, capacity, padded),
        grid_spec=pltpu.PrefetchScalarGridSpec(
            num_scalar_prefetch=1,
            grid=(1,),
            in_specs=[block] * sources
            + [pl.BlockSpec((1, rows, width), lambda f, p: (p[0], 0, 0))]
            + [block] * (sources - 1)
            + [
                pl.BlockSpec((1, width, size), lambda f, p: (p[0], 0, p[1])),
                pl.BlockSpec((1, size, width), lambda f, p: (p[0], p[1], 0)),
            ],
            out_specs=[
                pl.BlockSpec((width, size), lambda f, p: (0, 0)),
                pl.BlockSpec((size, width), lambda f, p: (0, 0)),
            ],
            scratch_shapes=[pltpu.VMEM((size, width), F32)] * 2,
        ),
        out_shape=[
            jax.ShapeDtypeStruct((width, size), BF),
            jax.ShapeDtypeStruct((size, width), BF),
        ],
        compiler_params=params(),
        cost_estimate=NO_COST,
    )(place, *us, c_rows, *c_far, w_in, w_out)


def finish_kernel(half, place_ref, *refs):
    own_in, own_out, refs = refs[0], refs[1], refs[2:]
    came_in, came_out, dense_ref = refs[:half], refs[half : 2 * half], refs[2 * half]
    a_out, b_out, *dense_outs = refs[2 * half + 1 : 2 * half + 7]
    held, sem = refs[2 * half + 7 :]
    at, last_step = pl.program_id(0), pl.num_programs(0) - 1
    dense = [
        pltpu.make_async_copy(held.at[which], dense_outs[which], sem.at[which]) for which in range(4)
    ]
    held[at] = dense_ref[...].astype(F32)
    for which in range(4):
        pl.when(at == which)(dense[which].start)

    @pl.when(at < half)
    def _():
        a_out[0] = own_in[0].astype(F32)
        b_out[0] = own_out[0].astype(F32)

    for step in range(half):

        @pl.when(at == half + step)
        def _(step=step):
            a_out[0] = came_in[step][...].astype(F32)
            b_out[0] = came_out[step][...].astype(F32)

    @pl.when(at == last_step)
    def _():
        for copy in dense:
            copy.wait()


def finish(places, own_in, own_out, came_in, came_out, dense):
    half, width, size = own_in.shape

    def whole(*shape):
        return pl.BlockSpec(shape, lambda e, p: (0, 0))

    def own(*shape):
        return pl.BlockSpec((1,) + shape, lambda e, p: (jnp.minimum(e, half - 1), 0, 0))

    def spec(*shape):
        return pl.BlockSpec((1,) + shape, lambda e, p: (p[e], 0, 0))

    return pl.pallas_call(
        functools.partial(finish_kernel, half),
        grid_spec=pltpu.PrefetchScalarGridSpec(
            num_scalar_prefetch=1,
            grid=(2 * half,),
            in_specs=[own(width, size), own(size, width)]
            + [whole(width, size)] * half
            + [whole(size, width)] * half
            + [pl.BlockSpec((width, width), lambda e, p: (e, 0))],
            out_specs=[spec(width, size), spec(size, width)]
            + [pl.BlockSpec(memory_space=pl.ANY)] * 4,
            scratch_shapes=[pltpu.VMEM((4, width, width), F32), pltpu.SemaphoreType.DMA((4,))],
        ),
        out_shape=[
            jax.ShapeDtypeStruct((2 * half, width, size), F32),
            jax.ShapeDtypeStruct((2 * half, size, width), F32),
        ]
        + [jax.ShapeDtypeStruct((width, width), F32)] * 4,
        compiler_params=params(),
    )(places, own_in, own_out, *came_in, *came_out, dense)


def tail_kernel(parts, sources, experts, capacity, padded, *refs):
    u_refs, refs = refs[: sources * experts], refs[sources * experts :]
    c_own, c_far, refs = refs[0], refs[1 : 1 + (sources - 1) * experts], refs[1 + (sources - 1) * experts :]
    (
        first_ref, second_ref, far_in, far_out, dense_o, dense_qkv, small_ref,
        own_in_ref, own_out_ref, came_in_ref, came_out_ref, dense_ref, total_ref,
        rows_u, rows_c, first_held, second_held, first_t, in_sum, out_sum, own_in, own_out,
        dense, dense_came, dense_over_dp, small, small_came,
        rows_sem, weight_sem, load_sem, far_send, far_recv, own_sem,
        half_send, half_recv, over_send, over_recv, back_send, back_recv, small_send, small_recv, keep_sem,
    ) = refs
    rows, width = rows_u.shape[2:]
    size = in_sum.shape[0]
    columns = size // parts
    exp_me, dp_me = lax.axis_index("exp"), lax.axis_index("dp")
    exp_bits, dp_bits = half_send.shape[2], over_send.shape[0]
    group, pair = dp_me % 2, dp_me // 2
    mesh_id = pl.DeviceIdType.MESH

    def exp_peer(bit):
        return {"exp": flipped(exp_me, 1 << bit)}

    def dp_peer(bit):
        return {"dp": flipped(dp_me, 1 << bit)}

    chain = dense.shape[0] // 2
    bits = list(range(exp_bits))
    split = 1 + (exp_bits - 1) // 2
    orders = (bits, bits[:1] + bits[split:] + bits[1:split])

    def region(which, depth):
        start = which * chain
        for level in range(depth):
            start = start + (exp_me // (1 << orders[which][level])) % 2 * (chain >> (level + 1))
        return pl.ds(pl.multiple_of(start, 16), chain >> depth)

    def other_half(which, depth):
        start = which * chain
        for level in range(depth):
            start = start + (exp_me // (1 << orders[which][level])) % 2 * (chain >> (level + 1))
        start = start + (1 - (exp_me // (1 << orders[which][depth])) % 2) * (chain >> (depth + 1))
        return pl.ds(pl.multiple_of(start, 16), chain >> (depth + 1))

    def came(which, depth):
        return pl.ds(which * chain + chain - (chain >> depth), chain >> (depth + 1))

    def columns_of(side):
        return pl.ds(side * (width // 2), width // 2)

    def halving(side, which, depth):
        return pltpu.make_async_remote_copy(
            src_ref=dense.at[other_half(which, depth), columns_of(side)],
            dst_ref=dense_came.at[came(which, depth), columns_of(side)],
            send_sem=half_send.at[side, which, depth],
            recv_sem=half_recv.at[side, which, depth],
            device_id=exp_peer(orders[which][depth]),
            device_id_type=mesh_id,
        )

    def over(side, which, bit):
        mine = dense.at[region(which, exp_bits), columns_of(side)]
        return pltpu.make_async_remote_copy(
            src_ref=mine if bit == 0 else dense_over_dp.at[1, bit - 1, side, which],
            dst_ref=dense_over_dp.at[0, bit, side, which],
            send_sem=over_send.at[bit, side, which],
            recv_sem=over_recv.at[bit, side, which],
            device_id=dp_peer(dp_bits - 1 - bit),
            device_id_type=mesh_id,
        )

    def keeping(side, which):
        return pltpu.make_async_copy(
            dense_over_dp.at[1, dp_bits - 1, side, which],
            dense_ref.at[region(which, exp_bits), columns_of(side)],
            keep_sem.at[side, which],
        )

    def returning(side, which, depth):
        place = dense_ref.at[region(which, depth + 1), columns_of(side)]
        return pltpu.make_async_remote_copy(
            src_ref=place,
            dst_ref=place,
            send_sem=back_send.at[side, which, depth],
            recv_sem=back_recv.at[side, which, depth],
            device_id=exp_peer(orders[which][depth]),
            device_id_type=mesh_id,
        )

    def small_copy(depth):
        return pltpu.make_async_remote_copy(
            src_ref=small.at[depth],
            dst_ref=small_came.at[depth],
            send_sem=small_send.at[depth],
            recv_sem=small_recv.at[depth],
            device_id=exp_peer(depth) if depth < exp_bits else dp_peer(depth - exp_bits),
            device_id_type=mesh_id,
        )

    def loads():
        return [
            pltpu.make_async_copy(dense_o, dense.at[pl.ds(3 * width, width)], load_sem.at[0]),
            pltpu.make_async_copy(dense_qkv, dense.at[pl.ds(0, 3 * width)], load_sem.at[1]),
            pltpu.make_async_copy(small_ref, small.at[0], load_sem.at[2]),
        ]

    def add_small(depth):
        small_copy(depth).wait_recv()
        small[depth + 1] = small[depth] + small_came[depth]

    def begin(side):
        if side == 0:
            for load in loads():
                load.wait()
            small_copy(0).start()
        for which in range(2):
            halving(side, which, 0).start()

    def halve(depth):
        def act(side):
            for which in range(2):
                halving(side, which, depth).wait_recv()
                place, new, here = region(which, depth + 1), came(which, depth), columns_of(side)
                dense[place, here] = (
                    dense[place, here].astype(F32) + dense_came[new, here].astype(F32)
                ).astype(BF)
                if depth + 1 < exp_bits:
                    halving(side, which, depth + 1).start()
                else:
                    over(side, which, 0).start()
            if side == 0:
                add_small(depth)
                small_copy(depth + 1).start()

        return act

    def sum_over(bit):
        def act(side):
            for which in range(2):
                over(side, which, bit).wait_recv()
                if bit == 0:
                    mine = dense[region(which, exp_bits), columns_of(side)]
                else:
                    mine = dense_over_dp[1, bit - 1, side, which]
                dense_over_dp[1, bit, side, which] = (
                    mine.astype(F32) + dense_over_dp[0, bit, side, which].astype(F32)
                ).astype(BF)
                if bit + 1 < dp_bits:
                    over(side, which, bit + 1).start()
                else:
                    keeping(side, which).start()
            if side == 0:
                add_small(exp_bits + bit)
                if bit + 1 < dp_bits:
                    small_copy(exp_bits + bit + 1).start()
            if bit + 1 == dp_bits:
                for which in range(2):
                    keeping(side, which).wait()
                    returning(side, which, exp_bits - 1).start()

        return act

    def give_back(depth):
        def act(side):
            for which in range(2):
                returning(side, which, depth).wait_recv()
                if depth > 0:
                    returning(side, which, depth - 1).start()

        return act

    stages = [begin] + [halve(depth) for depth in range(exp_bits)]
    stages += [sum_over(bit) for bit in range(dp_bits)]
    stages += [give_back(depth) for depth in reversed(range(exp_bits))]
    stages = [functools.partial(stage, side) for stage in stages for side in range(2)]

    steps, turns = experts, experts * sources

    def rows_copy(source, expert):
        if source == 0:
            c_from = c_own.at[group * experts + expert]
        else:
            c_from = c_far[expert * (sources - 1) + source - 1]
        return [
            pltpu.make_async_copy(
                u_refs[expert * sources + source],
                rows_u.at[source, expert],
                rows_sem.at[0, source, expert],
            ),
            pltpu.make_async_copy(
                c_from, rows_c.at[source, expert], rows_sem.at[1, source, expert]
            ),
        ]

    def weight_copy(step):
        expert = group * experts + step
        place = (pair * 2 + group) * size
        place = pl.ds(pl.multiple_of(place, 128), size)
        slot = step % 2
        return [
            pltpu.make_async_copy(
                first_ref.at[expert, :, place], first_held.at[slot], weight_sem.at[0, slot]
            ),
            pltpu.make_async_copy(
                second_ref.at[expert, place, :], second_held.at[slot], weight_sem.at[1, slot]
            ),
        ]

    far_parts = far_send.shape[1]

    def far_copy(index):
        kind, part = index % 2, index // 2
        held, target = ((far_in, came_in_ref), (far_out, came_out_ref))[kind]
        lines = held.shape[0] // far_parts
        place = pl.ds(part * lines, lines)
        return pltpu.make_async_remote_copy(
            src_ref=held.at[place],
            dst_ref=target.at[place],
            send_sem=far_send.at[kind, part],
            recv_sem=far_recv.at[kind, part],
            device_id=dp_peer(0),
            device_id_type=mesh_id,
        )

    def own_copy(expert):
        return [
            pltpu.make_async_copy(held.at[expert], target.at[expert], own_sem.at[kind, expert])
            for kind, (held, target) in enumerate(((own_in, own_in_ref), (own_out, own_out_ref)))
        ]

    for load in loads():
        load.start()
    for copy in weight_copy(0):
        copy.start()
    for expert in range(experts):
        for source in range(sources):
            for copy in rows_copy(source, expert):
                copy.start()
    barrier = pltpu.get_barrier_semaphore()
    for bit in range(exp_bits):
        pl.semaphore_signal(barrier, inc=1, device_id=exp_peer(bit), device_id_type=mesh_id)
    for bit in range(dp_bits):
        pl.semaphore_signal(barrier, inc=1, device_id=dp_peer(bit), device_id_type=mesh_id)
    pl.semaphore_wait(barrier, exp_bits + dp_bits)

    places = [0, 0, 1, 2, 3, 4, 5, 6]
    places = [place for place in places if place < turns][: len(stages)]
    starts = {4: 3}
    starts = {place: index for place, index in starts.items() if place < turns}
    pieces = 2 * far_parts

    def turn(at, carry):
        step, source = at // sources, at % sources
        expert, slot = step, step % 2
        for place, stage in zip(places, stages):
            pl.when(at == place)(stage)
        for place, index in starts.items():
            pl.when(at == place)(far_copy(index).start)

        @pl.when(source == 0)
        def _():
            for copy in weight_copy(step):
                copy.wait()

            @pl.when(step + 1 < steps)
            def _():
                for copy in weight_copy(step + 1):
                    copy.start()

            first_t[...] = first_held[slot].T

        for each_expert in range(experts):
            for each in range(sources):

                @pl.when(at == each_expert * sources + each)
                def _(each=each, each_expert=each_expert):
                    for copy in rows_copy(each, each_expert):
                        copy.wait()

        inputs, upstream = rows_u[source, expert], rows_c[source, expert]
        gate = jnp.zeros((1, rows), F32)
        for block in range(rows // padded):
            place = block * padded + capacity
            gate = gate + inputs[place : place + 1, :rows].astype(F32)
        for part in range(parts):
            here = slice(part * columns, (part + 1) * columns)
            value, slope = gelu_and_slope(mm_nt(first_t[here, :], inputs))
            inner = (mm_nt(second_held[slot, here, :], upstream) * (slope * gate)).astype(BF)
            in_term = mm(inner, inputs)
            out_term = mm((value * gate).astype(BF), upstream)
            fresh = source == 0
            in_sum[here, :] = jnp.where(fresh, 0.0, in_sum[here, :]) + in_term
            out_sum[here, :] = jnp.where(fresh, 0.0, out_sum[here, :]) + out_term

        for each_expert in range(experts):

            @pl.when((source == sources - 1) & (step == each_expert))
            def _(each_expert=each_expert):
                own_in[each_expert] = in_sum[...].T.astype(BF)
                own_out[each_expert] = out_sum[...].astype(BF)
                for copy in own_copy(each_expert):
                    copy.start()

        return carry

    for index in range(3):
        far_copy(index).start()
    lax.fori_loop(0, turns, turn, 0)
    for stage in stages[len(places) : len(places) + 2]:
        stage()
    for index in range(3 + len(starts), pieces):
        far_copy(index).start()
    for stage in stages[len(places) + 2 :]:
        stage()
    total_ref[...] = small[exp_bits + dp_bits]
    for index in range(pieces):
        far_copy(index).wait()
    for expert in range(experts):
        for copy in own_copy(expert):
            copy.wait()
    for side in range(2):
        for which in range(2):
            for depth in range(exp_bits):
                halving(side, which, depth).wait_send()
                returning(side, which, depth).wait_send()
            for bit in range(dp_bits):
                over(side, which, bit).wait_send()
    for depth in range(exp_bits + dp_bits):
        small_copy(depth).wait_send()


def tail(us, c_rows, c_far, w_in, w_out, far_in, far_out, size, dense_o, dense_qkv, small, capacity, padded, exp_n):
    sources, experts = len(us[0]), len(us)
    rows, width = us[0][0].shape
    far_parts = 4
    exp_bits, dp_bits = exp_n.bit_length() - 1, sources.bit_length() - 1
    lines = 4 * width
    anywhere = pl.BlockSpec(memory_space=pl.ANY)
    dma = pltpu.SemaphoreType.DMA
    return pl.pallas_call(
        functools.partial(tail_kernel, 3, sources, experts, capacity, padded),
        in_specs=[anywhere] * (experts * (2 * sources - 1) + 8),
        out_specs=[anywhere] * 5 + [pl.BlockSpec(memory_space=pltpu.VMEM)],
        out_shape=[
            jax.ShapeDtypeStruct((experts, width, size), BF),
            jax.ShapeDtypeStruct((experts, size, width), BF),
            jax.ShapeDtypeStruct((width, size), BF),
            jax.ShapeDtypeStruct((size, width), BF),
            jax.ShapeDtypeStruct((lines, width), BF),
            jax.ShapeDtypeStruct(small.shape, F32),
        ],
        scratch_shapes=[
            pltpu.VMEM((sources, experts, rows, width), BF),
            pltpu.VMEM((sources, experts, rows, width), BF),
            pltpu.VMEM((2, width, size), BF),
            pltpu.VMEM((2, size, width), BF),
            pltpu.VMEM((size, width), BF),
            pltpu.VMEM((size, width), F32),
            pltpu.VMEM((size, width), F32),
            pltpu.VMEM((experts, width, size), BF),
            pltpu.VMEM((experts, size, width), BF),
            pltpu.VMEM((lines, width), BF),
            pltpu.VMEM((lines, width), BF),
            pltpu.VMEM((2, dp_bits, 2, 2, lines // 2 >> exp_bits, width // 2), BF),
            pltpu.VMEM((exp_bits + dp_bits + 1,) + small.shape, F32),
            pltpu.VMEM((exp_bits + dp_bits,) + small.shape, F32),
            dma((2, sources, experts)),
            dma((2, 2)),
            dma((3,)),
            dma((2, far_parts)),
            dma((2, far_parts)),
            dma((2, experts)),
            dma((2, 2, exp_bits)),
            dma((2, 2, exp_bits)),
            dma((dp_bits, 2, 2)),
            dma((dp_bits, 2, 2)),
            dma((2, 2, exp_bits)),
            dma((2, 2, exp_bits)),
            dma((exp_bits + dp_bits,)),
            dma((exp_bits + dp_bits,)),
            dma((2, 2)),
        ],
        compiler_params=pltpu.CompilerParams(
            vmem_limit_bytes=58 * 2**20, collective_id=2, has_side_effects=True
        ),
        cost_estimate=NO_COST,
    )(*sum(us, []), c_rows, *sum(c_far, []), w_in, w_out, far_in, far_out, dense_o, dense_qkv, small)


def combine_kernel(
    parts, experts, slot_ref, expert_ref, gate_ref, probs_ref, h_ref, c_ref, o_ref,
    e_ref, d_ref, wo_ref, wr_ref, gain_ref, *refs
):
    sent_refs, refs = refs[:parts], refs[parts:]
    mixed_ref, dh_ref, do_ref, wo_ref_out, wr_sum, gain_sum = refs[:6]
    came_refs, refs = refs[6 : 6 + parts * experts], refs[6 + parts * experts :]
    wo_sum, e_held, d_held, load_sem, *sems = refs
    step = pl.program_id(0)
    me, blocks = lax.axis_index("exp"), sent_refs[0].shape[0]

    def loads():
        return [
            pltpu.make_async_copy(e_ref, e_held, load_sem.at[0]),
            pltpu.make_async_copy(d_ref, d_held, load_sem.at[1]),
        ]

    def transfers():
        copies = []
        for expert in range(experts):
            for part in range(parts):
                index = expert * parts + part
                copies += spread(me, sent_refs[part], expert, came_refs[index], sems, index)
        return copies

    @pl.when(step == 0)
    def _():
        for copy in loads():
            copy.start()
        greet(me, blocks)
        for copy in transfers():
            copy.start()
        for copy in loads():
            copy.wait()

    @pl.when(step == pl.num_programs(0) - 1)
    def _():
        for copy in transfers():
            copy.wait()

    tokens, slots = slot_ref.shape[1], e_ref.shape[0]
    slot = as_column(slot_ref[...].astype(F32)).astype(jnp.int32)
    picks = jnp.where(
        slot == lax.broadcasted_iota(jnp.int32, (tokens, slots), 1), 1.0, 0.0
    ).astype(BF)
    returned, arrived = mm(picks, e_held[...]), mm(picks, d_held[...])
    gate, probs, mixed = gate_ref[...], probs_ref[...], h_ref[...]
    upstream = c_ref[...].astype(F32)
    mixed_ref[...] = (mixed + gate * returned).astype(BF)
    gate_grad = jnp.sum(upstream * returned, axis=-1, keepdims=True)
    picked = jnp.where(expert_ref[...] == lax.broadcasted_iota(jnp.int32, probs.shape, 1), 1.0, 0.0)
    logit_grad = gate_grad * gate * (picked - probs)
    inv = lax.rsqrt(jnp.mean(mixed * mixed, axis=-1, keepdims=True) + EPSILON)
    unit = mixed * inv
    gain = gain_ref[...]
    lg_high, lg_low = halves(logit_grad)
    wr_high, wr_low = halves(wr_ref[...])
    through_router = mm_nt(lg_high, wr_high) + (mm_nt(lg_low, wr_high) + mm_nt(lg_high, wr_low))
    normed_grad = through_router + gate * arrived
    unit_grad = normed_grad * gain
    mixed_grad = upstream + inv * (
        unit_grad - unit * jnp.mean(unit_grad * unit, axis=-1, keepdims=True)
    )
    dh_ref[...] = mixed_grad
    low = mixed_grad.astype(BF)
    do_ref[...] = mm_nt(low, wo_ref[...]).astype(BF)

    @pl.when(step == 0)
    def _():
        wo_sum[...] = jnp.zeros_like(wo_sum)
        wr_sum[...] = jnp.zeros_like(wr_sum)
        gain_sum[...] = jnp.zeros_like(gain_sum)

    wo_sum[...] += mm(o_ref[...].T, low)
    n_high, n_low = halves(unit * gain)
    lg_high, lg_low = lg_high.T, lg_low.T
    wr_sum[...] += mm(lg_high, n_high) + (mm(lg_low, n_high) + mm(lg_high, n_low))
    gain_sum[...] += jnp.sum(normed_grad * unit, axis=0, keepdims=True)

    @pl.when(step == pl.num_programs(0) - 1)
    def _():
        wo_ref_out[...] = wo_sum[...].astype(BF)


def combine(slot, expert, gate, probs, h, c, o, e_out, du, wo, wr, gain, sent):
    parts, (blocks, local, padded, _) = len(sent), sent[0].shape
    spreads = parts * (local - 1)
    anywhere = pl.BlockSpec(memory_space=pl.ANY)
    tokens, width = h.shape
    slots, experts = e_out.shape[0], wr.shape[1]
    size = 256

    def rows(columns):
        return pl.BlockSpec((size, columns), lambda t: (t, 0))

    def whole(*shape):
        return pl.BlockSpec(shape, lambda t: (0, 0))

    return pl.pallas_call(
        functools.partial(combine_kernel, parts, local - 1),
        grid=(tokens // size,),
        in_specs=[pl.BlockSpec((1, size), lambda t: (0, t)), rows(1), rows(1), rows(experts), rows(width), rows(width), rows(width)]
        + [anywhere] * 2
        + [whole(width, width), whole(width, experts)]
        + [whole(1, width)]
        + [anywhere] * parts,
        out_specs=[rows(width), rows(width), rows(width), whole(width, width), whole(experts, width)]
        + [whole(1, width)]
        + [anywhere] * spreads,
        out_shape=[
            jax.ShapeDtypeStruct((tokens, width), BF),
            jax.ShapeDtypeStruct((tokens, width), F32),
            jax.ShapeDtypeStruct((tokens, width), BF),
            jax.ShapeDtypeStruct((width, width), BF),
            jax.ShapeDtypeStruct((experts, width), F32),
            jax.ShapeDtypeStruct((1, width), F32),
        ]
        + [jax.ShapeDtypeStruct((blocks, padded, width), BF)] * spreads,
        scratch_shapes=[
            pltpu.VMEM((width, width), F32),
            pltpu.VMEM((slots, width), BF),
            pltpu.VMEM((slots, width), BF),
            pltpu.SemaphoreType.DMA((2,)),
            *spread_sems(spreads, blocks),
        ],
        compiler_params=params(collective_id=5, has_side_effects=True),
        cost_estimate=NO_COST,
    )(slot, expert, gate, probs, h, c, o, e_out, du, wo, wr, gain, *sent)


def last_kernel(
    x_ref, dh_ref, dq_ref, dk_ref, dv_ref, wq_ref, wk_ref, wv_ref, gain_ref,
    grad_ref, sums_ref, gain_sum, q_sum, k_sum, v_sum,
):
    step = pl.program_id(0)
    width = x_ref.shape[1]

    @pl.when(step == 0)
    def _():
        for total in (q_sum, k_sum, v_sum, gain_sum):
            total[...] = jnp.zeros_like(total)

    rows = x_ref[...].astype(F32)
    inv = lax.rsqrt(jnp.mean(rows * rows, axis=-1, keepdims=True) + EPSILON)
    unit = rows * inv
    gain = gain_ref[...]
    normed_t = (unit * gain).astype(BF).T
    normed_grad = None
    for grad_ref_in, weight_ref, total in (
        (dq_ref, wq_ref, q_sum),
        (dk_ref, wk_ref, k_sum),
        (dv_ref, wv_ref, v_sum),
    ):
        grad = grad_ref_in[...]
        total[...] += mm(normed_t, grad)
        term = mm_nt(grad, weight_ref[...])
        normed_grad = term if normed_grad is None else normed_grad + term
    unit_grad = normed_grad * gain
    grad_ref[...] = dh_ref[...] + inv * (
        unit_grad - unit * jnp.mean(unit_grad * unit, axis=-1, keepdims=True)
    )
    gain_sum[...] += jnp.sum(normed_grad * unit, axis=0, keepdims=True)

    @pl.when(step == pl.num_programs(0) - 1)
    def _():
        for which, total in enumerate((q_sum, k_sum, v_sum)):
            sums_ref[which * width : (which + 1) * width, :] = total[...].astype(BF)


def last(x, dh, dq, dk, dv, wq, wk, wv, gain):
    tokens, width = x.shape
    size = 256
    rows = pl.BlockSpec((size, width), lambda t: (t, 0))
    square = pl.BlockSpec((width, width), lambda t: (0, 0))
    one = pl.BlockSpec((1, width), lambda t: (0, 0))
    return pl.pallas_call(
        last_kernel,
        grid=(tokens // size,),
        in_specs=[rows] * 5 + [square] * 3 + [one],
        out_specs=[rows, pl.BlockSpec((3 * width, width), lambda t: (0, 0)), one],
        out_shape=[
            jax.ShapeDtypeStruct((tokens, width), F32),
            jax.ShapeDtypeStruct((3 * width, width), BF),
            jax.ShapeDtypeStruct((1, width), F32),
        ],
        scratch_shapes=[pltpu.VMEM((width, width), F32)] * 3,
        compiler_params=params(),
        cost_estimate=NO_COST,
    )(x, dh, dq, dk, dv, wq, wk, wv, gain)


def per_device(
    tokens,
    w_query,
    w_key,
    w_value,
    w_output,
    norm_attn,
    norm_ffn,
    relative_bias_table,
    w_router,
    w_in,
    w_out,
    expert_index,
    priority,
    cotangent,
):
    tok_rows, width = tokens.shape
    local = w_in.shape[0]
    exp_n, dp_n = lax.axis_size("exp"), lax.axis_size("dp")
    exp_me, dp_me = lax.axis_index("exp"), lax.axis_index("dp")
    all_experts = local * exp_n
    capacity = (5 * tok_rows + 4 * all_experts - 1) // (4 * all_experts)
    padded = (capacity + 1 + 15) // 16 * 16
    block = local * padded
    buckets = relative_bias_table.shape[0]

    chosen = expert_index[:, 0]
    order = priority[0]
    ahead = (chosen[:, None] == chosen[None, :]) & (order[None, :] < order[:, None])
    rank = jnp.sum(ahead.astype(jnp.int32), axis=1)
    place = ((chosen // local) ^ exp_me) * block + (chosen % local) * padded + rank
    slots = jnp.where(rank < capacity, place, -1)
    slot_row = slots[None, :]
    half = local // 2
    group = dp_me % 2
    inside = chosen % local
    grouped = ((inside // half + group) % 2 * exp_n + place // block) * half + inside % half
    c_row = jnp.where(rank < capacity, grouped * padded + rank, -1)[None, :]

    def to_dp(rows, step):
        return lax.ppermute(rows, "dp", [(i, i ^ step) for i in range(dp_n)])

    def over_dp(mine, other):
        return [mine] + [to_dp(other if step % 2 else mine, step) for step in range(1, dp_n)]

    lines = jnp.dot(
        relative_bias_table.T, diagonal_onehot(buckets).T, precision=FULL_PRECISION
    ).reshape(HEADS, 4, TILE)
    lines = jnp.concatenate([lines, jnp.zeros_like(lines)], axis=1)
    gain_attn, gain_ffn = norm_attn[None, :], norm_ffn[None, :]
    q, k, v = qkv(tokens, gain_attn, w_query, w_key, w_value)
    c_sent = [
        part.reshape(exp_n, half, padded, width)
        for part in dispatch_by_group(c_row, cotangent, exp_n * half * padded)
    ]
    c_far = over_dp(*c_sent)[1:]
    context, lse, c_rows = attention(lines, c_sent, q, k, v)
    c_rows = c_rows.reshape(local, exp_n * padded, width)
    mixed, u, probs, gate, gate_row = router(
        context, tokens, w_output, gain_ffn, w_router, expert_index
    )
    sent = dispatch(slot_row, u, exp_n, block, gate=(gate_row, local, capacity, padded))
    u_rows, e_back, d_back = expert_pass(
        sent.reshape(exp_n, local, padded, width), c_rows, w_in, w_out
    )
    mine, other = u_rows[:half], u_rows[half:]
    mine[0], other[0], c_far[0] = lax.optimization_barrier((mine[0], other[0], c_far[0]))
    u_all = [over_dp(mine[0], other[0])]
    for expert in range(1, half):
        e_back, mine[expert], other[expert], *c_far[1:] = lax.optimization_barrier(
            (e_back, mine[expert], other[expert], *c_far[1:])
        )
        u_all.append([mine[expert], None] + [
            to_dp(other[expert] if step % 2 else mine[expert], step) for step in range(2, dp_n)
        ])
    e_back, d_back = e_back.reshape(-1, width), d_back.reshape(-1, width)
    mixed_out, mixed_grad, context_grad, output_part, router_part, norm_ffn_part, *c_early = combine(
        slot_row, expert_index, gate, probs, mixed, cotangent, context,
        e_back, d_back, w_output, w_router, gain_ffn, c_far,
    )
    for expert in range(1, half):
        context_grad, *u_all[0], other[expert] = lax.optimization_barrier(
            (context_grad, *u_all[0], other[expert])
        )
        u_all[expert][1] = to_dp(other[expert], 1)
    size = w_in.shape[2] // dp_n
    rows = exp_n * padded
    c_early = [part.reshape(rows, width) for part in c_early]
    c_spread = [c_early[at : at + dp_n - 1] for at in range(0, len(c_early), dp_n - 1)]

    def for_partner(expert):
        where = jnp.stack([group * half + expert, dp_me // 2 * 2 + 1 - group]).astype(jnp.int32)
        return weight_grads(
            where, u_all[expert], c_rows, c_spread[expert], w_in, w_out, size, capacity, padded
        )

    got = []
    for expert in range(half - 1):
        context_grad, *far = lax.optimization_barrier((context_grad, *for_partner(expert)))
        got += [to_dp(array, 1) for array in far]
    query_grad, key_grad, value_grad, sums, *c_late = attention_back(
        lines, q, k, v, context_grad, lse, c_far
    )
    c_spread.append([part.reshape(rows, width) for part in c_late])
    query_grad, far_in, far_out = lax.optimization_barrier((query_grad, *for_partner(half - 1)))
    table_part = jnp.dot(
        diagonal_onehot(buckets).T,
        sums[:, :4].reshape(HEADS, 4 * TILE).T,
        precision=FULL_PRECISION,
    )
    grad_tokens, qkv_part, norm_attn_part = last(
        tokens, mixed_grad, query_grad, key_grad, value_grad, w_query, w_key, w_value, gain_attn
    )

    table_line = jnp.pad(table_part.reshape(1, -1), ((0, 0), (0, width - table_part.size)))
    small = jnp.concatenate([router_part, norm_attn_part, norm_ffn_part, table_line], axis=0)
    small = jnp.pad(small, ((0, -small.shape[0] % 8), (0, 0)))
    own_in, own_out, came_in, came_out, dense, total = tail(
        u_all, c_rows, c_spread, w_in, w_out, far_in, far_out, size, output_part, qkv_part, small, capacity, padded, exp_n
    )
    experts = jnp.arange(local, dtype=jnp.int32)
    grad_in, grad_out, *dense_grads = finish(
        jnp.where(group == 0, experts, (experts + half) % local),
        own_in,
        own_out,
        got[0::2] + [came_in],
        got[1::2] + [came_out],
        dense,
    )
    return (
        mixed_out,
        grad_tokens,
        *dense_grads,
        total[all_experts],
        total[all_experts + 1],
        total[all_experts + 2, : table_part.size].reshape(table_part.shape),
        total[:all_experts].T,
        grad_in,
        grad_out,
    )


def solution(mesh):
    return jax.shard_map(
        per_device,
        mesh=mesh,
        in_specs=(
            P(("exp", "dp"), None),
            P(),
            P(),
            P(),
            P(),
            P(),
            P(),
            P(),
            P(),
            P("exp", None, None),
            P("exp", None, None),
            P(("exp", "dp"), None),
            P(("exp", "dp"), None),
            P(("exp", "dp"), None),
        ),
        out_specs=(
            P(("exp", "dp"), None),
            P(("exp", "dp"), None),
            P(),
            P(),
            P(),
            P(),
            P(),
            P(),
            P(),
            P(),
            P("exp", None, "dp"),
            P("exp", "dp", None),
        ),
        check_vma=False,
    )
```

```python
import functools

import jax
import jax.numpy as jnp
from jax import lax
from jax.experimental import pallas as pl
from jax.experimental.pallas import tpu as pltpu
from jax.sharding import PartitionSpec as P

HEADS = 12
HEAD_DIM = 64
SEQ = 512
LIMITS = (12, 16, 23, 32, 46, 64, 91)
EPSILON = 1e-06
FULL_PRECISION = lax.Precision.HIGHEST
BF = jnp.bfloat16
F32 = jnp.float32
PAIR = 2 * HEAD_DIM
TILE = 128
CHUNK = 256
GELU_A = 0.7978845608028654
GELU_B = 0.044715 * GELU_A
VMEM_MIB = 58
NO_COST = pl.CostEstimate(flops=0, bytes_accessed=2**16, transcendentals=0)


def params(**more):
    return pltpu.CompilerParams(vmem_limit_bytes=VMEM_MIB * 2**20, **more)


def mm(left, right):
    return jnp.dot(left, right, preferred_element_type=F32)


def mm_nt(left, right):
    return lax.dot_general(left, right, (((1,), (1,)), ((), ())), preferred_element_type=F32)


def flipped(index, step):
    bit = 1
    while bit <= step:
        if step & bit:
            index = index + bit * (1 - 2 * ((index // bit) % 2))
        bit *= 2
    return index


def greet(me, blocks, others=()):
    barrier = pltpu.get_barrier_semaphore()
    devices = [{"exp": flipped(me, block)} for block in range(1, blocks)] + list(others)
    for device in devices:
        pl.semaphore_signal(barrier, inc=1, device_id=device, device_id_type=pl.DeviceIdType.MESH)
    pl.semaphore_wait(barrier, len(devices))


def spread(me, sent, expert, came, sems, index):
    local_sem, send_sem, recv_sem = sems
    copies = [pltpu.make_async_copy(sent.at[0, expert], came.at[0], local_sem.at[index])]
    for block in range(1, came.shape[0]):
        copies.append(
            pltpu.make_async_remote_copy(
                src_ref=sent.at[block, expert],
                dst_ref=came.at[block],
                send_sem=send_sem.at[index, block],
                recv_sem=recv_sem.at[index, block],
                device_id={"exp": flipped(me, block)},
                device_id_type=pl.DeviceIdType.MESH,
            )
        )
    return copies


def spread_sems(count, blocks):
    dma = pltpu.SemaphoreType.DMA
    return [dma((count,)), dma((count, blocks)), dma((count, blocks))]


def halves(array):
    high = array.astype(BF)
    return high, (array - high.astype(F32)).astype(BF)


def as_column(line):
    size = line.shape[1]
    diagonal = lax.broadcasted_iota(jnp.int32, (size, size), 0) == lax.broadcasted_iota(
        jnp.int32, (size, size), 1
    )
    return jnp.sum(jnp.where(diagonal, line, 0.0), axis=1, keepdims=True)


def bucket_of(offset):
    distance = jnp.abs(offset)
    farther = jnp.zeros_like(distance)
    for limit in LIMITS:
        farther = farther + (distance >= limit).astype(jnp.int32)
    return jnp.where(distance < 8, distance, 8 + farther) + jnp.where(offset > 0, 16, 0)


def diagonal_onehot(count):
    places = jnp.arange(TILE, dtype=jnp.int32)
    offsets = jnp.concatenate([-places, TILE - places, 0 * places - SEQ, 0 * places + SEQ])
    return (bucket_of(offsets)[:, None] == jnp.arange(count, dtype=jnp.int32)[None, :]).astype(F32)


def dispatch_gate_kernel(experts, capacity, padded, slot_ref, gate_ref, rows_ref, out_ref):
    block, tokens = out_ref.shape[0], rows_ref.shape[0]
    width = out_ref.shape[1]
    step = pl.program_id(0)
    ids = lax.broadcasted_iota(jnp.int32, (block, tokens), 0) + step * block
    picks = jnp.where(slot_ref[...] == ids, 1.0, 0.0).astype(BF)
    out = mm(picks, rows_ref[...])
    gates = jnp.broadcast_to(gate_ref[...].astype(BF), (8, tokens))
    lanes = pl.num_programs(0) * padded
    in_slots = mm_nt(gates, picks)
    in_slots = jnp.concatenate([in_slots, jnp.zeros((8, lanes - block), F32)], axis=1)
    lane = lax.broadcasted_iota(jnp.int32, (8, lanes), 1)
    row = lax.broadcasted_iota(jnp.int32, (block, 1), 0)
    left = out[:, :lanes]
    for expert in range(experts):
        shift = lax.rem(step * padded - expert * padded + lanes, lanes)
        moved = pltpu.roll(in_slots, shift, 1)
        mine = (lane >= step * padded) & (lane < step * padded + capacity)
        moved = jnp.where(mine, moved, 0.0)[:1]
        left = jnp.where(row == expert * padded + capacity, moved, left)
    out_ref[:, :lanes] = left.astype(BF)
    out_ref[:, lanes:] = out[:, lanes:].astype(BF)


def dispatch(slot_row, rows, blocks, block, gate):
    tokens, width = rows.shape
    grid_spec = dict(
        grid=(blocks,),
        out_specs=pl.BlockSpec((block, width), lambda k: (k, 0)),
        out_shape=jax.ShapeDtypeStruct((blocks * block, width), BF),
    )
    line = pl.BlockSpec((1, tokens), lambda k: (0, 0))
    full = pl.BlockSpec((tokens, width), lambda k: (0, 0))
    values, experts, capacity, padded = gate
    return pl.pallas_call(
        functools.partial(dispatch_gate_kernel, experts, capacity, padded),
        in_specs=[line, line, full],
        compiler_params=params(),
        cost_estimate=NO_COST,
        **grid_spec,
    )(slot_row, values, rows)


def dispatch_by_group_kernel(slot_ref, rows_ref, mine_ref, other_ref):
    block, tokens = mine_ref.shape[0], rows_ref.shape[0]
    step = pl.program_id(0)
    ids = lax.broadcasted_iota(jnp.int32, (block, tokens), 0) + step * block
    picks = jnp.where(slot_ref[...] == ids, 1.0, 0.0).astype(BF)
    out = mm(picks, rows_ref[...]).astype(BF)
    first = step < pl.num_programs(0) // 2

    @pl.when(first)
    def _():
        mine_ref[...] = out

    @pl.when(jnp.logical_not(first))
    def _():
        other_ref[...] = out


def dispatch_by_group(slot_row, rows, slots):
    tokens, width = rows.shape
    block = 256
    steps = slots // block
    return pl.pallas_call(
        dispatch_by_group_kernel,
        grid=(2 * steps,),
        in_specs=[
            pl.BlockSpec((1, tokens), lambda k: (0, 0)),
            pl.BlockSpec((tokens, width), lambda k: (0, 0)),
        ],
        out_specs=[
            pl.BlockSpec((block, width), lambda k: (jnp.minimum(k, steps - 1), 0)),
            pl.BlockSpec((block, width), lambda k: (jnp.maximum(k - steps, 0), 0)),
        ],
        out_shape=[jax.ShapeDtypeStruct((slots, width), BF)] * 2,
        compiler_params=params(),
        cost_estimate=NO_COST,
    )(slot_row, rows)


def qkv_kernel(x_ref, gain_ref, wq_ref, wk_ref, wv_ref, q_ref, k_ref, v_ref):
    rows = x_ref[...].astype(F32)
    inv = lax.rsqrt(jnp.mean(rows * rows, axis=-1, keepdims=True) + EPSILON)
    normed = (rows * inv * gain_ref[...]).astype(BF)
    q_ref[...] = (mm(normed, wq_ref[...]).astype(BF).astype(F32) * HEAD_DIM**-0.5).astype(BF)
    k_ref[...] = mm(normed, wk_ref[...]).astype(BF)
    v_ref[...] = mm(normed, wv_ref[...]).astype(BF)


def qkv(x, gain, wq, wk, wv):
    tokens, width = x.shape
    rows = pl.BlockSpec((SEQ, width), lambda t: (t, 0))
    square = pl.BlockSpec((width, width), lambda t: (0, 0))
    one = pl.BlockSpec((1, width), lambda t: (0, 0))
    return pl.pallas_call(
        qkv_kernel,
        grid=(tokens // SEQ,),
        in_specs=[rows, one, square, square, square],
        out_specs=[rows] * 3,
        out_shape=[jax.ShapeDtypeStruct((tokens, width), BF)] * 3,
        compiler_params=params(),
        cost_estimate=NO_COST,
    )(x, gain, wq, wk, wv)


def fill_bias(lines_ref, bias_ref):
    upper_right = lax.broadcasted_iota(jnp.int32, (TILE, TILE), 0) <= lax.broadcasted_iota(
        jnp.int32, (TILE, TILE), 1
    )
    tiles = SEQ // TILE
    for head in range(2):

        def sheared(line):
            whole = jnp.broadcast_to(lines_ref[head, line : line + 1, :], (TILE, TILE))
            return pltpu.roll(whole, 0, 1, stride=1, stride_axis=0)

        negative, positive = sheared(0), sheared(1)
        far_negative = jnp.broadcast_to(lines_ref[head, 2:3, :], (TILE, TILE))
        far_positive = jnp.broadcast_to(lines_ref[head, 3:4, :], (TILE, TILE))
        same = jnp.where(upper_right, negative, positive)
        above = jnp.where(upper_right, positive, far_positive)
        below = jnp.where(upper_right, far_negative, negative)
        for key in range(tiles):
            for query in range(tiles):
                gap = key - query
                tile = (
                    same
                    if gap == 0
                    else above
                    if gap == 1
                    else below
                    if gap == -1
                    else far_positive
                    if gap > 0
                    else far_negative
                )
                bias_ref[head, pl.ds(key * TILE, TILE), pl.ds(query * TILE, TILE)] = tile


def head_lanes(head):
    lane = lax.broadcasted_iota(jnp.int32, (1, PAIR), 1)
    return (lane >= head * HEAD_DIM) & (lane < (head + 1) * HEAD_DIM)


def only(head, array):
    return jnp.where(head_lanes(head), array, jnp.zeros_like(array))


def attention_kernel(
    lines_ref, mine_ref, other_ref, q_ref, k_ref, v_ref, o_ref, lse_ref, came_ref,
    bias_ref, local_sem, send_sem, recv_sem
):
    pair, seq = pl.program_id(0), pl.program_id(1)
    blocks, half = mine_ref.shape[:2]
    me, group = lax.axis_index("exp"), lax.axis_index("dp") % 2

    def transfers():
        copies = []
        for kind, sent in enumerate((mine_ref, other_ref)):
            experts = pl.ds((group + kind) % 2 * half, half)
            copies.append(
                pltpu.make_async_copy(sent.at[0], came_ref.at[experts, 0], local_sem.at[kind])
            )
            for block in range(1, blocks):
                copies.append(
                    pltpu.make_async_remote_copy(
                        src_ref=sent.at[block],
                        dst_ref=came_ref.at[experts, block],
                        send_sem=send_sem.at[kind, block],
                        recv_sem=recv_sem.at[kind, block],
                        device_id={"exp": flipped(me, block)},
                        device_id_type=pl.DeviceIdType.MESH,
                    )
                )
        return copies

    @pl.when((pair == 0) & (seq == 0))
    def _():
        greet(me, blocks)
        for copy in transfers():
            copy.start()

    @pl.when(seq == 0)
    def _():
        fill_bias(lines_ref, bias_ref)

    keys = k_ref[...]
    values_t = v_ref[...].T
    masked = [only(head, keys) for head in range(2)]
    row = lax.broadcasted_iota(jnp.int32, (PAIR, 1), 0)
    for part in range(SEQ // CHUNK):
        places = pl.ds(part * CHUNK, CHUNK)
        queries = q_ref[places, :]
        out = None
        for head in range(2):
            scores = mm_nt(masked[head], queries) + bias_ref[head, :, places]
            highest = jnp.max(scores, axis=0, keepdims=True)
            weights = jnp.exp(scores - highest)
            total = jnp.sum(weights, axis=0, keepdims=True)
            lse_ref[0, 0, head : head + 1, places] = highest + jnp.log(total)
            mixed = mm(values_t, weights.astype(BF)) * (1.0 / total)
            out = mixed if out is None else jnp.where(row < HEAD_DIM, out, mixed)
        o_ref[places, :] = out.T.astype(BF)

    @pl.when((pair == pl.num_programs(0) - 1) & (seq == pl.num_programs(1) - 1))
    def _():
        for copy in transfers():
            copy.wait()


def attention(lines, sent, q, k, v):
    blocks, half, padded, width = sent[0].shape
    tokens, width = q.shape
    seqs, pairs = tokens // SEQ, width // PAIR
    block = pl.BlockSpec((SEQ, PAIR), lambda h, s: (s, h))
    return pl.pallas_call(
        attention_kernel,
        grid=(pairs, seqs),
        in_specs=[pl.BlockSpec((2, 8, TILE), lambda h, s: (h, 0, 0))]
        + [pl.BlockSpec(memory_space=pl.ANY)] * 2
        + [block, block, block],
        out_specs=[block, pl.BlockSpec((1, 1, 2, SEQ), lambda h, s: (h, s, 0, 0))]
        + [pl.BlockSpec(memory_space=pl.ANY)],
        out_shape=[
            jax.ShapeDtypeStruct((tokens, width), BF),
            jax.ShapeDtypeStruct((pairs, seqs, 2, SEQ), F32),
            jax.ShapeDtypeStruct((2 * half, blocks, padded, width), BF),
        ],
        scratch_shapes=[pltpu.VMEM((2, SEQ, SEQ), F32)] + spread_sems(2, blocks),
        compiler_params=params(collective_id=1, has_side_effects=True),
        cost_estimate=NO_COST,
    )(lines, *sent, q, k, v)


def attention_back_kernel(parts, lines_ref, q_ref, k_ref, v_ref, do_ref, lse_ref, *refs):
    sent_refs, refs = refs[:parts], refs[parts:]
    dq_ref, dk_ref, dv_ref, sums_ref = refs[:4]
    came_refs, refs = refs[4 : 4 + parts], refs[4 + parts :]
    bias_ref, diag_ref, *sems = refs
    pair, seq = pl.program_id(0), pl.program_id(1)
    blocks, expert = came_refs[0].shape[0], sent_refs[0].shape[1] - 1
    me = lax.axis_index("exp")

    def transfers():
        copies = []
        for part in range(parts):
            copies += spread(me, sent_refs[part], expert, came_refs[part], sems, part)
        return copies

    @pl.when((pair == 0) & (seq == 0))
    def _():
        greet(me, blocks)
        for copy in transfers():
            copy.start()

    @pl.when((pair == pl.num_programs(0) - 1) & (seq == pl.num_programs(1) - 1))
    def _():
        for copy in transfers():
            copy.wait()

    @pl.when(seq == 0)
    def _():
        fill_bias(lines_ref, bias_ref)
        diag_ref[...] = jnp.zeros_like(diag_ref)

    keys, values = k_ref[...], v_ref[...]
    keys_t = keys.T
    masked_k = [only(head, keys) for head in range(2)]
    masked_v = [only(head, values) for head in range(2)]
    row = lax.broadcasted_iota(jnp.int32, (PAIR, 1), 0)
    grads_k, grads_v = [None, None], [None, None]
    tiles = SEQ // TILE
    for part in range(SEQ // CHUNK):
        places = pl.ds(part * CHUNK, CHUNK)
        queries, upstream = q_ref[places, :], do_ref[places, :]
        grad_q = None
        for head in range(2):
            scores = mm_nt(masked_k[head], queries) + bias_ref[head, :, places]
            weights = jnp.exp(scores - lse_ref[0, 0, head : head + 1, places])
            products = weights * mm_nt(masked_v[head], upstream)
            scores_grad = products - weights * jnp.sum(products, axis=0, keepdims=True)
            low = scores_grad.astype(BF)
            value_term = mm(weights.astype(BF), upstream)
            key_term = mm(low, queries)
            grads_v[head] = value_term if part == 0 else grads_v[head] + value_term
            grads_k[head] = key_term if part == 0 else grads_k[head] + key_term
            query_term = mm(keys_t, low)
            grad_q = query_term if head == 0 else jnp.where(row < HEAD_DIM, grad_q, query_term)
            groups = {}
            for query in range(CHUNK // TILE):
                for key in range(tiles):
                    gap = key - (query + part * (CHUNK // TILE))
                    kind = 0 if gap == 0 else 1 if gap == 1 else 2 if gap == -1 else 3 if gap > 0 else 4
                    tile = scores_grad[
                        key * TILE : (key + 1) * TILE, query * TILE : (query + 1) * TILE
                    ]
                    groups[kind] = tile if kind not in groups else groups[kind] + tile
            for kind, tile in groups.items():
                diag_ref[head, kind] += tile
        dq_ref[places, :] = (grad_q * HEAD_DIM**-0.5).T.astype(BF)
    first = head_lanes(0)
    dk_ref[...] = jnp.where(first, grads_k[0], grads_k[1]).astype(BF)
    dv_ref[...] = jnp.where(first, grads_v[0], grads_v[1]).astype(BF)

    @pl.when(seq == pl.num_programs(1) - 1)
    def _():
        upper_right = lax.broadcasted_iota(jnp.int32, (TILE, TILE), 0) <= lax.broadcasted_iota(
            jnp.int32, (TILE, TILE), 1
        )
        sums_ref[...] = jnp.zeros_like(sums_ref)
        for head in range(2):
            same, above, below = diag_ref[head, 0], diag_ref[head, 1], diag_ref[head, 2]

            def gathered(array):
                row_id = lax.broadcasted_iota(jnp.int32, (TILE, 1), 0)
                bit = 1
                while bit < TILE:
                    turned = pltpu.roll(array, TILE - bit, 1)
                    array = jnp.where((row_id & bit) != 0, turned, array)
                    bit *= 2
                return jnp.sum(array, axis=0, keepdims=True)

            zero = jnp.zeros_like(same)
            sums_ref[head, 0:1, :] = gathered(jnp.where(upper_right, same, below))
            sums_ref[head, 1:2, :] = gathered(jnp.where(upper_right, above, same))
            sums_ref[head, 2:3, :] = jnp.sum(
                diag_ref[head, 4] + jnp.where(upper_right, below, zero), axis=0, keepdims=True
            )
            sums_ref[head, 3:4, :] = jnp.sum(
                diag_ref[head, 3] + jnp.where(upper_right, zero, above), axis=0, keepdims=True
            )


def attention_back(lines, q, k, v, do, lse, sent):
    parts = len(sent)
    blocks, _, padded, _ = sent[0].shape
    anywhere = pl.BlockSpec(memory_space=pl.ANY)
    tokens, width = q.shape
    seqs, pairs = tokens // SEQ, width // PAIR
    block = pl.BlockSpec((SEQ, PAIR), lambda h, s: (s, h))
    lines_spec = pl.BlockSpec((2, 8, TILE), lambda h, s: (h, 0, 0))
    return pl.pallas_call(
        functools.partial(attention_back_kernel, parts),
        grid=(pairs, seqs),
        in_specs=[lines_spec, block, block, block, block]
        + [pl.BlockSpec((1, 1, 2, SEQ), lambda h, s: (h, s, 0, 0))]
        + [anywhere] * parts,
        out_specs=[block, block, block, lines_spec] + [anywhere] * parts,
        out_shape=[jax.ShapeDtypeStruct((tokens, width), BF)] * 3
        + [jax.ShapeDtypeStruct((2 * pairs, 8, TILE), F32)]
        + [jax.ShapeDtypeStruct((blocks, padded, width), BF)] * parts,
        scratch_shapes=[
            pltpu.VMEM((2, SEQ, SEQ), F32),
            pltpu.VMEM((2, 5, TILE, TILE), F32),
            *spread_sems(parts, blocks),
        ],
        compiler_params=params(collective_id=4, has_side_effects=True),
        cost_estimate=pl.CostEstimate(
            flops=40 * pairs * seqs * SEQ * SEQ * PAIR,
            bytes_accessed=14 * tokens * width,
            transcendentals=2 * pairs * seqs * SEQ * SEQ,
        ),
    )(lines, q, k, v, do, lse, *sent)


def router_kernel(
    o_ref, x_ref, wo_ref, gain_ref, wr_ref, expert_ref, h_ref, u_ref, probs_ref, gate_ref, line_ref
):
    mixed = x_ref[...].astype(F32) + mm(o_ref[...], wo_ref[...])
    h_ref[...] = mixed
    inv = lax.rsqrt(jnp.mean(mixed * mixed, axis=-1, keepdims=True) + EPSILON)
    normed = mixed * inv * gain_ref[...]
    u_ref[...] = normed.astype(BF)
    high, low = halves(normed)
    wr_high, wr_low = halves(wr_ref[...])
    logits = mm(high, wr_high) + (mm(high, wr_low) + mm(low, wr_high))
    spread = jnp.exp(logits - jnp.max(logits, axis=-1, keepdims=True))
    probs = spread / jnp.sum(spread, axis=-1, keepdims=True)
    probs_ref[...] = probs
    picked = expert_ref[...] == lax.broadcasted_iota(jnp.int32, probs.shape, 1)
    gate = jnp.sum(jnp.where(picked, probs, 0.0), axis=-1, keepdims=True)
    gate_ref[...] = gate
    size = gate.shape[0]
    diagonal = lax.broadcasted_iota(jnp.int32, (size, size), 0) == lax.broadcasted_iota(
        jnp.int32, (size, size), 1
    )
    line_ref[...] = jnp.sum(jnp.where(diagonal, gate, 0.0), axis=0, keepdims=True)


def router(o, x, wo, gain, wr, expert):
    tokens, width = x.shape
    experts = wr.shape[1]
    size = 512

    def rows(columns):
        return pl.BlockSpec((size, columns), lambda t: (t, 0))

    def whole(*shape):
        return pl.BlockSpec(shape, lambda t: (0, 0))

    return pl.pallas_call(
        router_kernel,
        grid=(tokens // size,),
        in_specs=[rows(width), rows(width), whole(width, width), whole(1, width)]
        + [whole(width, experts), rows(1)],
        out_specs=[rows(width), rows(width), rows(experts), rows(1)]
        + [pl.BlockSpec((1, size), lambda t: (0, t))],
        out_shape=[
            jax.ShapeDtypeStruct((tokens, width), F32),
            jax.ShapeDtypeStruct((tokens, width), BF),
            jax.ShapeDtypeStruct((tokens, experts), F32),
            jax.ShapeDtypeStruct((tokens, 1), F32),
            jax.ShapeDtypeStruct((1, tokens), F32),
        ],
        compiler_params=params(),
        cost_estimate=NO_COST,
    )(o, x, wo, gain, wr, expert)


def gelu_and_slope(z):
    square = z * z
    half = 0.5 + 0.5 * jnp.tanh(z * (GELU_A + GELU_B * square))
    value = z * half
    slope = half + 2.0 * value * (1.0 - half) * (GELU_A + 3.0 * GELU_B * square)
    return value, slope


def send_back(me, held, target, which, place, sems, kind):
    send_sem, recv_sem, local_sem = sems
    copies = [pltpu.make_async_copy(held.at[0], target.at[0, which], local_sem.at[kind, place])]
    for block in range(1, held.shape[0]):
        copies.append(
            pltpu.make_async_remote_copy(
                src_ref=held.at[block],
                dst_ref=target.at[block, which],
                send_sem=send_sem.at[kind, place, block],
                recv_sem=recv_sem.at[kind, place, block],
                device_id={"exp": flipped(me, block)},
                device_id_type=pl.DeviceIdType.MESH,
            )
        )
    return copies


def expert_step(parts, rows, upstream, first_ref, second_ref, e_sum, d_sum):
    columns = first_ref.shape[2] // parts
    for part in range(parts):
        places = slice(part * columns, (part + 1) * columns)
        first, second = first_ref[0, :, places], second_ref[0, places, :]
        value, slope = gelu_and_slope(mm(rows, first))
        inner = (mm_nt(upstream, second) * slope).astype(BF)
        e_sum[...] += mm(value.astype(BF), second)
        d_sum[...] += mm_nt(inner, first)


def expert_kernel(parts, all_experts, sent_ref, c_ref, first_ref, second_ref, *refs):
    expert, step = pl.program_id(0), pl.program_id(1)
    count, last_step = pl.num_programs(0), pl.num_programs(1) - 1
    u_refs, u_late, refs = refs[:all_experts], refs[all_experts], refs[all_experts + 1 :]
    e_kept, d_kept, rows_ref, e_sum, d_sum, e_held, d_held, local_sem, send_sem, recv_sem = refs
    early, blocks, padded, width = e_held.shape
    me = lax.axis_index("exp")
    group, half = lax.axis_index("dp") % 2, all_experts // 2

    def outgoing(which, block):
        return pltpu.make_async_remote_copy(
            src_ref=sent_ref.at[block, which],
            dst_ref=rows_ref.at[which, block],
            send_sem=send_sem.at[which, block],
            recv_sem=recv_sem.at[which, block],
            device_id={"exp": flipped(me, block)},
            device_id_type=pl.DeviceIdType.MESH,
        )

    def own_in(which):
        return pltpu.make_async_copy(sent_ref.at[0, which], rows_ref.at[which, 0], local_sem.at[0, which])

    def keep(which, act):
        for each in range(2):
            target = u_refs[(which // half + each) % 2 * half + which % half]

            @pl.when(group == each)
            def _(target=target):
                act(pltpu.make_async_copy(rows_ref.at[which], target, local_sem.at[1, which]))

        if which >= early:
            act(
                pltpu.make_async_copy(
                    rows_ref.at[which], u_late.at[which - early], local_sem.at[2, which - early]
                )
            )

    def arrive(which):
        own_in(which).wait()
        for block in range(1, blocks):
            outgoing(which, block).wait_recv()
        keep(which, lambda copy: copy.start())

    def keep_result(which):
        return [
            pltpu.make_async_copy(e_held.at[which], e_kept.at[which], local_sem.at[3, which]),
            pltpu.make_async_copy(d_held.at[which], d_kept.at[which], local_sem.at[4, which]),
        ]

    @pl.when((expert == 0) & (step == 0))
    def _():
        greet(me, blocks)
        for which in range(all_experts):
            own_in(which).start()
            for block in range(1, blocks):
                outgoing(which, block).start()

    @pl.when(step == 0)
    def _():
        for which in range(early):

            @pl.when(expert == which)
            def _(which=which):
                arrive(which)

        e_sum[...] = jnp.zeros_like(e_sum)
        d_sum[...] = jnp.zeros_like(d_sum)

    rows = rows_ref[expert].reshape(blocks * padded, width)
    expert_step(parts, rows, c_ref[0], first_ref, second_ref, e_sum, d_sum)

    @pl.when(step == last_step)
    def _():
        e_held[expert] = e_sum[...].astype(BF).reshape(blocks, padded, width)
        d_held[expert] = d_sum[...].astype(BF).reshape(blocks, padded, width)
        for which in range(early):

            @pl.when(expert == which)
            def _(which=which):
                for copy in keep_result(which):
                    copy.start()

    @pl.when((step == last_step) & (expert == count - 1))
    def _():
        for which in range(early, all_experts):
            arrive(which)
        for which in range(all_experts):
            keep(which, lambda copy: copy.wait())
            for block in range(1, blocks):
                outgoing(which, block).wait_send()
        for which in range(early):
            for copy in keep_result(which):
                copy.wait()


def expert_rest_kernel(
    parts, u_ref, c_ref, first_ref, second_ref, e_kept, d_kept, e_ref, d_ref,
    e_sum, d_sum, e_held, d_held, back_send, back_recv, back_local,
):
    expert, step = pl.program_id(0), pl.program_id(1)
    count, last_step = pl.num_programs(0), pl.num_programs(1) - 1
    late, blocks, padded, width = e_held.shape
    kept = e_kept.shape[0]
    me = lax.axis_index("exp")
    sems = (back_send, back_recv, back_local)

    def back(which):
        if which < kept:
            e_from, d_from = e_kept.at[which], d_kept.at[which]
        else:
            e_from, d_from = e_held.at[which - kept], d_held.at[which - kept]
        return send_back(me, e_from, e_ref, which, which, sems, 0) + send_back(
            me, d_from, d_ref, which, which, sems, 1
        )

    @pl.when((expert == 0) & (step == 0))
    def _():
        greet(me, blocks)
        for which in range(kept):
            for copy in back(which):
                copy.start()

    @pl.when(step == 0)
    def _():
        e_sum[...] = jnp.zeros_like(e_sum)
        d_sum[...] = jnp.zeros_like(d_sum)

    rows = u_ref[0].reshape(blocks * padded, width)
    expert_step(parts, rows, c_ref[0], first_ref, second_ref, e_sum, d_sum)

    @pl.when(step == last_step)
    def _():
        e_held[expert] = e_sum[...].astype(BF).reshape(blocks, padded, width)
        d_held[expert] = d_sum[...].astype(BF).reshape(blocks, padded, width)
        for which in range(late):

            @pl.when(expert == which)
            def _(which=which):
                for copy in back(kept + which):
                    copy.start()

    @pl.when((step == last_step) & (expert == count - 1))
    def _():
        for which in range(kept + late):
            for copy in back(which):
                copy.wait()


def expert_pass(sent, c, w_in, w_out):
    blocks, experts, padded, width = sent.shape
    hidden = w_in.shape[2]
    size = 768
    rows = blocks * padded
    early = experts // 2
    late = experts - early
    anywhere = pl.BlockSpec(memory_space=pl.ANY)
    dma = pltpu.SemaphoreType.DMA

    def results(count):
        return jax.ShapeDtypeStruct((count, blocks, padded, width), BF)

    def weights(first):
        return [
            pl.BlockSpec((1, rows, width), lambda e, f: (first + e, 0, 0)),
            pl.BlockSpec((1, width, size), lambda e, f: (first + e, 0, f)),
            pl.BlockSpec((1, size, width), lambda e, f: (first + e, f, 0)),
        ]

    *u_rows, u_late, e_kept, d_kept = pl.pallas_call(
        functools.partial(expert_kernel, 3, experts),
        grid=(early, hidden // size),
        in_specs=[anywhere] + weights(0),
        out_specs=[anywhere] * (experts + 3),
        out_shape=[jax.ShapeDtypeStruct((blocks, padded, width), BF)] * experts
        + [results(late), results(early), results(early)],
        scratch_shapes=[
            pltpu.VMEM((experts, blocks, padded, width), BF),
            pltpu.VMEM((rows, width), F32),
            pltpu.VMEM((rows, width), F32),
            pltpu.VMEM((early, blocks, padded, width), BF),
            pltpu.VMEM((early, blocks, padded, width), BF),
            dma((5, experts)),
            dma((experts, blocks)),
            dma((experts, blocks)),
        ],
        compiler_params=params(collective_id=0, has_side_effects=True),
        cost_estimate=NO_COST,
    )(sent, c, w_in, w_out)
    u_rows = [part.reshape(rows, width) for part in u_rows]
    e_back, d_back = pl.pallas_call(
        functools.partial(expert_rest_kernel, 3),
        grid=(late, hidden // size),
        in_specs=[pl.BlockSpec((1, blocks, padded, width), lambda e, f: (e, 0, 0, 0))]
        + weights(early)
        + [anywhere] * 2,
        out_specs=[anywhere] * 2,
        out_shape=[jax.ShapeDtypeStruct((blocks, experts, padded, width), BF)] * 2,
        scratch_shapes=[
            pltpu.VMEM((rows, width), F32),
            pltpu.VMEM((rows, width), F32),
            pltpu.VMEM((late, blocks, padded, width), BF),
            pltpu.VMEM((late, blocks, padded, width), BF),
            dma((2, experts, blocks)),
            dma((2, experts, blocks)),
            dma((2, experts)),
        ],
        compiler_params=params(collective_id=3, has_side_effects=True),
        cost_estimate=pl.CostEstimate(
            flops=32 * rows * width * hidden, bytes_accessed=4 * width * hidden, transcendentals=0
        ),
    )(u_late, c, w_in, w_out, e_kept, d_kept)
    return u_rows, e_back, d_back


def weights_kernel(parts, sources, capacity, padded, place_ref, *refs):
    u_refs, c_refs = refs[:sources], refs[sources : 2 * sources]
    first_ref, second_ref, far_in, far_out, in_sum, out_sum = refs[2 * sources :]
    size = first_ref.shape[2]
    rows = u_refs[0].shape[0]
    columns = size // parts
    first_t = first_ref[0].T
    for source in range(sources):
        inputs, upstream = u_refs[source][...], c_refs[source][...].reshape(u_refs[source].shape)
        gate = jnp.zeros((1, rows), F32)
        for block in range(rows // padded):
            place = block * padded + capacity
            gate = gate + inputs[place : place + 1, :rows].astype(F32)
        for part in range(parts):
            places = slice(part * columns, (part + 1) * columns)
            value, slope = gelu_and_slope(mm_nt(first_t[places, :], inputs))
            inner = (mm_nt(second_ref[0, places, :], upstream) * (slope * gate)).astype(BF)
            in_term = mm(inner, inputs)
            out_term = mm((value * gate).astype(BF), upstream)
            if source == 0:
                in_sum[places, :] = in_term
                out_sum[places, :] = out_term
            else:
                in_sum[places, :] += in_term
                out_sum[places, :] += out_term
    far_in[...] = in_sum[...].T.astype(BF)
    far_out[...] = out_sum[...].astype(BF)


def weight_grads(place, us, c_rows, c_far, w_in, w_out, size, capacity, padded):
    sources = len(us)
    rows, width = us[0].shape
    block = pl.BlockSpec((rows, width), lambda f, p: (0, 0))
    return pl.pallas_call(
        functools.partial(weights_kernel, 1, sources, capacity, padded),
        grid_spec=pltpu.PrefetchScalarGridSpec(
            num_scalar_prefetch=1,
            grid=(1,),
            in_specs=[block] * sources
            + [pl.BlockSpec((1, rows, width), lambda f, p: (p[0], 0, 0))]
            + [block] * (sources - 1)
            + [
                pl.BlockSpec((1, width, size), lambda f, p: (p[0], 0, p[1])),
                pl.BlockSpec((1, size, width), lambda f, p: (p[0], p[1], 0)),
            ],
            out_specs=[
                pl.BlockSpec((width, size), lambda f, p: (0, 0)),
                pl.BlockSpec((size, width), lambda f, p: (0, 0)),
            ],
            scratch_shapes=[pltpu.VMEM((size, width), F32)] * 2,
        ),
        out_shape=[
            jax.ShapeDtypeStruct((width, size), BF),
            jax.ShapeDtypeStruct((size, width), BF),
        ],
        compiler_params=params(),
        cost_estimate=NO_COST,
    )(place, *us, c_rows, *c_far, w_in, w_out)


def finish_kernel(half, place_ref, *refs):
    own_in, own_out, refs = refs[0], refs[1], refs[2:]
    came_in, came_out, dense_ref = refs[:half], refs[half : 2 * half], refs[2 * half]
    a_out, b_out, *dense_outs = refs[2 * half + 1 : 2 * half + 7]
    held, sem = refs[2 * half + 7 :]
    at, last_step = pl.program_id(0), pl.num_programs(0) - 1
    dense = [
        pltpu.make_async_copy(held.at[which], dense_outs[which], sem.at[which]) for which in range(4)
    ]
    held[at] = dense_ref[...].astype(F32)
    for which in range(4):
        pl.when(at == which)(dense[which].start)

    @pl.when(at < half)
    def _():
        a_out[0] = own_in[0].astype(F32)
        b_out[0] = own_out[0].astype(F32)

    for step in range(half):

        @pl.when(at == half + step)
        def _(step=step):
            a_out[0] = came_in[step][...].astype(F32)
            b_out[0] = came_out[step][...].astype(F32)

    @pl.when(at == last_step)
    def _():
        for copy in dense:
            copy.wait()


def finish(places, own_in, own_out, came_in, came_out, dense):
    half, width, size = own_in.shape

    def whole(*shape):
        return pl.BlockSpec(shape, lambda e, p: (0, 0))

    def own(*shape):
        return pl.BlockSpec((1,) + shape, lambda e, p: (jnp.minimum(e, half - 1), 0, 0))

    def spec(*shape):
        return pl.BlockSpec((1,) + shape, lambda e, p: (p[e], 0, 0))

    return pl.pallas_call(
        functools.partial(finish_kernel, half),
        grid_spec=pltpu.PrefetchScalarGridSpec(
            num_scalar_prefetch=1,
            grid=(2 * half,),
            in_specs=[own(width, size), own(size, width)]
            + [whole(width, size)] * half
            + [whole(size, width)] * half
            + [pl.BlockSpec((width, width), lambda e, p: (e, 0))],
            out_specs=[spec(width, size), spec(size, width)]
            + [pl.BlockSpec(memory_space=pl.ANY)] * 4,
            scratch_shapes=[pltpu.VMEM((4, width, width), F32), pltpu.SemaphoreType.DMA((4,))],
        ),
        out_shape=[
            jax.ShapeDtypeStruct((2 * half, width, size), F32),
            jax.ShapeDtypeStruct((2 * half, size, width), F32),
        ]
        + [jax.ShapeDtypeStruct((width, width), F32)] * 4,
        compiler_params=params(),
    )(places, own_in, own_out, *came_in, *came_out, dense)


def tail_kernel(parts, sources, experts, capacity, padded, *refs):
    u_refs, refs = refs[: sources * experts], refs[sources * experts :]
    c_own, c_far, refs = refs[0], refs[1 : 1 + (sources - 1) * experts], refs[1 + (sources - 1) * experts :]
    (
        first_ref, second_ref, far_in, far_out, dense_o, dense_qkv, small_ref,
        own_in_ref, own_out_ref, came_in_ref, came_out_ref, dense_ref, total_ref,
        rows_u, rows_c, first_held, second_held, first_t, in_sum, out_sum, own_in, own_out,
        dense, dense_came, dense_over_dp, small, small_came,
        rows_sem, weight_sem, load_sem, far_send, far_recv, own_sem,
        half_send, half_recv, over_send, over_recv, back_send, back_recv, small_send, small_recv, keep_sem,
    ) = refs
    rows, width = rows_u.shape[2:]
    size = in_sum.shape[0]
    columns = size // parts
    exp_me, dp_me = lax.axis_index("exp"), lax.axis_index("dp")
    exp_bits, dp_bits = half_send.shape[2], over_send.shape[0]
    group, pair = dp_me % 2, dp_me // 2
    mesh_id = pl.DeviceIdType.MESH

    def exp_peer(bit):
        return {"exp": flipped(exp_me, 1 << bit)}

    def dp_peer(bit):
        return {"dp": flipped(dp_me, 1 << bit)}

    chain = dense.shape[0] // 2
    bits = list(range(exp_bits))
    split = 1 + (exp_bits - 1) // 2
    orders = (bits, bits[:1] + bits[split:] + bits[1:split])

    def region(which, depth):
        start = which * chain
        for level in range(depth):
            start = start + (exp_me // (1 << orders[which][level])) % 2 * (chain >> (level + 1))
        return pl.ds(pl.multiple_of(start, 16), chain >> depth)

    def other_half(which, depth):
        start = which * chain
        for level in range(depth):
            start = start + (exp_me // (1 << orders[which][level])) % 2 * (chain >> (level + 1))
        start = start + (1 - (exp_me // (1 << orders[which][depth])) % 2) * (chain >> (depth + 1))
        return pl.ds(pl.multiple_of(start, 16), chain >> (depth + 1))

    def came(which, depth):
        return pl.ds(which * chain + chain - (chain >> depth), chain >> (depth + 1))

    def columns_of(side):
        return pl.ds(side * (width // 2), width // 2)

    def halving(side, which, depth):
        return pltpu.make_async_remote_copy(
            src_ref=dense.at[other_half(which, depth), columns_of(side)],
            dst_ref=dense_came.at[came(which, depth), columns_of(side)],
            send_sem=half_send.at[side, which, depth],
            recv_sem=half_recv.at[side, which, depth],
            device_id=exp_peer(orders[which][depth]),
            device_id_type=mesh_id,
        )

    def over(side, which, bit):
        mine = dense.at[region(which, exp_bits), columns_of(side)]
        return pltpu.make_async_remote_copy(
            src_ref=mine if bit == 0 else dense_over_dp.at[1, bit - 1, side, which],
            dst_ref=dense_over_dp.at[0, bit, side, which],
            send_sem=over_send.at[bit, side, which],
            recv_sem=over_recv.at[bit, side, which],
            device_id=dp_peer(dp_bits - 1 - bit),
            device_id_type=mesh_id,
        )

    def keeping(side, which):
        return pltpu.make_async_copy(
            dense_over_dp.at[1, dp_bits - 1, side, which],
            dense_ref.at[region(which, exp_bits), columns_of(side)],
            keep_sem.at[side, which],
        )

    def returning(side, which, depth):
        place = dense_ref.at[region(which, depth + 1), columns_of(side)]
        return pltpu.make_async_remote_copy(
            src_ref=place,
            dst_ref=place,
            send_sem=back_send.at[side, which, depth],
            recv_sem=back_recv.at[side, which, depth],
            device_id=exp_peer(orders[which][depth]),
            device_id_type=mesh_id,
        )

    def small_copy(depth):
        return pltpu.make_async_remote_copy(
            src_ref=small.at[depth],
            dst_ref=small_came.at[depth],
            send_sem=small_send.at[depth],
            recv_sem=small_recv.at[depth],
            device_id=exp_peer(depth) if depth < exp_bits else dp_peer(depth - exp_bits),
            device_id_type=mesh_id,
        )

    def loads():
        return [
            pltpu.make_async_copy(dense_o, dense.at[pl.ds(3 * width, width)], load_sem.at[0]),
            pltpu.make_async_copy(dense_qkv, dense.at[pl.ds(0, 3 * width)], load_sem.at[1]),
            pltpu.make_async_copy(small_ref, small.at[0], load_sem.at[2]),
        ]

    def add_small(depth):
        small_copy(depth).wait_recv()
        small[depth + 1] = small[depth] + small_came[depth]

    def begin(side):
        if side == 0:
            for load in loads():
                load.wait()
            small_copy(0).start()
        for which in range(2):
            halving(side, which, 0).start()

    def halve(depth):
        def act(side):
            for which in range(2):
                halving(side, which, depth).wait_recv()
                place, new, here = region(which, depth + 1), came(which, depth), columns_of(side)
                dense[place, here] = (
                    dense[place, here].astype(F32) + dense_came[new, here].astype(F32)
                ).astype(BF)
                if depth + 1 < exp_bits:
                    halving(side, which, depth + 1).start()
                else:
                    over(side, which, 0).start()
            if side == 0:
                add_small(depth)
                small_copy(depth + 1).start()

        return act

    def sum_over(bit):
        def act(side):
            for which in range(2):
                over(side, which, bit).wait_recv()
                if bit == 0:
                    mine = dense[region(which, exp_bits), columns_of(side)]
                else:
                    mine = dense_over_dp[1, bit - 1, side, which]
                dense_over_dp[1, bit, side, which] = (
                    mine.astype(F32) + dense_over_dp[0, bit, side, which].astype(F32)
                ).astype(BF)
                if bit + 1 < dp_bits:
                    over(side, which, bit + 1).start()
                else:
                    keeping(side, which).start()
            if side == 0:
                add_small(exp_bits + bit)
                if bit + 1 < dp_bits:
                    small_copy(exp_bits + bit + 1).start()
            if bit + 1 == dp_bits:
                for which in range(2):
                    keeping(side, which).wait()
                    returning(side, which, exp_bits - 1).start()

        return act

    def give_back(depth):
        def act(side):
            for which in range(2):
                returning(side, which, depth).wait_recv()
                if depth > 0:
                    returning(side, which, depth - 1).start()

        return act

    stages = [begin] + [halve(depth) for depth in range(exp_bits)]
    stages += [sum_over(bit) for bit in range(dp_bits)]
    stages += [give_back(depth) for depth in reversed(range(exp_bits))]
    stages = [functools.partial(stage, side) for stage in stages for side in range(2)]

    steps, turns = experts, experts * sources

    def rows_copy(source, expert):
        if source == 0:
            c_from = c_own.at[group * experts + expert]
        else:
            c_from = c_far[expert * (sources - 1) + source - 1]
        return [
            pltpu.make_async_copy(
                u_refs[expert * sources + source],
                rows_u.at[source, expert],
                rows_sem.at[0, source, expert],
            ),
            pltpu.make_async_copy(
                c_from, rows_c.at[source, expert], rows_sem.at[1, source, expert]
            ),
        ]

    def weight_copy(step):
        expert = group * experts + step
        place = (pair * 2 + group) * size
        place = pl.ds(pl.multiple_of(place, 128), size)
        slot = step % 2
        return [
            pltpu.make_async_copy(
                first_ref.at[expert, :, place], first_held.at[slot], weight_sem.at[0, slot]
            ),
            pltpu.make_async_copy(
                second_ref.at[expert, place, :], second_held.at[slot], weight_sem.at[1, slot]
            ),
        ]

    far_parts = far_send.shape[1]

    def far_copy(index):
        kind, part = index % 2, index // 2
        held, target = ((far_in, came_in_ref), (far_out, came_out_ref))[kind]
        lines = held.shape[0] // far_parts
        place = pl.ds(part * lines, lines)
        return pltpu.make_async_remote_copy(
            src_ref=held.at[place],
            dst_ref=target.at[place],
            send_sem=far_send.at[kind, part],
            recv_sem=far_recv.at[kind, part],
            device_id=dp_peer(0),
            device_id_type=mesh_id,
        )

    def own_copy(expert):
        return [
            pltpu.make_async_copy(held.at[expert], target.at[expert], own_sem.at[kind, expert])
            for kind, (held, target) in enumerate(((own_in, own_in_ref), (own_out, own_out_ref)))
        ]

    for load in loads():
        load.start()
    for copy in weight_copy(0):
        copy.start()
    for expert in range(experts):
        for source in range(sources):
            for copy in rows_copy(source, expert):
                copy.start()
    barrier = pltpu.get_barrier_semaphore()
    for bit in range(exp_bits):
        pl.semaphore_signal(barrier, inc=1, device_id=exp_peer(bit), device_id_type=mesh_id)
    for bit in range(dp_bits):
        pl.semaphore_signal(barrier, inc=1, device_id=dp_peer(bit), device_id_type=mesh_id)
    pl.semaphore_wait(barrier, exp_bits + dp_bits)

    places = [0, 0, 1, 2, 3, 4, 5, 6]
    places = [place for place in places if place < turns][: len(stages)]
    starts = {4: 3}
    starts = {place: index for place, index in starts.items() if place < turns}
    pieces = 2 * far_parts

    def turn(at, carry):
        step, source = at // sources, at % sources
        expert, slot = step, step % 2
        for place, stage in zip(places, stages):
            pl.when(at == place)(stage)
        for place, index in starts.items():
            pl.when(at == place)(far_copy(index).start)

        @pl.when(source == 0)
        def _():
            for copy in weight_copy(step):
                copy.wait()

            @pl.when(step + 1 < steps)
            def _():
                for copy in weight_copy(step + 1):
                    copy.start()

            first_t[...] = first_held[slot].T

        for each_expert in range(experts):
            for each in range(sources):

                @pl.when(at == each_expert * sources + each)
                def _(each=each, each_expert=each_expert):
                    for copy in rows_copy(each, each_expert):
                        copy.wait()

        inputs, upstream = rows_u[source, expert], rows_c[source, expert]
        gate = jnp.zeros((1, rows), F32)
        for block in range(rows // padded):
            place = block * padded + capacity
            gate = gate + inputs[place : place + 1, :rows].astype(F32)
        for part in range(parts):
            here = slice(part * columns, (part + 1) * columns)
            value, slope = gelu_and_slope(mm_nt(first_t[here, :], inputs))
            inner = (mm_nt(second_held[slot, here, :], upstream) * (slope * gate)).astype(BF)
            in_term = mm(inner, inputs)
            out_term = mm((value * gate).astype(BF), upstream)
            fresh = source == 0
            in_sum[here, :] = jnp.where(fresh, 0.0, in_sum[here, :]) + in_term
            out_sum[here, :] = jnp.where(fresh, 0.0, out_sum[here, :]) + out_term

        for each_expert in range(experts):

            @pl.when((source == sources - 1) & (step == each_expert))
            def _(each_expert=each_expert):
                own_in[each_expert] = in_sum[...].T.astype(BF)
                own_out[each_expert] = out_sum[...].astype(BF)
                for copy in own_copy(each_expert):
                    copy.start()

        return carry

    for index in range(3):
        far_copy(index).start()
    lax.fori_loop(0, turns, turn, 0)
    for stage in stages[len(places) : len(places) + 2]:
        stage()
    for index in range(3 + len(starts), pieces):
        far_copy(index).start()
    for stage in stages[len(places) + 2 :]:
        stage()
    total_ref[...] = small[exp_bits + dp_bits]
    for index in range(pieces):
        far_copy(index).wait()
    for expert in range(experts):
        for copy in own_copy(expert):
            copy.wait()
    for side in range(2):
        for which in range(2):
            for depth in range(exp_bits):
                halving(side, which, depth).wait_send()
                returning(side, which, depth).wait_send()
            for bit in range(dp_bits):
                over(side, which, bit).wait_send()
    for depth in range(exp_bits + dp_bits):
        small_copy(depth).wait_send()


def tail(us, c_rows, c_far, w_in, w_out, far_in, far_out, size, dense_o, dense_qkv, small, capacity, padded, exp_n):
    sources, experts = len(us[0]), len(us)
    rows, width = us[0][0].shape
    far_parts = 4
    exp_bits, dp_bits = exp_n.bit_length() - 1, sources.bit_length() - 1
    lines = 4 * width
    anywhere = pl.BlockSpec(memory_space=pl.ANY)
    dma = pltpu.SemaphoreType.DMA
    return pl.pallas_call(
        functools.partial(tail_kernel, 3, sources, experts, capacity, padded),
        in_specs=[anywhere] * (experts * (2 * sources - 1) + 8),
        out_specs=[anywhere] * 5 + [pl.BlockSpec(memory_space=pltpu.VMEM)],
        out_shape=[
            jax.ShapeDtypeStruct((experts, width, size), BF),
            jax.ShapeDtypeStruct((experts, size, width), BF),
            jax.ShapeDtypeStruct((width, size), BF),
            jax.ShapeDtypeStruct((size, width), BF),
            jax.ShapeDtypeStruct((lines, width), BF),
            jax.ShapeDtypeStruct(small.shape, F32),
        ],
        scratch_shapes=[
            pltpu.VMEM((sources, experts, rows, width), BF),
            pltpu.VMEM((sources, experts, rows, width), BF),
            pltpu.VMEM((2, width, size), BF),
            pltpu.VMEM((2, size, width), BF),
            pltpu.VMEM((size, width), BF),
            pltpu.VMEM((size, width), F32),
            pltpu.VMEM((size, width), F32),
            pltpu.VMEM((experts, width, size), BF),
            pltpu.VMEM((experts, size, width), BF),
            pltpu.VMEM((lines, width), BF),
            pltpu.VMEM((lines, width), BF),
            pltpu.VMEM((2, dp_bits, 2, 2, lines // 2 >> exp_bits, width // 2), BF),
            pltpu.VMEM((exp_bits + dp_bits + 1,) + small.shape, F32),
            pltpu.VMEM((exp_bits + dp_bits,) + small.shape, F32),
            dma((2, sources, experts)),
            dma((2, 2)),
            dma((3,)),
            dma((2, far_parts)),
            dma((2, far_parts)),
            dma((2, experts)),
            dma((2, 2, exp_bits)),
            dma((2, 2, exp_bits)),
            dma((dp_bits, 2, 2)),
            dma((dp_bits, 2, 2)),
            dma((2, 2, exp_bits)),
            dma((2, 2, exp_bits)),
            dma((exp_bits + dp_bits,)),
            dma((exp_bits + dp_bits,)),
            dma((2, 2)),
        ],
        compiler_params=pltpu.CompilerParams(
            vmem_limit_bytes=58 * 2**20, collective_id=2, has_side_effects=True
        ),
        cost_estimate=NO_COST,
    )(*sum(us, []), c_rows, *sum(c_far, []), w_in, w_out, far_in, far_out, dense_o, dense_qkv, small)


def combine_kernel(
    parts, experts, slot_ref, expert_ref, gate_ref, probs_ref, h_ref, c_ref, o_ref,
    e_ref, d_ref, wo_ref, wr_ref, gain_ref, *refs
):
    sent_refs, refs = refs[:parts], refs[parts:]
    mixed_ref, dh_ref, do_ref, wo_ref_out, wr_sum, gain_sum = refs[:6]
    came_refs, refs = refs[6 : 6 + parts * experts], refs[6 + parts * experts :]
    wo_sum, e_held, d_held, load_sem, *sems = refs
    step = pl.program_id(0)
    me, blocks = lax.axis_index("exp"), sent_refs[0].shape[0]

    def loads():
        return [
            pltpu.make_async_copy(e_ref, e_held, load_sem.at[0]),
            pltpu.make_async_copy(d_ref, d_held, load_sem.at[1]),
        ]

    def transfers():
        copies = []
        for expert in range(experts):
            for part in range(parts):
                index = expert * parts + part
                copies += spread(me, sent_refs[part], expert, came_refs[index], sems, index)
        return copies

    @pl.when(step == 0)
    def _():
        for copy in loads():
            copy.start()
        greet(me, blocks)
        for copy in transfers():
            copy.start()
        for copy in loads():
            copy.wait()

    @pl.when(step == pl.num_programs(0) - 1)
    def _():
        for copy in transfers():
            copy.wait()

    tokens, slots = slot_ref.shape[1], e_ref.shape[0]
    slot = as_column(slot_ref[...].astype(F32)).astype(jnp.int32)
    picks = jnp.where(
        slot == lax.broadcasted_iota(jnp.int32, (tokens, slots), 1), 1.0, 0.0
    ).astype(BF)
    returned, arrived = mm(picks, e_held[...]), mm(picks, d_held[...])
    gate, probs, mixed = gate_ref[...], probs_ref[...], h_ref[...]
    upstream = c_ref[...].astype(F32)
    mixed_ref[...] = (mixed + gate * returned).astype(BF)
    gate_grad = jnp.sum(upstream * returned, axis=-1, keepdims=True)
    picked = jnp.where(expert_ref[...] == lax.broadcasted_iota(jnp.int32, probs.shape, 1), 1.0, 0.0)
    logit_grad = gate_grad * gate * (picked - probs)
    inv = lax.rsqrt(jnp.mean(mixed * mixed, axis=-1, keepdims=True) + EPSILON)
    unit = mixed * inv
    gain = gain_ref[...]
    lg_high, lg_low = halves(logit_grad)
    wr_high, wr_low = halves(wr_ref[...])
    through_router = mm_nt(lg_high, wr_high) + (mm_nt(lg_low, wr_high) + mm_nt(lg_high, wr_low))
    normed_grad = through_router + gate * arrived
    unit_grad = normed_grad * gain
    mixed_grad = upstream + inv * (
        unit_grad - unit * jnp.mean(unit_grad * unit, axis=-1, keepdims=True)
    )
    dh_ref[...] = mixed_grad
    low = mixed_grad.astype(BF)
    do_ref[...] = mm_nt(low, wo_ref[...]).astype(BF)

    @pl.when(step == 0)
    def _():
        wo_sum[...] = jnp.zeros_like(wo_sum)
        wr_sum[...] = jnp.zeros_like(wr_sum)
        gain_sum[...] = jnp.zeros_like(gain_sum)

    wo_sum[...] += mm(o_ref[...].T, low)
    n_high, n_low = halves(unit * gain)
    lg_high, lg_low = lg_high.T, lg_low.T
    wr_sum[...] += mm(lg_high, n_high) + (mm(lg_low, n_high) + mm(lg_high, n_low))
    gain_sum[...] += jnp.sum(normed_grad * unit, axis=0, keepdims=True)

    @pl.when(step == pl.num_programs(0) - 1)
    def _():
        wo_ref_out[...] = wo_sum[...].astype(BF)


def combine(slot, expert, gate, probs, h, c, o, e_out, du, wo, wr, gain, sent):
    parts, (blocks, local, padded, _) = len(sent), sent[0].shape
    spreads = parts * (local - 1)
    anywhere = pl.BlockSpec(memory_space=pl.ANY)
    tokens, width = h.shape
    slots, experts = e_out.shape[0], wr.shape[1]
    size = 256

    def rows(columns):
        return pl.BlockSpec((size, columns), lambda t: (t, 0))

    def whole(*shape):
        return pl.BlockSpec(shape, lambda t: (0, 0))

    return pl.pallas_call(
        functools.partial(combine_kernel, parts, local - 1),
        grid=(tokens // size,),
        in_specs=[pl.BlockSpec((1, size), lambda t: (0, t)), rows(1), rows(1), rows(experts), rows(width), rows(width), rows(width)]
        + [anywhere] * 2
        + [whole(width, width), whole(width, experts)]
        + [whole(1, width)]
        + [anywhere] * parts,
        out_specs=[rows(width), rows(width), rows(width), whole(width, width), whole(experts, width)]
        + [whole(1, width)]
        + [anywhere] * spreads,
        out_shape=[
            jax.ShapeDtypeStruct((tokens, width), BF),
            jax.ShapeDtypeStruct((tokens, width), F32),
            jax.ShapeDtypeStruct((tokens, width), BF),
            jax.ShapeDtypeStruct((width, width), BF),
            jax.ShapeDtypeStruct((experts, width), F32),
            jax.ShapeDtypeStruct((1, width), F32),
        ]
        + [jax.ShapeDtypeStruct((blocks, padded, width), BF)] * spreads,
        scratch_shapes=[
            pltpu.VMEM((width, width), F32),
            pltpu.VMEM((slots, width), BF),
            pltpu.VMEM((slots, width), BF),
            pltpu.SemaphoreType.DMA((2,)),
            *spread_sems(spreads, blocks),
        ],
        compiler_params=params(collective_id=5, has_side_effects=True),
        cost_estimate=NO_COST,
    )(slot, expert, gate, probs, h, c, o, e_out, du, wo, wr, gain, *sent)


def last_kernel(
    x_ref, dh_ref, dq_ref, dk_ref, dv_ref, wq_ref, wk_ref, wv_ref, gain_ref,
    grad_ref, sums_ref, gain_sum, q_sum, k_sum, v_sum,
):
    step = pl.program_id(0)
    width = x_ref.shape[1]

    @pl.when(step == 0)
    def _():
        for total in (q_sum, k_sum, v_sum, gain_sum):
            total[...] = jnp.zeros_like(total)

    rows = x_ref[...].astype(F32)
    inv = lax.rsqrt(jnp.mean(rows * rows, axis=-1, keepdims=True) + EPSILON)
    unit = rows * inv
    gain = gain_ref[...]
    normed_t = (unit * gain).astype(BF).T
    normed_grad = None
    for grad_ref_in, weight_ref, total in (
        (dq_ref, wq_ref, q_sum),
        (dk_ref, wk_ref, k_sum),
        (dv_ref, wv_ref, v_sum),
    ):
        grad = grad_ref_in[...]
        total[...] += mm(normed_t, grad)
        term = mm_nt(grad, weight_ref[...])
        normed_grad = term if normed_grad is None else normed_grad + term
    unit_grad = normed_grad * gain
    grad_ref[...] = dh_ref[...] + inv * (
        unit_grad - unit * jnp.mean(unit_grad * unit, axis=-1, keepdims=True)
    )
    gain_sum[...] += jnp.sum(normed_grad * unit, axis=0, keepdims=True)

    @pl.when(step == pl.num_programs(0) - 1)
    def _():
        for which, total in enumerate((q_sum, k_sum, v_sum)):
            sums_ref[which * width : (which + 1) * width, :] = total[...].astype(BF)


def last(x, dh, dq, dk, dv, wq, wk, wv, gain):
    tokens, width = x.shape
    size = 512
    rows = pl.BlockSpec((size, width), lambda t: (t, 0))
    square = pl.BlockSpec((width, width), lambda t: (0, 0))
    one = pl.BlockSpec((1, width), lambda t: (0, 0))
    return pl.pallas_call(
        last_kernel,
        grid=(tokens // size,),
        in_specs=[rows] * 5 + [square] * 3 + [one],
        out_specs=[rows, pl.BlockSpec((3 * width, width), lambda t: (0, 0)), one],
        out_shape=[
            jax.ShapeDtypeStruct((tokens, width), F32),
            jax.ShapeDtypeStruct((3 * width, width), BF),
            jax.ShapeDtypeStruct((1, width), F32),
        ],
        scratch_shapes=[pltpu.VMEM((width, width), F32)] * 3,
        compiler_params=params(),
        cost_estimate=NO_COST,
    )(x, dh, dq, dk, dv, wq, wk, wv, gain)


def per_device(
    tokens,
    w_query,
    w_key,
    w_value,
    w_output,
    norm_attn,
    norm_ffn,
    relative_bias_table,
    w_router,
    w_in,
    w_out,
    expert_index,
    priority,
    cotangent,
):
    tok_rows, width = tokens.shape
    local = w_in.shape[0]
    exp_n, dp_n = lax.axis_size("exp"), lax.axis_size("dp")
    exp_me, dp_me = lax.axis_index("exp"), lax.axis_index("dp")
    all_experts = local * exp_n
    capacity = (5 * tok_rows + 4 * all_experts - 1) // (4 * all_experts)
    padded = (capacity + 1 + 15) // 16 * 16
    block = local * padded
    buckets = relative_bias_table.shape[0]

    chosen = expert_index[:, 0]
    order = priority[0]
    ahead = (chosen[:, None] == chosen[None, :]) & (order[None, :] < order[:, None])
    rank = jnp.sum(ahead.astype(jnp.int32), axis=1)
    place = ((chosen // local) ^ exp_me) * block + (chosen % local) * padded + rank
    slots = jnp.where(rank < capacity, place, -1)
    slot_row = slots[None, :]
    half = local // 2
    group = dp_me % 2
    inside = chosen % local
    grouped = ((inside // half + group) % 2 * exp_n + place // block) * half + inside % half
    c_row = jnp.where(rank < capacity, grouped * padded + rank, -1)[None, :]

    def to_dp(rows, step):
        return lax.ppermute(rows, "dp", [(i, i ^ step) for i in range(dp_n)])

    def over_dp(mine, other):
        return [mine] + [to_dp(other if step % 2 else mine, step) for step in range(1, dp_n)]

    lines = jnp.dot(
        relative_bias_table.T, diagonal_onehot(buckets).T, precision=FULL_PRECISION
    ).reshape(HEADS, 4, TILE)
    lines = jnp.concatenate([lines, jnp.zeros_like(lines)], axis=1)
    gain_attn, gain_ffn = norm_attn[None, :], norm_ffn[None, :]
    q, k, v = qkv(tokens, gain_attn, w_query, w_key, w_value)
    c_sent = [
        part.reshape(exp_n, half, padded, width)
        for part in dispatch_by_group(c_row, cotangent, exp_n * half * padded)
    ]
    c_far = over_dp(*c_sent)[1:]
    context, lse, c_rows = attention(lines, c_sent, q, k, v)
    c_rows = c_rows.reshape(local, exp_n * padded, width)
    mixed, u, probs, gate, gate_row = router(
        context, tokens, w_output, gain_ffn, w_router, expert_index
    )
    sent = dispatch(slot_row, u, exp_n, block, gate=(gate_row, local, capacity, padded))
    u_rows, e_back, d_back = expert_pass(
        sent.reshape(exp_n, local, padded, width), c_rows, w_in, w_out
    )
    mine, other = u_rows[:half], u_rows[half:]
    mine[0], other[0], c_far[0] = lax.optimization_barrier((mine[0], other[0], c_far[0]))
    u_all = [over_dp(mine[0], other[0])]
    for expert in range(1, half):
        e_back, mine[expert], other[expert], *c_far[1:] = lax.optimization_barrier(
            (e_back, mine[expert], other[expert], *c_far[1:])
        )
        u_all.append([mine[expert], None] + [
            to_dp(other[expert] if step % 2 else mine[expert], step) for step in range(2, dp_n)
        ])
    e_back, d_back = e_back.reshape(-1, width), d_back.reshape(-1, width)
    mixed_out, mixed_grad, context_grad, output_part, router_part, norm_ffn_part, *c_early = combine(
        slot_row, expert_index, gate, probs, mixed, cotangent, context,
        e_back, d_back, w_output, w_router, gain_ffn, c_far,
    )
    for expert in range(1, half):
        context_grad, *u_all[0], other[expert] = lax.optimization_barrier(
            (context_grad, *u_all[0], other[expert])
        )
        u_all[expert][1] = to_dp(other[expert], 1)
    size = w_in.shape[2] // dp_n
    rows = exp_n * padded
    c_early = [part.reshape(rows, width) for part in c_early]
    c_spread = [c_early[at : at + dp_n - 1] for at in range(0, len(c_early), dp_n - 1)]

    def for_partner(expert):
        where = jnp.stack([group * half + expert, dp_me // 2 * 2 + 1 - group]).astype(jnp.int32)
        return weight_grads(
            where, u_all[expert], c_rows, c_spread[expert], w_in, w_out, size, capacity, padded
        )

    got = []
    for expert in range(half - 1):
        context_grad, *far = lax.optimization_barrier((context_grad, *for_partner(expert)))
        got += [to_dp(array, 1) for array in far]
    query_grad, key_grad, value_grad, sums, *c_late = attention_back(
        lines, q, k, v, context_grad, lse, c_far
    )
    c_spread.append([part.reshape(rows, width) for part in c_late])
    query_grad, far_in, far_out = lax.optimization_barrier((query_grad, *for_partner(half - 1)))
    table_part = jnp.dot(
        diagonal_onehot(buckets).T,
        sums[:, :4].reshape(HEADS, 4 * TILE).T,
        precision=FULL_PRECISION,
    )
    grad_tokens, qkv_part, norm_attn_part = last(
        tokens, mixed_grad, query_grad, key_grad, value_grad, w_query, w_key, w_value, gain_attn
    )

    table_line = jnp.pad(table_part.reshape(1, -1), ((0, 0), (0, width - table_part.size)))
    small = jnp.concatenate([router_part, norm_attn_part, norm_ffn_part, table_line], axis=0)
    small = jnp.pad(small, ((0, -small.shape[0] % 8), (0, 0)))
    own_in, own_out, came_in, came_out, dense, total = tail(
        u_all, c_rows, c_spread, w_in, w_out, far_in, far_out, size, output_part, qkv_part, small, capacity, padded, exp_n
    )
    experts = jnp.arange(local, dtype=jnp.int32)
    grad_in, grad_out, *dense_grads = finish(
        jnp.where(group == 0, experts, (experts + half) % local),
        own_in,
        own_out,
        got[0::2] + [came_in],
        got[1::2] + [came_out],
        dense,
    )
    return (
        mixed_out,
        grad_tokens,
        *dense_grads,
        total[all_experts],
        total[all_experts + 1],
        total[all_experts + 2, : table_part.size].reshape(table_part.shape),
        total[:all_experts].T,
        grad_in,
        grad_out,
    )


def solution(mesh):
    return jax.shard_map(
        per_device,
        mesh=mesh,
        in_specs=(
            P(("exp", "dp"), None),
            P(),
            P(),
            P(),
            P(),
            P(),
            P(),
            P(),
            P(),
            P("exp", None, None),
            P("exp", None, None),
            P(("exp", "dp"), None),
            P(("exp", "dp"), None),
            P(("exp", "dp"), None),
        ),
        out_specs=(
            P(("exp", "dp"), None),
            P(("exp", "dp"), None),
            P(),
            P(),
            P(),
            P(),
            P(),
            P(),
            P(),
            P(),
            P("exp", None, "dp"),
            P("exp", "dp", None),
        ),
        check_vma=False,
    )
```
